32 devices in a mesh: dp: 8 (over z, x), mp: 4 (over y, core).
Axes of the slice: x: 2, y: 2, z: 4, core: 2. Of those that a mesh axis runs over, the one named last changes fastest.
Arguments:
- tokens: bfloat16 [8192, 768], P(('dp', 'mp')), may hold values from -6 to 6
- cotangent: float32 [8192, 768], P(('dp', 'mp')), may hold values from -6 to 6
- lengths: int32 [8, 8], P('dp'), may hold values from 1 to 896, 1024 in all within a row
- key_mask: int32 [8192], P('dp'), may hold values 0 or 1
- qkv_weight: float32 [2, 768, 2304], P(None, 'dp'), may hold values from -0.21875 to 0.21875
- qkv_first: float32 [2, 768, 2304], P(None, 'dp'), may hold values from -768 to 768
- qkv_second: float32 [2, 768, 2304], P(None, 'dp'), may hold values from 18432 to 73728
- qkv_average: float32 [2, 768, 2304], P(None, 'dp'), may hold values from -0.21875 to 0.21875
- out_weight: float32 [2, 768, 768], P(None, 'dp'), may hold values from -4 to 4
- out_first: float32 [2, 768, 768], P(None, 'dp'), may hold values from -48 to 48
- out_second: float32 [2, 768, 768], P(None, 'dp'), may hold values from 66.3552 to 265.4208
- out_average: float32 [2, 768, 768], P(None, 'dp'), may hold values from -4 to 4
- gate_up_weight: float32 [2, 768, 2, 3072], P(None, 'dp', None, 'mp'), may hold values from -0.21875 to 0.21875
- gate_up_first: float32 [2, 768, 2, 3072], P(None, 'dp', None, 'mp'), may hold values from -160 to 160
- gate_up_second: float32 [2, 768, 2, 3072], P(None, 'dp', None, 'mp'), may hold values from 737.28 to 2949.12
- gate_up_average: float32 [2, 768, 2, 3072], P(None, 'dp', None, 'mp'), may hold values from -0.21875 to 0.21875
- down_weight: float32 [2, 768, 3072], P(None, 'dp', 'mp'), may hold values from -0.109375 to 0.109375
- down_first: float32 [2, 768, 3072], P(None, 'dp', 'mp'), may hold values from -448 to 448
- down_second: float32 [2, 768, 3072], P(None, 'dp', 'mp'), may hold values from 5242.88 to 20971.52
- down_average: float32 [2, 768, 3072], P(None, 'dp', 'mp'), may hold values from -0.109375 to 0.109375
- norm_gain: float32 [2, 2, 768], P(None, None, 'dp'), may hold values from 0.5 to 1.5
- gain_first: float32 [2, 2, 768], P(None, None, 'dp'), may hold values from -768 to 768
- gain_second: float32 [2, 2, 768], P(None, None, 'dp'), may hold values from 18432 to 73728
- gain_average: float32 [2, 2, 768], P(None, None, 'dp'), may hold values from 0.5 to 1.5
Outputs:
- activations: bfloat16 [8192, 768], P(('dp', 'mp'))
- input_grad: float32 [8192, 768], P(('dp', 'mp'))
- qkv_grad: float32 [2, 768, 2304], P(None, 'dp')
- qkv_first_new: float32 [2, 768, 2304], P(None, 'dp')
- qkv_second_new: float32 [2, 768, 2304], P(None, 'dp')
- qkv_new: float32 [2, 768, 2304], P(None, 'dp')
- qkv_average_new: float32 [2, 768, 2304], P(None, 'dp')
- out_grad: float32 [2, 768, 768], P(None, 'dp')
- out_first_new: float32 [2, 768, 768], P(None, 'dp')
- out_second_new: float32 [2, 768, 768], P(None, 'dp')
- out_new: float32 [2, 768, 768], P(None, 'dp')
- out_average_new: float32 [2, 768, 768], P(None, 'dp')
- gate_up_grad: float32 [2, 768, 2, 3072], P(None, 'dp', None, 'mp')
- gate_up_first_new: float32 [2, 768, 2, 3072], P(None, 'dp', None, 'mp')
- gate_up_second_new: float32 [2, 768, 2, 3072], P(None, 'dp', None, 'mp')
- gate_up_new: float32 [2, 768, 2, 3072], P(None, 'dp', None, 'mp')
- gate_up_average_new: float32 [2, 768, 2, 3072], P(None, 'dp', None, 'mp')
- down_grad: float32 [2, 768, 3072], P(None, 'dp', 'mp')
- down_first_new: float32 [2, 768, 3072], P(None, 'dp', 'mp')
- down_second_new: float32 [2, 768, 3072], P(None, 'dp', 'mp')
- down_new: float32 [2, 768, 3072], P(None, 'dp', 'mp')
- down_average_new: float32 [2, 768, 3072], P(None, 'dp', 'mp')
- gain_grad: float32 [2, 2, 768], P(None, None, 'dp')
- gain_first_new: float32 [2, 2, 768], P(None, None, 'dp')
- gain_second_new: float32 [2, 2, 768], P(None, None, 'dp')
- gain_new: float32 [2, 2, 768], P(None, None, 'dp')
- gain_average_new: float32 [2, 2, 768], P(None, None, 'dp')
The draws below stay inside these ranges and needn't reach their ends.
Inputs may be any that keep to these rules, and one draw needn't show every extreme that they name: Row p lists the lengths of the 8 documents of pack p in order; they sum to 1024.
All inputs are finite; a program needn't handle non-finite values. No bound on the sum of `key_mask` on one device may be relied on, other than what follows from the above.
Results may differ from the reference program's by a relative error of at most 0.03.
Values may be sent and summed in bfloat16 or wider, within the bound.
A program may use at most 192 MiB of HBM per device.

```python
import math
import jax
import jax.numpy as jnp
import numpy as np
from jax import lax

D = 768
HEADS = 12
HEAD_DIM = 64
FF = 3072
SEQ = 1024
DOCS = 8
LAYERS = 2
STEP = 10
PACKS = 8
TOKENS = 8192


def plant(entries, key, least, high):
    place = [jax.random.randint(jax.random.fold_in(key, axis), (), 0, length) for axis, length in enumerate(entries.shape)]
    widest = entries.shape.index(max(entries.shape))
    neighbour = place[:widest] + [(place[widest] + 1) % entries.shape[widest]] + place[widest + 1:]
    return entries.at[tuple(place)].set(least).at[tuple(neighbour)].set(high)


def levels(own_key, extent, split, smallest, largest):
    level = 1.0
    for dim, blocks in split:
        draws = jax.random.uniform(jax.random.fold_in(jax.random.fold_in(own_key, 6), dim), (blocks,), jnp.float32, smallest / len(split), largest / len(split))
        level = level * jnp.repeat(jnp.exp(draws), extent[dim] // blocks).reshape((-1,) + (1,) * (len(extent) - 1 - dim))
    return level


def profile(number_of, total, bound, skew):
    portions = [(1 << 20) // math.isqrt(rank ** skew) + 1 for rank in range(2, number_of + 1)]
    spare, holding = total - bound - (number_of - 1), [1] * (number_of - 1)
    while spare > 0:
        candidates = [i for i in range(number_of - 1) if holding[i] < bound]
        mass, left = sum([portions[i] for i in candidates]), spare
        for i in candidates:
            extra = min(bound - holding[i], max(1, left * portions[i] // mass), spare)
            holding[i] = holding[i] + extra
            spare = spare - extra
    return np.array([bound] + holding)


def uneven_parts(rng, number_of, total, limit, skew):
    if number_of == 2:
        one = jax.random.randint(rng, (), max(1, total - limit), min(limit, total - 1) + 1)
        return jnp.stack([one, total - one])
    tallies = jnp.asarray(profile(number_of, total, limit, skew), jnp.int32)
    twos = (number_of - 1) // 2
    source_of, sink = tallies[1:1 + 2 * twos:2], tallies[2:2 + 2 * twos:2]
    margin = jnp.minimum(source_of - 1, limit - sink)
    moved = jax.random.randint(jax.random.fold_in(rng, 1), (twos,), 0, 1 << 20) % (margin + 1)
    tallies = tallies.at[1:1 + 2 * twos:2].set(source_of - moved).at[2:2 + 2 * twos:2].set(sink + moved)
    return tallies[jax.random.permutation(jax.random.fold_in(rng, 2), number_of)]


def bell_draw(key, extent, scale, bound, shards=(), kind=jnp.bfloat16):
    factor_of = levels(key, extent, shards, -0.22, 0.18) if shards else 1.0
    entries = jax.random.normal(key, extent, jnp.float32) * scale * factor_of
    return jnp.minimum(jnp.maximum(entries, -bound), bound).astype(kind)


def setup_inputs(seed: int = 0) -> dict:
    key_list = jax.random.split(jax.random.key(seed), 25)
    tokens = bell_draw(key_list[0], (TOKENS, D), 1.0, 6.0, ((0, 32),))
    cotangent = bell_draw(key_list[1], (TOKENS, D), 1.0, 6.0, ((0, 32),), jnp.float32)
    lengths = jax.vmap(lambda own: uneven_parts(own, DOCS, SEQ, SEQ - SEQ // 8, 2))(jax.random.split(key_list[2], PACKS)).reshape((PACKS, DOCS)).astype(jnp.int32)
    key_mask = plant((jax.random.randint(key_list[3], (TOKENS,), 0, 8) < 7).astype(jnp.int32), jax.random.fold_in(key_list[3], 1), 0, 1)
    qkv_weight = bell_draw(key_list[4], (LAYERS, D, 3 * D), D ** -0.5, 0.21875, ((1, 8),), jnp.float32)
    qkv_first = bell_draw(key_list[5], (LAYERS, D, 3 * D), (1.5 * TOKENS ** 0.5), 768.0, ((1, 8),), jnp.float32)
    qkv_second = jnp.clip(jnp.exp(math.log(73728.0) - 1.3862944 * jax.random.uniform(key_list[6], (LAYERS, D, 3 * D), jnp.float32) ** levels(key_list[6], (LAYERS, D, 3 * D), ((1, 8),), -0.2, 0.2)), 18432.0, 73728.0)
    qkv_average = bell_draw(key_list[7], (LAYERS, D, 3 * D), D ** -0.5, 0.21875, ((1, 8),), jnp.float32)
    out_weight = bell_draw(key_list[8], (LAYERS, D, D), (3 * D // SEQ) ** -0.5, 4.0, ((1, 8),), jnp.float32)
    out_first = bell_draw(key_list[9], (LAYERS, D, D), (0.09 * TOKENS ** 0.5), 48.0, ((1, 8),), jnp.float32)
    out_second = jnp.clip(jnp.exp(math.log(265.4208) - 1.3862944 * jax.random.uniform(key_list[10], (LAYERS, D, D), jnp.float32) ** levels(key_list[10], (LAYERS, D, D), ((1, 8),), -0.2, 0.2)), 66.3552, 265.4208)
    out_average = bell_draw(key_list[11], (LAYERS, D, D), (3 * D // SEQ) ** -0.5, 4.0, ((1, 8),), jnp.float32)
    gate_up_weight = bell_draw(key_list[12], (LAYERS, D, 2, FF), D ** -0.5, 0.21875, ((1, 8), (3, 4)), jnp.float32)
    gate_up_first = bell_draw(key_list[13], (LAYERS, D, 2, FF), (0.3 * TOKENS ** 0.5), 160.0, ((1, 8), (3, 4)), jnp.float32)
    gate_up_second = jnp.clip(jnp.exp(math.log(2949.12) - 1.3862944 * jax.random.uniform(key_list[14], (LAYERS, D, 2, FF), jnp.float32) ** levels(key_list[14], (LAYERS, D, 2, FF), ((1, 8), (3, 4)), -0.2, 0.2)), 737.28, 2949.12)
    gate_up_average = bell_draw(key_list[15], (LAYERS, D, 2, FF), D ** -0.5, 0.21875, ((1, 8), (3, 4)), jnp.float32)
    down_weight = bell_draw(key_list[16], (LAYERS, D, FF), FF ** -0.5, 0.109375, ((1, 8), (2, 4)), jnp.float32)
    down_first = bell_draw(key_list[17], (LAYERS, D, FF), (0.8 * TOKENS ** 0.5), 448.0, ((1, 8), (2, 4)), jnp.float32)
    down_second = jnp.clip(jnp.exp(math.log(20971.52) - 1.3862944 * jax.random.uniform(key_list[18], (LAYERS, D, FF), jnp.float32) ** levels(key_list[18], (LAYERS, D, FF), ((1, 8), (2, 4)), -0.2, 0.2)), 5242.88, 20971.52)
    down_average = bell_draw(key_list[19], (LAYERS, D, FF), FF ** -0.5, 0.109375, ((1, 8), (2, 4)), jnp.float32)
    norm_gain = jnp.clip(1.0 + 0.1 * jax.random.normal(key_list[20], (LAYERS, 2, D), jnp.float32), 0.5, 1.5)
    gain_first = bell_draw(key_list[21], (LAYERS, 2, D), (1.5 * TOKENS ** 0.5), 768.0, ((2, 8),), jnp.float32)
    gain_second = jnp.clip(jnp.exp(math.log(73728.0) - 1.3862944 * jax.random.uniform(key_list[22], (LAYERS, 2, D), jnp.float32) ** levels(key_list[22], (LAYERS, 2, D), ((2, 8),), -0.2, 0.2)), 18432.0, 73728.0)
    gain_average = jnp.clip(1.0 + 0.1 * jax.random.normal(key_list[23], (LAYERS, 2, D), jnp.float32), 0.5, 1.5)
    return {"tokens": tokens, "cotangent": cotangent, "lengths": lengths, "key_mask": key_mask, "qkv_weight": qkv_weight, "qkv_first": qkv_first, "qkv_second": qkv_second, "qkv_average": qkv_average, "out_weight": out_weight, "out_first": out_first, "out_second": out_second, "out_average": out_average, "gate_up_weight": gate_up_weight, "gate_up_first": gate_up_first, "gate_up_second": gate_up_second, "gate_up_average": gate_up_average, "down_weight": down_weight, "down_first": down_first, "down_second": down_second, "down_average": down_average, "norm_gain": norm_gain, "gain_first": gain_first, "gain_second": gain_second, "gain_average": gain_average}


@jax.custom_vjp
def low(v):
    return lax.optimization_barrier(v.astype(jnp.bfloat16)).astype(jnp.float32)

@jax.custom_vjp
def low_back(v):
    return v

def low_keep(v):
    return (low(v), None)

def low_pass(kept, grad):
    return (grad,)

def back_keep(v):
    return (v, None)

def back_low(kept, grad):
    return (low(grad),)
low.defvjp(low_keep, low_pass)
low_back.defvjp(back_keep, back_low)
precise = lax.Precision.HIGHEST
rotary_base = 1000.0
norm_epsilon = 1e-05
masked_score = -1e+30
beta_first = 0.5
beta_second = 0.5
adam_epsilon = 1e-08
average_decay = 0.5

def both_round(value):
    return low_back(low(value))

def layer_norm(rows, gain):
    centered = rows - lax.optimization_barrier(jnp.mean(rows, axis=-1, keepdims=True))
    spread = lax.optimization_barrier(jnp.mean(centered * centered, axis=-1, keepdims=True))
    return centered * lax.rsqrt(spread + norm_epsilon) * gain

def pack_layout(length_row, mask_row):
    seq_len = mask_row.shape[0]
    doc_count = length_row.shape[0]
    ends = jnp.cumsum(length_row).astype(jnp.int32)
    starts = (ends - length_row).astype(jnp.int32)
    spots = jnp.arange(seq_len, dtype=jnp.int32)
    member = jnp.logical_and(spots[:, None] >= starts[None, :], spots[:, None] < ends[None, :])
    doc_number = lax.optimization_barrier(jnp.sum(jnp.where(member, jnp.arange(doc_count, dtype=jnp.int32)[None, :], 0), axis=1)).astype(jnp.int32)
    position = (spots - lax.optimization_barrier(jnp.sum(jnp.where(member, starts[None, :], 0), axis=1))).astype(jnp.int32)
    same_doc = doc_number[:, None] == doc_number[None, :]
    visible = jnp.logical_or(mask_row[None, :] == 1, spots[:, None] == spots[None, :])
    return (jnp.logical_and(same_doc, visible), position)

def rotary_tables(position):
    half = HEAD_DIM // 2
    freq = jnp.power(rotary_base, -2.0 * jnp.arange(half).astype(jnp.float32) / HEAD_DIM)
    angle = position.astype(jnp.float32)[..., None] * freq
    return (jnp.cos(angle), jnp.sin(angle))

def rotate(block, cos_rows, sin_rows):
    half = block.shape[-1] // 2
    front = block[..., :half]
    back_half = block[..., half:]
    cos_wide = cos_rows[..., None, :]
    sin_wide = sin_rows[..., None, :]
    return jnp.concatenate([front * cos_wide - back_half * sin_wide, back_half * cos_wide + front * sin_wide], axis=-1)

def pack_attention(parts):
    query, key_rows, value_rows, allowed = parts
    scale = HEAD_DIM ** (-0.5)

    def one_head(head_parts):
        head_query, head_keys, head_values = head_parts
        scores = low_back(jnp.dot(head_query, head_keys.T, precision=precise) * scale)
        scores = jnp.where(allowed, scores, masked_score)
        top = lax.optimization_barrier(jnp.max(scores, axis=1, keepdims=True))
        weights = jnp.exp(scores - top)
        probs = weights / lax.optimization_barrier(jnp.sum(weights, axis=1, keepdims=True))
        return jnp.dot(low(probs), head_values, precision=precise)
    return lax.map(jax.checkpoint(one_head), (query, key_rows, value_rows))

def one_layer(rows, qkv_layer, out_layer, gate_up_layer, down_layer, gain_pair, allowed, cos_rows, sin_rows):
    qkv_low = low(qkv_layer)
    out_low = low(out_layer)
    gate_up_low = low(gate_up_layer)
    down_low = low(down_layer)
    proj = low_back(jnp.dot(rows, qkv_low, precision=precise))
    proj = proj.reshape(PACKS, SEQ, 3, HEADS, HEAD_DIM)
    query = low(rotate(proj[:, :, 0], cos_rows, sin_rows)).transpose(0, 2, 1, 3)
    key_rows = low(rotate(proj[:, :, 1], cos_rows, sin_rows)).transpose(0, 2, 1, 3)
    value_rows = low(proj[:, :, 2]).transpose(0, 2, 1, 3)
    attended = lax.map(pack_attention, (query, key_rows, value_rows, allowed))
    attended = both_round(attended.transpose(0, 2, 1, 3).reshape(TOKENS, D))
    branch = low_back(jnp.dot(attended, out_low, precision=precise))
    first_out = layer_norm(rows + branch, gain_pair[0])
    first_low = low(first_out)
    gate = low_back(jnp.dot(first_low, gate_up_low[:, 0, :], precision=precise))
    upward = low_back(jnp.dot(first_low, gate_up_low[:, 1, :], precision=precise))
    hidden = low(jax.nn.silu(gate) * upward)
    ffn = low_back(jnp.dot(hidden, down_low.T, precision=precise))
    return low(layer_norm(first_out + ffn, gain_pair[1]))

def adamw(weight, first, second, average, gradient, rate, decay):
    first_new = beta_first * first + (1.0 - beta_first) * gradient
    second_new = beta_second * second + (1.0 - beta_second) * gradient * gradient
    first_hat = first_new / (1.0 - beta_first ** STEP)
    second_hat = second_new / (1.0 - beta_second ** STEP)
    weight_new = weight - rate * (first_hat / (jnp.sqrt(second_hat) + adam_epsilon) + decay * weight)
    average_new = average_decay * average + (1.0 - average_decay) * weight_new
    return (gradient, first_new, second_new, weight_new, average_new)

def reference(tokens, cotangent, lengths, key_mask, qkv_weight, qkv_first, qkv_second, qkv_average, out_weight, out_first, out_second, out_average, gate_up_weight, gate_up_first, gate_up_second, gate_up_average, down_weight, down_first, down_second, down_average, norm_gain, gain_first, gain_second, gain_average):
    allowed, position = jax.vmap(pack_layout)(lengths, key_mask.reshape(PACKS, SEQ))
    cos_rows, sin_rows = rotary_tables(position)

    def forward(rows, qkv_all, out_all, gate_up_all, down_all, gain_all):
        for layer in range(LAYERS):
            rows = one_layer(rows, qkv_all[layer], out_all[layer], gate_up_all[layer], down_all[layer], gain_all[layer], allowed, cos_rows, sin_rows)
        return rows
    result, pullback = jax.vjp(forward, tokens.astype(jnp.float32), qkv_weight, out_weight, gate_up_weight, down_weight, norm_gain)
    grads = pullback(cotangent.astype(jnp.float32))
    outputs = [result.astype(jnp.bfloat16), grads[0]]
    outputs.extend(adamw(qkv_weight, qkv_first, qkv_second, qkv_average, grads[1], 0.03, 0.01))
    outputs.extend(adamw(out_weight, out_first, out_second, out_average, grads[2], 0.5, 0.01))
    outputs.extend(adamw(gate_up_weight, gate_up_first, gate_up_second, gate_up_average, grads[3], 0.03, 0.01))
    outputs.extend(adamw(down_weight, down_first, down_second, down_average, grads[4], 0.02, 0.01))
    outputs.extend(adamw(norm_gain, gain_first, gain_second, gain_average, grads[5], 0.6, 0.0))
    return (outputs[0], outputs[1], outputs[2], outputs[3], outputs[4], outputs[5], outputs[6], outputs[7], outputs[8], outputs[9], outputs[10], outputs[11], outputs[12], outputs[13], outputs[14], outputs[15], outputs[16], outputs[17], outputs[18], outputs[19], outputs[20], outputs[21], outputs[22], outputs[23], outputs[24], outputs[25], outputs[26])
```

```python
import functools
import math

import jax
import jax.numpy as jnp
from jax import lax
from jax.experimental import pallas as pl
from jax.experimental.pallas import tpu as pltpu
from jax.sharding import PartitionSpec as P

HEADS = 12
HEAD_DIM = 64
LAYERS = 2
STEP = 10
GROUP = 4
OWN_HEADS = HEADS // GROUP
TILE = 2 * HEAD_DIM
PROJ = 5 * TILE

rotary_base = 1000.0
norm_epsilon = 1e-05
masked_score = -1e30
beta_first = 0.5
beta_second = 0.5
adam_epsilon = 1e-08
average_decay = 0.5
score_scale = HEAD_DIM ** (-0.5)
log2e = math.log2(math.e)

MESH = pl.DeviceIdType.MESH
ANY = pl.BlockSpec(memory_space=pl.ANY)
VMEM = pl.BlockSpec(memory_space=pltpu.VMEM)
f32 = jnp.float32
bf16 = jnp.bfloat16
VMEM_LIMIT = 127 * 2**19


def dot(a, b):
    return jnp.dot(a, b, preferred_element_type=f32)


def dot_nt(a, b):
    return lax.dot_general(a, b, (((1,), (1,)), ((), ())), preferred_element_type=f32)


def dot_tn(a, b):
    return lax.dot_general(a, b, (((0,), (0,)), ((), ())), preferred_element_type=f32)


def places():
    me = lax.axis_index("mp")
    core = lax.rem(me, 2)
    side = lax.div(me, 2)
    return me, me + 1 - 2 * core, me + 2 - 4 * side, 3 - me, core


def push(src, dst, sems, layer, number, who):
    return pltpu.make_async_remote_copy(
        src_ref=src,
        dst_ref=dst,
        send_sem=sems.at[0, layer, number],
        recv_sem=sems.at[1, layer, number],
        device_id={"mp": who},
        device_id_type=MESH,
    )


def greet(mate, across):
    barrier = pltpu.get_barrier_semaphore()
    for who in (mate, across):
        pl.semaphore_signal(barrier, inc=1, device_id={"mp": who}, device_id_type=MESH)
    pl.semaphore_wait(barrier, 2)


def rows_of(block, size, extent):
    return pl.ds(pl.multiple_of(block * size, size), extent)


def lane_iota(shape):
    return lax.broadcasted_iota(jnp.int32, shape, len(shape) - 1)


def half_masks():
    low = (lane_iota((1, TILE)) < HEAD_DIM).astype(f32)
    return low.astype(bf16), (1.0 - low).astype(bf16)


def turn(tile, cos_rows, sin_rows):
    lane = lane_iota(tile.shape) % HEAD_DIM
    half = HEAD_DIM // 2
    partner = jnp.where(
        lane < half, pltpu.roll(tile, TILE - half, 1), pltpu.roll(tile, half, 1)
    )
    return tile * cos_rows + partner * sin_rows


def write_bias(bias, doc_keys, doc_queries):
    seq = bias.shape[0]
    step = 128

    def body(i, carry):
        rows = rows_of(i, step, step)
        keys = doc_keys[rows, :][:, :1]
        same = keys == doc_queries[:1, :]
        spot = lax.broadcasted_iota(jnp.int32, (step, seq), 0) + i * step
        own = spot == lax.broadcasted_iota(jnp.int32, (step, seq), 1)
        bias[rows, :] = jnp.where(jnp.logical_or(same, own), 0.0, masked_score)
        return carry

    lax.fori_loop(0, seq // step, body, 0)


class Gather:
    def __init__(self, ref, layer, sems, first_sem, size, where):
        me, mate, across, far, core = where
        self.across, self.mate = [], []
        self.forward = []
        half = size // 2

        def piece(block, part):
            start = pl.multiple_of(block * size + part * half, half)
            return ref.at[layer, pl.ds(start, half)]

        for part in range(2):
            own = piece(me, part)
            theirs = piece(across, part)
            self.across.append(push(own, own, sems, layer, first_sem + part, across))
            self.mate.append(push(own, own, sems, layer, first_sem + 2 + part, mate))
            self.forward.append(push(theirs, theirs, sems, layer, first_sem + 4 + part, mate))

    def start(self):
        for copy in self.across + self.mate:
            copy.start()

    def wait_mate(self):
        for copy in self.mate:
            copy.wait_recv()

    def wait_across(self):
        for copy, onward in zip(self.across, self.forward):
            copy.wait_recv()
            onward.start()

    def wait_far(self):
        for copy in self.forward:
            copy.wait_recv()

    def finish(self):
        for copy in self.across + self.mate + self.forward:
            copy.wait_send()


class Scatter:
    def __init__(self, part, slot, got, layer, sems, first_sem, where):
        me, mate, across, far, core = where
        self.part, self.slot, self.got, self.layer = part, slot, got, layer
        self.far = push(part.at[slot, 0], got.at[layer, 0], sems, layer, first_sem, mate)
        self.over = push(part.at[slot, 1], got.at[layer, 1], sems, layer, first_sem + 1, across)
        self.near = push(part.at[slot, 2], got.at[layer, 2], sems, layer, first_sem + 2, mate)

    def send_far(self, block):
        self.part[self.slot, 0] = block.astype(bf16)
        self.far.start()

    def send_across(self, block):
        self.far.wait_recv()
        self.part[self.slot, 1] = (block + self.got[self.layer, 0].astype(f32)).astype(bf16)
        self.over.start()

    def send_mate(self, block):
        self.part[self.slot, 2] = block.astype(bf16)
        self.near.start()

    def total(self, block):
        self.near.wait_recv()
        self.over.wait_recv()
        return (
            block
            + self.got[self.layer, 1].astype(f32)
            + self.got[self.layer, 2].astype(f32)
        )

    def finish(self):
        for copy in (self.far, self.over, self.near):
            copy.wait_send()


def normed_rows(rows):
    centered = rows - jnp.mean(rows, axis=-1, keepdims=True)
    inverse = lax.rsqrt(jnp.mean(centered * centered, axis=-1, keepdims=True) + norm_epsilon)
    return centered * inverse, inverse


def forward_kernel(
    tok, wq_in, wo_in, wg_in, wd_in, gain, cos_rows, sin_rows, doc_keys, doc_queries,
    act_out, xf_out, qkv_out, lse_out, att_out, flow_out, gu_out, hid_out,
    n1_out, s1_out, n2_out, s2_out,
    wq, wo, wg, wd, xf, qkv, att, flow, gu, hid, bias, vt, k2, lse,
    n1, s1, n2, s2, first, act, part, got, sems, wsems, osems,
):
    where = places()
    me, mate, across, far, core = where
    size = tok.shape[0]
    seq = size * GROUP
    ff = hid.shape[2]
    weights = []
    for layer in range(LAYERS):
        for number, (source, target) in enumerate(((wq_in, wq), (wo_in, wo), (wg_in, wg), (wd_in, wd))):
            copy = pltpu.make_async_copy(source.at[layer], target.at[layer], wsems.at[layer, number])
            copy.start()
            weights.append(copy)
    xf[0, rows_of(me, size, size), :] = tok[...]
    greet(mate, across)
    pending = []
    stores = []

    def store(number, layer, source, target):
        copy = pltpu.make_async_copy(source.at[layer], target.at[layer], osems.at[layer, number])
        copy.start()
        stores.append(copy)

    row_gather = Gather(xf, 0, sems, 0, size, where)
    row_gather.start()
    write_bias(bias, doc_keys, doc_queries)
    low_mask, high_mask = half_masks()

    for layer in range(LAYERS):
        weights[4 * layer].wait()

        def project(block, layer=layer):
            rows = rows_of(block, size, size)
            proj = dot(xf[layer, rows, :], wq[layer])
            c, s = cos_rows[rows, :], sin_rows[rows, :]
            for tile in (0, 1, 3):
                piece = proj[:, tile * TILE:(tile + 1) * TILE]
                qkv[layer, rows, tile * TILE:(tile + 1) * TILE] = turn(piece, c, s).astype(bf16)
            for tile in (2, 4):
                piece = proj[:, tile * TILE:(tile + 1) * TILE]
                qkv[layer, rows, tile * TILE:(tile + 1) * TILE] = piece.astype(bf16)

        project(me)
        row_gather.wait_mate()
        project(mate)
        row_gather.wait_across()
        project(across)
        row_gather.wait_far()
        project(far)
        pending.append(row_gather)
        store(0, layer, xf, xf_out)
        store(1, layer, qkv, qkv_out)
        vt[0] = qkv[layer, :, 2 * TILE:3 * TILE].T
        vt[1] = qkv[layer, :, 4 * TILE:5 * TILE].T
        k2[...] = pltpu.roll(qkv[layer, :, 3 * TILE:4 * TILE].astype(f32), HEAD_DIM, 1).astype(bf16)

        sends = []
        forwards = []
        for head in range(OWN_HEADS):
            query_tile = (0, 0, 3)[head]
            mask = (low_mask, high_mask, low_mask)[head]

            def attend(i, carry, layer=layer, head=head, query_tile=query_tile, mask=mask):
                rows = rows_of(i, size, size)
                queries = qkv[layer, rows, query_tile * TILE:(query_tile + 1) * TILE] * mask
                keys = k2[...] if head == 2 else qkv[layer, :, TILE:2 * TILE]
                values = (vt.at[0, :HEAD_DIM], vt.at[0, HEAD_DIM:], vt.at[1, HEAD_DIM:])[head][...]
                scores = dot_nt(keys, queries) * (score_scale * log2e) + bias[:, rows]
                top = jnp.max(scores, axis=0, keepdims=True)
                probs = jnp.exp2(scores - top)
                total = jnp.sum(probs, axis=0, keepdims=True)
                result = dot(values, probs.astype(bf16)) / total
                spot = pl.ds(
                    pl.multiple_of(me * (OWN_HEADS * HEAD_DIM) + head * HEAD_DIM, HEAD_DIM), HEAD_DIM
                )
                att[layer, spot, rows] = result.astype(bf16)
                lse[layer, head:head + 1, rows] = top + jnp.log(total) * log2e
                return carry

            lax.fori_loop(0, seq // size, attend, 0)

            def features(block, head=head, layer=layer):
                start = block * (OWN_HEADS * HEAD_DIM) + head * HEAD_DIM
                return att.at[layer, pl.ds(pl.multiple_of(start, HEAD_DIM), HEAD_DIM)]

            own, theirs = features(me), features(across)
            to_across = push(own, own, sems, layer, 6 + head, across)
            to_mate = push(own, own, sems, layer, 9 + head, mate)
            onward = push(theirs, theirs, sems, layer, 12 + head, mate)
            to_across.start()
            to_mate.start()
            if head:
                sends[-2].wait_recv()
                forwards[-1].start()
            sends += [to_across, to_mate]
            forwards.append(onward)
        sends[-2].wait_recv()
        forwards[-1].start()
        for head in range(OWN_HEADS):
            sends[2 * head + 1].wait_recv()
            forwards[head].wait_recv()
        store(2, layer, lse, lse_out)
        store(3, layer, att, att_out)
        for number in range(1, 4):
            weights[4 * layer + number].wait()

        def feed(block, keep, layer=layer):
            rows = rows_of(block, size, size)
            branch = dot_tn(att[layer, :, rows], wo[layer])
            normed, inverse = normed_rows(xf[layer, rows, :].astype(f32) + branch)
            first_rows = normed * gain[layer, 0:1, :]
            if keep:
                n1[layer] = normed
                s1[layer] = jnp.broadcast_to(inverse, s1.shape[1:])
                first[...] = first_rows
            first_low = first_rows.astype(bf16)
            flow[layer, rows, :] = first_low
            gate_up = dot(first_low, wg[layer])
            gate, upward = gate_up[:, :ff], gate_up[:, ff:]
            gu[layer, rows, :] = gate_up.astype(bf16)
            hidden = (gate / (1.0 + jnp.exp(-gate)) * upward).astype(bf16)
            hid[layer, rows, :] = hidden
            return dot_nt(hidden, wd[layer])

        scatter = Scatter(part, layer, got, layer, sems, 15, where)
        scatter.send_far(feed(far, False))
        scatter.send_across(feed(across, False))
        scatter.send_mate(feed(mate, False))
        own_part = feed(me, True)
        store(4, layer, flow, flow_out)
        store(5, layer, gu, gu_out)
        store(6, layer, hid, hid_out)
        store(7, layer, n1, n1_out)
        store(8, layer, s1, s1_out)
        ffn = scatter.total(own_part)
        pending.append(scatter)
        normed, inverse = normed_rows(first[...] + ffn)
        n2[layer] = normed
        s2[layer] = jnp.broadcast_to(inverse, s2.shape[1:])
        result = (normed * gain[layer, 1:2, :]).astype(bf16)
        store(9, layer, n2, n2_out)
        store(10, layer, s2, s2_out)
        if layer + 1 < LAYERS:
            xf[layer + 1, rows_of(me, size, size), :] = result
            row_gather = Gather(xf, layer + 1, sems, 0, size, where)
            row_gather.start()
        else:
            act[...] = result
            copy = pltpu.make_async_copy(act, act_out, osems.at[0, 11])
            copy.start()
            stores.append(copy)
        for copy in sends + forwards:
            copy.wait_send()
    for item in pending:
        item.finish()
    for copy in stores:
        copy.wait()


def backward_kernel(
    cot, n1_in, s1_in, n2_in, s2_in, xf_in, qkv_in, lse_in, att_in, flow_in, gu_in, hid_in,
    wq_in, wo_in, wg_in, wd_in, gain, cos_rows, sin_rows, doc_keys, doc_queries,
    ig_out, gq_out, go_out, gg_out, gd_out, gain_out,
    n1, s1, n2, s2, xf, qkv, lse, att, flow, gu, hid, wq, wo, wg, wd,
    bias, dff, dbr, dgu, datt, dproj, dk, dv, dqt, kt, k2, grad, part, got,
    gq, go, gg, gd, sems, lsems, osems,
):
    where = places()
    me, mate, across, far, core = where
    size = cot.shape[0]
    seq = size * GROUP
    ff = hid.shape[1]
    feats = xf.shape[1]
    own_feats = OWN_HEADS * HEAD_DIM
    held = dict(
        n2=(n2_in, n2), s2=(s2_in, s2), wd=(wd_in, wd), gu=(gu_in, gu), wg=(wg_in, wg),
        hid=(hid_in, hid), n1=(n1_in, n1), s1=(s1_in, s1), flow=(flow_in, flow), wo=(wo_in, wo),
        qkv=(qkv_in, qkv), lse=(lse_in, lse), att=(att_in, att), wq=(wq_in, wq), xf=(xf_in, xf),
    )
    order = list(held)
    loads = {}

    def load(name, layer):
        if layer < 0:
            return
        source, target = held[name]
        copy = pltpu.make_async_copy(source.at[layer], target, lsems.at[order.index(name)])
        copy.start()
        loads[name] = copy

    for name in order:
        load(name, LAYERS - 1)
    greet(mate, across)
    write_bias(bias, doc_keys, doc_queries)
    low_mask, high_mask = half_masks()
    grad[...] = cot[...]
    pending = []
    scatters = []
    stores = {}

    def store(number, layer, source, target):
        copy = pltpu.make_async_copy(source, target.at[layer], osems.at[layer, number])
        copy.start()
        stores[number] = copy

    def stored(number):
        if number in stores:
            stores.pop(number).wait()

    for layer in range(LAYERS - 1, -1, -1):

        def norm_back(grad_rows, normed, inverse, row, layer=layer):
            gain_out[layer, row:row + 1, :] = jnp.sum(grad_rows * normed, axis=0, keepdims=True)
            scaled = grad_rows * gain[layer, row:row + 1, :]
            return (
                scaled
                - jnp.mean(scaled, axis=-1, keepdims=True)
                - normed * jnp.mean(scaled * normed, axis=-1, keepdims=True)
            ) * inverse

        loads["n2"].wait()
        loads["s2"].wait()
        dz = norm_back(grad[...], n2[...], s2[:, :1], 1)
        load("n2", layer - 1)
        load("s2", layer - 1)
        grad[...] = dz
        dff[layer, rows_of(me, size, size), :] = dz.astype(bf16)
        gather = Gather(dff, layer, sems, 0, size, where)
        gather.start()
        for name in ("wd", "gu", "wg"):
            loads[name].wait()

        def feed_back(block, layer=layer):
            rows = rows_of(block, size, size)
            grad_hidden = dot(dff[layer, rows, :], wd[...])
            gate = gu[rows, :ff].astype(f32)
            upward = gu[rows, ff:].astype(f32)
            sigma = 1.0 / (1.0 + jnp.exp(-gate))
            up_grad = grad_hidden * gate * sigma
            gate_grad = grad_hidden * upward * sigma * (1.0 + gate * (1.0 - sigma))
            dgu[rows, :ff] = gate_grad.astype(bf16)
            dgu[rows, ff:] = up_grad.astype(bf16)
            return dot_nt(dgu[rows, :], wg[...])

        if len(scatters) > 1:
            scatters[-2].finish()
        scatter = Scatter(part, 0, got, 2 * layer, sems, 6, where)
        scatters.append(scatter)
        own_part = feed_back(me)
        gather.wait_mate()
        scatter.send_mate(feed_back(mate))
        gather.wait_across()
        across_part = feed_back(across)
        gather.wait_far()
        scatter.send_far(feed_back(far))
        pending.append(gather)
        scatter.send_across(across_part)
        load("gu", layer - 1)
        load("wd", layer - 1)
        load("wg", layer - 1)
        loads["hid"].wait()

        stored(3)

        def down_weight(i, carry, layer=layer):
            cols = rows_of(i, 256, 256)
            gd[cols, :] = dot_tn(dff[layer, :, cols], hid[...]).astype(bf16)
            return carry

        lax.fori_loop(0, feats // 256, down_weight, 0)
        store(3, layer, gd, gd_out)
        load("hid", layer - 1)

        dfirst = grad[...] + scatter.total(own_part)
        loads["n1"].wait()
        loads["s1"].wait()
        dr = norm_back(dfirst, n1[...], s1[:, :1], 0)
        load("n1", layer - 1)
        load("s1", layer - 1)
        grad[...] = dr
        dbr[layer, rows_of(me, size, size), :] = dr.astype(bf16)
        gather = Gather(dbr, layer, sems, 9, size, where)
        gather.start()
        loads["flow"].wait()

        stored(2)

        def gate_up_weight(i, carry, layer=layer):
            cols = rows_of(i, 256, 256)
            gg[cols, :] = dot_tn(flow[:, cols], dgu[...]).astype(bf16)
            return carry

        lax.fori_loop(0, feats // 256, gate_up_weight, 0)
        store(2, layer, gg, gg_out)
        load("flow", layer - 1)

        loads["wo"].wait()

        def att_back(block, layer=layer):
            rows = rows_of(block, size, size)
            for tile, start in enumerate((0, HEAD_DIM)):
                spot = pl.ds(pl.multiple_of(me * own_feats + start, HEAD_DIM), TILE)
                datt[rows, tile * TILE:(tile + 1) * TILE] = dot_nt(
                    dbr[layer, rows, :], wo[spot, :]
                ).astype(bf16)

        att_back(me)
        gather.wait_mate()
        att_back(mate)
        gather.wait_across()
        att_back(across)
        gather.wait_far()
        att_back(far)
        pending.append(gather)
        load("wo", layer - 1)

        loads["qkv"].wait()
        loads["lse"].wait()
        kt[0] = qkv[:, TILE:2 * TILE].T
        kt[1] = qkv[:, 3 * TILE:4 * TILE].T
        k2[...] = pltpu.roll(qkv[:, 3 * TILE:4 * TILE].astype(f32), HEAD_DIM, 1).astype(bf16)
        dk[...] = jnp.zeros_like(dk)
        dv[...] = jnp.zeros_like(dv)
        for head in range(OWN_HEADS):
            tile = head // 2
            query_tile = (0, 0, 3)[head]
            value_tile = (2, 2, 4)[head]
            query_mask = (low_mask, high_mask, low_mask)[head]
            value_mask = (low_mask, high_mask, high_mask)[head]

            def attend(i, carry, head=head, tile=tile, query_tile=query_tile, value_tile=value_tile,
                       query_mask=query_mask, value_mask=value_mask):
                rows = rows_of(i, size, size)
                queries = qkv[rows, query_tile * TILE:(query_tile + 1) * TILE] * query_mask
                keys = k2[...] if head == 2 else qkv[:, TILE:2 * TILE]
                scores = dot_nt(keys, queries) * (score_scale * log2e) + bias[:, rows]
                probs = jnp.exp2(scores - lse[head:head + 1, rows])
                outs = datt[rows, tile * TILE:(tile + 1) * TILE] * value_mask
                grad_probs = dot_nt(qkv[:, value_tile * TILE:(value_tile + 1) * TILE], outs)
                delta = jnp.sum(probs * grad_probs, axis=0, keepdims=True)
                grad_scores = (probs * (grad_probs - delta)).astype(bf16)
                dv[tile] = dv[tile] + dot(probs.astype(bf16), outs)
                dk[tile] = dk[tile] + dot(grad_scores, queries)
                keys_t = (kt.at[0, :HEAD_DIM], kt.at[0, HEAD_DIM:], kt.at[1, HEAD_DIM:])[head][...]
                spot = (0, HEAD_DIM, 0)[head]
                dqt[tile, spot:spot + HEAD_DIM, rows] = dot(keys_t, grad_scores)
                return carry

            lax.fori_loop(0, seq // size, attend, 0)

        def unrotate(i, carry):
            rows = rows_of(i, size, size)
            c, s = cos_rows[rows, :], -sin_rows[rows, :]
            dproj[rows, :TILE] = turn(dqt[0, :, rows].T * score_scale, c, s).astype(bf16)
            dproj[rows, TILE:2 * TILE] = turn(dk[0, rows, :] * score_scale, c, s).astype(bf16)
            dproj[rows, 2 * TILE:3 * TILE] = dv[0, rows, :].astype(bf16)
            lower = lane_iota((size, TILE)) < HEAD_DIM
            mixed = jnp.where(lower, dqt[1, :, rows].T, pltpu.roll(dk[1, rows, :], HEAD_DIM, 1))
            dproj[rows, 3 * TILE:4 * TILE] = turn(mixed * score_scale, c, s).astype(bf16)
            dproj[rows, 4 * TILE:] = dv[1, rows, :].astype(bf16)
            return carry

        lax.fori_loop(0, seq // size, unrotate, 0)
        load("qkv", layer - 1)
        load("lse", layer - 1)
        loads["wq"].wait()

        def input_part(block):
            return dot_nt(dproj[rows_of(block, size, size), :], wq[...])

        if len(scatters) > 1:
            scatters[-2].finish()
        scatter = Scatter(part, 1, got, 2 * layer + 1, sems, 6, where)
        scatters.append(scatter)
        scatter.send_far(input_part(far))
        scatter.send_across(input_part(across))
        scatter.send_mate(input_part(mate))
        own_part = input_part(me)
        load("wq", layer - 1)
        loads["xf"].wait()

        stored(0)

        def qkv_weight(i, carry, layer=layer):
            cols = rows_of(i, 256, 256)
            gq[cols, :] = dot_tn(xf[:, cols], dproj[...]).astype(bf16)
            return carry

        lax.fori_loop(0, feats // 256, qkv_weight, 0)
        store(0, layer, gq, gq_out)
        load("xf", layer - 1)
        loads["att"].wait()

        stored(1)

        def out_weight(i, carry, layer=layer):
            rows = rows_of(i, 256, 256)
            half = feats // 2
            cols = pl.ds(pl.multiple_of(core * half, half), half)
            go[rows, :] = dot(att[rows, :], dbr[layer, :, cols]).astype(bf16)
            return carry

        lax.fori_loop(0, feats // 256, out_weight, 0)
        store(1, layer, go, go_out)
        load("att", layer - 1)
        grad[...] = grad[...] + scatter.total(own_part)
    copy = pltpu.make_async_copy(grad, ig_out, osems.at[0, 4])
    copy.start()
    copy.wait()
    for item in pending + scatters[-2:]:
        item.finish()
    for number in range(4):
        stored(number)


def pack_documents(length_row, mask_row):
    seq = mask_row.shape[0]
    ends = jnp.cumsum(length_row)
    spots = jnp.arange(seq, dtype=jnp.int32)
    past = spots[:, None] >= ends[None, :]
    number = jnp.sum(past.astype(jnp.int32), axis=1)
    starts = jnp.max(jnp.where(past, ends[None, :], 0), axis=1)
    position = spots - starts
    keys = jnp.where(mask_row == 1, number, -1)
    doc_keys = jnp.broadcast_to(keys[:, None], (seq, 128))
    doc_queries = jnp.broadcast_to(number[None, :], (8, seq))
    half = HEAD_DIM // 2
    freq = jnp.power(rotary_base, -2.0 * jnp.arange(half).astype(f32) / HEAD_DIM)
    angle = position.astype(f32)[:, None] * freq
    c, s = jnp.cos(angle), jnp.sin(angle)
    cos_rows = jnp.concatenate([c, c, c, c], axis=1)
    sin_rows = jnp.concatenate([-s, s, -s, s], axis=1)
    return cos_rows, sin_rows, doc_keys, doc_queries


def own_projection(weight, me):
    layers, rows, _ = weight.shape
    split = weight.reshape(layers, rows, 3, HEADS * HEAD_DIM)
    own = lax.dynamic_slice_in_dim(split, me * OWN_HEADS * HEAD_DIM, OWN_HEADS * HEAD_DIM, 3)
    own = own.astype(bf16)
    pairs = own[..., :TILE].reshape(layers, rows, 3 * TILE)
    last = own[..., TILE:]
    return jnp.concatenate(
        [pairs, last[:, :, 0], last[:, :, 1], jnp.zeros_like(last[:, :, 0]), last[:, :, 2]], axis=-1
    )


def whole_projection(grad):
    group, layers, rows, _ = grad.shape
    pairs = grad[..., :3 * TILE].reshape(group, layers, rows, 3, TILE)
    last = jnp.stack(
        [
            grad[..., 3 * TILE:3 * TILE + HEAD_DIM],
            grad[..., 3 * TILE + HEAD_DIM:4 * TILE],
            grad[..., 4 * TILE + HEAD_DIM:],
        ],
        axis=3,
    )
    full = jnp.concatenate([pairs, last], axis=-1)
    return full.transpose(1, 2, 3, 0, 4).reshape(layers, rows, 3 * HEADS * HEAD_DIM)


def run_forward(tokens, weights, gain, tables):
    size, feats = tokens.shape
    seq = size * GROUP
    ff = weights[3].shape[2]
    shapes = dict(
        act=((size, feats), bf16),
        xf=((LAYERS, seq, feats), bf16),
        qkv=((LAYERS, seq, PROJ), bf16),
        lse=((LAYERS, 8, seq), f32),
        att=((LAYERS, feats, seq), bf16),
        flow=((LAYERS, seq, feats), bf16),
        gu=((LAYERS, seq, 2 * ff), bf16),
        hid=((LAYERS, seq, ff), bf16),
        n1=((LAYERS, size, feats), f32),
        s1=((LAYERS, size, 128), f32),
        n2=((LAYERS, size, feats), f32),
        s2=((LAYERS, size, 128), f32),
    )
    held = {name: pltpu.VMEM(*shape) for name, shape in shapes.items()}
    scratch = [pltpu.VMEM(w.shape, bf16) for w in weights]
    scratch += [held[n] for n in ("xf", "qkv", "att", "flow", "gu", "hid")]
    scratch += [
        pltpu.VMEM((seq, seq), f32),
        pltpu.VMEM((2, TILE, seq), bf16),
        pltpu.VMEM((seq, TILE), bf16),
        held["lse"],
    ]
    scratch += [held[n] for n in ("n1", "s1", "n2", "s2")]
    scratch += [
        pltpu.VMEM((size, feats), f32),
        held["act"],
        pltpu.VMEM((LAYERS, 3, size, feats), bf16),
        pltpu.VMEM((LAYERS, 3, size, feats), bf16),
        pltpu.SemaphoreType.DMA((2, LAYERS, 18)),
        pltpu.SemaphoreType.DMA((LAYERS, 4)),
        pltpu.SemaphoreType.DMA((LAYERS, 12)),
    ]
    return pl.pallas_call(
        forward_kernel,
        out_shape=[jax.ShapeDtypeStruct(*shape) for shape in shapes.values()],
        in_specs=[VMEM] + [ANY] * 4 + [VMEM] * 5,
        out_specs=[ANY] * len(shapes),
        scratch_shapes=scratch,
        compiler_params=pltpu.CompilerParams(
            collective_id=0, has_side_effects=True, vmem_limit_bytes=VMEM_LIMIT
        ),
        cost_estimate=pl.CostEstimate(
            flops=12 * 10**9, bytes_accessed=60 * 10**6, transcendentals=10**7
        ),
        name="forward",
    )(tokens, *weights, gain, *tables)


def run_backward(cotangent, kept, weights, gain, tables):
    size, feats = cotangent.shape
    seq = size * GROUP
    xf, qkv, lse, att, flow, gu, hid, n1, s1, n2, s2 = kept
    ff = hid.shape[2]
    wq, wo, wg, wd = weights
    loaded = [n1, s1, n2, s2, xf, qkv, lse, att, flow, gu, hid, wq, wo, wg, wd]
    outs = [
        ((size, feats), f32),
        (wq.shape, bf16),
        ((LAYERS, feats, feats // 2), bf16),
        (wg.shape, bf16),
        (wd.shape, bf16),
        ((LAYERS, 2, feats), f32),
    ]
    scratch = [pltpu.VMEM(a.shape[1:], a.dtype) for a in loaded]
    scratch += [
        pltpu.VMEM((seq, seq), f32),
        pltpu.VMEM((LAYERS, seq, feats), bf16),
        pltpu.VMEM((LAYERS, seq, feats), bf16),
        pltpu.VMEM((seq, 2 * ff), bf16),
        pltpu.VMEM((seq, 2 * TILE), bf16),
        pltpu.VMEM((seq, PROJ), bf16),
        pltpu.VMEM((2, seq, TILE), f32),
        pltpu.VMEM((2, seq, TILE), f32),
        pltpu.VMEM((2, TILE, seq), f32),
        pltpu.VMEM((2, TILE, seq), bf16),
        pltpu.VMEM((seq, TILE), bf16),
        pltpu.VMEM((size, feats), f32),
        pltpu.VMEM((2, 3, size, feats), bf16),
        pltpu.VMEM((2 * LAYERS, 3, size, feats), bf16),
    ]
    scratch += [pltpu.VMEM(shape[1:], kind) for shape, kind in outs[1:5]]
    scratch += [
        pltpu.SemaphoreType.DMA((2, 2 * LAYERS, 15)),
        pltpu.SemaphoreType.DMA((len(loaded),)),
        pltpu.SemaphoreType.DMA((LAYERS, 5)),
    ]
    return pl.pallas_call(
        backward_kernel,
        out_shape=[jax.ShapeDtypeStruct(*shape) for shape in outs],
        in_specs=[VMEM] + [ANY] * 15 + [VMEM] * 5,
        out_specs=[ANY] * 5 + [VMEM],
        scratch_shapes=scratch,
        compiler_params=pltpu.CompilerParams(
            collective_id=1, has_side_effects=True, vmem_limit_bytes=VMEM_LIMIT
        ),
        cost_estimate=pl.CostEstimate(
            flops=24 * 10**9, bytes_accessed=60 * 10**6, transcendentals=10**7
        ),
        name="backward",
    )(cotangent, *loaded, gain, *tables)


def adamw(weight, first, second, average, gradient, rate, decay):
    first_new = beta_first * first + (1.0 - beta_first) * gradient
    second_new = beta_second * second + (1.0 - beta_second) * gradient * gradient
    first_hat = first_new / (1.0 - beta_first**STEP)
    second_hat = second_new / (1.0 - beta_second**STEP)
    weight_new = weight - rate * (
        first_hat / (jnp.sqrt(second_hat) + adam_epsilon) + decay * weight
    )
    average_new = average_decay * average + (1.0 - average_decay) * weight_new
    return (gradient, first_new, second_new, weight_new, average_new)


def shards(
    tokens,
    cotangent,
    lengths,
    key_mask,
    qkv_weight,
    qkv_first,
    qkv_second,
    qkv_average,
    out_weight,
    out_first,
    out_second,
    out_average,
    gate_up_weight,
    gate_up_first,
    gate_up_second,
    gate_up_average,
    down_weight,
    down_first,
    down_second,
    down_average,
    norm_gain,
    gain_first,
    gain_second,
    gain_average,
):
    me = lax.axis_index("mp")
    own = gate_up_weight.shape[1]
    ff = gate_up_weight.shape[3]
    gain = lax.all_gather(norm_gain, "dp", axis=2, tiled=True)
    tables = pack_documents(lengths[0], key_mask)
    owned = (
        own_projection(qkv_weight, me),
        out_weight.astype(bf16),
        gate_up_weight.reshape(LAYERS, own, 2 * ff).astype(bf16),
        down_weight.astype(bf16),
    )
    weights = [lax.all_gather(w, "dp", axis=1, tiled=True) for w in owned]
    act, *kept = run_forward(tokens, weights, gain, tables)
    input_grad, gq, go, gg, gd, gain_part = run_backward(cotangent, kept, weights, gain, tables)
    gq, go, gg, gd = [
        lax.psum_scatter(g, "dp", scatter_dimension=1, tiled=True) for g in (gq, go, gg, gd)
    ]
    qkv_grad = whole_projection(lax.all_gather(gq, "mp").astype(f32))
    go = lax.all_gather(go, "mp")
    out_grad = jnp.concatenate([go[0], go[1]], axis=-1).astype(f32)
    gate_up_grad = gg.reshape(LAYERS, own, 2, ff).astype(f32)
    down_grad = gd.astype(f32)
    gain_grad = lax.psum_scatter(
        lax.psum(gain_part, "mp"), "dp", scatter_dimension=2, tiled=True
    )
    results = [act, input_grad]
    results.extend(adamw(qkv_weight, qkv_first, qkv_second, qkv_average, qkv_grad, 0.03, 0.01))
    results.extend(adamw(out_weight, out_first, out_second, out_average, out_grad, 0.5, 0.01))
    results.extend(
        adamw(
            gate_up_weight, gate_up_first, gate_up_second, gate_up_average, gate_up_grad, 0.03, 0.01
        )
    )
    results.extend(
        adamw(down_weight, down_first, down_second, down_average, down_grad, 0.02, 0.01)
    )
    results.extend(adamw(norm_gain, gain_first, gain_second, gain_average, gain_grad, 0.6, 0.0))
    return tuple(results)


def solution(mesh):
    return jax.shard_map(
        shards,
        mesh=mesh,
        in_specs=(
            P(("dp", "mp"), None),
            P(("dp", "mp"), None),
            P("dp", None),
            P("dp"),
            P(None, "dp", None),
            P(None, "dp", None),
            P(None, "dp", None),
            P(None, "dp", None),
            P(None, "dp", None),
            P(None, "dp", None),
            P(None, "dp", None),
            P(None, "dp", None),
            P(None, "dp", None, "mp"),
            P(None, "dp", None, "mp"),
            P(None, "dp", None, "mp"),
            P(None, "dp", None, "mp"),
            P(None, "dp", "mp"),
            P(None, "dp", "mp"),
            P(None, "dp", "mp"),
            P(None, "dp", "mp"),
            P(None, None, "dp"),
            P(None, None, "dp"),
            P(None, None, "dp"),
            P(None, None, "dp"),
        ),
        out_specs=(
            P(("dp", "mp"), None),
            P(("dp", "mp"), None),
            P(None, "dp", None),
            P(None, "dp", None),
            P(None, "dp", None),
            P(None, "dp", None),
            P(None, "dp", None),
            P(None, "dp", None),
            P(None, "dp", None),
            P(None, "dp", None),
            P(None, "dp", None),
            P(None, "dp", None),
            P(None, "dp", None, "mp"),
            P(None, "dp", None, "mp"),
            P(None, "dp", None, "mp"),
            P(None, "dp", None, "mp"),
            P(None, "dp", None, "mp"),
            P(None, "dp", "mp"),
            P(None, "dp", "mp"),
            P(None, "dp", "mp"),
            P(None, "dp", "mp"),
            P(None, "dp", "mp"),
            P(None, None, "dp"),
            P(None, None, "dp"),
            P(None, None, "dp"),
            P(None, None, "dp"),
            P(None, None, "dp"),
        ),
        check_vma=False,
    )
```

```python
import functools
import math

import jax
import jax.numpy as jnp
from jax import lax
from jax.experimental import pallas as pl
from jax.experimental.pallas import tpu as pltpu
from jax.sharding import PartitionSpec as P

HEADS = 12
HEAD_DIM = 64
LAYERS = 2
STEP = 10
GROUP = 4
DEPTH = 4
OWN_HEADS = HEADS // GROUP
TILE = 2 * HEAD_DIM
PROJ = 5 * TILE

rotary_base = 1000.0
norm_epsilon = 1e-05
masked_score = -1e30
beta_first = 0.5
beta_second = 0.5
adam_epsilon = 1e-08
average_decay = 0.5
score_scale = HEAD_DIM ** (-0.5)
log2e = math.log2(math.e)

MESH = pl.DeviceIdType.MESH
ANY = pl.BlockSpec(memory_space=pl.ANY)
VMEM = pl.BlockSpec(memory_space=pltpu.VMEM)
f32 = jnp.float32
bf16 = jnp.bfloat16
VMEM_LIMIT = 127 * 2**19


def dot(a, b):
    return jnp.dot(a, b, preferred_element_type=f32)


def dot_nt(a, b):
    return lax.dot_general(a, b, (((1,), (1,)), ((), ())), preferred_element_type=f32)


def dot_tn(a, b):
    return lax.dot_general(a, b, (((0,), (0,)), ((), ())), preferred_element_type=f32)


def places():
    me = lax.axis_index("mp")
    core = lax.rem(me, 2)
    side = lax.div(me, 2)
    return me, me + 1 - 2 * core, me + 2 - 4 * side, 3 - me, core


def push(src, dst, sems, layer, number, who):
    return pltpu.make_async_remote_copy(
        src_ref=src,
        dst_ref=dst,
        send_sem=sems.at[0, layer, number],
        recv_sem=sems.at[1, layer, number],
        device_id={"mp": who},
        device_id_type=MESH,
    )


class Spread:
    def __init__(self, own):
        index = lax.axis_index("dp")
        self.own = own
        self.z, self.x = lax.div(index, 2), lax.rem(index, 2)

    def device(self, step):
        return 2 * lax.rem(self.z + step, DEPTH) + self.x

    def beside(self, step):
        return 2 * lax.rem(self.z + step, DEPTH) + 1 - self.x

    def rows(self, index):
        return pl.ds(pl.multiple_of(index * self.own, self.own), self.own)


def greet(mate, across, far=None, spread=None):
    barrier = pltpu.get_barrier_semaphore()
    packs = [mate, across] if far is None else [mate, across, far]
    for who in packs:
        pl.semaphore_signal(barrier, inc=1, device_id={"mp": who}, device_id_type=MESH)
    others = []
    if spread is not None:
        others = [spread.beside(0)] + [spread.device(step) for step in range(1, DEPTH)]
        for who in others:
            pl.semaphore_signal(barrier, inc=1, device_id={"dp": who}, device_id_type=MESH)
    pl.semaphore_wait(barrier, len(packs) + len(others))


def ship(src, dst, sems, piece, number, who):
    return pltpu.make_async_remote_copy(
        src_ref=src,
        dst_ref=dst,
        send_sem=sems.at[0, piece, number],
        recv_sem=sems.at[1, piece, number],
        device_id={"dp": who},
        device_id_type=MESH,
    )


class WeightGather:
    def __init__(self, source, target, layer, piece, sems, local, spread, cols=None):
        self.target, self.layer, self.cols = target, layer, cols
        self.piece, self.sems, self.spread = piece, sems, spread
        z, x = spread.z, spread.x
        own = source.at[layer] if cols is None else source.at[layer, :, cols]
        place = self.view(z, x)
        self.local = pltpu.make_async_copy(
            source.at[layer], target.at[layer, spread.rows(2 * z + x)], local
        )
        self.beside = self.send(own, place, 0, 0, 2 * z + 1 - x)
        self.up = self.send(own, place, 1, 1 + z, 2 * jnp.minimum(z + 1, DEPTH - 1) + x)
        self.down = self.send(own, place, 2, 1 + z, 2 * jnp.maximum(z - 1, 0) + x)
        self.hops = [(far, way) for far in range(1, DEPTH) for way in (-1, 1)]
        self.todo = list(self.hops)

    def view(self, z, x):
        rows = self.spread.rows(2 * z + x)
        if self.cols is None:
            return self.target.at[self.layer, rows]
        return self.target.at[self.layer, rows, self.cols]

    def send(self, src, dst, out, into, who):
        return pltpu.make_async_remote_copy(
            src_ref=src,
            dst_ref=dst,
            send_sem=self.sems.at[0, self.piece, out],
            recv_sem=self.sems.at[1, self.piece, into],
            device_id={"dp": who},
            device_id_type=MESH,
        )

    def start(self):
        self.local.start()
        pl.when(self.spread.z < DEPTH - 1)(self.up.start)
        pl.when(self.spread.z > 0)(self.down.start)
        self.beside.start()

    def hop(self, far, way):
        z, x = self.spread.z, self.spread.x
        source = jnp.clip(z + way * far, 0, DEPTH - 1)
        block = self.view(source, x)
        onward = jnp.clip(z - way, 0, DEPTH - 1)
        arrive = self.send(block, block, 3 + source, 1 + source, 2 * source + x)
        over = self.send(block, block, 3 + source, 1 + DEPTH + source, 2 * z + 1 - x)
        along = self.send(block, block, 3 + DEPTH + source, 1 + source, 2 * onward + x)
        comes = z >= far if way < 0 else z + far < DEPTH
        goes = z > 0 if way > 0 else z < DEPTH - 1
        return arrive, over, along, comes, jnp.logical_and(comes, goes)

    def serve(self, count=2 * DEPTH):
        while self.todo and count:
            count -= 1
            arrive, over, along, comes, goes = self.hop(*self.todo.pop(0))

            def receive():
                arrive.wait_recv()
                over.start()

            pl.when(comes)(receive)
            pl.when(goes)(along.start)

    def wait(self):
        self.serve()
        self.local.wait()
        self.beside.wait_recv()
        z, x = self.spread.z, self.spread.x
        for step in range(1, DEPTH):
            source = lax.rem(z + step, DEPTH)
            block = self.view(source, 1 - x)
            self.send(block, block, 3, 1 + DEPTH + source, 2 * z + 1 - x).wait_recv()

    def finish(self):
        self.beside.wait_send()
        pl.when(self.spread.z < DEPTH - 1)(self.up.wait_send)
        pl.when(self.spread.z > 0)(self.down.wait_send)
        for far, way in self.hops:
            arrive, over, along, comes, goes = self.hop(far, way)
            pl.when(comes)(over.wait_send)
            pl.when(goes)(along.wait_send)


class HalfGather(WeightGather):
    def __init__(self, source, target, layer, piece, sems, local, spread, half, pack_sems, where):
        me, mate, across, far, core = where
        cols = pl.ds(pl.multiple_of(core * half, half), half)
        super().__init__(source, target, layer, piece, sems, local, spread, cols)
        self.swap = []
        for step in range(DEPTH):
            z = lax.rem(spread.z + step, DEPTH)
            for number, x in enumerate((spread.x, 1 - spread.x)):
                if step or number:
                    block = self.view(z, x)
                    self.swap.append(
                        push(block, block, pack_sems, layer, 2 * step + number - 1, mate)
                    )

    def share(self):
        super().wait()
        for copy in self.swap:
            copy.start()

    def wait(self):
        for copy in self.swap:
            copy.wait_recv()

    def finish(self):
        super().finish()
        for copy in self.swap:
            copy.wait_send()


class WeightSum:
    def __init__(self, grad, near, apart, piece, sems, spread, credits, again, more, total):
        self.grad, self.near, self.apart, self.spread = grad, near, apart, spread
        self.near_credit, self.apart_credit = credits
        self.again, self.more = again, more
        self.sum = total
        self.beside = [
            ship(grad.at[spread.rows(spread.beside(step))], near.at[step], sems, piece, step,
                 spread.beside(0))
            for step in range(DEPTH)
        ]
        self.along = [
            ship(grad.at[spread.rows(spread.device(step))], apart.at[step - 1], sems, piece,
                 DEPTH - 1 + step, spread.device(step))
            for step in range(1, DEPTH)
        ]

    def start(self):
        if self.again:
            pl.semaphore_wait(self.near_credit, 1)
        for copy in self.beside[1:] + self.beside[:1]:
            copy.start()

    def credit(self, sem, who):
        pl.semaphore_signal(sem, inc=1, device_id={"dp": who}, device_id_type=MESH)

    def add(self):
        if self.again:
            pl.semaphore_wait(self.apart_credit, DEPTH - 1)
        for step in range(1, DEPTH):
            self.beside[step].wait_recv()
            rows = self.spread.rows(self.spread.device(step))
            self.grad[rows, :] = (
                self.grad[rows, :].astype(f32) + self.near[step].astype(f32)
            ).astype(bf16)
            self.along[step - 1].start()
        self.beside[0].wait_recv()
        rows = self.spread.rows(self.spread.device(0))
        self.sum[...] = self.grad[rows, :].astype(f32) + self.near[0].astype(f32)
        if self.more:
            self.credit(self.near_credit, self.spread.beside(0))

    def total(self):
        for copy in self.along:
            copy.wait_recv()
        result = self.sum[...]
        for step in range(DEPTH - 1):
            result = result + self.apart[step].astype(f32)
        if self.more:
            for step in range(1, DEPTH):
                self.credit(self.apart_credit, self.spread.device(step))
        return result

    def finish(self):
        for copy in self.beside + self.along:
            copy.wait_send()


def rows_of(block, size, extent):
    return pl.ds(pl.multiple_of(block * size, size), extent)


def lane_iota(shape):
    return lax.broadcasted_iota(jnp.int32, shape, len(shape) - 1)


def half_masks():
    low = (lane_iota((1, TILE)) < HEAD_DIM).astype(f32)
    return low.astype(bf16), (1.0 - low).astype(bf16)


def turn(tile, cos_rows, sin_rows):
    lane = lane_iota(tile.shape) % HEAD_DIM
    half = HEAD_DIM // 2
    partner = jnp.where(
        lane < half, pltpu.roll(tile, TILE - half, 1), pltpu.roll(tile, half, 1)
    )
    return tile * cos_rows + partner * sin_rows


def write_bias(bias, doc_keys, doc_queries):
    seq = bias.shape[0]
    step = 128

    def body(i, carry):
        rows = rows_of(i, step, step)
        keys = doc_keys[rows, :][:, :1]
        same = keys == doc_queries[:1, :]
        spot = lax.broadcasted_iota(jnp.int32, (step, seq), 0) + i * step
        own = spot == lax.broadcasted_iota(jnp.int32, (step, seq), 1)
        bias[rows, :] = jnp.where(jnp.logical_or(same, own), 0.0, masked_score)
        return carry

    lax.fori_loop(0, seq // step, body, 0)


class Gather:
    def __init__(self, ref, slot, layer, sems, first_sem, size, where):
        me, mate, across, far, core = where
        self.across, self.mate = [], []
        self.forward = []
        half = size // 2

        def piece(block, part):
            start = pl.multiple_of(block * size + part * half, half)
            return ref.at[slot, pl.ds(start, half)]

        for part in range(2):
            own = piece(me, part)
            theirs = piece(across, part)
            self.across.append(push(own, own, sems, layer, first_sem + part, across))
            self.mate.append(push(own, own, sems, layer, first_sem + 2 + part, mate))
            self.forward.append(push(theirs, theirs, sems, layer, first_sem + 4 + part, mate))

    def start(self):
        for copy in self.across + self.mate:
            copy.start()

    def wait_mate(self):
        for copy in self.mate:
            copy.wait_recv()

    def wait_across(self):
        for copy, onward in zip(self.across, self.forward):
            copy.wait_recv()
            onward.start()

    def wait_far(self):
        for copy in self.forward:
            copy.wait_recv()

    def finish(self):
        for copy in self.across + self.mate + self.forward:
            copy.wait_send()


class Share:
    def __init__(self, ref, layer, sems, first_sem, where):
        me, mate, across, far, core = where
        own, theirs = ref.at[layer, me], ref.at[layer, across]
        self.ref, self.layer, self.me = ref, layer, me
        self.over = push(own, own, sems, layer, first_sem, across)
        self.near = push(own, own, sems, layer, first_sem + 1, mate)
        self.onward = push(theirs, theirs, sems, layer, first_sem + 2, mate)

    def start(self, block):
        self.ref[self.layer, self.me] = block
        self.over.start()
        self.near.start()

    def serve(self):
        self.over.wait_recv()
        self.onward.start()

    def finish(self):
        self.near.wait_recv()
        self.onward.wait_recv()
        for copy in (self.over, self.near, self.onward):
            copy.wait_send()


class Scatter:
    def __init__(self, part, slot, got, layer, sems, first_sem, where):
        me, mate, across, far, core = where
        self.part, self.slot, self.got = part, slot, got
        self.far = push(part.at[slot, 0], got.at[slot, 0], sems, layer, first_sem, mate)
        self.over = push(part.at[slot, 1], got.at[slot, 1], sems, layer, first_sem + 1, across)
        self.near = push(part.at[slot, 2], got.at[slot, 2], sems, layer, first_sem + 2, mate)

    def send_far(self, block):
        self.part[self.slot, 0] = block.astype(bf16)
        self.far.start()

    def send_across(self, block):
        self.far.wait_recv()
        self.part[self.slot, 1] = (block + self.got[self.slot, 0].astype(f32)).astype(bf16)
        self.over.start()

    def send_mate(self, block):
        self.part[self.slot, 2] = block.astype(bf16)
        self.near.start()

    def total(self, block):
        self.near.wait_recv()
        self.over.wait_recv()
        return (
            block
            + self.got[self.slot, 1].astype(f32)
            + self.got[self.slot, 2].astype(f32)
        )

    def finish(self):
        for copy in (self.far, self.over, self.near):
            copy.wait_send()


def normed_rows(rows):
    centered = rows - jnp.mean(rows, axis=-1, keepdims=True)
    inverse = lax.rsqrt(jnp.mean(centered * centered, axis=-1, keepdims=True) + norm_epsilon)
    return centered * inverse, inverse


def forward_kernel(
    spreading, tok, wq_in, wo_in, wg_in, wd_in, gain_in, cos_rows, sin_rows, doc_keys, doc_queries,
    act_out, xf_out, qkv_out, lse_out, att_out, flow_out, gu_out, hid_out,
    n1_out, s1_out, n2_out, s2_out, wq_out, wo_out, wg_out, wd_out, gain,
    wq, wo, wg, wd, xf, qkv, att, flow, gu, hid, bias, vt, k2, lse,
    n1, s1, n2, s2, first, act, part, got, sems, wsems, osems, dsems, ssems, gside, gdeep, gsems,
):
    where = places()
    me, mate, across, far, core = where
    weight_outs = (wq_out, wo_out, wg_out, wd_out)
    size = tok.shape[0]
    seq = size * GROUP
    ff = hid.shape[2]
    spread = Spread(wq_in.shape[1]) if spreading else None
    weights = []
    for layer in range(LAYERS):
        for number, (source, target) in enumerate(((wq_in, wq), (wo_in, wo), (wg_in, wg), (wd_in, wd))):
            local = wsems.at[layer, number]
            if not spreading:
                weights.append(pltpu.make_async_copy(source.at[layer], target.at[layer], local))
            elif number == 1:
                weights.append(
                    HalfGather(source, target, layer, 4 * layer + 1, dsems, local, spread,
                               wo.shape[2] // 2, ssems, where)
                )
            else:
                weights.append(
                    WeightGather(source, target, layer, 4 * layer + number, dsems, local, spread)
                )
    xf[0, rows_of(me, size, size), :] = tok[...]
    greet(mate, across, None, spread)
    gains = []
    if spreading:
        gdeep[spread.z] = gain_in[...]
        own = gdeep.at[spread.z]
        for step in range(1, DEPTH):
            gains.append(ship(own, own, gsems, 0, step, spread.device(step)))
            gains[-1].start()
    else:
        gain[...] = gain_in[...]
    for item in weights:
        item.start()

    def gain_stage(stage):
        if not spreading:
            return
        if stage == 0:
            for copy in gains:
                copy.wait_recv()
            gside[spread.x] = gdeep[0] + gdeep[1] + gdeep[2] + gdeep[3]
            own = gside.at[spread.x]
            gains.append(ship(own, own, gsems, 0, 0, spread.beside(0)))
            gains[-1].start()
        else:
            gains[-1].wait_recv()
            gain[...] = gside[0] + gside[1]
            for copy in gains:
                copy.wait_send()

    def serve(layer, number, count=2 * DEPTH):
        if spreading and layer < LAYERS:
            item = weights[4 * layer + number]
            if number == 1:
                item.share()
            else:
                item.serve(count)
    pending = []
    stores = []

    def store(number, layer, source, target):
        copy = pltpu.make_async_copy(source.at[layer], target.at[layer], osems.at[layer, number])
        copy.start()
        stores.append(copy)

    row_gather = Gather(xf, 0, 0, sems, 0, size, where)
    row_gather.start()
    write_bias(bias, doc_keys, doc_queries)
    low_mask, high_mask = half_masks()

    for layer in range(LAYERS):
        weights[4 * layer].wait()
        serve(layer, 1)
        if layer == 0:
            gain_stage(0)

        def project(block, layer=layer):
            rows = rows_of(block, size, size)
            proj = dot(xf[layer, rows, :], wq[layer])
            c, s = cos_rows[rows, :], sin_rows[rows, :]
            for tile in (0, 1, 3):
                piece = proj[:, tile * TILE:(tile + 1) * TILE]
                qkv[layer, rows, tile * TILE:(tile + 1) * TILE] = turn(piece, c, s).astype(bf16)
            for tile in (2, 4):
                piece = proj[:, tile * TILE:(tile + 1) * TILE]
                qkv[layer, rows, tile * TILE:(tile + 1) * TILE] = piece.astype(bf16)

        project(me)
        row_gather.wait_mate()
        project(mate)
        row_gather.wait_across()
        project(across)
        row_gather.wait_far()
        project(far)
        pending.append(row_gather)
        store(0, layer, xf, xf_out)
        store(1, layer, qkv, qkv_out)
        vt[0] = qkv[layer, :, 2 * TILE:3 * TILE].T
        vt[1] = qkv[layer, :, 4 * TILE:5 * TILE].T
        k2[...] = pltpu.roll(qkv[layer, :, 3 * TILE:4 * TILE].astype(f32), HEAD_DIM, 1).astype(bf16)

        sends = []
        forwards = []
        for head in range(OWN_HEADS):
            query_tile = (0, 0, 3)[head]
            mask = (low_mask, high_mask, low_mask)[head]

            def attend(i, carry, layer=layer, head=head, query_tile=query_tile, mask=mask):
                rows = rows_of(i, size, size)
                queries = qkv[layer, rows, query_tile * TILE:(query_tile + 1) * TILE] * mask
                keys = k2[...] if head == 2 else qkv[layer, :, TILE:2 * TILE]
                values = (vt.at[0, :HEAD_DIM], vt.at[0, HEAD_DIM:], vt.at[1, HEAD_DIM:])[head][...]
                scores = dot_nt(keys, queries) * (score_scale * log2e) + bias[:, rows]
                top = jnp.max(scores, axis=0, keepdims=True)
                probs = jnp.exp2(scores - top)
                total = jnp.sum(probs, axis=0, keepdims=True)
                result = dot(values, probs.astype(bf16)) / total
                spot = pl.ds(
                    pl.multiple_of(me * (OWN_HEADS * HEAD_DIM) + head * HEAD_DIM, HEAD_DIM), HEAD_DIM
                )
                att[layer, spot, rows] = result.astype(bf16)
                lse[layer, head:head + 1, rows] = top + jnp.log(total) * log2e
                return carry

            lax.fori_loop(0, seq // size, attend, 0)

            def features(block, head=head, layer=layer):
                start = block * (OWN_HEADS * HEAD_DIM) + head * HEAD_DIM
                return att.at[layer, pl.ds(pl.multiple_of(start, HEAD_DIM), HEAD_DIM)]

            own, theirs = features(me), features(across)
            to_across = push(own, own, sems, layer, 6 + head, across)
            to_mate = push(own, own, sems, layer, 9 + head, mate)
            onward = push(theirs, theirs, sems, layer, 12 + head, mate)
            to_across.start()
            to_mate.start()
            if head:
                sends[-2].wait_recv()
                forwards[-1].start()
            serve(layer, 2, 2)
            sends += [to_across, to_mate]
            forwards.append(onward)
        sends[-2].wait_recv()
        forwards[-1].start()
        for head in range(OWN_HEADS):
            sends[2 * head + 1].wait_recv()
            forwards[head].wait_recv()
        store(2, layer, lse, lse_out)
        store(3, layer, att, att_out)
        serve(layer, 3)
        if layer == 0:
            gain_stage(1)
        for number in range(1, 4):
            weights[4 * layer + number].wait()

        def feed(block, keep, layer=layer):
            rows = rows_of(block, size, size)
            branch = dot_tn(att[layer, :, rows], wo[layer])
            normed, inverse = normed_rows(xf[layer, rows, :].astype(f32) + branch)
            first_rows = normed * gain[2 * layer:2 * layer + 1, :]
            if keep:
                n1[layer] = normed
                s1[layer] = jnp.broadcast_to(inverse, s1.shape[1:])
                first[...] = first_rows
            first_low = first_rows.astype(bf16)
            flow[layer, rows, :] = first_low
            gate_up = dot(first_low, wg[layer])
            gate, upward = gate_up[:, :ff], gate_up[:, ff:]
            gu[layer, rows, :] = gate_up.astype(bf16)
            hidden = (gate / (1.0 + jnp.exp(-gate)) * upward).astype(bf16)
            hid[layer, rows, :] = hidden
            return dot_nt(hidden, wd[layer])

        scatter = Scatter(part, layer, got, layer, sems, 15, where)
        scatter.send_far(feed(far, False))
        scatter.send_across(feed(across, False))
        scatter.send_mate(feed(mate, False))
        own_part = feed(me, True)
        serve(layer + 1, 0)
        store(4, layer, flow, flow_out)
        store(5, layer, gu, gu_out)
        store(6, layer, hid, hid_out)
        store(7, layer, n1, n1_out)
        store(8, layer, s1, s1_out)
        ffn = scatter.total(own_part)
        pending.append(scatter)
        normed, inverse = normed_rows(first[...] + ffn)
        n2[layer] = normed
        s2[layer] = jnp.broadcast_to(inverse, s2.shape[1:])
        result = (normed * gain[2 * layer + 1:2 * layer + 2, :]).astype(bf16)
        store(9, layer, n2, n2_out)
        store(10, layer, s2, s2_out)
        if layer + 1 < LAYERS:
            xf[layer + 1, rows_of(me, size, size), :] = result
            row_gather = Gather(xf, layer + 1, layer + 1, sems, 0, size, where)
            row_gather.start()
        else:
            act[...] = result
            copy = pltpu.make_async_copy(act, act_out, osems.at[0, 11])
            copy.start()
            stores.append(copy)
        for copy in sends + forwards:
            copy.wait_send()
        if spreading:
            for number, held in enumerate((wq, wo, wg, wd)):
                store(12 + number, layer, held, weight_outs[number])
    if spreading:
        pending += weights
    for item in pending:
        item.finish()
    for copy in stores:
        copy.wait()


BACK_LOADED = (
    "n1", "s1", "n2", "s2", "xf", "qkv", "lse", "att", "flow", "gu", "hid", "wq", "wo", "wg", "wd",
)
BACK_TABLES = ("gain", "cos_rows", "sin_rows", "doc_keys", "doc_queries")
BACK_SCRATCH = (
    "bias", "dff", "dbr", "datt", "dproj", "dk", "dv", "dqt", "kt", "k2", "grad", "part", "got",
    "gq", "go", "gg", "gd", "sems", "lsems", "osems",
)
BACK_SPREAD = (
    "gsum", "gpack", "gside", "gdeep", "gsems", "csems", "qshare", "oshare",
    "near_d", "near_g", "near_u", "near_q", "near_o",
    "apart_d", "apart_g", "apart_u", "apart_q", "apart_o",
    "sum_d", "sum_g", "sum_u", "sum_q", "sum_o", "dsems",
)


def backward_kernel(spreading, names, *refs):
    r = dict(zip(names, refs))
    cot = r["cot"]
    gain, cos_rows, sin_rows, doc_keys, doc_queries = (r[n] for n in BACK_TABLES)
    (
        bias, dff, dbr, datt, dproj, dk, dv, dqt, kt, k2, grad, part, got,
        gq, go, gg, gd, sems, lsems, osems,
    ) = (r[n] for n in BACK_SCRATCH)
    n1, s1, n2, s2, qkv, lse, att, gu, hid, wq, wo, wg, wd = (
        r[n] for n in BACK_LOADED if n not in ("xf", "flow")
    )
    xf = flow = r["rows"]
    where = places()
    me, mate, across, far, core = where
    size = cot.shape[0]
    seq = size * GROUP
    ff = hid.shape[1]
    feats = xf.shape[1]
    own_feats = OWN_HEADS * HEAD_DIM
    held = {n: (r[n + "_in"], r.get(n, r["rows"])) for n in BACK_LOADED}
    order = list(held)
    loads = {}

    def load(name, layer):
        if layer < 0:
            return
        source, target = held[name]
        copy = pltpu.make_async_copy(source.at[layer], target, lsems.at[order.index(name)])
        copy.start()
        loads[name] = copy

    for name in ("n2", "s2", "wd", "gu", "wg", "hid", "n1", "s1", "flow", "wo", "qkv", "lse", "att", "wq"):
        load(name, LAYERS - 1)
    spread = Spread(feats // (2 * DEPTH)) if spreading else None
    greet(mate, across, far if spreading else None, spread)
    write_bias(bias, doc_keys, doc_queries)
    low_mask, high_mask = half_masks()
    grad[...] = cot[...]
    pending = []
    scatters = []
    stores = {}
    sums = {}
    shares = []
    pieces = dict(
        d=gd.at[:, :], g=gg.at[:, :ff], u=gg.at[:, ff:], q=gq.at[:, :], o=go.at[:, :]
    )
    gsum = r["gsum"] if spreading else r["gain_out"]
    gsum[...] = jnp.zeros_like(gsum)

    def begin(name, layer):
        if not spreading:
            if name == "u":
                store(2, layer, gg, r["g_out"])
            elif name != "g":
                number = "qogd".index(name)
                store(number, layer, (gq, go, gg, gd)[number], r[name + "_out"])
            return
        index = "dguqo".index(name)
        item = WeightSum(
            pieces[name], r["near_" + name], r["apart_" + name], 5 * layer + index, r["dsems"],
            spread, (r["csems"].at[0, index], r["csems"].at[1, index]),
            layer < LAYERS - 1, layer > 0, r["sum_" + name],
        )
        item.start()
        sums[name, layer] = item

    def add(name, layer):
        if spreading and (name, layer) in sums:
            sums[name, layer].add()

    def total(name, layer):
        if not spreading or (name, layer) not in sums:
            return
        result = sums[name, layer].total()
        if name == "q":
            share = Share(r["qshare"], layer, sems, 15, where)
            share.start(result.astype(bf16))
            shares.append(share)
        elif name == "o":
            oshare = r["oshare"]
            oshare[layer, core] = result.astype(bf16)
            copy = push(oshare.at[layer, core], oshare.at[layer, core], sems, layer, 18, mate)
            copy.start()
            oshares.append(copy)
        elif name == "d":
            r["d_res"][layer] = result
        else:
            half = "gu".index(name)
            r["g_res"][layer, :, half * ff:(half + 1) * ff] = result

    def ready(name, layer):
        if not spreading:
            if name != "u":
                stored("qogd".index(name))
        elif (name, layer + 1) in sums:
            sums[name, layer + 1].finish()

    oshares = []
    gains = []

    def gain_stage(stage):
        if not spreading:
            return
        gpack, gside, gdeep, gsems = (r[n] for n in ("gpack", "gside", "gdeep", "gsems"))
        if stage == 0:
            gpack[me] = gsum[...]
            for number, who in enumerate((mate, across, far)):
                gains.append(push(gpack.at[me], gpack.at[me], gsems, 0, number, who))
        elif stage == 1:
            for copy in gains[:3]:
                copy.wait_recv()
            gside[spread.x] = gpack[0] + gpack[1] + gpack[2] + gpack[3]
            own = gside.at[spread.x]
            gains.append(ship(own, own, gsems, 0, 3, spread.beside(0)))
        elif stage == 2:
            gains[3].wait_recv()
            gdeep[spread.z] = gside[0] + gside[1]
            own = gdeep.at[spread.z]
            for step in range(1, DEPTH):
                gains.append(ship(own, own, gsems, 0, 3 + step, spread.device(step)))
        else:
            for copy in gains[4:]:
                copy.wait_recv()
            r["gain_out"][...] = gdeep[0] + gdeep[1] + gdeep[2] + gdeep[3]
            for copy in gains:
                copy.wait_send()
            return
        for copy in gains[(0, 3, 4)[stage]:]:
            copy.start()

    def store(number, layer, source, target):
        copy = pltpu.make_async_copy(source, target.at[layer], osems.at[layer, number])
        copy.start()
        stores[number] = copy

    def stored(number):
        if number in stores:
            stores.pop(number).wait()

    for layer in range(LAYERS - 1, -1, -1):

        def norm_back(grad_rows, normed, inverse, row, layer=layer):
            gsum[2 * layer + row:2 * layer + row + 1, :] = jnp.sum(
                grad_rows * normed, axis=0, keepdims=True
            )
            scaled = grad_rows * gain[2 * layer + row:2 * layer + row + 1, :]
            return (
                scaled
                - jnp.mean(scaled, axis=-1, keepdims=True)
                - normed * jnp.mean(scaled * normed, axis=-1, keepdims=True)
            ) * inverse

        loads["n2"].wait()
        loads["s2"].wait()
        dz = norm_back(grad[...], n2[...], s2[:, :1], 1)
        load("n2", layer - 1)
        load("s2", layer - 1)
        grad[...] = dz
        dff[0, rows_of(me, size, size), :] = dz.astype(bf16)
        gather = Gather(dff, 0, layer, sems, 0, size, where)
        gather.start()
        for name in ("wd", "gu", "wg"):
            loads[name].wait()

        def feed_back(block, layer=layer):
            rows = rows_of(block, size, size)
            grad_hidden = dot(dff[0, rows, :], wd[...])
            gate = gu[rows, :ff].astype(f32)
            upward = gu[rows, ff:].astype(f32)
            sigma = 1.0 / (1.0 + jnp.exp(-gate))
            up_grad = grad_hidden * gate * sigma
            gate_grad = grad_hidden * upward * sigma * (1.0 + gate * (1.0 - sigma))
            gu[rows, :ff] = gate_grad.astype(bf16)
            gu[rows, ff:] = up_grad.astype(bf16)
            return dot_nt(gu[rows, :], wg[...])

        if len(scatters) > 1:
            scatters[-2].finish()
        scatter = Scatter(part, 0, got, 2 * layer, sems, 6, where)
        scatters.append(scatter)
        own_part = feed_back(me)
        gather.wait_mate()
        scatter.send_mate(feed_back(mate))
        gather.wait_across()
        across_part = feed_back(across)
        gather.wait_far()
        scatter.send_far(feed_back(far))
        scatter.send_across(across_part)
        load("wd", layer - 1)
        load("wg", layer - 1)
        loads["hid"].wait()
        add("q", layer + 1)
        ready("d", layer)

        def down_weight(i, carry, layer=layer):
            cols = rows_of(i, 256, 256)
            gd[cols, :] = dot_tn(dff[0, :, cols], hid[...]).astype(bf16)
            return carry

        lax.fori_loop(0, feats // 256, down_weight, 0)
        begin("d", layer)
        gather.finish()
        load("hid", layer - 1)
        add("o", layer + 1)

        dfirst = grad[...] + scatter.total(own_part)
        loads["n1"].wait()
        loads["s1"].wait()
        dr = norm_back(dfirst, n1[...], s1[:, :1], 0)
        load("n1", layer - 1)
        load("s1", layer - 1)
        grad[...] = dr
        dbr[layer, rows_of(me, size, size), :] = dr.astype(bf16)
        gather = Gather(dbr, layer, layer, sems, 9, size, where)
        gather.start()
        loads["flow"].wait()

        if layer == 0:
            gain_stage(0)
        for name, first_col in (("g", 0), ("u", ff)):
            ready(name, layer)

            def gate_up_weight(i, carry, first_col=first_col):
                cols = rows_of(i, 256, 256)
                gg[cols, first_col:first_col + ff] = dot_tn(
                    flow[:, cols], gu[:, first_col:first_col + ff]
                ).astype(bf16)
                return carry

            lax.fori_loop(0, feats // 256, gate_up_weight, 0)
            begin(name, layer)
        load("gu", layer - 1)
        load("xf", layer)
        for name in "dgu":
            total(name, layer + 1)

        loads["wo"].wait()

        def weigh_out(layer):
            loads["att"].wait()
            ready("o", layer)

            def out_weight(i, carry):
                rows = rows_of(i, 256, 256)
                half = feats // 2
                cols = pl.ds(pl.multiple_of(core * half, half), half)
                go[rows, :] = dot(att[rows, :], dbr[layer, :, cols]).astype(bf16)
                return carry

            lax.fori_loop(0, feats // 256, out_weight, 0)
            begin("o", layer)
            load("att", layer - 1)

        def att_back(block, layer=layer):
            rows = rows_of(block, size, size)
            for tile, start in enumerate((0, HEAD_DIM)):
                spot = pl.ds(pl.multiple_of(me * own_feats + start, HEAD_DIM), TILE)
                datt[rows, tile * TILE:(tile + 1) * TILE] = dot_nt(
                    dbr[layer, rows, :], wo[spot, :]
                ).astype(bf16)

        att_back(me)
        gather.wait_mate()
        att_back(mate)
        gather.wait_across()
        att_back(across)
        gather.wait_far()
        att_back(far)
        pending.append(gather)
        load("wo", layer - 1)
        if layer == 0:
            weigh_out(layer)
            gain_stage(1)
        add("d", layer)
        total("q", layer + 1)
        total("o", layer + 1)

        loads["qkv"].wait()
        loads["lse"].wait()
        kt[0] = qkv[:, TILE:2 * TILE].T
        kt[1] = qkv[:, 3 * TILE:4 * TILE].T
        k2[...] = pltpu.roll(qkv[:, 3 * TILE:4 * TILE].astype(f32), HEAD_DIM, 1).astype(bf16)
        dk[...] = jnp.zeros_like(dk)
        dv[...] = jnp.zeros_like(dv)
        for head in range(OWN_HEADS):
            tile = head // 2
            query_tile = (0, 0, 3)[head]
            value_tile = (2, 2, 4)[head]
            query_mask = (low_mask, high_mask, low_mask)[head]
            value_mask = (low_mask, high_mask, high_mask)[head]

            def attend(i, carry, head=head, tile=tile, query_tile=query_tile, value_tile=value_tile,
                       query_mask=query_mask, value_mask=value_mask):
                rows = rows_of(i, size, size)
                queries = qkv[rows, query_tile * TILE:(query_tile + 1) * TILE] * query_mask
                keys = k2[...] if head == 2 else qkv[:, TILE:2 * TILE]
                scores = dot_nt(keys, queries) * (score_scale * log2e) + bias[:, rows]
                probs = jnp.exp2(scores - lse[head:head + 1, rows])
                outs = datt[rows, tile * TILE:(tile + 1) * TILE] * value_mask
                grad_probs = dot_nt(qkv[:, value_tile * TILE:(value_tile + 1) * TILE], outs)
                delta = jnp.sum(probs * grad_probs, axis=0, keepdims=True)
                grad_scores = (probs * (grad_probs - delta)).astype(bf16)
                dv[tile] = dv[tile] + dot(probs.astype(bf16), outs)
                dk[tile] = dk[tile] + dot(grad_scores, queries)
                keys_t = (kt.at[0, :HEAD_DIM], kt.at[0, HEAD_DIM:], kt.at[1, HEAD_DIM:])[head][...]
                spot = (0, HEAD_DIM, 0)[head]
                dqt[tile, spot:spot + HEAD_DIM, rows] = dot(keys_t, grad_scores)
                return carry

            lax.fori_loop(0, seq // size, attend, 0)
            if head == 0:
                add("g", layer)
                for share in shares:
                    share.serve()
            if head == 1 and layer == 0:
                add("o", layer)
            if layer == 0 and head < 2:
                gain_stage(2 + head)

        add("u", layer)

        def unrotate(i, carry):
            rows = rows_of(i, size, size)
            c, s = cos_rows[rows, :], -sin_rows[rows, :]
            dproj[rows, :TILE] = turn(dqt[0, :, rows].T * score_scale, c, s).astype(bf16)
            dproj[rows, TILE:2 * TILE] = turn(dk[0, rows, :] * score_scale, c, s).astype(bf16)
            dproj[rows, 2 * TILE:3 * TILE] = dv[0, rows, :].astype(bf16)
            lower = lane_iota((size, TILE)) < HEAD_DIM
            mixed = jnp.where(lower, dqt[1, :, rows].T, pltpu.roll(dk[1, rows, :], HEAD_DIM, 1))
            dproj[rows, 3 * TILE:4 * TILE] = turn(mixed * score_scale, c, s).astype(bf16)
            dproj[rows, 4 * TILE:] = dv[1, rows, :].astype(bf16)
            return carry

        lax.fori_loop(0, seq // size, unrotate, 0)
        load("qkv", layer - 1)
        load("lse", layer - 1)
        loads["wq"].wait()

        def input_part(block):
            return dot_nt(dproj[rows_of(block, size, size), :], wq[...])

        if len(scatters) > 1:
            scatters[-2].finish()
        scatter = Scatter(part, 1, got, 2 * layer + 1, sems, 6, where)
        scatters.append(scatter)
        scatter.send_far(input_part(far))
        scatter.send_across(input_part(across))
        scatter.send_mate(input_part(mate))
        own_part = input_part(me)
        load("wq", layer - 1)
        loads["xf"].wait()

        ready("q", layer)

        def qkv_weight(i, carry, layer=layer):
            cols = rows_of(i, 256, 256)
            gq[cols, :] = dot_tn(xf[:, cols], dproj[...]).astype(bf16)
            return carry

        lax.fori_loop(0, feats // 256, qkv_weight, 0)
        begin("q", layer)
        load("flow", layer - 1)
        if layer:
            weigh_out(layer)
        grad[...] = grad[...] + scatter.total(own_part)
    input_copy = pltpu.make_async_copy(grad, r["ig_out"], osems.at[0, 4])
    input_copy.start()
    for name in "dguo":
        total(name, 0)
    add("q", 0)
    total("q", 0)
    if spreading:
        shares[-1].serve()
    input_copy.wait()
    for item in pending + scatters[-2:]:
        item.finish()
    for number in range(4):
        stored(number)
    for item in shares:
        item.finish()
    for copy in oshares:
        copy.wait()
    if spreading:
        for name in "dguqo":
            sums[name, 0].finish()
        for number, held in enumerate(((r["qshare"], r["q_out"]), (r["oshare"], r["o_out"]))):
            copy = pltpu.make_async_copy(*held, osems.at[1, number])
            copy.start()
            copy.wait()


def pack_documents(length_row, mask_row):
    seq = mask_row.shape[0]
    ends = jnp.cumsum(length_row)
    spots = jnp.arange(seq, dtype=jnp.int32)
    past = spots[:, None] >= ends[None, :]
    number = jnp.sum(past.astype(jnp.int32), axis=1)
    starts = jnp.max(jnp.where(past, ends[None, :], 0), axis=1)
    position = spots - starts
    keys = jnp.where(mask_row == 1, number, -1)
    doc_keys = jnp.broadcast_to(keys[:, None], (seq, 128))
    doc_queries = jnp.broadcast_to(number[None, :], (8, seq))
    half = HEAD_DIM // 2
    freq = jnp.power(rotary_base, -2.0 * jnp.arange(half).astype(f32) / HEAD_DIM)
    angle = position.astype(f32)[:, None] * freq
    c, s = jnp.cos(angle), jnp.sin(angle)
    cos_rows = jnp.concatenate([c, c, c, c], axis=1)
    sin_rows = jnp.concatenate([-s, s, -s, s], axis=1)
    return cos_rows, sin_rows, doc_keys, doc_queries


def own_projection(weight, me):
    layers, rows, _ = weight.shape
    split = weight.reshape(layers, rows, 3, HEADS * HEAD_DIM)
    own = lax.dynamic_slice_in_dim(split, me * OWN_HEADS * HEAD_DIM, OWN_HEADS * HEAD_DIM, 3)
    own = own.astype(bf16)
    pairs = own[..., :TILE].reshape(layers, rows, 3 * TILE)
    last = own[..., TILE:]
    return jnp.concatenate(
        [pairs, last[:, :, 0], last[:, :, 1], jnp.zeros_like(last[:, :, 0]), last[:, :, 2]], axis=-1
    )


def whole_projection(grad):
    group, layers, rows, _ = grad.shape
    pairs = grad[..., :3 * TILE].reshape(group, layers, rows, 3, TILE)
    last = jnp.stack(
        [
            grad[..., 3 * TILE:3 * TILE + HEAD_DIM],
            grad[..., 3 * TILE + HEAD_DIM:4 * TILE],
            grad[..., 4 * TILE + HEAD_DIM:],
        ],
        axis=3,
    )
    full = jnp.concatenate([pairs, last], axis=-1)
    return full.transpose(1, 2, 3, 0, 4).reshape(layers, rows, 3 * HEADS * HEAD_DIM)


def run_forward(spreading, tokens, weights, gain, tables):
    size, feats = tokens.shape
    seq = size * GROUP
    ff = weights[3].shape[2]
    shapes = dict(
        act=((size, feats), bf16),
        xf=((LAYERS, seq, feats), bf16),
        qkv=((LAYERS, seq, PROJ), bf16),
        lse=((LAYERS, 8, seq), f32),
        att=((LAYERS, feats, seq), bf16),
        flow=((LAYERS, seq, feats), bf16),
        gu=((LAYERS, seq, 2 * ff), bf16),
        hid=((LAYERS, seq, ff), bf16),
        n1=((LAYERS, size, feats), f32),
        s1=((LAYERS, size, 128), f32),
        n2=((LAYERS, size, feats), f32),
        s2=((LAYERS, size, 128), f32),
        wq=((LAYERS, feats, PROJ), bf16),
        wo=((LAYERS, feats, feats), bf16),
        wg=((LAYERS, feats, 2 * ff), bf16),
        wd=((LAYERS, feats, ff), bf16),
        gain=((8, feats), f32),
    )
    held = {name: pltpu.VMEM(*shape) for name, shape in shapes.items()}
    scratch = [held[n] for n in ("wq", "wo", "wg", "wd", "xf", "qkv", "att", "flow", "gu", "hid")]
    scratch += [
        pltpu.VMEM((seq, seq), f32),
        pltpu.VMEM((2, TILE, seq), bf16),
        pltpu.VMEM((seq, TILE), bf16),
        held["lse"],
    ]
    scratch += [held[n] for n in ("n1", "s1", "n2", "s2")]
    scratch += [
        pltpu.VMEM((size, feats), f32),
        held["act"],
        pltpu.VMEM((LAYERS, 3, size, feats), bf16),
        pltpu.VMEM((LAYERS, 3, size, feats), bf16),
        pltpu.SemaphoreType.DMA((2, LAYERS, 18)),
        pltpu.SemaphoreType.DMA((LAYERS, 4)),
        pltpu.SemaphoreType.DMA((LAYERS, 16)),
        pltpu.SemaphoreType.DMA((2, 4 * LAYERS, 3 + 2 * DEPTH)),
        pltpu.SemaphoreType.DMA((2, LAYERS, 7)),
        pltpu.VMEM((2, 8, feats), f32),
        pltpu.VMEM((DEPTH, 8, feats), f32),
        pltpu.SemaphoreType.DMA((2, 1, DEPTH)),
    ]
    return pl.pallas_call(
        functools.partial(forward_kernel, spreading),
        out_shape=[jax.ShapeDtypeStruct(*shape) for shape in shapes.values()],
        in_specs=[VMEM] + [ANY] * 4 + [VMEM] * 5,
        out_specs=[ANY] * (len(shapes) - 1) + [VMEM],
        scratch_shapes=scratch,
        compiler_params=pltpu.CompilerParams(
            collective_id=0, has_side_effects=True, vmem_limit_bytes=VMEM_LIMIT
        ),
        cost_estimate=pl.CostEstimate(
            flops=12 * 10**9, bytes_accessed=60 * 10**6, transcendentals=10**7
        ),
        name="forward",
    )(tokens, *weights, gain, *tables)


def run_backward(spreading, cotangent, kept, weights, gain, tables):
    size, feats = cotangent.shape
    seq = size * GROUP
    xf, qkv, lse, att, flow, gu, hid, n1, s1, n2, s2 = kept
    ff = hid.shape[2]
    wq, wo, wg, wd = weights
    loaded = [n1, s1, n2, s2, xf, qkv, lse, att, flow, gu, hid, wq, wo, wg, wd]
    own = feats // (2 * DEPTH)
    half = feats // 2
    widths = dict(d=ff, g=ff, u=ff, q=PROJ, o=half)
    if spreading:
        outs = dict(
            ig_out=((size, feats), f32),
            q_out=((LAYERS, GROUP, own, PROJ), bf16),
            o_out=((LAYERS, 2, own, half), bf16),
            d_res=((LAYERS, own, ff), f32),
            g_res=((LAYERS, own, 2 * ff), f32),
            gain_out=((8, feats), f32),
        )
    else:
        outs = dict(
            ig_out=((size, feats), f32),
            q_out=(wq.shape, bf16),
            o_out=((LAYERS, feats, half), bf16),
            d_out=(wd.shape, bf16),
            g_out=(wg.shape, bf16),
            gain_out=((8, feats), f32),
        )
    names = ["cot"] + [n + "_in" for n in BACK_LOADED] + list(BACK_TABLES) + list(outs)
    scratch = dict(
        bias=pltpu.VMEM((seq, seq), f32),
        dff=pltpu.VMEM((1, seq, feats), bf16),
        dbr=pltpu.VMEM((LAYERS, seq, feats), bf16),
        datt=pltpu.VMEM((seq, 2 * TILE), bf16),
        dproj=pltpu.VMEM((seq, PROJ), bf16),
        dk=pltpu.VMEM((2, seq, TILE), f32),
        dv=pltpu.VMEM((2, seq, TILE), f32),
        dqt=pltpu.VMEM((2, TILE, seq), f32),
        kt=pltpu.VMEM((2, TILE, seq), bf16),
        k2=pltpu.VMEM((seq, TILE), bf16),
        grad=pltpu.VMEM((size, feats), f32),
        part=pltpu.VMEM((2, 3, size, feats), bf16),
        got=pltpu.VMEM((2, 3, size, feats), bf16),
        gq=pltpu.VMEM((feats, PROJ), bf16),
        go=pltpu.VMEM((feats, half), bf16),
        gg=pltpu.VMEM((feats, 2 * ff), bf16),
        gd=pltpu.VMEM((feats, ff), bf16),
        sems=pltpu.SemaphoreType.DMA((2, 2 * LAYERS, 19)),
        lsems=pltpu.SemaphoreType.DMA((len(loaded),)),
        osems=pltpu.SemaphoreType.DMA((LAYERS, 5)),
        rows=pltpu.VMEM((seq, feats), bf16),
    )
    for name, array in zip(BACK_LOADED, loaded):
        if name not in ("xf", "flow"):
            scratch[name] = pltpu.VMEM(array.shape[1:], array.dtype)
    if spreading:
        scratch.update(
            gsum=pltpu.VMEM((8, feats), f32),
            gpack=pltpu.VMEM((GROUP, 8, feats), f32),
            gside=pltpu.VMEM((2, 8, feats), f32),
            gdeep=pltpu.VMEM((DEPTH, 8, feats), f32),
            gsems=pltpu.SemaphoreType.DMA((2, 1, 7)),
            csems=pltpu.SemaphoreType.REGULAR((2, 5)),
            qshare=pltpu.VMEM((LAYERS, GROUP, own, PROJ), bf16),
            oshare=pltpu.VMEM((LAYERS, 2, own, half), bf16),
            dsems=pltpu.SemaphoreType.DMA((2, 5 * LAYERS, 7)),
        )
        for name, width in widths.items():
            scratch["near_" + name] = pltpu.VMEM((DEPTH, own, width), bf16)
            scratch["apart_" + name] = pltpu.VMEM((DEPTH - 1, own, width), bf16)
            scratch["sum_" + name] = pltpu.VMEM((own, width), f32)
    in_vmem = ("d_res", "g_res", "gain_out")
    return pl.pallas_call(
        functools.partial(backward_kernel, spreading, tuple(names + list(scratch))),
        out_shape=[jax.ShapeDtypeStruct(*shape) for shape in outs.values()],
        in_specs=[VMEM] + [ANY] * 15 + [VMEM] * 5,
        out_specs=[VMEM if name in in_vmem else ANY for name in outs],
        scratch_shapes=list(scratch.values()),
        compiler_params=pltpu.CompilerParams(
            collective_id=1, has_side_effects=True, vmem_limit_bytes=VMEM_LIMIT
        ),
        cost_estimate=pl.CostEstimate(
            flops=24 * 10**9, bytes_accessed=60 * 10**6, transcendentals=10**7
        ),
        name="backward",
    )(cotangent, *loaded, gain, *tables)


def adamw(weight, first, second, average, gradient, rate, decay):
    first_new = beta_first * first + (1.0 - beta_first) * gradient
    second_new = beta_second * second + (1.0 - beta_second) * gradient * gradient
    first_hat = first_new / (1.0 - beta_first**STEP)
    second_hat = second_new / (1.0 - beta_second**STEP)
    weight_new = weight - rate * (
        first_hat / (jnp.sqrt(second_hat) + adam_epsilon) + decay * weight
    )
    average_new = average_decay * average + (1.0 - average_decay) * weight_new
    return (gradient, first_new, second_new, weight_new, average_new)


def shards(
    spreading,
    tokens,
    cotangent,
    lengths,
    key_mask,
    qkv_weight,
    qkv_first,
    qkv_second,
    qkv_average,
    out_weight,
    out_first,
    out_second,
    out_average,
    gate_up_weight,
    gate_up_first,
    gate_up_second,
    gate_up_average,
    down_weight,
    down_first,
    down_second,
    down_average,
    norm_gain,
    gain_first,
    gain_second,
    gain_average,
):
    me = lax.axis_index("mp")
    own = gate_up_weight.shape[1]
    ff = gate_up_weight.shape[3]
    feats = tokens.shape[1]
    if spreading:
        gain = jnp.zeros((8, feats), f32)
        gain = lax.dynamic_update_slice(
            gain, norm_gain.reshape(2 * LAYERS, own), (0, lax.axis_index("dp") * own)
        )
    else:
        gain = lax.all_gather(norm_gain, "dp", axis=2, tiled=True).reshape(2 * LAYERS, feats)
        gain = jnp.concatenate([gain, jnp.zeros((8 - 2 * LAYERS, feats), f32)], axis=0)
    tables = pack_documents(lengths[0], key_mask)
    owned = (
        own_projection(qkv_weight, me),
        out_weight.astype(bf16),
        gate_up_weight.reshape(LAYERS, own, 2 * ff).astype(bf16),
        down_weight.astype(bf16),
    )
    if not spreading:
        owned = [lax.all_gather(w, "dp", axis=1, tiled=True) for w in owned]
    act, *kept = run_forward(spreading, tokens, owned, gain, tables)
    weights, kept, gain = kept[-5:-1], kept[:-5], kept[-1]
    backward = run_backward(spreading, cotangent, kept, weights, gain, tables)
    if spreading:
        input_grad, gq, go, gd, gg, gain_sum = backward
        gq, go = gq.transpose(1, 0, 2, 3), go.transpose(1, 0, 2, 3)
        gain_grad = lax.dynamic_slice_in_dim(
            gain_sum[:2 * LAYERS].reshape(LAYERS, 2, -1), lax.axis_index("dp") * own, own, 2
        )
    else:
        input_grad, gq, go, gd, gg, gain_sum = backward
        gq, go, gg, gd = [
            lax.psum_scatter(g, "dp", scatter_dimension=1, tiled=True) for g in (gq, go, gg, gd)
        ]
        gq, go = lax.all_gather(gq, "mp"), lax.all_gather(go, "mp")
        gain_part = gain_sum[:2 * LAYERS].reshape(LAYERS, 2, -1)
        gain_grad = lax.psum_scatter(
            lax.psum(gain_part, "mp"), "dp", scatter_dimension=2, tiled=True
        )
    qkv_grad = whole_projection(gq.astype(f32))
    out_grad = jnp.concatenate([go[0], go[1]], axis=-1).astype(f32)
    gate_up_grad = gg.reshape(LAYERS, own, 2, ff).astype(f32)
    down_grad = gd.astype(f32)
    results = [act, input_grad]
    results.extend(adamw(qkv_weight, qkv_first, qkv_second, qkv_average, qkv_grad, 0.03, 0.01))
    results.extend(adamw(out_weight, out_first, out_second, out_average, out_grad, 0.5, 0.01))
    results.extend(
        adamw(
            gate_up_weight, gate_up_first, gate_up_second, gate_up_average, gate_up_grad, 0.03, 0.01
        )
    )
    results.extend(
        adamw(down_weight, down_first, down_second, down_average, down_grad, 0.02, 0.01)
    )
    results.extend(adamw(norm_gain, gain_first, gain_second, gain_average, gain_grad, 0.6, 0.0))
    return tuple(results)


def solution(mesh):
    spreading = mesh.shape["dp"] == 2 * DEPTH
    return jax.shard_map(
        functools.partial(shards, spreading),
        mesh=mesh,
        in_specs=(
            P(("dp", "mp"), None),
            P(("dp", "mp"), None),
            P("dp", None),
            P("dp"),
            P(None, "dp", None),
            P(None, "dp", None),
            P(None, "dp", None),
            P(None, "dp", None),
            P(None, "dp", None),
            P(None, "dp", None),
            P(None, "dp", None),
            P(None, "dp", None),
            P(None, "dp", None, "mp"),
            P(None, "dp", None, "mp"),
            P(None, "dp", None, "mp"),
            P(None, "dp", None, "mp"),
            P(None, "dp", "mp"),
            P(None, "dp", "mp"),
            P(None, "dp", "mp"),
            P(None, "dp", "mp"),
            P(None, None, "dp"),
            P(None, None, "dp"),
            P(None, None, "dp"),
            P(None, None, "dp"),
        ),
        out_specs=(
            P(("dp", "mp"), None),
            P(("dp", "mp"), None),
            P(None, "dp", None),
            P(None, "dp", None),
            P(None, "dp", None),
            P(None, "dp", None),
            P(None, "dp", None),
            P(None, "dp", None),
            P(None, "dp", None),
            P(None, "dp", None),
            P(None, "dp", None),
            P(None, "dp", None),
            P(None, "dp", None, "mp"),
            P(None, "dp", None, "mp"),
            P(None, "dp", None, "mp"),
            P(None, "dp", None, "mp"),
            P(None, "dp", None, "mp"),
            P(None, "dp", "mp"),
            P(None, "dp", "mp"),
            P(None, "dp", "mp"),
            P(None, "dp", "mp"),
            P(None, "dp", "mp"),
            P(None, None, "dp"),
            P(None, None, "dp"),
            P(None, None, "dp"),
            P(None, None, "dp"),
            P(None, None, "dp"),
        ),
        check_vma=False,
    )
```

```python
import functools
import math

import jax
import jax.numpy as jnp
from jax import lax
from jax.experimental import pallas as pl
from jax.experimental.pallas import tpu as pltpu
from jax.sharding import PartitionSpec as P

HEADS = 12
HEAD_DIM = 64
LAYERS = 2
STEP = 10
GROUP = 4
DEPTH = 4
LEAD = 1
PIECES = 4
OWN_HEADS = HEADS // GROUP
TILE = 2 * HEAD_DIM
PROJ = 5 * TILE

rotary_base = 1000.0
norm_epsilon = 1e-05
masked_score = -1e30
beta_first = 0.5
beta_second = 0.5
adam_epsilon = 1e-08
average_decay = 0.5
score_scale = HEAD_DIM ** (-0.5)
log2e = math.log2(math.e)

MESH = pl.DeviceIdType.MESH
ANY = pl.BlockSpec(memory_space=pl.ANY)
VMEM = pl.BlockSpec(memory_space=pltpu.VMEM)
f32 = jnp.float32
bf16 = jnp.bfloat16
VMEM_LIMIT = 127 * 2**19


def dot(a, b):
    return jnp.dot(a, b, preferred_element_type=f32)


def dot_nt(a, b):
    return lax.dot_general(a, b, (((1,), (1,)), ((), ())), preferred_element_type=f32)


def dot_tn(a, b):
    return lax.dot_general(a, b, (((0,), (0,)), ((), ())), preferred_element_type=f32)


def places():
    me = lax.axis_index("mp")
    core = lax.rem(me, 2)
    side = lax.div(me, 2)
    return me, me + 1 - 2 * core, me + 2 - 4 * side, 3 - me, core


def push(src, dst, sems, layer, number, who):
    return pltpu.make_async_remote_copy(
        src_ref=src,
        dst_ref=dst,
        send_sem=sems.at[0, layer, number],
        recv_sem=sems.at[1, layer, number],
        device_id={"mp": who},
        device_id_type=MESH,
    )


class Spread:
    def __init__(self, own):
        index = lax.axis_index("dp")
        self.own = own
        self.z, self.x = lax.div(index, 2), lax.rem(index, 2)

    def device(self, step):
        return 2 * lax.rem(self.z + step, DEPTH) + self.x

    def beside(self, step):
        return 2 * lax.rem(self.z + step, DEPTH) + 1 - self.x

    def rows(self, index):
        return pl.ds(pl.multiple_of(index * self.own, self.own), self.own)


def greet(mate, across, far=None, spread=None):
    barrier = pltpu.get_barrier_semaphore()
    packs = [mate, across] if far is None else [mate, across, far]
    for who in packs:
        pl.semaphore_signal(barrier, inc=1, device_id={"mp": who}, device_id_type=MESH)
    others = []
    if spread is not None:
        others = [spread.beside(0)] + [spread.device(step) for step in range(1, DEPTH)]
        for who in others:
            pl.semaphore_signal(barrier, inc=1, device_id={"dp": who}, device_id_type=MESH)
    pl.semaphore_wait(barrier, len(packs) + len(others))


def ship(src, dst, sems, piece, number, who):
    return pltpu.make_async_remote_copy(
        src_ref=src,
        dst_ref=dst,
        send_sem=sems.at[0, piece, number],
        recv_sem=sems.at[1, piece, number],
        device_id={"dp": who},
        device_id_type=MESH,
    )


class WeightGather:
    def __init__(self, source, target, layer, piece, sems, local, spread, cols=None):
        self.target, self.layer, self.cols = target, layer, cols
        self.piece, self.sems, self.spread = piece, sems, spread
        z, x = spread.z, spread.x
        own = source.at[layer] if cols is None else source.at[layer, :, cols]
        place = self.view(z, x)
        self.local = pltpu.make_async_copy(own, place, local)
        self.beside = self.send(own, place, 0, 0, 2 * z + 1 - x)
        self.up = self.send(own, place, 1, 1 + z, 2 * jnp.minimum(z + 1, DEPTH - 1) + x)
        self.down = self.send(own, place, 2, 1 + z, 2 * jnp.maximum(z - 1, 0) + x)
        self.hops = [(far, way) for far in range(1, DEPTH) for way in (-1, 1)]
        self.todo = list(self.hops)

    def view(self, z, x):
        rows = self.spread.rows(2 * z + x)
        if self.cols is None:
            return self.target.at[self.layer, rows]
        return self.target.at[self.layer, rows, self.cols]

    def send(self, src, dst, out, into, who):
        return pltpu.make_async_remote_copy(
            src_ref=src,
            dst_ref=dst,
            send_sem=self.sems.at[0, self.piece, out],
            recv_sem=self.sems.at[1, self.piece, into],
            device_id={"dp": who},
            device_id_type=MESH,
        )

    def start(self):
        self.local.start()
        pl.when(self.spread.z < DEPTH - 1)(self.up.start)
        pl.when(self.spread.z > 0)(self.down.start)
        self.beside.start()

    def hop(self, far, way):
        z, x = self.spread.z, self.spread.x
        source = jnp.clip(z + way * far, 0, DEPTH - 1)
        block = self.view(source, x)
        onward = jnp.clip(z - way, 0, DEPTH - 1)
        arrive = self.send(block, block, 3 + source, 1 + source, 2 * source + x)
        over = self.send(block, block, 3 + source, 1 + DEPTH + source, 2 * z + 1 - x)
        along = self.send(block, block, 3 + DEPTH + source, 1 + source, 2 * onward + x)
        comes = z >= far if way < 0 else z + far < DEPTH
        goes = z > 0 if way > 0 else z < DEPTH - 1
        return arrive, over, along, comes, jnp.logical_and(comes, goes)

    def serve(self, count=2 * DEPTH):
        while self.todo and count:
            count -= 1
            arrive, over, along, comes, goes = self.hop(*self.todo.pop(0))

            pl.when(comes)(arrive.wait_recv)
            pl.when(goes)(along.start)
            pl.when(comes)(over.start)

    def wait(self):
        self.serve()
        self.local.wait()
        self.beside.wait_recv()
        z, x = self.spread.z, self.spread.x
        for step in range(1, DEPTH):
            source = lax.rem(z + step, DEPTH)
            block = self.view(source, 1 - x)
            self.send(block, block, 3, 1 + DEPTH + source, 2 * z + 1 - x).wait_recv()

    def finish(self):
        self.beside.wait_send()
        pl.when(self.spread.z < DEPTH - 1)(self.up.wait_send)
        pl.when(self.spread.z > 0)(self.down.wait_send)
        for far, way in self.hops:
            arrive, over, along, comes, goes = self.hop(far, way)
            pl.when(comes)(over.wait_send)
            pl.when(goes)(along.wait_send)


class HalfGather(WeightGather):
    def __init__(self, source, target, layer, piece, sems, local, spread, half, pack_sems, where):
        me, mate, across, far, core = where
        cols = pl.ds(pl.multiple_of(core * half, half), half)
        super().__init__(source, target, layer, piece, sems, local, spread, cols)
        here = spread.rows(2 * spread.z + spread.x)
        self.local = pltpu.make_async_copy(source.at[layer], target.at[layer, here], local)
        self.swap = []
        for step in range(DEPTH):
            z = lax.rem(spread.z + step, DEPTH)
            for number, x in enumerate((spread.x, 1 - spread.x)):
                if step or number:
                    block = self.view(z, x)
                    self.swap.append(
                        push(block, block, pack_sems, layer, 2 * step + number - 1, mate)
                    )

    def share(self):
        super().wait()
        for copy in self.swap:
            copy.start()

    def wait(self):
        for copy in self.swap:
            copy.wait_recv()

    def finish(self):
        super().finish()
        for copy in self.swap:
            copy.wait_send()


class WeightSum:
    def __init__(self, grad, near, apart, piece, sems, spread, credits, again, more, total):
        self.grad, self.near, self.apart, self.spread = grad, near, apart, spread
        self.near_credit, self.apart_credit = credits
        self.again, self.more = again, more
        self.sum = total
        self.beside = [
            ship(grad.at[spread.rows(spread.beside(step))], near.at[step], sems, piece, step,
                 spread.beside(0))
            for step in range(DEPTH)
        ]
        self.along = [
            ship(grad.at[spread.rows(spread.device(step))], apart.at[step - 1], sems, piece,
                 DEPTH - 1 + step, spread.device(step))
            for step in range(1, DEPTH)
        ]

    def start(self):
        if self.again:
            pl.semaphore_wait(self.near_credit, 1)
        for copy in self.beside[1:] + self.beside[:1]:
            copy.start()

    def credit(self, sem, who):
        pl.semaphore_signal(sem, inc=1, device_id={"dp": who}, device_id_type=MESH)

    def add(self):
        if self.again:
            pl.semaphore_wait(self.apart_credit, DEPTH - 1)
        for step in range(1, DEPTH):
            self.beside[step].wait_recv()
            rows = self.spread.rows(self.spread.device(step))
            self.grad[rows, :] = (
                self.grad[rows, :].astype(f32) + self.near[step].astype(f32)
            ).astype(bf16)
            self.along[step - 1].start()
        self.beside[0].wait_recv()
        rows = self.spread.rows(self.spread.device(0))
        self.sum[...] = self.grad[rows, :].astype(f32) + self.near[0].astype(f32)
        if self.more:
            self.credit(self.near_credit, self.spread.beside(0))

    def total(self):
        for copy in self.along:
            copy.wait_recv()
        result = self.sum[...]
        for step in range(DEPTH - 1):
            result = result + self.apart[step].astype(f32)
        if self.more:
            for step in range(1, DEPTH):
                self.credit(self.apart_credit, self.spread.device(step))
        return result

    def finish(self):
        for copy in self.beside + self.along:
            copy.wait_send()


def rows_of(block, size, extent):
    return pl.ds(pl.multiple_of(block * size, size), extent)


def lane_iota(shape):
    return lax.broadcasted_iota(jnp.int32, shape, len(shape) - 1)


def half_masks():
    low = (lane_iota((1, TILE)) < HEAD_DIM).astype(f32)
    return low.astype(bf16), (1.0 - low).astype(bf16)


def turn(tile, cos_rows, sin_rows):
    lane = lane_iota(tile.shape) % HEAD_DIM
    half = HEAD_DIM // 2
    partner = jnp.where(
        lane < half, pltpu.roll(tile, TILE - half, 1), pltpu.roll(tile, half, 1)
    )
    return tile * cos_rows + partner * sin_rows


def write_bias(bias, doc_keys, doc_queries):
    seq = bias.shape[0]
    step = 128

    def body(i, carry):
        rows = rows_of(i, step, step)
        keys = doc_keys[rows, :][:, :1]
        same = keys == doc_queries[:1, :]
        spot = lax.broadcasted_iota(jnp.int32, (step, seq), 0) + i * step
        own = spot == lax.broadcasted_iota(jnp.int32, (step, seq), 1)
        bias[rows, :] = jnp.where(jnp.logical_or(same, own), 0.0, masked_score)
        return carry

    lax.fori_loop(0, seq // step, body, 0)


class Gather:
    def __init__(self, ref, slot, layer, sems, first_sem, size, where):
        me, mate, across, far, core = where
        self.across, self.mate = [], []
        self.forward = []
        half = size // 2

        def piece(block, part):
            start = pl.multiple_of(block * size + part * half, half)
            return ref.at[slot, pl.ds(start, half)]

        for part in range(2):
            own = piece(me, part)
            theirs = piece(across, part)
            self.across.append(push(own, own, sems, layer, first_sem + part, across))
            self.mate.append(push(own, own, sems, layer, first_sem + 2 + part, mate))
            self.forward.append(push(theirs, theirs, sems, layer, first_sem + 4 + part, mate))

    def start(self):
        for copy in self.across + self.mate:
            copy.start()

    def wait_mate(self):
        for copy in self.mate:
            copy.wait_recv()

    def wait_across(self):
        for copy, onward in zip(self.across, self.forward):
            copy.wait_recv()
            onward.start()

    def wait_far(self):
        for copy in self.forward:
            copy.wait_recv()

    def finish(self):
        for copy in self.across + self.mate + self.forward:
            copy.wait_send()


class Share:
    def __init__(self, ref, layer, sems, first_sem, where):
        me, mate, across, far, core = where
        own, theirs = ref.at[layer, me], ref.at[layer, across]
        self.ref, self.layer, self.me = ref, layer, me
        self.over = push(own, own, sems, layer, first_sem, across)
        self.near = push(own, own, sems, layer, first_sem + 1, mate)
        self.onward = push(theirs, theirs, sems, layer, first_sem + 2, mate)

    def start(self, block):
        self.ref[self.layer, self.me] = block
        self.over.start()
        self.near.start()

    def serve(self):
        self.over.wait_recv()
        self.onward.start()

    def finish(self):
        self.near.wait_recv()
        self.onward.wait_recv()
        for copy in (self.over, self.near, self.onward):
            copy.wait_send()


class Scatter:
    def __init__(self, part, slot, got, layer, sems, first_sem, where):
        me, mate, across, far, core = where
        self.part, self.slot, self.got = part, slot, got
        self.far = push(part.at[slot, 0], got.at[slot, 0], sems, layer, first_sem, mate)
        self.over = push(part.at[slot, 1], got.at[slot, 1], sems, layer, first_sem + 1, across)
        self.near = push(part.at[slot, 2], got.at[slot, 2], sems, layer, first_sem + 2, mate)

    def send_far(self, block):
        self.part[self.slot, 0] = block.astype(bf16)
        self.far.start()

    def send_across(self, block):
        self.far.wait_recv()
        self.part[self.slot, 1] = (block + self.got[self.slot, 0].astype(f32)).astype(bf16)
        self.over.start()

    def send_mate(self, block):
        self.part[self.slot, 2] = block.astype(bf16)
        self.near.start()

    def total(self, block):
        self.near.wait_recv()
        self.over.wait_recv()
        return (
            block
            + self.got[self.slot, 1].astype(f32)
            + self.got[self.slot, 2].astype(f32)
        )

    def finish(self):
        for copy in (self.far, self.over, self.near):
            copy.wait_send()


def normed_rows(rows):
    centered = rows - jnp.mean(rows, axis=-1, keepdims=True)
    inverse = lax.rsqrt(jnp.mean(centered * centered, axis=-1, keepdims=True) + norm_epsilon)
    return centered * inverse, inverse


def forward_kernel(
    spreading, tok, wq_in, wo_in, wg_in, wd_in, gain_in, cos_rows, sin_rows, doc_keys, doc_queries,
    act_out, xf_out, qkv_out, lse_out, att_out, flow_out, gu_out, hid_out,
    n1_out, s1_out, n2_out, s2_out, wq_out, wo_out, wg_out, wd_out, gain,
    wq, wo, wg, wd, xf, qkv, att, flow, gu, hid, bias, vt, k2, lse,
    n1, s1, n2, s2, first, act, part, got, sems, wsems, osems, dsems, ssems, gside, gdeep, gsems,
):
    where = places()
    me, mate, across, far, core = where
    weight_outs = (wq_out, wo_out, wg_out, wd_out)
    size = tok.shape[0]
    seq = size * GROUP
    ff = hid.shape[2]
    spread = Spread(wq_in.shape[1]) if spreading else None
    weights = []
    parts = (
        (wq_in, wq, None), (wo_in, wo, None), (wg_in, wg, None), (wd_in, wd, None),
    )
    for layer in range(LAYERS):
        for number, (source, target, cols) in enumerate(parts):
            local = wsems.at[layer, number]
            piece = PIECES * layer + number
            if not spreading:
                if cols is not None:
                    source, target = source.at[:, :, cols], target.at[:, :, cols]
                weights.append(pltpu.make_async_copy(source.at[layer], target.at[layer], local))
            elif number == 1:
                weights.append(
                    HalfGather(source, target, layer, piece, dsems, local, spread,
                               wo.shape[2] // 2, ssems, where)
                )
            else:
                weights.append(
                    WeightGather(source, target, layer, piece, dsems, local, spread, cols)
                )
    xf[0, rows_of(me, size, size), :] = tok[...]
    greet(mate, across, None, spread)
    gains = []
    if spreading:
        gdeep[spread.z] = gain_in[...]
        own = gdeep.at[spread.z]
        for step in range(1, DEPTH):
            gains.append(ship(own, own, gsems, 0, step, spread.device(step)))
            gains[-1].start()
    else:
        gain[...] = gain_in[...]
    ahead = LEAD if spreading else len(weights)
    for item in weights[:ahead]:
        item.start()

    def gain_stage(stage):
        if not spreading:
            return
        if stage == 0:
            for copy in gains:
                copy.wait_recv()
            gside[spread.x] = gdeep[0] + gdeep[1] + gdeep[2] + gdeep[3]
            own = gside.at[spread.x]
            gains.append(ship(own, own, gsems, 0, 0, spread.beside(0)))
            gains[-1].start()
        else:
            gains[-1].wait_recv()
            gain[...] = gside[0] + gside[1]
            for copy in gains:
                copy.wait_send()

    queue = [(k, hop) for k in range(len(weights)) for hop in range(6)] if spreading else []

    def pump(count):
        for number in range(min(count, len(queue))):
            k, hop = queue.pop(0)
            if hop == 0 and k + ahead < len(weights):
                weights[k + ahead].start()
            weights[k].serve(1)

    pending = []
    stores = []

    def store(number, layer, source, target):
        copy = pltpu.make_async_copy(source.at[layer], target.at[layer], osems.at[layer, number])
        copy.start()
        stores.append(copy)

    row_gather = Gather(xf, 0, 0, sems, 0, size, where)
    row_gather.start()
    write_bias(bias, doc_keys, doc_queries)
    low_mask, high_mask = half_masks()

    for layer in range(LAYERS):
        if layer == 0:
            pump(12)
        weights[PIECES * layer].wait()

        def project(block, layer=layer):
            rows = rows_of(block, size, size)
            proj = dot(xf[layer, rows, :], wq[layer])
            c, s = cos_rows[rows, :], sin_rows[rows, :]
            for tile in (0, 1, 3):
                piece = proj[:, tile * TILE:(tile + 1) * TILE]
                qkv[layer, rows, tile * TILE:(tile + 1) * TILE] = turn(piece, c, s).astype(bf16)
            for tile in (2, 4):
                piece = proj[:, tile * TILE:(tile + 1) * TILE]
                qkv[layer, rows, tile * TILE:(tile + 1) * TILE] = piece.astype(bf16)

        project(me)
        row_gather.wait_mate()
        project(mate)
        row_gather.wait_across()
        if layer:
            pump(2)
        project(across)
        row_gather.wait_far()
        project(far)
        if layer == 0:
            gain_stage(0)
        pending.append(row_gather)
        store(0, layer, xf, xf_out)
        store(1, layer, qkv, qkv_out)
        vt[0] = qkv[layer, :, 2 * TILE:3 * TILE].T
        vt[1] = qkv[layer, :, 4 * TILE:5 * TILE].T
        k2[...] = pltpu.roll(qkv[layer, :, 3 * TILE:4 * TILE].astype(f32), HEAD_DIM, 1).astype(bf16)

        sends = []
        forwards = []
        for head in range(OWN_HEADS):
            query_tile = (0, 0, 3)[head]
            mask = (low_mask, high_mask, low_mask)[head]

            def attend(i, carry, layer=layer, head=head, query_tile=query_tile, mask=mask):
                rows = rows_of(i, size, size)
                queries = qkv[layer, rows, query_tile * TILE:(query_tile + 1) * TILE] * mask
                keys = k2[...] if head == 2 else qkv[layer, :, TILE:2 * TILE]
                values = (vt.at[0, :HEAD_DIM], vt.at[0, HEAD_DIM:], vt.at[1, HEAD_DIM:])[head][...]
                scores = dot_nt(keys, queries) * (score_scale * log2e) + bias[:, rows]
                top = jnp.max(scores, axis=0, keepdims=True)
                probs = jnp.exp2(scores - top)
                total = jnp.sum(probs, axis=0, keepdims=True)
                result = dot(values, probs.astype(bf16)) / total
                spot = pl.ds(
                    pl.multiple_of(me * (OWN_HEADS * HEAD_DIM) + head * HEAD_DIM, HEAD_DIM), HEAD_DIM
                )
                att[layer, spot, rows] = result.astype(bf16)
                lse[layer, head:head + 1, rows] = top + jnp.log(total) * log2e
                return carry

            lax.fori_loop(0, seq // size, attend, 0)

            def features(block, head=head, layer=layer):
                start = block * (OWN_HEADS * HEAD_DIM) + head * HEAD_DIM
                return att.at[layer, pl.ds(pl.multiple_of(start, HEAD_DIM), HEAD_DIM)]

            own, theirs = features(me), features(across)
            to_across = push(own, own, sems, layer, 6 + head, across)
            to_mate = push(own, own, sems, layer, 9 + head, mate)
            onward = push(theirs, theirs, sems, layer, 12 + head, mate)
            to_across.start()
            to_mate.start()
            if head:
                sends[-2].wait_recv()
                forwards[-1].start()
            if spreading and head == 0:
                weights[PIECES * layer + 1].share()
            pump(2)
            sends += [to_across, to_mate]
            forwards.append(onward)
        sends[-2].wait_recv()
        forwards[-1].start()
        for head in range(OWN_HEADS):
            sends[2 * head + 1].wait_recv()
            forwards[head].wait_recv()
        store(2, layer, lse, lse_out)
        store(3, layer, att, att_out)
        pump(6 - 2 * layer)
        if layer == 0:
            gain_stage(1)
        for number in range(1, PIECES):
            weights[PIECES * layer + number].wait()
        for number, held in enumerate((wq, wo, wg, wd)):
            store(12 + number, layer, held, weight_outs[number])

        def feed(block, keep, layer=layer):
            rows = rows_of(block, size, size)
            branch = dot_tn(att[layer, :, rows], wo[layer])
            normed, inverse = normed_rows(xf[layer, rows, :].astype(f32) + branch)
            first_rows = normed * gain[2 * layer:2 * layer + 1, :]
            if keep:
                n1[layer] = normed
                s1[layer] = jnp.broadcast_to(inverse, s1.shape[1:])
                first[...] = first_rows
            first_low = first_rows.astype(bf16)
            flow[layer, rows, :] = first_low
            gate_up = dot(first_low, wg[layer])
            gate, upward = gate_up[:, :ff], gate_up[:, ff:]
            gu[layer, rows, :] = gate_up.astype(bf16)
            hidden = (gate / (1.0 + jnp.exp(-gate)) * upward).astype(bf16)
            hid[layer, rows, :] = hidden
            return dot_nt(hidden, wd[layer])

        scatter = Scatter(part, layer, got, layer, sems, 15, where)
        scatter.send_far(feed(far, False))
        pump(2)
        scatter.send_across(feed(across, False))
        pump(2)
        scatter.send_mate(feed(mate, False))
        pump(2)
        own_part = feed(me, True)
        pump(2)
        store(4, layer, flow, flow_out)
        store(5, layer, gu, gu_out)
        store(6, layer, hid, hid_out)
        store(7, layer, n1, n1_out)
        store(8, layer, s1, s1_out)
        pump(2)
        ffn = scatter.total(own_part)
        pending.append(scatter)
        normed, inverse = normed_rows(first[...] + ffn)
        n2[layer] = normed
        s2[layer] = jnp.broadcast_to(inverse, s2.shape[1:])
        result = (normed * gain[2 * layer + 1:2 * layer + 2, :]).astype(bf16)
        store(9, layer, n2, n2_out)
        store(10, layer, s2, s2_out)
        if layer + 1 < LAYERS:
            xf[layer + 1, rows_of(me, size, size), :] = result
            row_gather = Gather(xf, layer + 1, layer + 1, sems, 0, size, where)
            row_gather.start()
            pump(2)
        else:
            act[...] = result
            copy = pltpu.make_async_copy(act, act_out, osems.at[0, 11])
            copy.start()
            stores.append(copy)
        for copy in sends + forwards:
            copy.wait_send()
    if spreading:
        pending += weights
    for item in pending:
        item.finish()
    for copy in stores:
        copy.wait()


BACK_LOADED = (
    "n1", "s1", "n2", "s2", "xf", "qkv", "lse", "att", "flow", "gu", "hid", "wq", "wo", "wg", "wd",
)
BACK_TABLES = ("gain", "cos_rows", "sin_rows", "doc_keys", "doc_queries")
BACK_SCRATCH = (
    "bias", "dff", "dbr", "datt", "dproj", "dk", "dv", "dqt", "kt", "k2", "grad", "part", "got",
    "gq", "go", "gg", "gd", "sems", "lsems", "osems",
)
BACK_SPREAD = (
    "gsum", "gpack", "gside", "gdeep", "gsems", "csems", "qshare", "oshare",
    "near_d", "near_g", "near_u", "near_q", "near_o",
    "apart_d", "apart_g", "apart_u", "apart_q", "apart_o",
    "sum_d", "sum_g", "sum_u", "sum_q", "sum_o", "dsems",
)


def backward_kernel(spreading, names, *refs):
    r = dict(zip(names, refs))
    cot = r["cot"]
    gain, cos_rows, sin_rows, doc_keys, doc_queries = (r[n] for n in BACK_TABLES)
    (
        bias, dff, dbr, datt, dproj, dk, dv, dqt, kt, k2, grad, part, got,
        gq, go, gg, gd, sems, lsems, osems,
    ) = (r[n] for n in BACK_SCRATCH)
    n1, s1, n2, s2, qkv, lse, att, gu, hid, wq, wo, wg, wd = (
        r[n] for n in BACK_LOADED if n not in ("xf", "flow")
    )
    xf = flow = r["rows"]
    where = places()
    me, mate, across, far, core = where
    size = cot.shape[0]
    seq = size * GROUP
    ff = hid.shape[1]
    feats = xf.shape[1]
    own_feats = OWN_HEADS * HEAD_DIM
    held = {n: (r[n + "_in"], r.get(n, r["rows"])) for n in BACK_LOADED}
    order = list(held)
    loads = {}

    def load(name, layer):
        if layer < 0:
            return
        source, target = held[name]
        copy = pltpu.make_async_copy(source.at[layer], target, lsems.at[order.index(name)])
        copy.start()
        loads[name] = copy

    for name in ("n2", "s2", "wd", "gu", "wg", "hid", "n1", "s1", "flow", "wo", "qkv", "lse", "att", "wq"):
        load(name, LAYERS - 1)
    spread = Spread(feats // (2 * DEPTH)) if spreading else None
    greet(mate, across, far if spreading else None, spread)
    write_bias(bias, doc_keys, doc_queries)
    low_mask, high_mask = half_masks()
    grad[...] = cot[...]
    pending = []
    scatters = []
    stores = {}
    sums = {}
    shares = []
    pieces = dict(
        d=gd.at[:, :], g=gg.at[:, :ff], u=gg.at[:, ff:], q=gq.at[:, :], o=go.at[:, :]
    )
    gsum = r["gsum"] if spreading else r["gain_out"]
    gsum[...] = jnp.zeros_like(gsum)

    def begin(name, layer):
        if not spreading:
            if name == "u":
                store(2, layer, gg, r["g_out"])
            elif name != "g":
                number = "qogd".index(name)
                store(number, layer, (gq, go, gg, gd)[number], r[name + "_out"])
            return
        index = "dguqo".index(name)
        item = WeightSum(
            pieces[name], r["near_" + name], r["apart_" + name], 5 * layer + index, r["dsems"],
            spread, (r["csems"].at[0, index], r["csems"].at[1, index]),
            layer < LAYERS - 1, layer > 0, r["sum_" + name],
        )
        item.start()
        sums[name, layer] = item

    def add(name, layer):
        if spreading and (name, layer) in sums:
            sums[name, layer].add()

    def total(name, layer):
        if not spreading or (name, layer) not in sums:
            return
        result = sums[name, layer].total()
        if name == "q":
            share = Share(r["qshare"], layer, sems, 15, where)
            share.start(result.astype(bf16))
            shares.append(share)
        elif name == "o":
            oshare = r["oshare"]
            oshare[layer, core] = result.astype(bf16)
            copy = push(oshare.at[layer, core], oshare.at[layer, core], sems, layer, 18, mate)
            copy.start()
            oshares.append(copy)
        elif name == "d":
            r["d_res"][layer] = result
        else:
            half = "gu".index(name)
            r["g_res"][layer, :, half * ff:(half + 1) * ff] = result

    def ready(name, layer):
        if not spreading:
            if name != "u":
                stored("qogd".index(name))
        elif (name, layer + 1) in sums:
            sums[name, layer + 1].finish()

    oshares = []
    gains = []

    def gain_stage(stage):
        if not spreading:
            return
        gpack, gside, gdeep, gsems = (r[n] for n in ("gpack", "gside", "gdeep", "gsems"))
        if stage == 0:
            gpack[me] = gsum[...]
            for number, who in enumerate((mate, across, far)):
                gains.append(push(gpack.at[me], gpack.at[me], gsems, 0, number, who))
        elif stage == 1:
            for copy in gains[:3]:
                copy.wait_recv()
            gside[spread.x] = gpack[0] + gpack[1] + gpack[2] + gpack[3]
            own = gside.at[spread.x]
            gains.append(ship(own, own, gsems, 0, 3, spread.beside(0)))
        elif stage == 2:
            gains[3].wait_recv()
            gdeep[spread.z] = gside[0] + gside[1]
            own = gdeep.at[spread.z]
            for step in range(1, DEPTH):
                gains.append(ship(own, own, gsems, 0, 3 + step, spread.device(step)))
        else:
            for copy in gains[4:]:
                copy.wait_recv()
            r["gain_out"][...] = gdeep[0] + gdeep[1] + gdeep[2] + gdeep[3]
            for copy in gains:
                copy.wait_send()
            return
        for copy in gains[(0, 3, 4)[stage]:]:
            copy.start()

    def store(number, layer, source, target):
        copy = pltpu.make_async_copy(source, target.at[layer], osems.at[layer, number])
        copy.start()
        stores[number] = copy

    def stored(number):
        if number in stores:
            stores.pop(number).wait()

    for layer in range(LAYERS - 1, -1, -1):

        def norm_back(grad_rows, normed, inverse, row, layer=layer):
            gsum[2 * layer + row:2 * layer + row + 1, :] = jnp.sum(
                grad_rows * normed, axis=0, keepdims=True
            )
            scaled = grad_rows * gain[2 * layer + row:2 * layer + row + 1, :]
            return (
                scaled
                - jnp.mean(scaled, axis=-1, keepdims=True)
                - normed * jnp.mean(scaled * normed, axis=-1, keepdims=True)
            ) * inverse

        loads["n2"].wait()
        loads["s2"].wait()
        dz = norm_back(grad[...], n2[...], s2[:, :1], 1)
        load("n2", layer - 1)
        load("s2", layer - 1)
        grad[...] = dz
        dff[0, rows_of(me, size, size), :] = dz.astype(bf16)
        gather = Gather(dff, 0, layer, sems, 0, size, where)
        gather.start()
        for name in ("wd", "gu", "wg"):
            loads[name].wait()

        def feed_back(block, layer=layer):
            rows = rows_of(block, size, size)
            grad_hidden = dot(dff[0, rows, :], wd[...])
            gate = gu[rows, :ff].astype(f32)
            upward = gu[rows, ff:].astype(f32)
            sigma = 1.0 / (1.0 + jnp.exp(-gate))
            up_grad = grad_hidden * gate * sigma
            gate_grad = grad_hidden * upward * sigma * (1.0 + gate * (1.0 - sigma))
            gu[rows, :ff] = gate_grad.astype(bf16)
            gu[rows, ff:] = up_grad.astype(bf16)
            return dot_nt(gu[rows, :], wg[...])

        if len(scatters) > 1:
            scatters[-2].finish()
        scatter = Scatter(part, 0, got, 2 * layer, sems, 6, where)
        scatters.append(scatter)
        own_part = feed_back(me)
        gather.wait_mate()
        scatter.send_mate(feed_back(mate))
        gather.wait_across()
        across_part = feed_back(across)
        gather.wait_far()
        scatter.send_far(feed_back(far))
        scatter.send_across(across_part)
        load("wd", layer - 1)
        load("wg", layer - 1)
        loads["hid"].wait()
        add("q", layer + 1)
        ready("d", layer)

        def down_weight(i, carry, layer=layer):
            cols = rows_of(i, 256, 256)
            gd[cols, :] = dot_tn(dff[0, :, cols], hid[...]).astype(bf16)
            return carry

        lax.fori_loop(0, feats // 256, down_weight, 0)
        begin("d", layer)
        gather.finish()
        load("hid", layer - 1)
        add("o", layer + 1)

        dfirst = grad[...] + scatter.total(own_part)
        loads["n1"].wait()
        loads["s1"].wait()
        dr = norm_back(dfirst, n1[...], s1[:, :1], 0)
        load("n1", layer - 1)
        load("s1", layer - 1)
        grad[...] = dr
        dbr[layer, rows_of(me, size, size), :] = dr.astype(bf16)
        gather = Gather(dbr, layer, layer, sems, 9, size, where)
        gather.start()
        loads["flow"].wait()

        if layer == 0:
            gain_stage(0)
        for name, first_col in (("g", 0), ("u", ff)):
            ready(name, layer)

            def gate_up_weight(i, carry, first_col=first_col):
                cols = rows_of(i, 256, 256)
                gg[cols, first_col:first_col + ff] = dot_tn(
                    flow[:, cols], gu[:, first_col:first_col + ff]
                ).astype(bf16)
                return carry

            lax.fori_loop(0, feats // 256, gate_up_weight, 0)
            begin(name, layer)
        load("gu", layer - 1)
        load("xf", layer)
        for name in "dgu":
            total(name, layer + 1)

        loads["wo"].wait()

        def weigh_out(layer):
            loads["att"].wait()
            ready("o", layer)

            def out_weight(i, carry):
                rows = rows_of(i, 256, 256)
                half = feats // 2
                cols = pl.ds(pl.multiple_of(core * half, half), half)
                go[rows, :] = dot(att[rows, :], dbr[layer, :, cols]).astype(bf16)
                return carry

            lax.fori_loop(0, feats // 256, out_weight, 0)
            begin("o", layer)
            load("att", layer - 1)

        def att_back(block, layer=layer):
            rows = rows_of(block, size, size)
            for tile, start in enumerate((0, HEAD_DIM)):
                spot = pl.ds(pl.multiple_of(me * own_feats + start, HEAD_DIM), TILE)
                datt[rows, tile * TILE:(tile + 1) * TILE] = dot_nt(
                    dbr[layer, rows, :], wo[spot, :]
                ).astype(bf16)

        att_back(me)
        gather.wait_mate()
        att_back(mate)
        gather.wait_across()
        att_back(across)
        gather.wait_far()
        att_back(far)
        pending.append(gather)
        load("wo", layer - 1)
        if layer == 0:
            weigh_out(layer)
            gain_stage(1)
            add("d", layer)
        total("q", layer + 1)
        total("o", layer + 1)

        loads["qkv"].wait()
        loads["lse"].wait()
        kt[0] = qkv[:, TILE:2 * TILE].T
        kt[1] = qkv[:, 3 * TILE:4 * TILE].T
        k2[...] = pltpu.roll(qkv[:, 3 * TILE:4 * TILE].astype(f32), HEAD_DIM, 1).astype(bf16)
        dk[...] = jnp.zeros_like(dk)
        dv[...] = jnp.zeros_like(dv)
        for head in range(OWN_HEADS):
            tile = head // 2
            query_tile = (0, 0, 3)[head]
            value_tile = (2, 2, 4)[head]
            query_mask = (low_mask, high_mask, low_mask)[head]
            value_mask = (low_mask, high_mask, high_mask)[head]

            def attend(i, carry, head=head, tile=tile, query_tile=query_tile, value_tile=value_tile,
                       query_mask=query_mask, value_mask=value_mask):
                rows = rows_of(i, size, size)
                queries = qkv[rows, query_tile * TILE:(query_tile + 1) * TILE] * query_mask
                keys = k2[...] if head == 2 else qkv[:, TILE:2 * TILE]
                scores = dot_nt(keys, queries) * (score_scale * log2e) + bias[:, rows]
                probs = jnp.exp2(scores - lse[head:head + 1, rows])
                outs = datt[rows, tile * TILE:(tile + 1) * TILE] * value_mask
                grad_probs = dot_nt(qkv[:, value_tile * TILE:(value_tile + 1) * TILE], outs)
                delta = jnp.sum(probs * grad_probs, axis=0, keepdims=True)
                grad_scores = (probs * (grad_probs - delta)).astype(bf16)
                dv[tile] = dv[tile] + dot(probs.astype(bf16), outs)
                dk[tile] = dk[tile] + dot(grad_scores, queries)
                keys_t = (kt.at[0, :HEAD_DIM], kt.at[0, HEAD_DIM:], kt.at[1, HEAD_DIM:])[head][...]
                spot = (0, HEAD_DIM, 0)[head]
                dqt[tile, spot:spot + HEAD_DIM, rows] = dot(keys_t, grad_scores)
                return carry

            lax.fori_loop(0, seq // size, attend, 0)
            if head == 0:
                add("g" if layer == 0 else "d", layer)
                for share in shares:
                    share.serve()
            if head == 1 and layer:
                add("g", layer)
            if layer == 0 and head < 2:
                gain_stage(2 + head)


        def unrotate(i, carry):
            rows = rows_of(i, size, size)
            c, s = cos_rows[rows, :], -sin_rows[rows, :]
            dproj[rows, :TILE] = turn(dqt[0, :, rows].T * score_scale, c, s).astype(bf16)
            dproj[rows, TILE:2 * TILE] = turn(dk[0, rows, :] * score_scale, c, s).astype(bf16)
            dproj[rows, 2 * TILE:3 * TILE] = dv[0, rows, :].astype(bf16)
            lower = lane_iota((size, TILE)) < HEAD_DIM
            mixed = jnp.where(lower, dqt[1, :, rows].T, pltpu.roll(dk[1, rows, :], HEAD_DIM, 1))
            dproj[rows, 3 * TILE:4 * TILE] = turn(mixed * score_scale, c, s).astype(bf16)
            dproj[rows, 4 * TILE:] = dv[1, rows, :].astype(bf16)
            return carry

        lax.fori_loop(0, seq // size, unrotate, 0)
        if layer == 0:
            add("u", layer)
        load("qkv", layer - 1)
        load("lse", layer - 1)
        loads["wq"].wait()

        def input_part(block):
            return dot_nt(dproj[rows_of(block, size, size), :], wq[...])

        if len(scatters) > 1:
            scatters[-2].finish()
        scatter = Scatter(part, 1, got, 2 * layer + 1, sems, 6, where)
        scatters.append(scatter)
        scatter.send_far(input_part(far))
        scatter.send_across(input_part(across))
        scatter.send_mate(input_part(mate))
        own_part = input_part(me)
        load("wq", layer - 1)
        loads["xf"].wait()

        ready("q", layer)

        def qkv_weight(i, carry, layer=layer):
            cols = rows_of(i, 256, 256)
            gq[cols, :] = dot_tn(xf[:, cols], dproj[...]).astype(bf16)
            return carry

        lax.fori_loop(0, feats // 256, qkv_weight, 0)
        begin("q", layer)
        if layer:
            add("u", layer)
        else:
            add("o", layer)
        load("flow", layer - 1)
        if layer:
            weigh_out(layer)
        grad[...] = grad[...] + scatter.total(own_part)
    input_copy = pltpu.make_async_copy(grad, r["ig_out"], osems.at[0, 4])
    input_copy.start()
    for name in "dguo":
        total(name, 0)
    add("q", 0)
    total("q", 0)
    if spreading:
        shares[-1].serve()
    input_copy.wait()
    for item in pending + scatters[-2:]:
        item.finish()
    for number in range(4):
        stored(number)
    for item in shares:
        item.finish()
    for copy in oshares:
        copy.wait()
    if spreading:
        for name in "dguqo":
            sums[name, 0].finish()
        for number, held in enumerate(((r["qshare"], r["q_out"]), (r["oshare"], r["o_out"]))):
            copy = pltpu.make_async_copy(*held, osems.at[1, number])
            copy.start()
            copy.wait()


RATES = ((0.03, 0.01), (0.5, 0.01), (0.03, 0.01), (0.02, 0.01), (0.6, 0.0))


def adam_step(weight, first, second, average, gradient, rate, decay):
    first_new = beta_first * first + (1.0 - beta_first) * gradient
    second_new = beta_second * second + (1.0 - beta_second) * gradient * gradient
    first_hat = first_new / (1.0 - beta_first**STEP)
    second_hat = second_new / (1.0 - beta_second**STEP)
    weight_new = weight - rate * (
        first_hat / (jnp.sqrt(second_hat) + adam_epsilon) + decay * weight
    )
    average_new = average_decay * average + (1.0 - average_decay) * weight_new
    return first_new, second_new, weight_new, average_new


def adam_kernel(*refs):
    states = [refs[4 * f:4 * f + 4] for f in range(5)]
    grads = refs[20:25]
    outs = [refs[25 + 5 * f:30 + 5 * f] for f in range(5)]
    (qs, os, ds, gs, qg, og, gg, qb, ob, gb, db, gsems, isems, usems) = refs[50:]
    width = ob.shape[3]
    for number, target in enumerate((qs, os, gs, ds)):
        pltpu.make_async_copy(grads[number], target, gsems.at[number]).start()
    chunks = []
    for family, held, grad in ((3, db, ds), (2, gb, gg), (1, ob, og), (0, qb, qg)):
        for layer in range(LAYERS):
            for part in range(3 if family == 0 else 1):
                spot = 3 * layer + part if family == 0 else layer
                chunks.append((family, held, grad, layer, part, spot))

    def view(ref, family, layer, part):
        if family:
            return ref.at[layer]
        return ref.at[layer, :, pl.ds(part * width, width)]

    arrivals = []
    for number, (family, held, grad, layer, part, spot) in enumerate(chunks):
        copies = [
            pltpu.make_async_copy(
                view(states[family][k], family, layer, part), held.at[k, spot], isems.at[number, k]
            )
            for k in range(4)
        ]
        for copy in copies:
            copy.start()
        arrivals.append(copies)

    def wait_grad(number, target):
        pltpu.make_async_copy(grads[number], target, gsems.at[number]).wait()

    gain = [ref[...] for ref in states[4]]
    gradient = grads[4][...]
    new = adam_step(*gain, gradient, *RATES[4])
    for ref, value in zip(outs[4], (gradient,) + new):
        ref[...] = value

    low = lane_iota((qs.shape[2], TILE)) < HEAD_DIM
    leaving = []
    for number, (family, held, grad, layer, part, spot) in enumerate(chunks):
        first_of = layer == 0 and part == 0
        if family == 3 and first_of:
            wait_grad(3, ds)
        if family == 2:
            if first_of:
                wait_grad(2, gs)
            for half in range(2):
                gg[layer, :, half, :] = gs[layer, :, half * width:(half + 1) * width]
        if family == 1:
            if first_of:
                wait_grad(1, os)
            half = width // 2
            og[layer, :, :half] = os[layer, 0].astype(f32)
            og[layer, :, half:] = os[layer, 1].astype(f32)
        if family == 0:
            if first_of:
                wait_grad(0, qs)

            def pair(j):
                return qs[layer, j, :, part * TILE:(part + 1) * TILE].astype(f32)

            def last(j, upper):
                tile = 4 if part == 2 else 3
                value = qs[layer, j, :, tile * TILE:(tile + 1) * TILE].astype(f32)
                return value if upper == (part > 0) else pltpu.roll(value, HEAD_DIM, 1)

            for j in (0, 2):
                turned = pltpu.roll(pair(j + 1), HEAD_DIM, 1)
                tiles = (
                    pair(j),
                    jnp.where(low, last(j, False), turned),
                    jnp.where(low, turned, last(j + 1, True)),
                )
                for k, value in enumerate(tiles):
                    start = (3 * (j // 2) + k) * TILE
                    qg[spot, :, start:start + TILE] = value
        for copy in arrivals[number]:
            copy.wait()
        rows = 32

        def body(i, carry, family=family, held=held, grad=grad, spot=spot):
            at = pl.ds(pl.multiple_of(i * rows, rows), rows)
            values = [held[k, spot, at] for k in range(4)]
            first, second, weight, average = adam_step(*values, grad[spot, at], *RATES[family])
            for k, value in enumerate((weight, first, second, average)):
                held[k, spot, at] = value
            return carry

        lax.fori_loop(0, ob.shape[2] // rows, body, 0)
        sources = (grad.at[spot],) + tuple(held.at[k, spot] for k in (1, 2, 0, 3))
        for k, source in enumerate(sources):
            copy = pltpu.make_async_copy(
                source, view(outs[family][k], family, layer, part), usems.at[number, k]
            )
            copy.start()
            leaving.append(copy)
    for copy in leaving:
        copy.wait()


def pack_documents(length_row, mask_row):
    seq = mask_row.shape[0]
    ends = jnp.cumsum(length_row)
    spots = jnp.arange(seq, dtype=jnp.int32)
    past = spots[:, None] >= ends[None, :]
    number = jnp.sum(past.astype(jnp.int32), axis=1)
    starts = jnp.max(jnp.where(past, ends[None, :], 0), axis=1)
    position = spots - starts
    keys = jnp.where(mask_row == 1, number, -1)
    doc_keys = jnp.broadcast_to(keys[:, None], (seq, 128))
    doc_queries = jnp.broadcast_to(number[None, :], (8, seq))
    half = HEAD_DIM // 2
    freq = jnp.power(rotary_base, -2.0 * jnp.arange(half).astype(f32) / HEAD_DIM)
    angle = position.astype(f32)[:, None] * freq
    c, s = jnp.cos(angle), jnp.sin(angle)
    cos_rows = jnp.concatenate([c, c, c, c], axis=1)
    sin_rows = jnp.concatenate([-s, s, -s, s], axis=1)
    return cos_rows, sin_rows, doc_keys, doc_queries


def own_projection(weight, me):
    layers, rows, _ = weight.shape
    split = weight.reshape(layers, rows, 3, HEADS * HEAD_DIM)
    own = lax.dynamic_slice_in_dim(split, me * OWN_HEADS * HEAD_DIM, OWN_HEADS * HEAD_DIM, 3)
    own = own.astype(bf16)
    pairs = own[..., :TILE].reshape(layers, rows, 3 * TILE)
    last = own[..., TILE:]
    return jnp.concatenate(
        [pairs, last[:, :, 0], last[:, :, 1], jnp.zeros_like(last[:, :, 0]), last[:, :, 2]], axis=-1
    )


def whole_projection(grad):
    group, layers, rows, _ = grad.shape
    pairs = grad[..., :3 * TILE].reshape(group, layers, rows, 3, TILE)
    last = jnp.stack(
        [
            grad[..., 3 * TILE:3 * TILE + HEAD_DIM],
            grad[..., 3 * TILE + HEAD_DIM:4 * TILE],
            grad[..., 4 * TILE + HEAD_DIM:],
        ],
        axis=3,
    )
    full = jnp.concatenate([pairs, last], axis=-1)
    return full.transpose(1, 2, 3, 0, 4).reshape(layers, rows, 3 * HEADS * HEAD_DIM)


def run_forward(spreading, tokens, weights, gain, tables):
    size, feats = tokens.shape
    seq = size * GROUP
    ff = weights[3].shape[2]
    shapes = dict(
        act=((size, feats), bf16),
        xf=((LAYERS, seq, feats), bf16),
        qkv=((LAYERS, seq, PROJ), bf16),
        lse=((LAYERS, 8, seq), f32),
        att=((LAYERS, feats, seq), bf16),
        flow=((LAYERS, seq, feats), bf16),
        gu=((LAYERS, seq, 2 * ff), bf16),
        hid=((LAYERS, seq, ff), bf16),
        n1=((LAYERS, size, feats), f32),
        s1=((LAYERS, size, 128), f32),
        n2=((LAYERS, size, feats), f32),
        s2=((LAYERS, size, 128), f32),
        wq=((LAYERS, feats, PROJ), bf16),
        wo=((LAYERS, feats, feats), bf16),
        wg=((LAYERS, feats, 2 * ff), bf16),
        wd=((LAYERS, feats, ff), bf16),
        gain=((8, feats), f32),
    )
    held = {name: pltpu.VMEM(*shape) for name, shape in shapes.items()}
    scratch = [held[n] for n in ("wq", "wo", "wg", "wd", "xf", "qkv", "att", "flow", "gu", "hid")]
    scratch += [
        pltpu.VMEM((seq, seq), f32),
        pltpu.VMEM((2, TILE, seq), bf16),
        pltpu.VMEM((seq, TILE), bf16),
        held["lse"],
    ]
    scratch += [held[n] for n in ("n1", "s1", "n2", "s2")]
    scratch += [
        pltpu.VMEM((size, feats), f32),
        held["act"],
        pltpu.VMEM((LAYERS, 3, size, feats), bf16),
        pltpu.VMEM((LAYERS, 3, size, feats), bf16),
        pltpu.SemaphoreType.DMA((2, LAYERS, 18)),
        pltpu.SemaphoreType.DMA((LAYERS, PIECES)),
        pltpu.SemaphoreType.DMA((LAYERS, 16)),
        pltpu.SemaphoreType.DMA((2, PIECES * LAYERS, 3 + 2 * DEPTH)),
        pltpu.SemaphoreType.DMA((2, LAYERS, 7)),
        pltpu.VMEM((2, 8, feats), f32),
        pltpu.VMEM((DEPTH, 8, feats), f32),
        pltpu.SemaphoreType.DMA((2, 1, DEPTH)),
    ]
    return pl.pallas_call(
        functools.partial(forward_kernel, spreading),
        out_shape=[jax.ShapeDtypeStruct(*shape) for shape in shapes.values()],
        in_specs=[VMEM] + [ANY] * 4 + [VMEM] * 5,
        out_specs=[ANY] * (len(shapes) - 1) + [VMEM],
        scratch_shapes=scratch,
        compiler_params=pltpu.CompilerParams(
            collective_id=0, has_side_effects=True, vmem_limit_bytes=VMEM_LIMIT
        ),
        cost_estimate=pl.CostEstimate(
            flops=12 * 10**9, bytes_accessed=60 * 10**6, transcendentals=10**7
        ),
        name="forward",
    )(tokens, *weights, gain, *tables)


def run_backward(spreading, cotangent, kept, weights, gain, tables):
    size, feats = cotangent.shape
    seq = size * GROUP
    xf, qkv, lse, att, flow, gu, hid, n1, s1, n2, s2 = kept
    ff = hid.shape[2]
    wq, wo, wg, wd = weights
    loaded = [n1, s1, n2, s2, xf, qkv, lse, att, flow, gu, hid, wq, wo, wg, wd]
    own = feats // (2 * DEPTH)
    half = feats // 2
    widths = dict(d=ff, g=ff, u=ff, q=PROJ, o=half)
    if spreading:
        outs = dict(
            ig_out=((size, feats), f32),
            q_out=((LAYERS, GROUP, own, PROJ), bf16),
            o_out=((LAYERS, 2, own, half), bf16),
            d_res=((LAYERS, own, ff), f32),
            g_res=((LAYERS, own, 2 * ff), f32),
            gain_out=((8, feats), f32),
        )
    else:
        outs = dict(
            ig_out=((size, feats), f32),
            q_out=(wq.shape, bf16),
            o_out=((LAYERS, feats, half), bf16),
            d_out=(wd.shape, bf16),
            g_out=(wg.shape, bf16),
            gain_out=((8, feats), f32),
        )
    names = ["cot"] + [n + "_in" for n in BACK_LOADED] + list(BACK_TABLES) + list(outs)
    scratch = dict(
        bias=pltpu.VMEM((seq, seq), f32),
        dff=pltpu.VMEM((1, seq, feats), bf16),
        dbr=pltpu.VMEM((LAYERS, seq, feats), bf16),
        datt=pltpu.VMEM((seq, 2 * TILE), bf16),
        dproj=pltpu.VMEM((seq, PROJ), bf16),
        dk=pltpu.VMEM((2, seq, TILE), f32),
        dv=pltpu.VMEM((2, seq, TILE), f32),
        dqt=pltpu.VMEM((2, TILE, seq), f32),
        kt=pltpu.VMEM((2, TILE, seq), bf16),
        k2=pltpu.VMEM((seq, TILE), bf16),
        grad=pltpu.VMEM((size, feats), f32),
        part=pltpu.VMEM((2, 3, size, feats), bf16),
        got=pltpu.VMEM((2, 3, size, feats), bf16),
        gq=pltpu.VMEM((feats, PROJ), bf16),
        go=pltpu.VMEM((feats, half), bf16),
        gg=pltpu.VMEM((feats, 2 * ff), bf16),
        gd=pltpu.VMEM((feats, ff), bf16),
        sems=pltpu.SemaphoreType.DMA((2, 2 * LAYERS, 19)),
        lsems=pltpu.SemaphoreType.DMA((len(loaded),)),
        osems=pltpu.SemaphoreType.DMA((LAYERS, 5)),
        rows=pltpu.VMEM((seq, feats), bf16),
    )
    for name, array in zip(BACK_LOADED, loaded):
        if name not in ("xf", "flow"):
            scratch[name] = pltpu.VMEM(array.shape[1:], array.dtype)
    if spreading:
        scratch.update(
            gsum=pltpu.VMEM((8, feats), f32),
            gpack=pltpu.VMEM((GROUP, 8, feats), f32),
            gside=pltpu.VMEM((2, 8, feats), f32),
            gdeep=pltpu.VMEM((DEPTH, 8, feats), f32),
            gsems=pltpu.SemaphoreType.DMA((2, 1, 7)),
            csems=pltpu.SemaphoreType.REGULAR((2, 5)),
            qshare=pltpu.VMEM((LAYERS, GROUP, own, PROJ), bf16),
            oshare=pltpu.VMEM((LAYERS, 2, own, half), bf16),
            dsems=pltpu.SemaphoreType.DMA((2, 5 * LAYERS, 7)),
        )
        for name, width in widths.items():
            scratch["near_" + name] = pltpu.VMEM((DEPTH, own, width), bf16)
            scratch["apart_" + name] = pltpu.VMEM((DEPTH - 1, own, width), bf16)
            scratch["sum_" + name] = pltpu.VMEM((own, width), f32)
    in_vmem = ("d_res", "g_res", "gain_out")
    return pl.pallas_call(
        functools.partial(backward_kernel, spreading, tuple(names + list(scratch))),
        out_shape=[jax.ShapeDtypeStruct(*shape) for shape in outs.values()],
        in_specs=[VMEM] + [ANY] * 15 + [VMEM] * 5,
        out_specs=[VMEM if name in in_vmem else ANY for name in outs],
        scratch_shapes=list(scratch.values()),
        compiler_params=pltpu.CompilerParams(
            collective_id=1, has_side_effects=True, vmem_limit_bytes=VMEM_LIMIT
        ),
        cost_estimate=pl.CostEstimate(
            flops=24 * 10**9, bytes_accessed=60 * 10**6, transcendentals=10**7
        ),
        name="backward",
    )(cotangent, *loaded, gain, *tables)


def run_adam(states, grads):
    outs = []
    for family in range(5):
        shape = jax.ShapeDtypeStruct(states[4 * family].shape, f32)
        outs += [shape] * 5
    layers, own, _, width = states[8].shape
    scratch = [
        pltpu.VMEM(grads[0].shape, bf16),
        pltpu.VMEM(grads[1].shape, bf16),
        pltpu.VMEM(grads[3].shape, f32),
        pltpu.VMEM(grads[2].shape, f32),
        pltpu.VMEM((3 * layers, own, width), f32),
        pltpu.VMEM((layers, own, width), f32),
        pltpu.VMEM((layers, own, 2, width), f32),
        pltpu.VMEM((4, 3 * layers, own, width), f32),
        pltpu.VMEM((4, layers, own, width), f32),
        pltpu.VMEM((4, layers, own, 2, width), f32),
        pltpu.VMEM((4, layers, own, width), f32),
        pltpu.SemaphoreType.DMA((4,)),
        pltpu.SemaphoreType.DMA((6 * layers, 4)),
        pltpu.SemaphoreType.DMA((6 * layers, 5)),
    ]
    return pl.pallas_call(
        adam_kernel,
        out_shape=outs,
        in_specs=[ANY] * 16 + [VMEM] * 4 + [ANY] * 4 + [VMEM],
        out_specs=[ANY] * 20 + [VMEM] * 5,
        scratch_shapes=scratch,
        compiler_params=pltpu.CompilerParams(vmem_limit_bytes=VMEM_LIMIT),
        cost_estimate=pl.CostEstimate(
            flops=2 * 10**7, bytes_accessed=37 * 10**6, transcendentals=10**6
        ),
        name="adam",
    )(*states, *grads)


def adamw(weight, first, second, average, gradient, rate, decay):
    first_new = beta_first * first + (1.0 - beta_first) * gradient
    second_new = beta_second * second + (1.0 - beta_second) * gradient * gradient
    first_hat = first_new / (1.0 - beta_first**STEP)
    second_hat = second_new / (1.0 - beta_second**STEP)
    weight_new = weight - rate * (
        first_hat / (jnp.sqrt(second_hat) + adam_epsilon) + decay * weight
    )
    average_new = average_decay * average + (1.0 - average_decay) * weight_new
    return (gradient, first_new, second_new, weight_new, average_new)


def shards(
    spreading,
    tokens,
    cotangent,
    lengths,
    key_mask,
    qkv_weight,
    qkv_first,
    qkv_second,
    qkv_average,
    out_weight,
    out_first,
    out_second,
    out_average,
    gate_up_weight,
    gate_up_first,
    gate_up_second,
    gate_up_average,
    down_weight,
    down_first,
    down_second,
    down_average,
    norm_gain,
    gain_first,
    gain_second,
    gain_average,
):
    me = lax.axis_index("mp")
    own = gate_up_weight.shape[1]
    ff = gate_up_weight.shape[3]
    feats = tokens.shape[1]
    if spreading:
        gain = jnp.zeros((8, feats), f32)
        gain = lax.dynamic_update_slice(
            gain, norm_gain.reshape(2 * LAYERS, own), (0, lax.axis_index("dp") * own)
        )
    else:
        gain = lax.all_gather(norm_gain, "dp", axis=2, tiled=True).reshape(2 * LAYERS, feats)
        gain = jnp.concatenate([gain, jnp.zeros((8 - 2 * LAYERS, feats), f32)], axis=0)
    tables = pack_documents(lengths[0], key_mask)
    owned = (
        own_projection(qkv_weight, me),
        out_weight.astype(bf16),
        gate_up_weight.reshape(LAYERS, own, 2 * ff).astype(bf16),
        down_weight.astype(bf16),
    )
    if not spreading:
        owned = [lax.all_gather(w, "dp", axis=1, tiled=True) for w in owned]
    act, *kept = run_forward(spreading, tokens, owned, gain, tables)
    weights, kept, gain = kept[-5:-1], kept[:-5], kept[-1]
    backward = run_backward(spreading, cotangent, kept, weights, gain, tables)
    if spreading:
        input_grad, gq, go, gd, gg, gain_sum = backward
        gain_grad = lax.dynamic_slice_in_dim(
            gain_sum[:2 * LAYERS].reshape(LAYERS, 2, -1), lax.axis_index("dp") * own, own, 2
        )
        states = (
            qkv_weight, qkv_first, qkv_second, qkv_average,
            out_weight, out_first, out_second, out_average,
            gate_up_weight, gate_up_first, gate_up_second, gate_up_average,
            down_weight, down_first, down_second, down_average,
            norm_gain, gain_first, gain_second, gain_average,
        )
        return (act, input_grad, *run_adam(states, (gq, go, gg, gd, gain_grad)))
    else:
        input_grad, gq, go, gd, gg, gain_sum = backward
        gq, go, gg, gd = [
            lax.psum_scatter(g, "dp", scatter_dimension=1, tiled=True) for g in (gq, go, gg, gd)
        ]
        gq, go = lax.all_gather(gq, "mp"), lax.all_gather(go, "mp")
        gain_part = gain_sum[:2 * LAYERS].reshape(LAYERS, 2, -1)
        gain_grad = lax.psum_scatter(
            lax.psum(gain_part, "mp"), "dp", scatter_dimension=2, tiled=True
        )
    qkv_grad = whole_projection(gq.astype(f32))
    out_grad = jnp.concatenate([go[0], go[1]], axis=-1).astype(f32)
    gate_up_grad = gg.reshape(LAYERS, own, 2, ff).astype(f32)
    down_grad = gd.astype(f32)
    results = [act, input_grad]
    results.extend(adamw(qkv_weight, qkv_first, qkv_second, qkv_average, qkv_grad, 0.03, 0.01))
    results.extend(adamw(out_weight, out_first, out_second, out_average, out_grad, 0.5, 0.01))
    results.extend(
        adamw(
            gate_up_weight, gate_up_first, gate_up_second, gate_up_average, gate_up_grad, 0.03, 0.01
        )
    )
    results.extend(
        adamw(down_weight, down_first, down_second, down_average, down_grad, 0.02, 0.01)
    )
    results.extend(adamw(norm_gain, gain_first, gain_second, gain_average, gain_grad, 0.6, 0.0))
    return tuple(results)


def solution(mesh):
    spreading = mesh.shape["dp"] == 2 * DEPTH
    return jax.shard_map(
        functools.partial(shards, spreading),
        mesh=mesh,
        in_specs=(
            P(("dp", "mp"), None),
            P(("dp", "mp"), None),
            P("dp", None),
            P("dp"),
            P(None, "dp", None),
            P(None, "dp", None),
            P(None, "dp", None),
            P(None, "dp", None),
            P(None, "dp", None),
            P(None, "dp", None),
            P(None, "dp", None),
            P(None, "dp", None),
            P(None, "dp", None, "mp"),
            P(None, "dp", None, "mp"),
            P(None, "dp", None, "mp"),
            P(None, "dp", None, "mp"),
            P(None, "dp", "mp"),
            P(None, "dp", "mp"),
            P(None, "dp", "mp"),
            P(None, "dp", "mp"),
            P(None, None, "dp"),
            P(None, None, "dp"),
            P(None, None, "dp"),
            P(None, None, "dp"),
        ),
        out_specs=(
            P(("dp", "mp"), None),
            P(("dp", "mp"), None),
            P(None, "dp", None),
            P(None, "dp", None),
            P(None, "dp", None),
            P(None, "dp", None),
            P(None, "dp", None),
            P(None, "dp", None),
            P(None, "dp", None),
            P(None, "dp", None),
            P(None, "dp", None),
            P(None, "dp", None),
            P(None, "dp", None, "mp"),
            P(None, "dp", None, "mp"),
            P(None, "dp", None, "mp"),
            P(None, "dp", None, "mp"),
            P(None, "dp", None, "mp"),
            P(None, "dp", "mp"),
            P(None, "dp", "mp"),
            P(None, "dp", "mp"),
            P(None, "dp", "mp"),
            P(None, "dp", "mp"),
            P(None, None, "dp"),
            P(None, None, "dp"),
            P(None, None, "dp"),
            P(None, None, "dp"),
            P(None, None, "dp"),
        ),
        check_vma=False,
    )
```

```python
import functools
import math

import jax
import jax.numpy as jnp
from jax import lax
from jax.experimental import pallas as pl
from jax.experimental.pallas import tpu as pltpu
from jax.sharding import PartitionSpec as P

HEADS = 12
HEAD_DIM = 64
LAYERS = 2
STEP = 10
GROUP = 4
DEPTH = 4
LEAD = 1
PIECES = 4
OWN_HEADS = HEADS // GROUP
TILE = 2 * HEAD_DIM
PROJ = 5 * TILE

rotary_base = 1000.0
norm_epsilon = 1e-05
masked_score = -1e30
beta_first = 0.5
beta_second = 0.5
adam_epsilon = 1e-08
average_decay = 0.5
score_scale = HEAD_DIM ** (-0.5)
log2e = math.log2(math.e)

MESH = pl.DeviceIdType.MESH
ANY = pl.BlockSpec(memory_space=pl.ANY)
VMEM = pl.BlockSpec(memory_space=pltpu.VMEM)
f32 = jnp.float32
bf16 = jnp.bfloat16
VMEM_LIMIT = 127 * 2**19


def dot(a, b):
    return jnp.dot(a, b, preferred_element_type=f32)


def dot_nt(a, b):
    return lax.dot_general(a, b, (((1,), (1,)), ((), ())), preferred_element_type=f32)


def dot_tn(a, b):
    return lax.dot_general(a, b, (((0,), (0,)), ((), ())), preferred_element_type=f32)


def places():
    me = lax.axis_index("mp")
    core = lax.rem(me, 2)
    side = lax.div(me, 2)
    return me, me + 1 - 2 * core, me + 2 - 4 * side, 3 - me, core


def push(src, dst, sems, layer, number, who):
    return pltpu.make_async_remote_copy(
        src_ref=src,
        dst_ref=dst,
        send_sem=sems.at[0, layer, number],
        recv_sem=sems.at[1, layer, number],
        device_id={"mp": who},
        device_id_type=MESH,
    )


class Spread:
    def __init__(self, own):
        index = lax.axis_index("dp")
        self.own = own
        self.z, self.x = lax.div(index, 2), lax.rem(index, 2)

    def device(self, step):
        return 2 * lax.rem(self.z + step, DEPTH) + self.x

    def beside(self, step):
        return 2 * lax.rem(self.z + step, DEPTH) + 1 - self.x

    def rows(self, index):
        return pl.ds(pl.multiple_of(index * self.own, self.own), self.own)


def greet(mate, across, far=None, spread=None):
    barrier = pltpu.get_barrier_semaphore()
    packs = [mate, across] if far is None else [mate, across, far]
    for who in packs:
        pl.semaphore_signal(barrier, inc=1, device_id={"mp": who}, device_id_type=MESH)
    others = []
    if spread is not None:
        others = [spread.beside(0)] + [spread.device(step) for step in range(1, DEPTH)]
        for who in others:
            pl.semaphore_signal(barrier, inc=1, device_id={"dp": who}, device_id_type=MESH)
    pl.semaphore_wait(barrier, len(packs) + len(others))


def ship(src, dst, sems, piece, number, who):
    return pltpu.make_async_remote_copy(
        src_ref=src,
        dst_ref=dst,
        send_sem=sems.at[0, piece, number],
        recv_sem=sems.at[1, piece, number],
        device_id={"dp": who},
        device_id_type=MESH,
    )


class WeightGather:
    def __init__(self, source, target, layer, piece, sems, local, spread, cols=None):
        self.target, self.layer, self.cols = target, layer, cols
        self.piece, self.sems, self.spread = piece, sems, spread
        z, x = spread.z, spread.x
        own = source.at[layer] if cols is None else source.at[layer, :, cols]
        place = self.view(z, x)
        self.local = pltpu.make_async_copy(own, place, local)
        self.beside = self.send(own, place, 0, 0, 2 * z + 1 - x)
        self.up = self.send(own, place, 1, 1 + z, 2 * jnp.minimum(z + 1, DEPTH - 1) + x)
        self.down = self.send(own, place, 2, 1 + z, 2 * jnp.maximum(z - 1, 0) + x)
        self.hops = [(far, way) for far in range(1, DEPTH) for way in (-1, 1)]
        self.todo = list(self.hops)

    def view(self, z, x):
        rows = self.spread.rows(2 * z + x)
        if self.cols is None:
            return self.target.at[self.layer, rows]
        return self.target.at[self.layer, rows, self.cols]

    def send(self, src, dst, out, into, who):
        return pltpu.make_async_remote_copy(
            src_ref=src,
            dst_ref=dst,
            send_sem=self.sems.at[0, self.piece, out],
            recv_sem=self.sems.at[1, self.piece, into],
            device_id={"dp": who},
            device_id_type=MESH,
        )

    def start(self):
        self.local.start()
        pl.when(self.spread.z < DEPTH - 1)(self.up.start)
        pl.when(self.spread.z > 0)(self.down.start)
        self.beside.start()

    def hop(self, far, way):
        z, x = self.spread.z, self.spread.x
        source = jnp.clip(z + way * far, 0, DEPTH - 1)
        block = self.view(source, x)
        onward = jnp.clip(z - way, 0, DEPTH - 1)
        arrive = self.send(block, block, 3 + source, 1 + source, 2 * source + x)
        over = self.send(block, block, 3 + source, 1 + DEPTH + source, 2 * z + 1 - x)
        along = self.send(block, block, 3 + DEPTH + source, 1 + source, 2 * onward + x)
        comes = z >= far if way < 0 else z + far < DEPTH
        goes = z > 0 if way > 0 else z < DEPTH - 1
        return arrive, over, along, comes, jnp.logical_and(comes, goes)

    def serve(self, count=2 * DEPTH):
        while self.todo and count:
            count -= 1
            arrive, over, along, comes, goes = self.hop(*self.todo.pop(0))

            pl.when(comes)(arrive.wait_recv)
            pl.when(goes)(along.start)
            pl.when(comes)(over.start)

    def wait(self):
        self.serve()
        self.local.wait()
        self.beside.wait_recv()
        z, x = self.spread.z, self.spread.x
        for step in range(1, DEPTH):
            source = lax.rem(z + step, DEPTH)
            block = self.view(source, 1 - x)
            self.send(block, block, 3, 1 + DEPTH + source, 2 * z + 1 - x).wait_recv()

    def finish(self):
        self.beside.wait_send()
        pl.when(self.spread.z < DEPTH - 1)(self.up.wait_send)
        pl.when(self.spread.z > 0)(self.down.wait_send)
        for far, way in self.hops:
            arrive, over, along, comes, goes = self.hop(far, way)
            pl.when(comes)(over.wait_send)
            pl.when(goes)(along.wait_send)


class HalfGather(WeightGather):
    def __init__(self, source, target, layer, piece, sems, local, spread, half, pack_sems, where):
        me, mate, across, far, core = where
        cols = pl.ds(pl.multiple_of(core * half, half), half)
        super().__init__(source, target, layer, piece, sems, local, spread, cols)
        here = spread.rows(2 * spread.z + spread.x)
        self.local = pltpu.make_async_copy(source.at[layer], target.at[layer, here], local)
        self.swap = []
        for step in range(DEPTH):
            z = lax.rem(spread.z + step, DEPTH)
            for number, x in enumerate((spread.x, 1 - spread.x)):
                if step or number:
                    block = self.view(z, x)
                    self.swap.append(
                        push(block, block, pack_sems, layer, 2 * step + number - 1, mate)
                    )

    def share(self):
        super().wait()
        for copy in self.swap:
            copy.start()

    def wait(self):
        for copy in self.swap:
            copy.wait_recv()

    def finish(self):
        super().finish()
        for copy in self.swap:
            copy.wait_send()


class WeightSum:
    def __init__(self, grad, near, apart, piece, sems, spread, credits, again, more, total):
        self.grad, self.near, self.apart, self.spread = grad, near, apart, spread
        self.near_credit, self.apart_credit = credits
        self.again, self.more = again, more
        self.sum = total
        self.beside = [
            ship(grad.at[spread.rows(spread.beside(step))], near.at[step], sems, piece, step,
                 spread.beside(0))
            for step in range(DEPTH)
        ]
        self.along = [
            ship(grad.at[spread.rows(spread.device(step))], apart.at[step - 1], sems, piece,
                 DEPTH - 1 + step, spread.device(step))
            for step in range(1, DEPTH)
        ]

    def start(self):
        if self.again:
            pl.semaphore_wait(self.near_credit, 1)
        for copy in self.beside[1:] + self.beside[:1]:
            copy.start()

    def credit(self, sem, who):
        pl.semaphore_signal(sem, inc=1, device_id={"dp": who}, device_id_type=MESH)

    def add(self):
        if self.again:
            pl.semaphore_wait(self.apart_credit, DEPTH - 1)
        for step in range(1, DEPTH):
            self.beside[step].wait_recv()
            rows = self.spread.rows(self.spread.device(step))
            self.grad[rows, :] = (
                self.grad[rows, :].astype(f32) + self.near[step].astype(f32)
            ).astype(bf16)
            self.along[step - 1].start()
        self.beside[0].wait_recv()
        rows = self.spread.rows(self.spread.device(0))
        self.sum[...] = self.grad[rows, :].astype(f32) + self.near[0].astype(f32)
        if self.more:
            self.credit(self.near_credit, self.spread.beside(0))

    def total(self):
        for copy in self.along:
            copy.wait_recv()
        result = self.sum[...]
        for step in range(DEPTH - 1):
            result = result + self.apart[step].astype(f32)
        if self.more:
            for step in range(1, DEPTH):
                self.credit(self.apart_credit, self.spread.device(step))
        return result

    def finish(self):
        for copy in self.beside + self.along:
            copy.wait_send()


def rows_of(block, size, extent):
    return pl.ds(pl.multiple_of(block * size, size), extent)


def lane_iota(shape):
    return lax.broadcasted_iota(jnp.int32, shape, len(shape) - 1)


def half_masks():
    low = (lane_iota((1, TILE)) < HEAD_DIM).astype(f32)
    return low.astype(bf16), (1.0 - low).astype(bf16)


def turn(tile, cos_rows, sin_rows):
    lane = lane_iota(tile.shape) % HEAD_DIM
    half = HEAD_DIM // 2
    partner = jnp.where(
        lane < half, pltpu.roll(tile, TILE - half, 1), pltpu.roll(tile, half, 1)
    )
    return tile * cos_rows + partner * sin_rows


def write_bias(bias, doc_keys, doc_queries):
    seq = bias.shape[0]
    step = 128

    def body(i, carry):
        rows = rows_of(i, step, step)
        keys = doc_keys[rows, :][:, :1]
        same = keys == doc_queries[:1, :]
        spot = lax.broadcasted_iota(jnp.int32, (step, seq), 0) + i * step
        own = spot == lax.broadcasted_iota(jnp.int32, (step, seq), 1)
        bias[rows, :] = jnp.where(jnp.logical_or(same, own), 0.0, masked_score)
        return carry

    lax.fori_loop(0, seq // step, body, 0)


class Gather:
    def __init__(self, ref, slot, layer, sems, first_sem, size, where):
        me, mate, across, far, core = where
        self.across, self.mate = [], []
        self.forward = []
        half = size // 2

        def piece(block, part):
            start = pl.multiple_of(block * size + part * half, half)
            return ref.at[slot, pl.ds(start, half)]

        for part in range(2):
            own = piece(me, part)
            theirs = piece(across, part)
            self.across.append(push(own, own, sems, layer, first_sem + part, across))
            self.mate.append(push(own, own, sems, layer, first_sem + 2 + part, mate))
            self.forward.append(push(theirs, theirs, sems, layer, first_sem + 4 + part, mate))

    def start(self):
        for copy in self.across + self.mate:
            copy.start()

    def wait_mate(self):
        for copy in self.mate:
            copy.wait_recv()

    def wait_across(self):
        for copy, onward in zip(self.across, self.forward):
            copy.wait_recv()
            onward.start()

    def wait_far(self):
        for copy in self.forward:
            copy.wait_recv()

    def finish(self):
        for copy in self.across + self.mate + self.forward:
            copy.wait_send()


class Share:
    def __init__(self, ref, layer, sems, first_sem, where):
        me, mate, across, far, core = where
        own, theirs = ref.at[layer, me], ref.at[layer, across]
        self.ref, self.layer, self.me = ref, layer, me
        self.over = push(own, own, sems, layer, first_sem, across)
        self.near = push(own, own, sems, layer, first_sem + 1, mate)
        self.onward = push(theirs, theirs, sems, layer, first_sem + 2, mate)

    def start(self, block):
        self.ref[self.layer, self.me] = block
        self.over.start()
        self.near.start()

    def serve(self):
        self.over.wait_recv()
        self.onward.start()

    def finish(self):
        self.near.wait_recv()
        self.onward.wait_recv()
        for copy in (self.over, self.near, self.onward):
            copy.wait_send()


class Scatter:
    def __init__(self, part, slot, got, layer, sems, first_sem, where):
        me, mate, across, far, core = where
        self.part, self.slot, self.got = part, slot, got
        self.far = push(part.at[slot, 0], got.at[slot, 0], sems, layer, first_sem, mate)
        self.over = push(part.at[slot, 1], got.at[slot, 1], sems, layer, first_sem + 1, across)
        self.near = push(part.at[slot, 2], got.at[slot, 2], sems, layer, first_sem + 2, mate)

    def send_far(self, block):
        self.part[self.slot, 0] = block.astype(bf16)
        self.far.start()

    def send_across(self, block):
        self.far.wait_recv()
        self.part[self.slot, 1] = (block + self.got[self.slot, 0].astype(f32)).astype(bf16)
        self.over.start()

    def send_mate(self, block):
        self.part[self.slot, 2] = block.astype(bf16)
        self.near.start()

    def total(self, block):
        self.near.wait_recv()
        self.over.wait_recv()
        return (
            block
            + self.got[self.slot, 1].astype(f32)
            + self.got[self.slot, 2].astype(f32)
        )

    def finish(self):
        for copy in (self.far, self.over, self.near):
            copy.wait_send()


def normed_rows(rows):
    centered = rows - jnp.mean(rows, axis=-1, keepdims=True)
    inverse = lax.rsqrt(jnp.mean(centered * centered, axis=-1, keepdims=True) + norm_epsilon)
    return centered * inverse, inverse


def forward_kernel(
    spreading, tok, wq_in, wo_in, wg_in, wd_in, gain_in, cos_rows, sin_rows, doc_keys, doc_queries,
    act_out, xf_out, qkv_out, lse_out, att_out, flow_out, gu_out, hid_out,
    n1_out, s1_out, n2_out, s2_out, wq_out, wo_out, wg_out, wd_out, gain,
    wq, wo, wg, wd, xf, qkv, att, flow, gu, hid, bias, vt, k2, lse,
    n1, s1, n2, s2, first, act, part, got, sems, wsems, osems, dsems, ssems, gside, gdeep, gsems,
):
    where = places()
    me, mate, across, far, core = where
    weight_outs = (wq_out, wo_out, wg_out, wd_out)
    size = tok.shape[0]
    seq = size * GROUP
    ff = hid.shape[2]
    spread = Spread(wq_in.shape[1]) if spreading else None
    weights = []
    parts = (
        (wq_in, wq, None), (wo_in, wo, None), (wg_in, wg, None), (wd_in, wd, None),
    )
    for layer in range(LAYERS):
        for number, (source, target, cols) in enumerate(parts):
            local = wsems.at[layer, number]
            piece = PIECES * layer + number
            if not spreading:
                if cols is not None:
                    source, target = source.at[:, :, cols], target.at[:, :, cols]
                weights.append(pltpu.make_async_copy(source.at[layer], target.at[layer], local))
            elif number == 1:
                weights.append(
                    HalfGather(source, target, layer, piece, dsems, local, spread,
                               wo.shape[2] // 2, ssems, where)
                )
            else:
                weights.append(
                    WeightGather(source, target, layer, piece, dsems, local, spread, cols)
                )
    xf[0, rows_of(me, size, size), :] = tok[...]
    greet(mate, across, None, spread)
    gains = []
    if spreading:
        gdeep[spread.z] = gain_in[...]
        own = gdeep.at[spread.z]
        for step in range(1, DEPTH):
            gains.append(ship(own, own, gsems, 0, step, spread.device(step)))
            gains[-1].start()
    else:
        gain[...] = gain_in[...]
    ahead = LEAD if spreading else len(weights)
    for item in weights[:ahead]:
        item.start()

    def gain_stage(stage):
        if not spreading:
            return
        if stage == 0:
            for copy in gains:
                copy.wait_recv()
            gside[spread.x] = gdeep[0] + gdeep[1] + gdeep[2] + gdeep[3]
            own = gside.at[spread.x]
            gains.append(ship(own, own, gsems, 0, 0, spread.beside(0)))
            gains[-1].start()
        else:
            gains[-1].wait_recv()
            gain[...] = gside[0] + gside[1]
            for copy in gains:
                copy.wait_send()

    queue = [(k, hop) for k in range(len(weights)) for hop in range(6)] if spreading else []

    def pump(count):
        for number in range(min(count, len(queue))):
            k, hop = queue.pop(0)
            if hop == 0 and k + ahead < len(weights):
                weights[k + ahead].start()
            weights[k].serve(1)

    pending = []
    stores = []

    def store(number, layer, source, target):
        copy = pltpu.make_async_copy(source.at[layer], target.at[layer], osems.at[layer, number])
        copy.start()
        stores.append(copy)

    row_gather = Gather(xf, 0, 0, sems, 0, size, where)
    row_gather.start()
    write_bias(bias, doc_keys, doc_queries)
    low_mask, high_mask = half_masks()

    for layer in range(LAYERS):
        if layer == 0:
            pump(12)
        weights[PIECES * layer].wait()

        def project(block, layer=layer):
            rows = rows_of(block, size, size)
            proj = dot(xf[layer, rows, :], wq[layer])
            c, s = cos_rows[rows, :], sin_rows[rows, :]
            for tile in (0, 1, 3):
                piece = proj[:, tile * TILE:(tile + 1) * TILE]
                qkv[layer, rows, tile * TILE:(tile + 1) * TILE] = turn(piece, c, s).astype(bf16)
            for tile in (2, 4):
                piece = proj[:, tile * TILE:(tile + 1) * TILE]
                qkv[layer, rows, tile * TILE:(tile + 1) * TILE] = piece.astype(bf16)

        project(me)
        row_gather.wait_mate()
        project(mate)
        row_gather.wait_across()
        if layer:
            pump(2)
        project(across)
        row_gather.wait_far()
        project(far)
        if layer == 0:
            gain_stage(0)
        pending.append(row_gather)
        store(0, layer, xf, xf_out)
        store(1, layer, qkv, qkv_out)
        vt[0] = qkv[layer, :, 2 * TILE:3 * TILE].T
        vt[1] = qkv[layer, :, 4 * TILE:5 * TILE].T
        k2[...] = pltpu.roll(qkv[layer, :, 3 * TILE:4 * TILE].astype(f32), HEAD_DIM, 1).astype(bf16)

        sends = []
        forwards = []
        for head in range(OWN_HEADS):
            query_tile = (0, 0, 3)[head]
            mask = (low_mask, high_mask, low_mask)[head]

            def attend(i, carry, layer=layer, head=head, query_tile=query_tile, mask=mask):
                rows = rows_of(i, size, size)
                queries = qkv[layer, rows, query_tile * TILE:(query_tile + 1) * TILE] * mask
                keys = k2[...] if head == 2 else qkv[layer, :, TILE:2 * TILE]
                values = (vt.at[0, :HEAD_DIM], vt.at[0, HEAD_DIM:], vt.at[1, HEAD_DIM:])[head][...]
                scores = dot_nt(keys, queries) * (score_scale * log2e) + bias[:, rows]
                top = jnp.max(scores, axis=0, keepdims=True)
                probs = jnp.exp2(scores - top)
                total = jnp.sum(probs, axis=0, keepdims=True)
                result = dot(values, probs.astype(bf16)) / total
                spot = pl.ds(
                    pl.multiple_of(me * (OWN_HEADS * HEAD_DIM) + head * HEAD_DIM, HEAD_DIM), HEAD_DIM
                )
                att[layer, spot, rows] = result.astype(bf16)
                lse[layer, head:head + 1, rows] = top + jnp.log(total) * log2e
                return carry

            lax.fori_loop(0, seq // size, attend, 0)

            def features(block, head=head, layer=layer):
                start = block * (OWN_HEADS * HEAD_DIM) + head * HEAD_DIM
                return att.at[layer, pl.ds(pl.multiple_of(start, HEAD_DIM), HEAD_DIM)]

            own, theirs = features(me), features(across)
            to_across = push(own, own, sems, layer, 6 + head, across)
            to_mate = push(own, own, sems, layer, 9 + head, mate)
            onward = push(theirs, theirs, sems, layer, 12 + head, mate)
            to_across.start()
            to_mate.start()
            if head:
                sends[-2].wait_recv()
                forwards[-1].start()
            if spreading and head == 0:
                weights[PIECES * layer + 1].share()
            pump(2)
            sends += [to_across, to_mate]
            forwards.append(onward)
        sends[-2].wait_recv()
        forwards[-1].start()
        for head in range(OWN_HEADS):
            sends[2 * head + 1].wait_recv()
            forwards[head].wait_recv()
        store(2, layer, lse, lse_out)
        store(3, layer, att, att_out)
        pump(6 - 2 * layer)
        if layer == 0:
            gain_stage(1)
        for number in range(1, PIECES):
            weights[PIECES * layer + number].wait()
        for number, held in enumerate((wq, wo, wg, wd)):
            store(12 + number, layer, held, weight_outs[number])

        def feed(block, keep, layer=layer):
            rows = rows_of(block, size, size)
            branch = dot_tn(att[layer, :, rows], wo[layer])
            normed, inverse = normed_rows(xf[layer, rows, :].astype(f32) + branch)
            first_rows = normed * gain[2 * layer:2 * layer + 1, :]
            if keep:
                n1[layer] = normed
                s1[layer] = jnp.broadcast_to(inverse, s1.shape[1:])
                first[...] = first_rows
            first_low = first_rows.astype(bf16)
            flow[layer, rows, :] = first_low
            gate_up = dot(first_low, wg[layer])
            gate, upward = gate_up[:, :ff], gate_up[:, ff:]
            gu[layer, rows, :] = gate_up.astype(bf16)
            hidden = (gate / (1.0 + jnp.exp(-gate)) * upward).astype(bf16)
            hid[layer, rows, :] = hidden
            return dot_nt(hidden, wd[layer])

        scatter = Scatter(part, layer, got, layer, sems, 15, where)
        scatter.send_far(feed(far, False))
        pump(2)
        scatter.send_across(feed(across, False))
        pump(2)
        scatter.send_mate(feed(mate, False))
        pump(2)
        own_part = feed(me, True)
        pump(2)
        store(4, layer, flow, flow_out)
        store(5, layer, gu, gu_out)
        store(6, layer, hid, hid_out)
        store(7, layer, n1, n1_out)
        store(8, layer, s1, s1_out)
        pump(2)
        ffn = scatter.total(own_part)
        pending.append(scatter)
        normed, inverse = normed_rows(first[...] + ffn)
        n2[layer] = normed
        s2[layer] = jnp.broadcast_to(inverse, s2.shape[1:])
        result = (normed * gain[2 * layer + 1:2 * layer + 2, :]).astype(bf16)
        store(9, layer, n2, n2_out)
        store(10, layer, s2, s2_out)
        if layer + 1 < LAYERS:
            xf[layer + 1, rows_of(me, size, size), :] = result
            row_gather = Gather(xf, layer + 1, layer + 1, sems, 0, size, where)
            row_gather.start()
            pump(2)
        else:
            act[...] = result
            copy = pltpu.make_async_copy(act, act_out, osems.at[0, 11])
            copy.start()
            stores.append(copy)
        for copy in sends + forwards:
            copy.wait_send()
    if spreading:
        pending += weights
    for item in pending:
        item.finish()
    for copy in stores:
        copy.wait()


BACK_LOADED = (
    "n1", "s1", "n2", "s2", "xf", "qkv", "lse", "att", "flow", "gu", "hid", "wq", "wo", "wg", "wd",
)
BACK_TABLES = ("gain", "cos_rows", "sin_rows", "doc_keys", "doc_queries")
BACK_SCRATCH = (
    "bias", "dff", "dbr", "datt", "dproj", "dk", "dv", "dqt", "kt", "k2", "grad", "part", "got",
    "gq", "go", "gg", "gd", "sems", "lsems", "osems",
)

def backward_kernel(spreading, names, *refs):
    r = dict(zip(names, refs))
    cot = r["cot"]
    gain, cos_rows, sin_rows, doc_keys, doc_queries = (r[n] for n in BACK_TABLES)
    (
        bias, dff, dbr, datt, dproj, dk, dv, dqt, kt, k2, grad, part, got,
        gq, go, gg, gd, sems, lsems, osems,
    ) = (r[n] for n in BACK_SCRATCH)
    n1, s1, n2, s2, qkv, lse, att, gu, hid, wq, wo, wg, wd = (
        r[n] for n in BACK_LOADED if n not in ("xf", "flow")
    )
    xf = flow = r["rows"]
    where = places()
    me, mate, across, far, core = where
    size = cot.shape[0]
    seq = size * GROUP
    ff = hid.shape[1]
    feats = xf.shape[1]
    own_feats = OWN_HEADS * HEAD_DIM
    held = {n: (r[n + "_in"], r.get(n, r["rows"])) for n in BACK_LOADED}
    order = list(held)
    loads = {}

    def load(name, layer):
        if layer < 0:
            return
        source, target = held[name]
        copy = pltpu.make_async_copy(source.at[layer], target, lsems.at[order.index(name)])
        copy.start()
        loads[name] = copy

    for name in ("n2", "s2", "wd", "gu", "wg", "hid", "n1", "s1", "flow", "wo", "qkv", "lse", "att", "wq"):
        load(name, LAYERS - 1)
    spread = Spread(feats // (2 * DEPTH)) if spreading else None
    greet(mate, across, far if spreading else None, spread)
    write_bias(bias, doc_keys, doc_queries)
    low_mask, high_mask = half_masks()
    grad[...] = cot[...]
    pending = []
    scatters = []
    stores = {}
    sums = {}
    shares = []
    pieces = dict(
        d=gd.at[:, :], g=gg.at[:, :ff], u=gg.at[:, ff:],
        a=gq.at[:, :3 * TILE], b=gq.at[:, 3 * TILE:], o=go.at[:, :],
    )
    gsum = r["gsum"] if spreading else r["gain_out"]
    gsum[...] = jnp.zeros_like(gsum)

    def begin(name, layer):
        if not spreading:
            if name not in "ga":
                number = "boud".index(name)
                store(number, layer, (gq, go, gg, gd)[number], r["qogd"[number] + "_out"])
            return
        index = "dguabo".index(name)
        item = WeightSum(
            pieces[name], r["near_" + name], r["apart_" + name], 6 * layer + index, r["dsems"],
            spread, (r["csems"].at[0, index], r["csems"].at[1, index]),
            layer < LAYERS - 1, layer > 0, r["sum_" + name],
        )
        item.start()
        sums[name, layer] = item

    def add(name, layer):
        if spreading and (name, layer) in sums:
            sums[name, layer].add()

    def total(name, layer):
        if not spreading or (name, layer) not in sums:
            return
        result = sums[name, layer].total()
        if name in "ab":
            share = Share(r[name + "share"], layer, sems, 15 if name == "a" else 18, where)
            share.start(result.astype(bf16))
            shares.append(share)
        elif name == "o":
            oshare = r["oshare"]
            oshare[layer, core] = result.astype(bf16)
            copy = push(oshare.at[layer, core], oshare.at[layer, core], sems, layer, 21, mate)
            copy.start()
            oshares.append(copy)
        elif name == "d":
            r["d_res"][layer] = result
        else:
            half = "gu".index(name)
            r["g_res"][layer, :, half * ff:(half + 1) * ff] = result

    def ready(name, layer):
        if not spreading:
            if name not in "ub":
                stored("aogd".index(name))
        elif (name, layer + 1) in sums:
            sums[name, layer + 1].finish()

    oshares = []
    gains = []

    def gain_stage(stage):
        if not spreading:
            return
        gpack, gside, gdeep, gsems = (r[n] for n in ("gpack", "gside", "gdeep", "gsems"))
        if stage == 0:
            gpack[me] = gsum[...]
            for number, who in enumerate((mate, across, far)):
                gains.append(push(gpack.at[me], gpack.at[me], gsems, 0, number, who))
        elif stage == 1:
            for copy in gains[:3]:
                copy.wait_recv()
            gside[spread.x] = gpack[0] + gpack[1] + gpack[2] + gpack[3]
            own = gside.at[spread.x]
            gains.append(ship(own, own, gsems, 0, 3, spread.beside(0)))
        elif stage == 2:
            gains[3].wait_recv()
            gdeep[spread.z] = gside[0] + gside[1]
            own = gdeep.at[spread.z]
            for step in range(1, DEPTH):
                gains.append(ship(own, own, gsems, 0, 3 + step, spread.device(step)))
        else:
            for copy in gains[4:]:
                copy.wait_recv()
            r["gain_out"][...] = gdeep[0] + gdeep[1] + gdeep[2] + gdeep[3]
            for copy in gains:
                copy.wait_send()
            return
        for copy in gains[(0, 3, 4)[stage]:]:
            copy.start()

    def store(number, layer, source, target):
        copy = pltpu.make_async_copy(source, target.at[layer], osems.at[layer, number])
        copy.start()
        stores[number] = copy

    def stored(number):
        if number in stores:
            stores.pop(number).wait()

    for layer in range(LAYERS - 1, -1, -1):

        def norm_back(grad_rows, normed, inverse, row, layer=layer):
            gsum[2 * layer + row:2 * layer + row + 1, :] = jnp.sum(
                grad_rows * normed, axis=0, keepdims=True
            )
            scaled = grad_rows * gain[2 * layer + row:2 * layer + row + 1, :]
            return (
                scaled
                - jnp.mean(scaled, axis=-1, keepdims=True)
                - normed * jnp.mean(scaled * normed, axis=-1, keepdims=True)
            ) * inverse

        loads["n2"].wait()
        loads["s2"].wait()
        dz = norm_back(grad[...], n2[...], s2[:, :1], 1)
        load("n2", layer - 1)
        load("s2", layer - 1)
        grad[...] = dz
        dff[0, rows_of(me, size, size), :] = dz.astype(bf16)
        gather = Gather(dff, 0, layer, sems, 0, size, where)
        gather.start()
        for name in ("wd", "gu", "wg"):
            loads[name].wait()
        add("o", layer + 1)

        def feed_back(block):
            rows = rows_of(block, size, size)
            grad_hidden = dot(dff[0, rows, :], wd[...])
            gate = gu[rows, :ff].astype(f32)
            upward = gu[rows, ff:].astype(f32)
            sigma = 1.0 / (1.0 + jnp.exp(-gate))
            up_grad = grad_hidden * gate * sigma
            gate_grad = grad_hidden * upward * sigma * (1.0 + gate * (1.0 - sigma))
            gu[rows, :ff] = gate_grad.astype(bf16)
            gu[rows, ff:] = up_grad.astype(bf16)
            return dot_nt(gu[rows, :], wg[...])

        if len(scatters) > 1:
            scatters[-2].finish()
        scatter = Scatter(part, 0, got, 2 * layer, sems, 6, where)
        scatters.append(scatter)
        own_part = feed_back(me)
        gather.wait_mate()
        scatter.send_mate(feed_back(mate))
        gather.wait_across()
        loads["hid"].wait()
        add("a", layer + 1)
        gather.wait_far()
        ready("d", layer)

        def down_weight(i, carry):
            cols = rows_of(i, 256, 256)
            gd[cols, :] = dot_tn(dff[0, :, cols], hid[...]).astype(bf16)
            return carry

        lax.fori_loop(0, feats // 256, down_weight, 0)
        begin("d", layer)
        scatter.send_far(feed_back(far))
        scatter.send_across(feed_back(across))
        gather.finish()
        load("hid", layer - 1)
        load("wd", layer - 1)
        load("wg", layer - 1)
        add("b", layer + 1)
        loads["flow"].wait()
        for name, first_col in (("g", 0), ("u", ff)):
            ready(name, layer)

            def gate_up_weight(i, carry, first_col=first_col):
                cols = rows_of(i, 256, 256)
                gg[cols, first_col:first_col + ff] = dot_tn(
                    flow[:, cols], gu[:, first_col:first_col + ff]
                ).astype(bf16)
                return carry

            lax.fori_loop(0, feats // 256, gate_up_weight, 0)
            begin(name, layer)
        load("gu", layer - 1)
        load("xf", layer)
        for name in "dgu":
            total(name, layer + 1)

        dfirst = grad[...] + scatter.total(own_part)
        loads["n1"].wait()
        loads["s1"].wait()
        dr = norm_back(dfirst, n1[...], s1[:, :1], 0)
        load("n1", layer - 1)
        load("s1", layer - 1)
        grad[...] = dr
        dbr[layer, rows_of(me, size, size), :] = dr.astype(bf16)
        gather = Gather(dbr, layer, layer, sems, 9, size, where)
        gather.start()
        if layer == 0:
            gain_stage(0)
        for name in ("wo", "qkv", "lse"):
            loads[name].wait()

        def att_back(block, layer=layer):
            rows = rows_of(block, size, size)
            for tile, start in enumerate((0, HEAD_DIM)):
                spot = pl.ds(pl.multiple_of(me * own_feats + start, HEAD_DIM), TILE)
                datt[rows, tile * TILE:(tile + 1) * TILE] = dot_nt(
                    dbr[layer, rows, :], wo[spot, :]
                ).astype(bf16)

        kt[0] = qkv[:, TILE:2 * TILE].T
        kt[1] = qkv[:, 3 * TILE:4 * TILE].T
        k2[...] = pltpu.roll(qkv[:, 3 * TILE:4 * TILE].astype(f32), HEAD_DIM, 1).astype(bf16)
        dk[...] = jnp.zeros_like(dk)
        dv[...] = jnp.zeros_like(dv)

        def attend(head, first, second):
            tile = head // 2
            query_tile = (0, 0, 3)[head]
            value_tile = (2, 2, 4)[head]
            query_mask = (low_mask, high_mask, low_mask)[head]
            value_mask = (low_mask, high_mask, high_mask)[head]

            def body(i, carry):
                rows = rows_of(first + i * (second - first), size, size)
                queries = qkv[rows, query_tile * TILE:(query_tile + 1) * TILE] * query_mask
                keys = k2[...] if head == 2 else qkv[:, TILE:2 * TILE]
                scores = dot_nt(keys, queries) * (score_scale * log2e) + bias[:, rows]
                probs = jnp.exp2(scores - lse[head:head + 1, rows])
                outs = datt[rows, tile * TILE:(tile + 1) * TILE] * value_mask
                grad_probs = dot_nt(qkv[:, value_tile * TILE:(value_tile + 1) * TILE], outs)
                delta = jnp.sum(probs * grad_probs, axis=0, keepdims=True)
                grad_scores = (probs * (grad_probs - delta)).astype(bf16)
                dv[tile] = dv[tile] + dot(probs.astype(bf16), outs)
                dk[tile] = dk[tile] + dot(grad_scores, queries)
                keys_t = (kt.at[0, :HEAD_DIM], kt.at[0, HEAD_DIM:], kt.at[1, HEAD_DIM:])[head][...]
                spot = (0, HEAD_DIM, 0)[head]
                dqt[tile, spot:spot + HEAD_DIM, rows] = dot(keys_t, grad_scores)
                return carry

            lax.fori_loop(0, 2, body, 0)

        att_back(me)
        gather.wait_mate()
        att_back(mate)
        if layer == 0:
            add("d", layer)
        for head in range(OWN_HEADS):
            attend(head, me, mate)
        gather.wait_across()
        att_back(across)
        if layer == 0:
            gain_stage(1)
            add("g", layer)
        else:
            add("d", layer)
        gather.wait_far()
        att_back(far)
        pending.append(gather)
        load("wo", layer - 1)
        loads["att"].wait()
        ready("o", layer)

        def out_weight(i, carry, layer=layer):
            rows = rows_of(i, 256, 256)
            half = feats // 2
            cols = pl.ds(pl.multiple_of(core * half, half), half)
            go[rows, :] = dot(att[rows, :], dbr[layer, :, cols]).astype(bf16)
            return carry

        lax.fori_loop(0, feats // 256, out_weight, 0)
        begin("o", layer)
        load("att", layer - 1)
        for name in "oab":
            total(name, layer + 1)
        attend(0, across, far)
        attend(1, across, far)
        for share in shares:
            share.serve()

        def unrotate_pairs(i, carry):
            rows = rows_of(i, size, size)
            c, s = cos_rows[rows, :], -sin_rows[rows, :]
            dproj[rows, :TILE] = turn(dqt[0, :, rows].T * score_scale, c, s).astype(bf16)
            dproj[rows, TILE:2 * TILE] = turn(dk[0, rows, :] * score_scale, c, s).astype(bf16)
            dproj[rows, 2 * TILE:3 * TILE] = dv[0, rows, :].astype(bf16)
            return carry

        def unrotate_last(i, carry):
            rows = rows_of(i, size, size)
            c, s = cos_rows[rows, :], -sin_rows[rows, :]
            lower = lane_iota((size, TILE)) < HEAD_DIM
            mixed = jnp.where(lower, dqt[1, :, rows].T, pltpu.roll(dk[1, rows, :], HEAD_DIM, 1))
            dproj[rows, 3 * TILE:4 * TILE] = turn(mixed * score_scale, c, s).astype(bf16)
            dproj[rows, 4 * TILE:] = dv[1, rows, :].astype(bf16)
            return carry

        def weigh_projection(first, last):
            def qkv_weight(i, carry):
                cols = rows_of(i, 256, 256)
                gq[cols, first:last] = dot_tn(xf[:, cols], dproj[:, first:last]).astype(bf16)
                return carry

            lax.fori_loop(0, feats // 256, qkv_weight, 0)

        lax.fori_loop(0, seq // size, unrotate_pairs, 0)
        loads["xf"].wait()
        ready("a", layer)
        weigh_projection(0, 3 * TILE)
        begin("a", layer)
        if layer:
            add("g", layer)
        else:
            gain_stage(2)
            add("u", layer)
        attend(2, across, far)
        lax.fori_loop(0, seq // size, unrotate_last, 0)
        load("qkv", layer - 1)
        load("lse", layer - 1)
        loads["wq"].wait()

        def input_part(block):
            return dot_nt(dproj[rows_of(block, size, size), :], wq[...])

        if len(scatters) > 1:
            scatters[-2].finish()
        scatter = Scatter(part, 1, got, 2 * layer + 1, sems, 6, where)
        scatters.append(scatter)
        if layer == 0:
            ready("b", layer)
            weigh_projection(3 * TILE, PROJ)
            begin("b", layer)
        scatter.send_far(input_part(far))
        scatter.send_across(input_part(across))
        scatter.send_mate(input_part(mate))
        own_part = input_part(me)
        load("wq", layer - 1)
        if layer:
            ready("b", layer)
            weigh_projection(3 * TILE, PROJ)
            begin("b", layer)
            add("u", layer)
        else:
            gain_stage(3)
            add("o", layer)
            add("a", layer)
            for name in "dg":
                total(name, 0)
            add("b", layer)
        load("flow", layer - 1)
        grad[...] = grad[...] + scatter.total(own_part)
    input_copy = pltpu.make_async_copy(grad, r["ig_out"], osems.at[0, 4])
    input_copy.start()
    for name in "uoab":
        total(name, 0)
    if spreading:
        for share in shares[-2:]:
            share.serve()
    input_copy.wait()
    for item in pending + scatters[-2:]:
        item.finish()
    for number in range(4):
        stored(number)
    for item in shares:
        item.finish()
    for copy in oshares:
        copy.wait()
    if spreading:
        for name in "dguabo":
            sums[name, 0].finish()
        q_out = r["q_out"]
        ends = (
            (r["ashare"], q_out.at[:, :, :, pl.ds(0, 3 * TILE)]),
            (r["bshare"], q_out.at[:, :, :, pl.ds(3 * TILE, 2 * TILE)]),
            (r["oshare"], r["o_out"]),
        )
        last = []
        for number, held in enumerate(ends):
            last.append(pltpu.make_async_copy(*held, osems.at[1, number]))
            last[-1].start()
        for copy in last:
            copy.wait()


RATES = ((0.03, 0.01), (0.5, 0.01), (0.03, 0.01), (0.02, 0.01), (0.6, 0.0))


def adam_step(weight, first, second, average, gradient, rate, decay):
    first_new = beta_first * first + (1.0 - beta_first) * gradient
    second_new = beta_second * second + (1.0 - beta_second) * gradient * gradient
    first_hat = first_new / (1.0 - beta_first**STEP)
    second_hat = second_new / (1.0 - beta_second**STEP)
    weight_new = weight - rate * (
        first_hat / (jnp.sqrt(second_hat) + adam_epsilon) + decay * weight
    )
    average_new = average_decay * average + (1.0 - average_decay) * weight_new
    return first_new, second_new, weight_new, average_new


def adam_kernel(*refs):
    states = [refs[4 * f:4 * f + 4] for f in range(5)]
    grads = refs[20:25]
    outs = [refs[25 + 5 * f:30 + 5 * f] for f in range(5)]
    (qs, os, ds, gs, qg, og, gg, qb, ob, gb, db, gsems, isems, usems) = refs[50:]
    width = ob.shape[3]
    for number, target in enumerate((qs, os, gs, ds)):
        pltpu.make_async_copy(grads[number], target, gsems.at[number]).start()
    chunks = []
    for family, held, grad in ((3, db, ds), (2, gb, gg), (1, ob, og), (0, qb, qg)):
        for layer in range(LAYERS):
            for part in range(3 if family == 0 else 1):
                spot = 3 * layer + part if family == 0 else layer
                chunks.append((family, held, grad, layer, part, spot))

    def view(ref, family, layer, part):
        if family:
            return ref.at[layer]
        return ref.at[layer, :, pl.ds(part * width, width)]

    arrivals = []
    for number, (family, held, grad, layer, part, spot) in enumerate(chunks):
        copies = [
            pltpu.make_async_copy(
                view(states[family][k], family, layer, part), held.at[k, spot], isems.at[number, k]
            )
            for k in range(4)
        ]
        for copy in copies:
            copy.start()
        arrivals.append(copies)

    def wait_grad(number, target):
        pltpu.make_async_copy(grads[number], target, gsems.at[number]).wait()

    gain = [ref[...] for ref in states[4]]
    gradient = grads[4][...]
    new = adam_step(*gain, gradient, *RATES[4])
    for ref, value in zip(outs[4], (gradient,) + new):
        ref[...] = value

    low = lane_iota((qs.shape[2], TILE)) < HEAD_DIM
    leaving = []
    for number, (family, held, grad, layer, part, spot) in enumerate(chunks):
        first_of = layer == 0 and part == 0
        if family == 3 and first_of:
            wait_grad(3, ds)
        if family == 2:
            if first_of:
                wait_grad(2, gs)
            for half in range(2):
                gg[layer, :, half, :] = gs[layer, :, half * width:(half + 1) * width]
        if family == 1:
            if first_of:
                wait_grad(1, os)
            half = width // 2
            og[layer, :, :half] = os[layer, 0].astype(f32)
            og[layer, :, half:] = os[layer, 1].astype(f32)
        if family == 0:
            if first_of:
                wait_grad(0, qs)

            def pair(j):
                return qs[layer, j, :, part * TILE:(part + 1) * TILE].astype(f32)

            def last(j, upper):
                tile = 4 if part == 2 else 3
                value = qs[layer, j, :, tile * TILE:(tile + 1) * TILE].astype(f32)
                return value if upper == (part > 0) else pltpu.roll(value, HEAD_DIM, 1)

            for j in (0, 2):
                turned = pltpu.roll(pair(j + 1), HEAD_DIM, 1)
                tiles = (
                    pair(j),
                    jnp.where(low, last(j, False), turned),
                    jnp.where(low, turned, last(j + 1, True)),
                )
                for k, value in enumerate(tiles):
                    start = (3 * (j // 2) + k) * TILE
                    qg[spot, :, start:start + TILE] = value
        for copy in arrivals[number]:
            copy.wait()
        rows = 32

        def body(i, carry, family=family, held=held, grad=grad, spot=spot):
            at = pl.ds(pl.multiple_of(i * rows, rows), rows)
            values = [held[k, spot, at] for k in range(4)]
            first, second, weight, average = adam_step(*values, grad[spot, at], *RATES[family])
            for k, value in enumerate((weight, first, second, average)):
                held[k, spot, at] = value
            return carry

        lax.fori_loop(0, ob.shape[2] // rows, body, 0)
        sources = (grad.at[spot],) + tuple(held.at[k, spot] for k in (1, 2, 0, 3))
        for k, source in enumerate(sources):
            copy = pltpu.make_async_copy(
                source, view(outs[family][k], family, layer, part), usems.at[number, k]
            )
            copy.start()
            leaving.append(copy)
    for copy in leaving:
        copy.wait()


def pack_documents(length_row, mask_row):
    seq = mask_row.shape[0]
    ends = jnp.cumsum(length_row)
    spots = jnp.arange(seq, dtype=jnp.int32)
    past = spots[:, None] >= ends[None, :]
    number = jnp.sum(past.astype(jnp.int32), axis=1)
    starts = jnp.max(jnp.where(past, ends[None, :], 0), axis=1)
    position = spots - starts
    keys = jnp.where(mask_row == 1, number, -1)
    doc_keys = jnp.broadcast_to(keys[:, None], (seq, 128))
    doc_queries = jnp.broadcast_to(number[None, :], (8, seq))
    half = HEAD_DIM // 2
    freq = jnp.power(rotary_base, -2.0 * jnp.arange(half).astype(f32) / HEAD_DIM)
    angle = position.astype(f32)[:, None] * freq
    c, s = jnp.cos(angle), jnp.sin(angle)
    cos_rows = jnp.concatenate([c, c, c, c], axis=1)
    sin_rows = jnp.concatenate([-s, s, -s, s], axis=1)
    return cos_rows, sin_rows, doc_keys, doc_queries


def own_projection(weight, me):
    layers, rows, _ = weight.shape
    split = weight.reshape(layers, rows, 3, HEADS * HEAD_DIM)
    own = lax.dynamic_slice_in_dim(split, me * OWN_HEADS * HEAD_DIM, OWN_HEADS * HEAD_DIM, 3)
    own = own.astype(bf16)
    pairs = own[..., :TILE].reshape(layers, rows, 3 * TILE)
    last = own[..., TILE:]
    return jnp.concatenate(
        [pairs, last[:, :, 0], last[:, :, 1], jnp.zeros_like(last[:, :, 0]), last[:, :, 2]], axis=-1
    )


def whole_projection(grad):
    group, layers, rows, _ = grad.shape
    pairs = grad[..., :3 * TILE].reshape(group, layers, rows, 3, TILE)
    last = jnp.stack(
        [
            grad[..., 3 * TILE:3 * TILE + HEAD_DIM],
            grad[..., 3 * TILE + HEAD_DIM:4 * TILE],
            grad[..., 4 * TILE + HEAD_DIM:],
        ],
        axis=3,
    )
    full = jnp.concatenate([pairs, last], axis=-1)
    return full.transpose(1, 2, 3, 0, 4).reshape(layers, rows, 3 * HEADS * HEAD_DIM)


def run_forward(spreading, tokens, weights, gain, tables):
    size, feats = tokens.shape
    seq = size * GROUP
    ff = weights[3].shape[2]
    shapes = dict(
        act=((size, feats), bf16),
        xf=((LAYERS, seq, feats), bf16),
        qkv=((LAYERS, seq, PROJ), bf16),
        lse=((LAYERS, 8, seq), f32),
        att=((LAYERS, feats, seq), bf16),
        flow=((LAYERS, seq, feats), bf16),
        gu=((LAYERS, seq, 2 * ff), bf16),
        hid=((LAYERS, seq, ff), bf16),
        n1=((LAYERS, size, feats), f32),
        s1=((LAYERS, size, 128), f32),
        n2=((LAYERS, size, feats), f32),
        s2=((LAYERS, size, 128), f32),
        wq=((LAYERS, feats, PROJ), bf16),
        wo=((LAYERS, feats, feats), bf16),
        wg=((LAYERS, feats, 2 * ff), bf16),
        wd=((LAYERS, feats, ff), bf16),
        gain=((8, feats), f32),
    )
    held = {name: pltpu.VMEM(*shape) for name, shape in shapes.items()}
    scratch = [held[n] for n in ("wq", "wo", "wg", "wd", "xf", "qkv", "att", "flow", "gu", "hid")]
    scratch += [
        pltpu.VMEM((seq, seq), f32),
        pltpu.VMEM((2, TILE, seq), bf16),
        pltpu.VMEM((seq, TILE), bf16),
        held["lse"],
    ]
    scratch += [held[n] for n in ("n1", "s1", "n2", "s2")]
    scratch += [
        pltpu.VMEM((size, feats), f32),
        held["act"],
        pltpu.VMEM((LAYERS, 3, size, feats), bf16),
        pltpu.VMEM((LAYERS, 3, size, feats), bf16),
        pltpu.SemaphoreType.DMA((2, LAYERS, 18)),
        pltpu.SemaphoreType.DMA((LAYERS, PIECES)),
        pltpu.SemaphoreType.DMA((LAYERS, 16)),
        pltpu.SemaphoreType.DMA((2, PIECES * LAYERS, 3 + 2 * DEPTH)),
        pltpu.SemaphoreType.DMA((2, LAYERS, 7)),
        pltpu.VMEM((2, 8, feats), f32),
        pltpu.VMEM((DEPTH, 8, feats), f32),
        pltpu.SemaphoreType.DMA((2, 1, DEPTH)),
    ]
    return pl.pallas_call(
        functools.partial(forward_kernel, spreading),
        out_shape=[jax.ShapeDtypeStruct(*shape) for shape in shapes.values()],
        in_specs=[VMEM] + [ANY] * 4 + [VMEM] * 5,
        out_specs=[ANY] * (len(shapes) - 1) + [VMEM],
        scratch_shapes=scratch,
        compiler_params=pltpu.CompilerParams(
            collective_id=0, has_side_effects=True, vmem_limit_bytes=VMEM_LIMIT
        ),
        cost_estimate=pl.CostEstimate(
            flops=12 * 10**9, bytes_accessed=60 * 10**6, transcendentals=10**7
        ),
        name="forward",
    )(tokens, *weights, gain, *tables)


def run_backward(spreading, cotangent, kept, weights, gain, tables):
    size, feats = cotangent.shape
    seq = size * GROUP
    xf, qkv, lse, att, flow, gu, hid, n1, s1, n2, s2 = kept
    ff = hid.shape[2]
    wq, wo, wg, wd = weights
    loaded = [n1, s1, n2, s2, xf, qkv, lse, att, flow, gu, hid, wq, wo, wg, wd]
    own = feats // (2 * DEPTH)
    half = feats // 2
    widths = dict(d=ff, g=ff, u=ff, a=3 * TILE, b=2 * TILE, o=half)
    if spreading:
        outs = dict(
            ig_out=((size, feats), f32),
            q_out=((LAYERS, GROUP, own, PROJ), bf16),
            o_out=((LAYERS, 2, own, half), bf16),
            d_res=((LAYERS, own, ff), f32),
            g_res=((LAYERS, own, 2 * ff), f32),
            gain_out=((8, feats), f32),
        )
    else:
        outs = dict(
            ig_out=((size, feats), f32),
            q_out=(wq.shape, bf16),
            o_out=((LAYERS, feats, half), bf16),
            d_out=(wd.shape, bf16),
            g_out=(wg.shape, bf16),
            gain_out=((8, feats), f32),
        )
    names = ["cot"] + [n + "_in" for n in BACK_LOADED] + list(BACK_TABLES) + list(outs)
    scratch = dict(
        bias=pltpu.VMEM((seq, seq), f32),
        dff=pltpu.VMEM((1, seq, feats), bf16),
        dbr=pltpu.VMEM((LAYERS, seq, feats), bf16),
        datt=pltpu.VMEM((seq, 2 * TILE), bf16),
        dproj=pltpu.VMEM((seq, PROJ), bf16),
        dk=pltpu.VMEM((2, seq, TILE), f32),
        dv=pltpu.VMEM((2, seq, TILE), f32),
        dqt=pltpu.VMEM((2, TILE, seq), f32),
        kt=pltpu.VMEM((2, TILE, seq), bf16),
        k2=pltpu.VMEM((seq, TILE), bf16),
        grad=pltpu.VMEM((size, feats), f32),
        part=pltpu.VMEM((2, 3, size, feats), bf16),
        got=pltpu.VMEM((2, 3, size, feats), bf16),
        gq=pltpu.VMEM((feats, PROJ), bf16),
        go=pltpu.VMEM((feats, half), bf16),
        gg=pltpu.VMEM((feats, 2 * ff), bf16),
        gd=pltpu.VMEM((feats, ff), bf16),
        sems=pltpu.SemaphoreType.DMA((2, 2 * LAYERS, 22)),
        lsems=pltpu.SemaphoreType.DMA((len(loaded),)),
        osems=pltpu.SemaphoreType.DMA((LAYERS, 5)),
        rows=pltpu.VMEM((seq, feats), bf16),
    )
    for name, array in zip(BACK_LOADED, loaded):
        if name not in ("xf", "flow"):
            scratch[name] = pltpu.VMEM(array.shape[1:], array.dtype)
    if spreading:
        scratch.update(
            gsum=pltpu.VMEM((8, feats), f32),
            gpack=pltpu.VMEM((GROUP, 8, feats), f32),
            gside=pltpu.VMEM((2, 8, feats), f32),
            gdeep=pltpu.VMEM((DEPTH, 8, feats), f32),
            gsems=pltpu.SemaphoreType.DMA((2, 1, 7)),
            csems=pltpu.SemaphoreType.REGULAR((2, 6)),
            ashare=pltpu.VMEM((LAYERS, GROUP, own, 3 * TILE), bf16),
            bshare=pltpu.VMEM((LAYERS, GROUP, own, 2 * TILE), bf16),
            oshare=pltpu.VMEM((LAYERS, 2, own, half), bf16),
            dsems=pltpu.SemaphoreType.DMA((2, 6 * LAYERS, 7)),
        )
        for name, width in widths.items():
            scratch["near_" + name] = pltpu.VMEM((DEPTH, own, width), bf16)
            scratch["apart_" + name] = pltpu.VMEM((DEPTH - 1, own, width), bf16)
            scratch["sum_" + name] = pltpu.VMEM((own, width), f32)
    in_vmem = ("d_res", "g_res", "gain_out")
    return pl.pallas_call(
        functools.partial(backward_kernel, spreading, tuple(names + list(scratch))),
        out_shape=[jax.ShapeDtypeStruct(*shape) for shape in outs.values()],
        in_specs=[VMEM] + [ANY] * 15 + [VMEM] * 5,
        out_specs=[VMEM if name in in_vmem else ANY for name in outs],
        scratch_shapes=list(scratch.values()),
        compiler_params=pltpu.CompilerParams(
            collective_id=1, has_side_effects=True, vmem_limit_bytes=VMEM_LIMIT
        ),
        cost_estimate=pl.CostEstimate(
            flops=24 * 10**9, bytes_accessed=60 * 10**6, transcendentals=10**7
        ),
        name="backward",
    )(cotangent, *loaded, gain, *tables)


def run_adam(states, grads):
    outs = []
    for family in range(5):
        shape = jax.ShapeDtypeStruct(states[4 * family].shape, f32)
        outs += [shape] * 5
    layers, own, _, width = states[8].shape
    scratch = [
        pltpu.VMEM(grads[0].shape, bf16),
        pltpu.VMEM(grads[1].shape, bf16),
        pltpu.VMEM(grads[3].shape, f32),
        pltpu.VMEM(grads[2].shape, f32),
        pltpu.VMEM((3 * layers, own, width), f32),
        pltpu.VMEM((layers, own, width), f32),
        pltpu.VMEM((layers, own, 2, width), f32),
        pltpu.VMEM((4, 3 * layers, own, width), f32),
        pltpu.VMEM((4, layers, own, width), f32),
        pltpu.VMEM((4, layers, own, 2, width), f32),
        pltpu.VMEM((4, layers, own, width), f32),
        pltpu.SemaphoreType.DMA((4,)),
        pltpu.SemaphoreType.DMA((6 * layers, 4)),
        pltpu.SemaphoreType.DMA((6 * layers, 5)),
    ]
    return pl.pallas_call(
        adam_kernel,
        out_shape=outs,
        in_specs=[ANY] * 16 + [VMEM] * 4 + [ANY] * 4 + [VMEM],
        out_specs=[ANY] * 20 + [VMEM] * 5,
        scratch_shapes=scratch,
        compiler_params=pltpu.CompilerParams(vmem_limit_bytes=VMEM_LIMIT),
        cost_estimate=pl.CostEstimate(
            flops=2 * 10**7, bytes_accessed=37 * 10**6, transcendentals=10**6
        ),
        name="adam",
    )(*states, *grads)


def adamw(weight, first, second, average, gradient, rate, decay):
    first_new = beta_first * first + (1.0 - beta_first) * gradient
    second_new = beta_second * second + (1.0 - beta_second) * gradient * gradient
    first_hat = first_new / (1.0 - beta_first**STEP)
    second_hat = second_new / (1.0 - beta_second**STEP)
    weight_new = weight - rate * (
        first_hat / (jnp.sqrt(second_hat) + adam_epsilon) + decay * weight
    )
    average_new = average_decay * average + (1.0 - average_decay) * weight_new
    return (gradient, first_new, second_new, weight_new, average_new)


def shards(
    spreading,
    tokens,
    cotangent,
    lengths,
    key_mask,
    qkv_weight,
    qkv_first,
    qkv_second,
    qkv_average,
    out_weight,
    out_first,
    out_second,
    out_average,
    gate_up_weight,
    gate_up_first,
    gate_up_second,
    gate_up_average,
    down_weight,
    down_first,
    down_second,
    down_average,
    norm_gain,
    gain_first,
    gain_second,
    gain_average,
):
    me = lax.axis_index("mp")
    own = gate_up_weight.shape[1]
    ff = gate_up_weight.shape[3]
    feats = tokens.shape[1]
    if spreading:
        gain = jnp.zeros((8, feats), f32)
        gain = lax.dynamic_update_slice(
            gain, norm_gain.reshape(2 * LAYERS, own), (0, lax.axis_index("dp") * own)
        )
    else:
        gain = lax.all_gather(norm_gain, "dp", axis=2, tiled=True).reshape(2 * LAYERS, feats)
        gain = jnp.concatenate([gain, jnp.zeros((8 - 2 * LAYERS, feats), f32)], axis=0)
    tables = pack_documents(lengths[0], key_mask)
    owned = (
        own_projection(qkv_weight, me),
        out_weight.astype(bf16),
        gate_up_weight.reshape(LAYERS, own, 2 * ff).astype(bf16),
        down_weight.astype(bf16),
    )
    if not spreading:
        owned = [lax.all_gather(w, "dp", axis=1, tiled=True) for w in owned]
    act, *kept = run_forward(spreading, tokens, owned, gain, tables)
    weights, kept, gain = kept[-5:-1], kept[:-5], kept[-1]
    backward = run_backward(spreading, cotangent, kept, weights, gain, tables)
    if spreading:
        input_grad, gq, go, gd, gg, gain_sum = backward
        gain_grad = lax.dynamic_slice_in_dim(
            gain_sum[:2 * LAYERS].reshape(LAYERS, 2, -1), lax.axis_index("dp") * own, own, 2
        )
        states = (
            qkv_weight, qkv_first, qkv_second, qkv_average,
            out_weight, out_first, out_second, out_average,
            gate_up_weight, gate_up_first, gate_up_second, gate_up_average,
            down_weight, down_first, down_second, down_average,
            norm_gain, gain_first, gain_second, gain_average,
        )
        return (act, input_grad, *run_adam(states, (gq, go, gg, gd, gain_grad)))
    else:
        input_grad, gq, go, gd, gg, gain_sum = backward
        gq, go, gg, gd = [
            lax.psum_scatter(g, "dp", scatter_dimension=1, tiled=True) for g in (gq, go, gg, gd)
        ]
        gq, go = lax.all_gather(gq, "mp"), lax.all_gather(go, "mp")
        gain_part = gain_sum[:2 * LAYERS].reshape(LAYERS, 2, -1)
        gain_grad = lax.psum_scatter(
            lax.psum(gain_part, "mp"), "dp", scatter_dimension=2, tiled=True
        )
    qkv_grad = whole_projection(gq.astype(f32))
    out_grad = jnp.concatenate([go[0], go[1]], axis=-1).astype(f32)
    gate_up_grad = gg.reshape(LAYERS, own, 2, ff).astype(f32)
    down_grad = gd.astype(f32)
    results = [act, input_grad]
    results.extend(adamw(qkv_weight, qkv_first, qkv_second, qkv_average, qkv_grad, 0.03, 0.01))
    results.extend(adamw(out_weight, out_first, out_second, out_average, out_grad, 0.5, 0.01))
    results.extend(
        adamw(
            gate_up_weight, gate_up_first, gate_up_second, gate_up_average, gate_up_grad, 0.03, 0.01
        )
    )
    results.extend(
        adamw(down_weight, down_first, down_second, down_average, down_grad, 0.02, 0.01)
    )
    results.extend(adamw(norm_gain, gain_first, gain_second, gain_average, gain_grad, 0.6, 0.0))
    return tuple(results)


def solution(mesh):
    spreading = mesh.shape["dp"] == 2 * DEPTH
    return jax.shard_map(
        functools.partial(shards, spreading),
        mesh=mesh,
        in_specs=(
            P(("dp", "mp"), None),
            P(("dp", "mp"), None),
            P("dp", None),
            P("dp"),
            P(None, "dp", None),
            P(None, "dp", None),
            P(None, "dp", None),
            P(None, "dp", None),
            P(None, "dp", None),
            P(None, "dp", None),
            P(None, "dp", None),
            P(None, "dp", None),
            P(None, "dp", None, "mp"),
            P(None, "dp", None, "mp"),
            P(None, "dp", None, "mp"),
            P(None, "dp", None, "mp"),
            P(None, "dp", "mp"),
            P(None, "dp", "mp"),
            P(None, "dp", "mp"),
            P(None, "dp", "mp"),
            P(None, None, "dp"),
            P(None, None, "dp"),
            P(None, None, "dp"),
            P(None, None, "dp"),
        ),
        out_specs=(
            P(("dp", "mp"), None),
            P(("dp", "mp"), None),
            P(None, "dp", None),
            P(None, "dp", None),
            P(None, "dp", None),
            P(None, "dp", None),
            P(None, "dp", None),
            P(None, "dp", None),
            P(None, "dp", None),
            P(None, "dp", None),
            P(None, "dp", None),
            P(None, "dp", None),
            P(None, "dp", None, "mp"),
            P(None, "dp", None, "mp"),
            P(None, "dp", None, "mp"),
            P(None, "dp", None, "mp"),
            P(None, "dp", None, "mp"),
            P(None, "dp", "mp"),
            P(None, "dp", "mp"),
            P(None, "dp", "mp"),
            P(None, "dp", "mp"),
            P(None, "dp", "mp"),
            P(None, None, "dp"),
            P(None, None, "dp"),
            P(None, None, "dp"),
            P(None, None, "dp"),
            P(None, None, "dp"),
        ),
        check_vma=False,
    )
```

```python
import functools
import math

import jax
import jax.numpy as jnp
import numpy as np
from jax import lax
from jax.experimental import pallas as pl
from jax.experimental.pallas import tpu as pltpu
from jax.sharding import PartitionSpec as P

HEADS = 12
HEAD_DIM = 64
LAYERS = 2
STEP = 10
GROUP = 4
DEPTH = 4
LEAD = 1
PIECES = 4
OWN_HEADS = HEADS // GROUP
TILE = 2 * HEAD_DIM
PROJ = 5 * TILE

rotary_base = 1000.0
norm_epsilon = 1e-05
masked_score = -1e30
beta_first = 0.5
beta_second = 0.5
adam_epsilon = 1e-08
average_decay = 0.5
score_scale = HEAD_DIM ** (-0.5)
log2e = math.log2(math.e)

MESH = pl.DeviceIdType.MESH
ANY = pl.BlockSpec(memory_space=pl.ANY)
VMEM = pl.BlockSpec(memory_space=pltpu.VMEM)
f32 = jnp.float32
bf16 = jnp.bfloat16
VMEM_LIMIT = 127 * 2**19


def dot(a, b):
    return jnp.dot(a, b, preferred_element_type=f32)


def dot_nt(a, b):
    return lax.dot_general(a, b, (((1,), (1,)), ((), ())), preferred_element_type=f32)


def dot_tn(a, b):
    return lax.dot_general(a, b, (((0,), (0,)), ((), ())), preferred_element_type=f32)


def places():
    me = lax.axis_index("mp")
    core = lax.rem(me, 2)
    side = lax.div(me, 2)
    return me, me + 1 - 2 * core, me + 2 - 4 * side, 3 - me, core


def push(src, dst, sems, layer, number, who):
    return pltpu.make_async_remote_copy(
        src_ref=src,
        dst_ref=dst,
        send_sem=sems.at[0, layer, number],
        recv_sem=sems.at[1, layer, number],
        device_id={"mp": who},
        device_id_type=MESH,
    )


class Spread:
    def __init__(self, own):
        index = lax.axis_index("dp")
        self.own = own
        self.z, self.x = lax.div(index, 2), lax.rem(index, 2)

    def device(self, step):
        return 2 * lax.rem(self.z + step, DEPTH) + self.x

    def beside(self, step):
        return 2 * lax.rem(self.z + step, DEPTH) + 1 - self.x

    def rows(self, index):
        return pl.ds(pl.multiple_of(index * self.own, self.own), self.own)


def greet(mate, across, far=None, spread=None):
    barrier = pltpu.get_barrier_semaphore()
    packs = [mate, across] if far is None else [mate, across, far]
    for who in packs:
        pl.semaphore_signal(barrier, inc=1, device_id={"mp": who}, device_id_type=MESH)
    others = []
    if spread is not None:
        others = [spread.beside(0)] + [spread.device(step) for step in range(1, DEPTH)]
        for who in others:
            pl.semaphore_signal(barrier, inc=1, device_id={"dp": who}, device_id_type=MESH)
    pl.semaphore_wait(barrier, len(packs) + len(others))


def ship(src, dst, sems, piece, number, who):
    return pltpu.make_async_remote_copy(
        src_ref=src,
        dst_ref=dst,
        send_sem=sems.at[0, piece, number],
        recv_sem=sems.at[1, piece, number],
        device_id={"dp": who},
        device_id_type=MESH,
    )


class WeightGather:
    def __init__(self, source, target, layer, piece, sems, local, spread, cols=None):
        self.target, self.layer, self.cols = target, layer, cols
        self.piece, self.sems, self.spread = piece, sems, spread
        z, x = spread.z, spread.x
        own = source.at[layer] if cols is None else source.at[layer, :, cols]
        place = self.view(z, x)
        self.local = pltpu.make_async_copy(own, place, local)
        self.beside = self.send(own, place, 0, 0, 2 * z + 1 - x)
        self.up = self.send(own, place, 1, 1 + z, 2 * jnp.minimum(z + 1, DEPTH - 1) + x)
        self.down = self.send(own, place, 2, 1 + z, 2 * jnp.maximum(z - 1, 0) + x)
        self.hops = [(far, way) for far in range(1, DEPTH) for way in (-1, 1)]
        self.todo = list(self.hops)

    def view(self, z, x):
        rows = self.spread.rows(2 * z + x)
        if self.cols is None:
            return self.target.at[self.layer, rows]
        return self.target.at[self.layer, rows, self.cols]

    def send(self, src, dst, out, into, who):
        return pltpu.make_async_remote_copy(
            src_ref=src,
            dst_ref=dst,
            send_sem=self.sems.at[0, self.piece, out],
            recv_sem=self.sems.at[1, self.piece, into],
            device_id={"dp": who},
            device_id_type=MESH,
        )

    def start(self):
        self.local.start()
        pl.when(self.spread.z < DEPTH - 1)(self.up.start)
        pl.when(self.spread.z > 0)(self.down.start)
        self.beside.start()

    def hop(self, far, way):
        z, x = self.spread.z, self.spread.x
        source = jnp.clip(z + way * far, 0, DEPTH - 1)
        block = self.view(source, x)
        onward = jnp.clip(z - way, 0, DEPTH - 1)
        arrive = self.send(block, block, 3 + source, 1 + source, 2 * source + x)
        over = self.send(block, block, 3 + source, 1 + DEPTH + source, 2 * z + 1 - x)
        along = self.send(block, block, 3 + DEPTH + source, 1 + source, 2 * onward + x)
        comes = z >= far if way < 0 else z + far < DEPTH
        goes = z > 0 if way > 0 else z < DEPTH - 1
        return arrive, over, along, comes, jnp.logical_and(comes, goes)

    def serve(self, count=2 * DEPTH):
        while self.todo and count:
            count -= 1
            arrive, over, along, comes, goes = self.hop(*self.todo.pop(0))

            pl.when(comes)(arrive.wait_recv)
            pl.when(goes)(along.start)
            pl.when(comes)(over.start)

    def wait(self):
        self.serve()
        self.local.wait()
        self.beside.wait_recv()
        z, x = self.spread.z, self.spread.x
        for step in range(1, DEPTH):
            source = lax.rem(z + step, DEPTH)
            block = self.view(source, 1 - x)
            self.send(block, block, 3, 1 + DEPTH + source, 2 * z + 1 - x).wait_recv()

    def finish(self):
        self.beside.wait_send()
        pl.when(self.spread.z < DEPTH - 1)(self.up.wait_send)
        pl.when(self.spread.z > 0)(self.down.wait_send)
        for far, way in self.hops:
            arrive, over, along, comes, goes = self.hop(far, way)
            pl.when(comes)(over.wait_send)
            pl.when(goes)(along.wait_send)


class HalfGather(WeightGather):
    def __init__(self, source, target, layer, piece, sems, local, spread, half, pack_sems, where):
        me, mate, across, far, core = where
        cols = pl.ds(pl.multiple_of(core * half, half), half)
        super().__init__(source, target, layer, piece, sems, local, spread, cols)
        here = spread.rows(2 * spread.z + spread.x)
        self.local = pltpu.make_async_copy(source.at[layer], target.at[layer, here], local)
        self.swap = []
        for step in range(DEPTH):
            z = lax.rem(spread.z + step, DEPTH)
            for number, x in enumerate((spread.x, 1 - spread.x)):
                if step or number:
                    block = self.view(z, x)
                    self.swap.append(
                        push(block, block, pack_sems, layer, 2 * step + number - 1, mate)
                    )

    def share(self):
        super().wait()
        for copy in self.swap:
            copy.start()

    def wait(self):
        for copy in self.swap:
            copy.wait_recv()

    def finish(self):
        super().finish()
        for copy in self.swap:
            copy.wait_send()


class WeightSum:
    def __init__(self, grad, near, apart, piece, sems, spread, credits, again, more, total):
        self.grad, self.near, self.apart, self.spread = grad, near, apart, spread
        self.near_credit, self.apart_credit = credits
        self.again, self.more = again, more
        self.sum = total
        self.beside = [
            ship(grad.at[spread.rows(spread.beside(step))], near.at[step], sems, piece, step,
                 spread.beside(0))
            for step in range(DEPTH)
        ]
        self.along = [
            ship(grad.at[spread.rows(spread.device(step))], apart.at[step - 1], sems, piece,
                 DEPTH - 1 + step, spread.device(step))
            for step in range(1, DEPTH)
        ]

    def start(self):
        if self.again:
            pl.semaphore_wait(self.near_credit, 1)
        for copy in self.beside[1:] + self.beside[:1]:
            copy.start()

    def credit(self, sem, who):
        pl.semaphore_signal(sem, inc=1, device_id={"dp": who}, device_id_type=MESH)

    def add(self):
        if self.again:
            pl.semaphore_wait(self.apart_credit, DEPTH - 1)
        for step in range(1, DEPTH):
            self.beside[step].wait_recv()
            rows = self.spread.rows(self.spread.device(step))
            self.grad[rows, :] = (
                self.grad[rows, :].astype(f32) + self.near[step].astype(f32)
            ).astype(bf16)
            self.along[step - 1].start()
        self.beside[0].wait_recv()
        rows = self.spread.rows(self.spread.device(0))
        self.sum[...] = self.grad[rows, :].astype(f32) + self.near[0].astype(f32)
        if self.more:
            self.credit(self.near_credit, self.spread.beside(0))

    def total(self):
        for copy in self.along:
            copy.wait_recv()
        result = self.sum[...]
        for step in range(DEPTH - 1):
            result = result + self.apart[step].astype(f32)
        if self.more:
            for step in range(1, DEPTH):
                self.credit(self.apart_credit, self.spread.device(step))
        return result

    def finish(self):
        for copy in self.beside + self.along:
            copy.wait_send()


def rows_of(block, size, extent):
    return pl.ds(pl.multiple_of(block * size, size), extent)


def lane_iota(shape):
    return lax.broadcasted_iota(jnp.int32, shape, len(shape) - 1)


def half_masks():
    low = (lane_iota((1, TILE)) < HEAD_DIM).astype(f32)
    return low.astype(bf16), (1.0 - low).astype(bf16)


def turn(tile, cos_rows, sin_rows):
    lane = lane_iota(tile.shape) % HEAD_DIM
    half = HEAD_DIM // 2
    partner = jnp.where(
        lane < half, pltpu.roll(tile, TILE - half, 1), pltpu.roll(tile, half, 1)
    )
    return tile * cos_rows + partner * sin_rows


def write_bias(bias, doc_keys, doc_queries):
    seq = bias.shape[0]
    step = 128

    def body(i, carry):
        rows = rows_of(i, step, step)
        keys = doc_keys[rows, :][:, :1]
        same = keys == doc_queries[:1, :]
        spot = lax.broadcasted_iota(jnp.int32, (step, seq), 0) + i * step
        own = spot == lax.broadcasted_iota(jnp.int32, (step, seq), 1)
        bias[rows, :] = jnp.where(jnp.logical_or(same, own), 0.0, masked_score)
        return carry

    lax.fori_loop(0, seq // step, body, 0)


def write_tables(lengths, mask_row, freq, cos_rows, sin_rows, doc_keys, doc_queries):
    ends = []
    for doc in range(lengths.shape[1]):
        ends.append(lengths[0, doc] + (ends[-1] if ends else 0))

    def document(spots):
        number = jnp.zeros(spots.shape, jnp.int32)
        for end in ends:
            number = number + (spots >= end).astype(jnp.int32)
        return number

    seq = cos_rows.shape[0]
    doc_queries[...] = document(lane_iota(doc_queries.shape))
    step = 128

    def body(i, carry):
        rows = rows_of(i, step, step)
        spots = lax.broadcasted_iota(jnp.int32, (step, 128), 0) + i * step
        start = jnp.zeros(spots.shape, jnp.int32)
        for end in ends:
            start = jnp.maximum(start, jnp.where(spots >= end, end, 0))
        seen = jnp.broadcast_to(mask_row[:, rows].astype(f32), (step, step)).T
        doc_keys[rows, :] = jnp.where(seen > 0.5, document(spots), -1)
        angle = (spots - start).astype(f32) * freq[:1, :]
        sine = jnp.sin(angle)
        cos_rows[rows, :] = jnp.cos(angle)
        lower = lane_iota(spots.shape) % HEAD_DIM < HEAD_DIM // 2
        sin_rows[rows, :] = jnp.where(lower, -sine, sine)
        return carry

    lax.fori_loop(0, seq // step, body, 0)


class Gather:
    def __init__(self, ref, slot, layer, sems, first_sem, size, where):
        me, mate, across, far, core = where
        self.across, self.mate = [], []
        self.forward = []
        half = size // 2

        def piece(block, part):
            start = pl.multiple_of(block * size + part * half, half)
            return ref.at[slot, pl.ds(start, half)]

        for part in range(2):
            own = piece(me, part)
            theirs = piece(across, part)
            self.across.append(push(own, own, sems, layer, first_sem + part, across))
            self.mate.append(push(own, own, sems, layer, first_sem + 2 + part, mate))
            self.forward.append(push(theirs, theirs, sems, layer, first_sem + 4 + part, mate))

    def start(self):
        for copy in self.across + self.mate:
            copy.start()

    def wait_mate(self):
        for copy in self.mate:
            copy.wait_recv()

    def wait_across(self):
        for copy, onward in zip(self.across, self.forward):
            copy.wait_recv()
            onward.start()

    def wait_far(self):
        for copy in self.forward:
            copy.wait_recv()

    def finish(self):
        for copy in self.across + self.mate + self.forward:
            copy.wait_send()


class Share:
    def __init__(self, ref, layer, sems, first_sem, where):
        me, mate, across, far, core = where
        own, theirs = ref.at[layer, me], ref.at[layer, across]
        self.ref, self.layer, self.me = ref, layer, me
        self.over = push(own, own, sems, layer, first_sem, across)
        self.near = push(own, own, sems, layer, first_sem + 1, mate)
        self.onward = push(theirs, theirs, sems, layer, first_sem + 2, mate)

    def start(self, block):
        self.ref[self.layer, self.me] = block
        self.over.start()
        self.near.start()

    def serve(self):
        self.over.wait_recv()
        self.onward.start()

    def finish(self):
        self.near.wait_recv()
        self.onward.wait_recv()
        for copy in (self.over, self.near, self.onward):
            copy.wait_send()


class Scatter:
    def __init__(self, part, slot, got, layer, sems, first_sem, where):
        me, mate, across, far, core = where
        self.part, self.slot, self.got = part, slot, got
        self.far = push(part.at[slot, 0], got.at[slot, 0], sems, layer, first_sem, mate)
        self.over = push(part.at[slot, 1], got.at[slot, 1], sems, layer, first_sem + 1, across)
        self.near = push(part.at[slot, 2], got.at[slot, 2], sems, layer, first_sem + 2, mate)

    def send_far(self, block):
        self.part[self.slot, 0] = block.astype(bf16)
        self.far.start()

    def send_across(self, block):
        self.far.wait_recv()
        self.part[self.slot, 1] = (block + self.got[self.slot, 0].astype(f32)).astype(bf16)
        self.over.start()

    def send_mate(self, block):
        self.part[self.slot, 2] = block.astype(bf16)
        self.near.start()

    def total(self, block):
        self.near.wait_recv()
        self.over.wait_recv()
        return (
            block
            + self.got[self.slot, 1].astype(f32)
            + self.got[self.slot, 2].astype(f32)
        )

    def finish(self):
        for copy in (self.far, self.over, self.near):
            copy.wait_send()


def normed_rows(rows):
    centered = rows - jnp.mean(rows, axis=-1, keepdims=True)
    inverse = lax.rsqrt(jnp.mean(centered * centered, axis=-1, keepdims=True) + norm_epsilon)
    return centered * inverse, inverse


def forward_kernel(
    spreading, tok, wq_in, wo_in, wg_in, wd_in, gain_in, lengths, mask_row, freq,
    act_out, xf_out, qkv_out, lse_out, att_out, flow_out, gu_out, hid_out,
    n1_out, s1_out, n2_out, s2_out, wq_out, wo_out, wg_out, wd_out, gain,
    cos_rows, sin_rows, doc_keys, doc_queries,
    wq, wo, wg, wd, xf, qkv, att, flow, gu, hid, bias, vt, k2, lse,
    n1, s1, n2, s2, first, act, part, got, sems, wsems, osems, dsems, ssems, gside, gdeep, gsems, *own_low,
):
    where = places()
    me, mate, across, far, core = where
    weight_outs = (wq_out, wo_out, wg_out, wd_out)
    size = tok.shape[0]
    seq = size * GROUP
    ff = hid.shape[2]
    spread = Spread(wq_in.shape[1]) if spreading else None
    weights = []
    cast = ()
    if spreading:
        cast = ((wo_in, own_low[0]), (wg_in, own_low[1]), (wd_in, own_low[2]))
        wo_in, wg_in, wd_in = own_low
    parts = (
        (wq_in, wq, None), (wo_in, wo, None), (wg_in, wg, None), (wd_in, wd, None),
    )
    for layer in range(LAYERS):
        for number, (source, target, cols) in enumerate(parts):
            local = wsems.at[layer, number]
            piece = PIECES * layer + number
            if not spreading:
                if cols is not None:
                    source, target = source.at[:, :, cols], target.at[:, :, cols]
                weights.append(pltpu.make_async_copy(source.at[layer], target.at[layer], local))
            elif number == 1:
                weights.append(
                    HalfGather(source, target, layer, piece, dsems, local, spread,
                               wo.shape[2] // 2, ssems, where)
                )
            else:
                weights.append(
                    WeightGather(source, target, layer, piece, dsems, local, spread, cols)
                )
    xf[0, rows_of(me, size, size), :] = tok[...]
    greet(mate, across, None, spread)
    gains = []
    if spreading:
        gdeep[spread.z] = gain_in[...]
        own = gdeep.at[spread.z]
        for step in range(1, DEPTH):
            gains.append(ship(own, own, gsems, 0, step, spread.device(step)))
            gains[-1].start()
    else:
        gain[...] = gain_in[...]
    ahead = LEAD if spreading else len(weights)
    for item in weights[:ahead]:
        item.start()

    def gain_stage(stage):
        if not spreading:
            return
        if stage == 0:
            for copy in gains:
                copy.wait_recv()
            gside[spread.x] = gdeep[0] + gdeep[1] + gdeep[2] + gdeep[3]
            own = gside.at[spread.x]
            gains.append(ship(own, own, gsems, 0, 0, spread.beside(0)))
            gains[-1].start()
        else:
            gains[-1].wait_recv()
            gain[...] = gside[0] + gside[1]
            for copy in gains:
                copy.wait_send()

    queue = [(k, hop) for k in range(len(weights)) for hop in range(6)] if spreading else []

    def pump(count):
        for number in range(min(count, len(queue))):
            k, hop = queue.pop(0)
            if hop == 0 and k + ahead < len(weights):
                weights[k + ahead].start()
            weights[k].serve(1)

    pending = []
    stores = []

    def store(number, layer, source, target):
        copy = pltpu.make_async_copy(source.at[layer], target.at[layer], osems.at[layer, number])
        copy.start()
        stores.append(copy)

    row_gather = Gather(xf, 0, 0, sems, 0, size, where)
    row_gather.start()
    for source, target in cast:
        if len(source.shape) == 3:
            target[...] = source[...].astype(bf16)
        else:
            for layer in range(LAYERS):
                for half in range(2):
                    target[layer, :, half * ff:(half + 1) * ff] = source[layer, :, half, :].astype(bf16)
    write_tables(lengths, mask_row, freq, cos_rows, sin_rows, doc_keys, doc_queries)
    write_bias(bias, doc_keys, doc_queries)
    low_mask, high_mask = half_masks()

    for layer in range(LAYERS):
        if layer == 0:
            pump(12)
        weights[PIECES * layer].wait()

        def project(block, layer=layer):
            rows = rows_of(block, size, size)
            proj = dot(xf[layer, rows, :], wq[layer])
            c, s = cos_rows[rows, :], sin_rows[rows, :]
            for tile in (0, 1, 3):
                piece = proj[:, tile * TILE:(tile + 1) * TILE]
                qkv[layer, rows, tile * TILE:(tile + 1) * TILE] = turn(piece, c, s).astype(bf16)
            for tile in (2, 4):
                piece = proj[:, tile * TILE:(tile + 1) * TILE]
                qkv[layer, rows, tile * TILE:(tile + 1) * TILE] = piece.astype(bf16)

        project(me)
        row_gather.wait_mate()
        project(mate)
        row_gather.wait_across()
        pump(2)
        project(across)
        row_gather.wait_far()
        project(far)
        if layer == 0:
            gain_stage(0)
        pending.append(row_gather)
        store(0, layer, xf, xf_out)
        store(1, layer, qkv, qkv_out)
        vt[0] = qkv[layer, :, 2 * TILE:3 * TILE].T
        vt[1] = qkv[layer, :, 4 * TILE:5 * TILE].T
        k2[...] = pltpu.roll(qkv[layer, :, 3 * TILE:4 * TILE].astype(f32), HEAD_DIM, 1).astype(bf16)

        sends = []
        forwards = []
        for head in range(OWN_HEADS):
            query_tile = (0, 0, 3)[head]
            mask = (low_mask, high_mask, low_mask)[head]

            def attend(i, carry, layer=layer, head=head, query_tile=query_tile, mask=mask):
                rows = rows_of(i, size, size)
                queries = qkv[layer, rows, query_tile * TILE:(query_tile + 1) * TILE] * mask
                keys = k2[...] if head == 2 else qkv[layer, :, TILE:2 * TILE]
                values = (vt.at[0, :HEAD_DIM], vt.at[0, HEAD_DIM:], vt.at[1, HEAD_DIM:])[head][...]
                scores = dot_nt(keys, queries) * (score_scale * log2e) + bias[:, rows]
                top = jnp.max(scores, axis=0, keepdims=True)
                probs = jnp.exp2(scores - top)
                total = jnp.sum(probs, axis=0, keepdims=True)
                result = dot(values, probs.astype(bf16)) / total
                spot = pl.ds(
                    pl.multiple_of(me * (OWN_HEADS * HEAD_DIM) + head * HEAD_DIM, HEAD_DIM), HEAD_DIM
                )
                att[layer, spot, rows] = result.astype(bf16)
                lse[layer, head:head + 1, rows] = top + jnp.log(total) * log2e
                return carry

            lax.fori_loop(0, seq // size, attend, 0)

            def features(block, head=head, layer=layer):
                start = block * (OWN_HEADS * HEAD_DIM) + head * HEAD_DIM
                return att.at[layer, pl.ds(pl.multiple_of(start, HEAD_DIM), HEAD_DIM)]

            own, theirs = features(me), features(across)
            to_across = push(own, own, sems, layer, 6 + head, across)
            to_mate = push(own, own, sems, layer, 9 + head, mate)
            onward = push(theirs, theirs, sems, layer, 12 + head, mate)
            to_across.start()
            to_mate.start()
            if head:
                sends[-2].wait_recv()
                forwards[-1].start()
            if spreading and head == 0:
                weights[PIECES * layer + 1].share()
            pump(2)
            sends += [to_across, to_mate]
            forwards.append(onward)
        sends[-2].wait_recv()
        forwards[-1].start()
        for head in range(OWN_HEADS):
            sends[2 * head + 1].wait_recv()
            forwards[head].wait_recv()
        store(2, layer, lse, lse_out)
        store(3, layer, att, att_out)
        if layer == 0:
            gain_stage(1)
        pump(2)
        for number in (1, 2):
            weights[PIECES * layer + number].wait()

        def feed(block, keep, layer=layer):
            rows = rows_of(block, size, size)
            branch = dot_tn(att[layer, :, rows], wo[layer])
            normed, inverse = normed_rows(xf[layer, rows, :].astype(f32) + branch)
            first_rows = normed * gain[2 * layer:2 * layer + 1, :]
            if keep:
                n1[layer] = normed
                s1[layer] = jnp.broadcast_to(inverse, s1.shape[1:])
                first[...] = first_rows
            first_low = first_rows.astype(bf16)
            flow[layer, rows, :] = first_low
            gate_up = dot(first_low, wg[layer])
            gate, upward = gate_up[:, :ff], gate_up[:, ff:]
            gu[layer, rows, :] = gate_up.astype(bf16)
            hid[layer, rows, :] = (gate / (1.0 + jnp.exp(-gate)) * upward).astype(bf16)

        def down(block, layer=layer):
            return dot_nt(hid[layer, rows_of(block, size, size), :], wd[layer])

        for number, block in enumerate((far, across, mate, me)):
            feed(block, number == 3)
            pump(2)
        weights[PIECES * layer + 3].wait()
        for number, held in enumerate((wq, wo, wg, wd)):
            store(12 + number, layer, held, weight_outs[number])
        scatter = Scatter(part, layer, got, layer, sems, 15, where)
        scatter.send_far(down(far))
        scatter.send_across(down(across))
        scatter.send_mate(down(mate))
        own_part = down(me)
        pump(2)
        store(4, layer, flow, flow_out)
        store(5, layer, gu, gu_out)
        store(6, layer, hid, hid_out)
        store(7, layer, n1, n1_out)
        store(8, layer, s1, s1_out)
        pump(4)
        ffn = scatter.total(own_part)
        pending.append(scatter)
        normed, inverse = normed_rows(first[...] + ffn)
        n2[layer] = normed
        s2[layer] = jnp.broadcast_to(inverse, s2.shape[1:])
        result = (normed * gain[2 * layer + 1:2 * layer + 2, :]).astype(bf16)
        store(9, layer, n2, n2_out)
        store(10, layer, s2, s2_out)
        if layer + 1 < LAYERS:
            xf[layer + 1, rows_of(me, size, size), :] = result
            row_gather = Gather(xf, layer + 1, layer + 1, sems, 0, size, where)
            row_gather.start()
            pump(2)
        else:
            act[...] = result
            copy = pltpu.make_async_copy(act, act_out, osems.at[0, 11])
            copy.start()
            stores.append(copy)
        for copy in sends + forwards:
            copy.wait_send()
    if spreading:
        pending += weights
    for item in pending:
        item.finish()
    for copy in stores:
        copy.wait()


BACK_LOADED = (
    "n1", "s1", "n2", "s2", "xf", "qkv", "lse", "att", "flow", "gu", "hid", "wq", "wo", "wg", "wd",
)
BACK_TABLES = ("gain", "cos_rows", "sin_rows", "doc_keys", "doc_queries")
BACK_SCRATCH = (
    "bias", "dff", "dbr", "datt", "dproj", "dk", "dv", "dqt", "kt", "k2", "grad", "part", "got",
    "gq", "go", "gg", "gd", "sems", "lsems", "osems",
)

def backward_kernel(spreading, names, *refs):
    r = dict(zip(names, refs))
    cot = r["cot"]
    gain, cos_rows, sin_rows, doc_keys, doc_queries = (r[n] for n in BACK_TABLES)
    (
        bias, dff, dbr, datt, dproj, dk, dv, dqt, kt, k2, grad, part, got,
        gq, go, gg, gd, sems, lsems, osems,
    ) = (r[n] for n in BACK_SCRATCH)
    n1, s1, n2, s2, qkv, lse, att, gu, hid, wq, wo, wg, wd = (
        r[n] for n in BACK_LOADED if n not in ("xf", "flow")
    )
    xf = flow = r["rows"]
    where = places()
    me, mate, across, far, core = where
    size = cot.shape[0]
    seq = size * GROUP
    ff = hid.shape[1]
    feats = xf.shape[1]
    own_feats = OWN_HEADS * HEAD_DIM
    held = {n: (r[n + "_in"], r.get(n, r["rows"])) for n in BACK_LOADED}
    order = list(held)
    loads = {}

    def load(name, layer):
        if layer < 0:
            return
        source, target = held[name]
        copy = pltpu.make_async_copy(source.at[layer], target, lsems.at[order.index(name)])
        copy.start()
        loads[name] = copy

    for name in ("n2", "s2", "wd", "gu", "wg", "hid", "n1", "s1", "flow", "wo", "qkv", "lse", "att", "wq"):
        load(name, LAYERS - 1)
    spread = Spread(feats // (2 * DEPTH)) if spreading else None
    greet(mate, across, far if spreading else None, spread)
    low_mask, high_mask = half_masks()
    grad[...] = cot[...]
    pending = []
    scatters = []
    stores = {}
    sums = {}
    shares = []
    pieces = dict(
        d=gd.at[:, :], g=gg.at[:, :ff], u=gg.at[:, ff:],
        a=gq.at[:, :3 * TILE], b=gq.at[:, 3 * TILE:], o=go.at[:, :],
    )
    gsum = r["gsum"] if spreading else r["gain_out"]
    gsum[...] = jnp.zeros_like(gsum)

    def begin(name, layer):
        if not spreading:
            if name not in "ga":
                number = "boud".index(name)
                store(number, layer, (gq, go, gg, gd)[number], r["qogd"[number] + "_out"])
            return
        index = "dguabo".index(name)
        item = WeightSum(
            pieces[name], r["near_" + name], r["apart_" + name], 6 * layer + index, r["dsems"],
            spread, (r["csems"].at[0, index], r["csems"].at[1, index]),
            layer < LAYERS - 1, layer > 0, r["sum_" + name],
        )
        item.start()
        sums[name, layer] = item

    def add(name, layer):
        if spreading and (name, layer) in sums:
            sums[name, layer].add()

    def total(name, layer):
        if not spreading or (name, layer) not in sums:
            return
        result = sums[name, layer].total()
        if name in "ab":
            share = Share(r[name + "share"], layer, sems, 15 if name == "a" else 18, where)
            share.start(result.astype(bf16))
            shares.append(share)
        elif name == "o":
            oshare = r["oshare"]
            oshare[layer, core] = result.astype(bf16)
            copy = push(oshare.at[layer, core], oshare.at[layer, core], sems, layer, 21, mate)
            copy.start()
            oshares.append(copy)
        elif name == "d":
            r["d_res"][layer] = result
        else:
            half = "gu".index(name)
            r["g_res"][layer, :, half * ff:(half + 1) * ff] = result

    def ready(name, layer):
        if not spreading:
            if name not in "ub":
                stored("aogd".index(name))
        elif (name, layer + 1) in sums:
            sums[name, layer + 1].finish()

    oshares = []
    gains = []

    def gain_stage(stage):
        if not spreading:
            return
        gpack, gside, gdeep, gsems = (r[n] for n in ("gpack", "gside", "gdeep", "gsems"))
        if stage == 0:
            gpack[me] = gsum[...]
            for number, who in enumerate((mate, across, far)):
                gains.append(push(gpack.at[me], gpack.at[me], gsems, 0, number, who))
        elif stage == 1:
            for copy in gains[:3]:
                copy.wait_recv()
            gside[spread.x] = gpack[0] + gpack[1] + gpack[2] + gpack[3]
            own = gside.at[spread.x]
            gains.append(ship(own, own, gsems, 0, 3, spread.beside(0)))
        elif stage == 2:
            gains[3].wait_recv()
            gdeep[spread.z] = gside[0] + gside[1]
            own = gdeep.at[spread.z]
            for step in range(1, DEPTH):
                gains.append(ship(own, own, gsems, 0, 3 + step, spread.device(step)))
        else:
            for copy in gains[4:]:
                copy.wait_recv()
            r["gain_out"][...] = gdeep[0] + gdeep[1] + gdeep[2] + gdeep[3]
            for copy in gains:
                copy.wait_send()
            return
        for copy in gains[(0, 3, 4)[stage]:]:
            copy.start()

    def store(number, layer, source, target):
        copy = pltpu.make_async_copy(source, target.at[layer], osems.at[layer, number])
        copy.start()
        stores[number] = copy

    def stored(number):
        if number in stores:
            stores.pop(number).wait()

    for layer in range(LAYERS - 1, -1, -1):

        def norm_back(grad_rows, normed, inverse, row, layer=layer):
            gsum[2 * layer + row:2 * layer + row + 1, :] = jnp.sum(
                grad_rows * normed, axis=0, keepdims=True
            )
            scaled = grad_rows * gain[2 * layer + row:2 * layer + row + 1, :]
            return (
                scaled
                - jnp.mean(scaled, axis=-1, keepdims=True)
                - normed * jnp.mean(scaled * normed, axis=-1, keepdims=True)
            ) * inverse

        loads["n2"].wait()
        loads["s2"].wait()
        dz = norm_back(grad[...], n2[...], s2[:, :1], 1)
        load("n2", layer - 1)
        load("s2", layer - 1)
        grad[...] = dz
        dff[0, rows_of(me, size, size), :] = dz.astype(bf16)
        gather = Gather(dff, 0, layer, sems, 0, size, where)
        gather.start()
        if layer == LAYERS - 1:
            write_bias(bias, doc_keys, doc_queries)
        for name in ("wd", "gu", "wg"):
            loads[name].wait()
        add("o", layer + 1)

        def feed_back(block):
            rows = rows_of(block, size, size)
            grad_hidden = dot(dff[0, rows, :], wd[...])
            gate = gu[rows, :ff].astype(f32)
            upward = gu[rows, ff:].astype(f32)
            sigma = 1.0 / (1.0 + jnp.exp(-gate))
            up_grad = grad_hidden * gate * sigma
            gate_grad = grad_hidden * upward * sigma * (1.0 + gate * (1.0 - sigma))
            gu[rows, :ff] = gate_grad.astype(bf16)
            gu[rows, ff:] = up_grad.astype(bf16)
            return dot_nt(gu[rows, :], wg[...])

        if len(scatters) > 1:
            scatters[-2].finish()
        scatter = Scatter(part, 0, got, 2 * layer, sems, 6, where)
        scatters.append(scatter)
        own_part = feed_back(me)
        gather.wait_mate()
        scatter.send_mate(feed_back(mate))
        gather.wait_across()
        loads["hid"].wait()
        add("a", layer + 1)
        gather.wait_far()
        ready("d", layer)

        def down_weight(i, carry):
            cols = rows_of(i, 256, 256)
            gd[cols, :] = dot_tn(dff[0, :, cols], hid[...]).astype(bf16)
            return carry

        lax.fori_loop(0, feats // 256, down_weight, 0)
        begin("d", layer)
        scatter.send_far(feed_back(far))
        scatter.send_across(feed_back(across))
        gather.finish()
        load("hid", layer - 1)
        load("wd", layer - 1)
        load("wg", layer - 1)
        add("b", layer + 1)
        loads["flow"].wait()
        for name, first_col in (("g", 0), ("u", ff)):
            ready(name, layer)

            def gate_up_weight(i, carry, first_col=first_col):
                cols = rows_of(i, 256, 256)
                gg[cols, first_col:first_col + ff] = dot_tn(
                    flow[:, cols], gu[:, first_col:first_col + ff]
                ).astype(bf16)
                return carry

            lax.fori_loop(0, feats // 256, gate_up_weight, 0)
            begin(name, layer)
        load("gu", layer - 1)
        load("xf", layer)
        for name in "dgu":
            total(name, layer + 1)

        dfirst = grad[...] + scatter.total(own_part)
        loads["n1"].wait()
        loads["s1"].wait()
        dr = norm_back(dfirst, n1[...], s1[:, :1], 0)
        load("n1", layer - 1)
        load("s1", layer - 1)
        grad[...] = dr
        dbr[layer, rows_of(me, size, size), :] = dr.astype(bf16)
        gather = Gather(dbr, layer, layer, sems, 9, size, where)
        gather.start()
        if layer == 0:
            gain_stage(0)
        for name in ("wo", "qkv", "lse"):
            loads[name].wait()

        def att_back(block, layer=layer):
            rows = rows_of(block, size, size)
            for tile, start in enumerate((0, HEAD_DIM)):
                spot = pl.ds(pl.multiple_of(me * own_feats + start, HEAD_DIM), TILE)
                datt[rows, tile * TILE:(tile + 1) * TILE] = dot_nt(
                    dbr[layer, rows, :], wo[spot, :]
                ).astype(bf16)

        kt[0] = qkv[:, TILE:2 * TILE].T
        kt[1] = qkv[:, 3 * TILE:4 * TILE].T
        k2[...] = pltpu.roll(qkv[:, 3 * TILE:4 * TILE].astype(f32), HEAD_DIM, 1).astype(bf16)
        dk[...] = jnp.zeros_like(dk)
        dv[...] = jnp.zeros_like(dv)

        def attend(head, first, second):
            tile = head // 2
            query_tile = (0, 0, 3)[head]
            value_tile = (2, 2, 4)[head]
            query_mask = (low_mask, high_mask, low_mask)[head]
            value_mask = (low_mask, high_mask, high_mask)[head]

            def body(i, carry):
                rows = rows_of(first + i * (second - first), size, size)
                queries = qkv[rows, query_tile * TILE:(query_tile + 1) * TILE] * query_mask
                keys = k2[...] if head == 2 else qkv[:, TILE:2 * TILE]
                scores = dot_nt(keys, queries) * (score_scale * log2e) + bias[:, rows]
                probs = jnp.exp2(scores - lse[head:head + 1, rows])
                outs = datt[rows, tile * TILE:(tile + 1) * TILE] * value_mask
                grad_probs = dot_nt(qkv[:, value_tile * TILE:(value_tile + 1) * TILE], outs)
                delta = jnp.sum(probs * grad_probs, axis=0, keepdims=True)
                grad_scores = (probs * (grad_probs - delta)).astype(bf16)
                dv[tile] = dv[tile] + dot(probs.astype(bf16), outs)
                dk[tile] = dk[tile] + dot(grad_scores, queries)
                keys_t = (kt.at[0, :HEAD_DIM], kt.at[0, HEAD_DIM:], kt.at[1, HEAD_DIM:])[head][...]
                spot = (0, HEAD_DIM, 0)[head]
                dqt[tile, spot:spot + HEAD_DIM, rows] = dot(keys_t, grad_scores)
                return carry

            lax.fori_loop(0, 2, body, 0)

        att_back(me)
        gather.wait_mate()
        att_back(mate)
        if layer == 0:
            add("d", layer)
        for head in range(OWN_HEADS):
            attend(head, me, mate)
        gather.wait_across()
        att_back(across)
        if layer == 0:
            gain_stage(1)
            add("g", layer)
        else:
            add("d", layer)
        gather.wait_far()
        att_back(far)
        pending.append(gather)
        load("wo", layer - 1)
        loads["att"].wait()
        ready("o", layer)

        def out_weight(i, carry, layer=layer):
            rows = rows_of(i, 256, 256)
            half = feats // 2
            cols = pl.ds(pl.multiple_of(core * half, half), half)
            go[rows, :] = dot(att[rows, :], dbr[layer, :, cols]).astype(bf16)
            return carry

        lax.fori_loop(0, feats // 256, out_weight, 0)
        begin("o", layer)
        load("att", layer - 1)
        for name in "oab":
            total(name, layer + 1)
        attend(0, across, far)
        attend(1, across, far)
        for share in shares:
            share.serve()

        def unrotate_pairs(i, carry):
            rows = rows_of(i, size, size)
            c, s = cos_rows[rows, :], -sin_rows[rows, :]
            dproj[rows, :TILE] = turn(dqt[0, :, rows].T * score_scale, c, s).astype(bf16)
            dproj[rows, TILE:2 * TILE] = turn(dk[0, rows, :] * score_scale, c, s).astype(bf16)
            dproj[rows, 2 * TILE:3 * TILE] = dv[0, rows, :].astype(bf16)
            return carry

        def unrotate_last(i, carry):
            rows = rows_of(i, size, size)
            c, s = cos_rows[rows, :], -sin_rows[rows, :]
            lower = lane_iota((size, TILE)) < HEAD_DIM
            mixed = jnp.where(lower, dqt[1, :, rows].T, pltpu.roll(dk[1, rows, :], HEAD_DIM, 1))
            dproj[rows, 3 * TILE:4 * TILE] = turn(mixed * score_scale, c, s).astype(bf16)
            dproj[rows, 4 * TILE:] = dv[1, rows, :].astype(bf16)
            return carry

        def weigh_projection(first, last):
            def qkv_weight(i, carry):
                cols = rows_of(i, 256, 256)
                gq[cols, first:last] = dot_tn(xf[:, cols], dproj[:, first:last]).astype(bf16)
                return carry

            lax.fori_loop(0, feats // 256, qkv_weight, 0)

        lax.fori_loop(0, seq // size, unrotate_pairs, 0)
        loads["xf"].wait()
        ready("a", layer)
        weigh_projection(0, 3 * TILE)
        begin("a", layer)
        if layer:
            add("g", layer)
        else:
            gain_stage(2)
            add("u", layer)
        attend(2, across, far)
        lax.fori_loop(0, seq // size, unrotate_last, 0)
        load("qkv", layer - 1)
        load("lse", layer - 1)
        loads["wq"].wait()

        def input_part(block):
            return dot_nt(dproj[rows_of(block, size, size), :], wq[...])

        if len(scatters) > 1:
            scatters[-2].finish()
        scatter = Scatter(part, 1, got, 2 * layer + 1, sems, 6, where)
        scatters.append(scatter)
        if layer == 0:
            ready("b", layer)
            weigh_projection(3 * TILE, PROJ)
            begin("b", layer)
        scatter.send_far(input_part(far))
        scatter.send_across(input_part(across))
        scatter.send_mate(input_part(mate))
        own_part = input_part(me)
        load("wq", layer - 1)
        if layer:
            ready("b", layer)
            weigh_projection(3 * TILE, PROJ)
            begin("b", layer)
            add("u", layer)
        else:
            gain_stage(3)
            add("o", layer)
            add("a", layer)
            for name in "dg":
                total(name, 0)
            add("b", layer)
        load("flow", layer - 1)
        grad[...] = grad[...] + scatter.total(own_part)
    input_copy = pltpu.make_async_copy(grad, r["ig_out"], osems.at[0, 4])
    input_copy.start()
    for name in "uoab":
        total(name, 0)
    if spreading:
        for share in shares[-2:]:
            share.serve()
    input_copy.wait()
    for item in pending + scatters[-2:]:
        item.finish()
    for number in range(4):
        stored(number)
    for item in shares:
        item.finish()
    for copy in oshares:
        copy.wait()
    if spreading:
        for name in "dguabo":
            sums[name, 0].finish()
        q_out = r["q_out"]
        ends = (
            (r["ashare"], q_out.at[:, :, :, pl.ds(0, 3 * TILE)]),
            (r["bshare"], q_out.at[:, :, :, pl.ds(3 * TILE, 2 * TILE)]),
            (r["oshare"], r["o_out"]),
        )
        last = []
        for number, held in enumerate(ends):
            last.append(pltpu.make_async_copy(*held, osems.at[1, number]))
            last[-1].start()
        for copy in last:
            copy.wait()


RATES = ((0.03, 0.01), (0.5, 0.01), (0.03, 0.01), (0.02, 0.01), (0.6, 0.0))


def adam_step(weight, first, second, average, gradient, rate, decay):
    first_new = beta_first * first + (1.0 - beta_first) * gradient
    second_new = beta_second * second + (1.0 - beta_second) * gradient * gradient
    first_hat = first_new / (1.0 - beta_first**STEP)
    second_hat = second_new / (1.0 - beta_second**STEP)
    weight_new = weight - rate * (
        first_hat / (jnp.sqrt(second_hat) + adam_epsilon) + decay * weight
    )
    average_new = average_decay * average + (1.0 - average_decay) * weight_new
    return first_new, second_new, weight_new, average_new


def adam_kernel(*refs):
    states = [refs[4 * f:4 * f + 4] for f in range(5)]
    grads = refs[20:25]
    outs = [refs[25 + 5 * f:30 + 5 * f] for f in range(5)]
    (qs, os, ds, gs, qg, og, gg, qb, ob, gb, db, gsems, isems, usems) = refs[50:]
    width = ob.shape[3]
    for number, target in enumerate((qs, os, gs, ds)):
        pltpu.make_async_copy(grads[number], target, gsems.at[number]).start()
    chunks = []
    for family, held, grad in ((3, db, ds), (2, gb, gg), (1, ob, og), (0, qb, qg)):
        for layer in range(LAYERS):
            for part in range(3 if family == 0 else 1):
                spot = 3 * layer + part if family == 0 else layer
                chunks.append((family, held, grad, layer, part, spot))

    def view(ref, family, layer, part):
        if family:
            return ref.at[layer]
        return ref.at[layer, :, pl.ds(part * width, width)]

    arrivals = []
    for number, (family, held, grad, layer, part, spot) in enumerate(chunks):
        copies = [
            pltpu.make_async_copy(
                view(states[family][k], family, layer, part), held.at[k, spot], isems.at[number, k]
            )
            for k in range(4)
        ]
        for copy in copies:
            copy.start()
        arrivals.append(copies)

    def wait_grad(number, target):
        pltpu.make_async_copy(grads[number], target, gsems.at[number]).wait()

    gain = [ref[...] for ref in states[4]]
    gradient = grads[4][...]
    new = adam_step(*gain, gradient, *RATES[4])
    for ref, value in zip(outs[4], (gradient,) + new):
        ref[...] = value

    low = lane_iota((qs.shape[2], TILE)) < HEAD_DIM
    leaving = []
    for number, (family, held, grad, layer, part, spot) in enumerate(chunks):
        first_of = layer == 0 and part == 0
        if family == 3 and first_of:
            wait_grad(3, ds)
        if family == 2:
            if first_of:
                wait_grad(2, gs)
            for half in range(2):
                gg[layer, :, half, :] = gs[layer, :, half * width:(half + 1) * width]
        if family == 1:
            if first_of:
                wait_grad(1, os)
            half = width // 2
            og[layer, :, :half] = os[layer, 0].astype(f32)
            og[layer, :, half:] = os[layer, 1].astype(f32)
        if family == 0:
            if first_of:
                wait_grad(0, qs)

            def pair(j):
                return qs[layer, j, :, part * TILE:(part + 1) * TILE].astype(f32)

            def last(j, upper):
                tile = 4 if part == 2 else 3
                value = qs[layer, j, :, tile * TILE:(tile + 1) * TILE].astype(f32)
                return value if upper == (part > 0) else pltpu.roll(value, HEAD_DIM, 1)

            for j in (0, 2):
                turned = pltpu.roll(pair(j + 1), HEAD_DIM, 1)
                tiles = (
                    pair(j),
                    jnp.where(low, last(j, False), turned),
                    jnp.where(low, turned, last(j + 1, True)),
                )
                for k, value in enumerate(tiles):
                    start = (3 * (j // 2) + k) * TILE
                    qg[spot, :, start:start + TILE] = value
        for copy in arrivals[number]:
            copy.wait()
        rows = 32

        def body(i, carry, family=family, held=held, grad=grad, spot=spot):
            at = pl.ds(pl.multiple_of(i * rows, rows), rows)
            values = [held[k, spot, at] for k in range(4)]
            first, second, weight, average = adam_step(*values, grad[spot, at], *RATES[family])
            for k, value in enumerate((weight, first, second, average)):
                held[k, spot, at] = value
            return carry

        lax.fori_loop(0, ob.shape[2] // rows, body, 0)
        sources = (grad.at[spot],) + tuple(held.at[k, spot] for k in (1, 2, 0, 3))
        for k, source in enumerate(sources):
            copy = pltpu.make_async_copy(
                source, view(outs[family][k], family, layer, part), usems.at[number, k]
            )
            copy.start()
            leaving.append(copy)
    for copy in leaving:
        copy.wait()


def frequencies():
    half = HEAD_DIM // 2
    freq = rotary_base ** (-2.0 * np.arange(half) / HEAD_DIM)
    return jnp.asarray(np.tile(freq, (8, 4)).astype(np.float32))


def own_projection(weight, me):
    layers, rows, _ = weight.shape
    split = weight.reshape(layers, rows, 3, HEADS * HEAD_DIM)
    own = lax.dynamic_slice_in_dim(split, me * OWN_HEADS * HEAD_DIM, OWN_HEADS * HEAD_DIM, 3)
    own = own.astype(bf16)
    pairs = own[..., :TILE].reshape(layers, rows, 3 * TILE)
    last = own[..., TILE:]
    return jnp.concatenate(
        [pairs, last[:, :, 0], last[:, :, 1], jnp.zeros_like(last[:, :, 0]), last[:, :, 2]], axis=-1
    )


def whole_projection(grad):
    group, layers, rows, _ = grad.shape
    pairs = grad[..., :3 * TILE].reshape(group, layers, rows, 3, TILE)
    last = jnp.stack(
        [
            grad[..., 3 * TILE:3 * TILE + HEAD_DIM],
            grad[..., 3 * TILE + HEAD_DIM:4 * TILE],
            grad[..., 4 * TILE + HEAD_DIM:],
        ],
        axis=3,
    )
    full = jnp.concatenate([pairs, last], axis=-1)
    return full.transpose(1, 2, 3, 0, 4).reshape(layers, rows, 3 * HEADS * HEAD_DIM)


def run_forward(spreading, tokens, weights, gain, lengths, mask_row):
    size, feats = tokens.shape
    seq = size * GROUP
    ff = weights[3].shape[2]
    own = weights[0].shape[1]
    shapes = dict(
        act=((size, feats), bf16),
        xf=((LAYERS, seq, feats), bf16),
        qkv=((LAYERS, seq, PROJ), bf16),
        lse=((LAYERS, 8, seq), f32),
        att=((LAYERS, feats, seq), bf16),
        flow=((LAYERS, seq, feats), bf16),
        gu=((LAYERS, seq, 2 * ff), bf16),
        hid=((LAYERS, seq, ff), bf16),
        n1=((LAYERS, size, feats), f32),
        s1=((LAYERS, size, 128), f32),
        n2=((LAYERS, size, feats), f32),
        s2=((LAYERS, size, 128), f32),
        wq=((LAYERS, feats, PROJ), bf16),
        wo=((LAYERS, feats, feats), bf16),
        wg=((LAYERS, feats, 2 * ff), bf16),
        wd=((LAYERS, feats, ff), bf16),
        gain=((8, feats), f32),
        cos_rows=((seq, 128), f32),
        sin_rows=((seq, 128), f32),
        doc_keys=((seq, 128), jnp.int32),
        doc_queries=((8, seq), jnp.int32),
    )
    held = {name: pltpu.VMEM(*shape) for name, shape in shapes.items()}
    scratch = [held[n] for n in ("wq", "wo", "wg", "wd", "xf", "qkv", "att", "flow", "gu", "hid")]
    scratch += [
        pltpu.VMEM((seq, seq), f32),
        pltpu.VMEM((2, TILE, seq), bf16),
        pltpu.VMEM((seq, TILE), bf16),
        held["lse"],
    ]
    scratch += [held[n] for n in ("n1", "s1", "n2", "s2")]
    scratch += [
        pltpu.VMEM((size, feats), f32),
        held["act"],
        pltpu.VMEM((LAYERS, 3, size, feats), bf16),
        pltpu.VMEM((LAYERS, 3, size, feats), bf16),
        pltpu.SemaphoreType.DMA((2, LAYERS, 18)),
        pltpu.SemaphoreType.DMA((LAYERS, PIECES)),
        pltpu.SemaphoreType.DMA((LAYERS, 16)),
        pltpu.SemaphoreType.DMA((2, PIECES * LAYERS, 3 + 2 * DEPTH)),
        pltpu.SemaphoreType.DMA((2, LAYERS, 7)),
        pltpu.VMEM((2, 8, feats), f32),
        pltpu.VMEM((DEPTH, 8, feats), f32),
        pltpu.SemaphoreType.DMA((2, 1, DEPTH)),
    ]
    if spreading:
        scratch += [
            pltpu.VMEM((LAYERS, own, feats), bf16),
            pltpu.VMEM((LAYERS, own, 2 * ff), bf16),
            pltpu.VMEM((LAYERS, own, ff), bf16),
        ]
    return pl.pallas_call(
        functools.partial(forward_kernel, spreading),
        out_shape=[jax.ShapeDtypeStruct(*shape) for shape in shapes.values()],
        in_specs=[VMEM, ANY] + [VMEM if spreading else ANY] * 3
        + [VMEM, pl.BlockSpec(memory_space=pltpu.SMEM), VMEM, VMEM],
        out_specs=[ANY] * (len(shapes) - 5) + [VMEM] * 5,
        scratch_shapes=scratch,
        compiler_params=pltpu.CompilerParams(
            collective_id=0, has_side_effects=True, vmem_limit_bytes=VMEM_LIMIT
        ),
        cost_estimate=pl.CostEstimate(
            flops=12 * 10**9, bytes_accessed=60 * 10**6, transcendentals=10**7
        ),
        name="forward",
    )(tokens, *weights, gain, lengths, mask_row, frequencies())


def run_backward(spreading, cotangent, kept, weights, gain, tables):
    size, feats = cotangent.shape
    seq = size * GROUP
    xf, qkv, lse, att, flow, gu, hid, n1, s1, n2, s2 = kept
    ff = hid.shape[2]
    wq, wo, wg, wd = weights
    loaded = [n1, s1, n2, s2, xf, qkv, lse, att, flow, gu, hid, wq, wo, wg, wd]
    own = feats // (2 * DEPTH)
    half = feats // 2
    widths = dict(d=ff, g=ff, u=ff, a=3 * TILE, b=2 * TILE, o=half)
    if spreading:
        outs = dict(
            ig_out=((size, feats), f32),
            q_out=((LAYERS, GROUP, own, PROJ), bf16),
            o_out=((LAYERS, 2, own, half), bf16),
            d_res=((LAYERS, own, ff), f32),
            g_res=((LAYERS, own, 2 * ff), f32),
            gain_out=((8, feats), f32),
        )
    else:
        outs = dict(
            ig_out=((size, feats), f32),
            q_out=(wq.shape, bf16),
            o_out=((LAYERS, feats, half), bf16),
            d_out=(wd.shape, bf16),
            g_out=(wg.shape, bf16),
            gain_out=((8, feats), f32),
        )
    names = ["cot"] + [n + "_in" for n in BACK_LOADED] + list(BACK_TABLES) + list(outs)
    scratch = dict(
        bias=pltpu.VMEM((seq, seq), f32),
        dff=pltpu.VMEM((1, seq, feats), bf16),
        dbr=pltpu.VMEM((LAYERS, seq, feats), bf16),
        datt=pltpu.VMEM((seq, 2 * TILE), bf16),
        dproj=pltpu.VMEM((seq, PROJ), bf16),
        dk=pltpu.VMEM((2, seq, TILE), f32),
        dv=pltpu.VMEM((2, seq, TILE), f32),
        dqt=pltpu.VMEM((2, TILE, seq), f32),
        kt=pltpu.VMEM((2, TILE, seq), bf16),
        k2=pltpu.VMEM((seq, TILE), bf16),
        grad=pltpu.VMEM((size, feats), f32),
        part=pltpu.VMEM((2, 3, size, feats), bf16),
        got=pltpu.VMEM((2, 3, size, feats), bf16),
        gq=pltpu.VMEM((feats, PROJ), bf16),
        go=pltpu.VMEM((feats, half), bf16),
        gg=pltpu.VMEM((feats, 2 * ff), bf16),
        gd=pltpu.VMEM((feats, ff), bf16),
        sems=pltpu.SemaphoreType.DMA((2, 2 * LAYERS, 22)),
        lsems=pltpu.SemaphoreType.DMA((len(loaded),)),
        osems=pltpu.SemaphoreType.DMA((LAYERS, 5)),
        rows=pltpu.VMEM((seq, feats), bf16),
    )
    for name, array in zip(BACK_LOADED, loaded):
        if name not in ("xf", "flow"):
            scratch[name] = pltpu.VMEM(array.shape[1:], array.dtype)
    if spreading:
        scratch.update(
            gsum=pltpu.VMEM((8, feats), f32),
            gpack=pltpu.VMEM((GROUP, 8, feats), f32),
            gside=pltpu.VMEM((2, 8, feats), f32),
            gdeep=pltpu.VMEM((DEPTH, 8, feats), f32),
            gsems=pltpu.SemaphoreType.DMA((2, 1, 7)),
            csems=pltpu.SemaphoreType.REGULAR((2, 6)),
            ashare=pltpu.VMEM((LAYERS, GROUP, own, 3 * TILE), bf16),
            bshare=pltpu.VMEM((LAYERS, GROUP, own, 2 * TILE), bf16),
            oshare=pltpu.VMEM((LAYERS, 2, own, half), bf16),
            dsems=pltpu.SemaphoreType.DMA((2, 6 * LAYERS, 7)),
        )
        for name, width in widths.items():
            scratch["near_" + name] = pltpu.VMEM((DEPTH, own, width), bf16)
            scratch["apart_" + name] = pltpu.VMEM((DEPTH - 1, own, width), bf16)
            scratch["sum_" + name] = pltpu.VMEM((own, width), f32)
    in_vmem = ("d_res", "g_res", "gain_out")
    return pl.pallas_call(
        functools.partial(backward_kernel, spreading, tuple(names + list(scratch))),
        out_shape=[jax.ShapeDtypeStruct(*shape) for shape in outs.values()],
        in_specs=[VMEM] + [ANY] * 15 + [VMEM] * 5,
        out_specs=[VMEM if name in in_vmem else ANY for name in outs],
        scratch_shapes=list(scratch.values()),
        compiler_params=pltpu.CompilerParams(
            collective_id=1, has_side_effects=True, vmem_limit_bytes=VMEM_LIMIT
        ),
        cost_estimate=pl.CostEstimate(
            flops=24 * 10**9, bytes_accessed=60 * 10**6, transcendentals=10**7
        ),
        name="backward",
    )(cotangent, *loaded, gain, *tables)


def run_adam(states, grads):
    outs = []
    for family in range(5):
        shape = jax.ShapeDtypeStruct(states[4 * family].shape, f32)
        outs += [shape] * 5
    layers, own, _, width = states[8].shape
    scratch = [
        pltpu.VMEM(grads[0].shape, bf16),
        pltpu.VMEM(grads[1].shape, bf16),
        pltpu.VMEM(grads[3].shape, f32),
        pltpu.VMEM(grads[2].shape, f32),
        pltpu.VMEM((3 * layers, own, width), f32),
        pltpu.VMEM((layers, own, width), f32),
        pltpu.VMEM((layers, own, 2, width), f32),
        pltpu.VMEM((4, 3 * layers, own, width), f32),
        pltpu.VMEM((4, layers, own, width), f32),
        pltpu.VMEM((4, layers, own, 2, width), f32),
        pltpu.VMEM((4, layers, own, width), f32),
        pltpu.SemaphoreType.DMA((4,)),
        pltpu.SemaphoreType.DMA((6 * layers, 4)),
        pltpu.SemaphoreType.DMA((6 * layers, 5)),
    ]
    return pl.pallas_call(
        adam_kernel,
        out_shape=outs,
        in_specs=[ANY] * 16 + [VMEM] * 4 + [ANY] * 4 + [VMEM],
        out_specs=[ANY] * 20 + [VMEM] * 5,
        scratch_shapes=scratch,
        compiler_params=pltpu.CompilerParams(vmem_limit_bytes=VMEM_LIMIT),
        cost_estimate=pl.CostEstimate(
            flops=2 * 10**7, bytes_accessed=37 * 10**6, transcendentals=10**6
        ),
        name="adam",
    )(*states, *grads)


def adamw(weight, first, second, average, gradient, rate, decay):
    first_new = beta_first * first + (1.0 - beta_first) * gradient
    second_new = beta_second * second + (1.0 - beta_second) * gradient * gradient
    first_hat = first_new / (1.0 - beta_first**STEP)
    second_hat = second_new / (1.0 - beta_second**STEP)
    weight_new = weight - rate * (
        first_hat / (jnp.sqrt(second_hat) + adam_epsilon) + decay * weight
    )
    average_new = average_decay * average + (1.0 - average_decay) * weight_new
    return (gradient, first_new, second_new, weight_new, average_new)


def shards(
    spreading,
    tokens,
    cotangent,
    lengths,
    key_mask,
    qkv_weight,
    qkv_first,
    qkv_second,
    qkv_average,
    out_weight,
    out_first,
    out_second,
    out_average,
    gate_up_weight,
    gate_up_first,
    gate_up_second,
    gate_up_average,
    down_weight,
    down_first,
    down_second,
    down_average,
    norm_gain,
    gain_first,
    gain_second,
    gain_average,
):
    me = lax.axis_index("mp")
    own = gate_up_weight.shape[1]
    ff = gate_up_weight.shape[3]
    feats = tokens.shape[1]
    if spreading:
        gain = jnp.zeros((8, feats), f32)
        gain = lax.dynamic_update_slice(
            gain, norm_gain.reshape(2 * LAYERS, own), (0, lax.axis_index("dp") * own)
        )
    else:
        gain = lax.all_gather(norm_gain, "dp", axis=2, tiled=True).reshape(2 * LAYERS, feats)
        gain = jnp.concatenate([gain, jnp.zeros((8 - 2 * LAYERS, feats), f32)], axis=0)
    if spreading:
        owned = (own_projection(qkv_weight, me), out_weight, gate_up_weight, down_weight)
    else:
        owned = (
            own_projection(qkv_weight, me),
            out_weight.astype(bf16),
            gate_up_weight.reshape(LAYERS, own, 2 * ff).astype(bf16),
            down_weight.astype(bf16),
        )
        owned = [lax.all_gather(w, "dp", axis=1, tiled=True) for w in owned]
    act, *kept = run_forward(spreading, tokens, owned, gain, lengths, key_mask[None, :])
    weights, gain, tables, kept = kept[-9:-5], kept[-5], kept[-4:], kept[:-9]
    backward = run_backward(spreading, cotangent, kept, weights, gain, tables)
    if spreading:
        input_grad, gq, go, gd, gg, gain_sum = backward
        gain_grad = lax.dynamic_slice_in_dim(
            gain_sum[:2 * LAYERS].reshape(LAYERS, 2, -1), lax.axis_index("dp") * own, own, 2
        )
        states = (
            qkv_weight, qkv_first, qkv_second, qkv_average,
            out_weight, out_first, out_second, out_average,
            gate_up_weight, gate_up_first, gate_up_second, gate_up_average,
            down_weight, down_first, down_second, down_average,
            norm_gain, gain_first, gain_second, gain_average,
        )
        return (act, input_grad, *run_adam(states, (gq, go, gg, gd, gain_grad)))
    else:
        input_grad, gq, go, gd, gg, gain_sum = backward
        gq, go, gg, gd = [
            lax.psum_scatter(g, "dp", scatter_dimension=1, tiled=True) for g in (gq, go, gg, gd)
        ]
        gq, go = lax.all_gather(gq, "mp"), lax.all_gather(go, "mp")
        gain_part = gain_sum[:2 * LAYERS].reshape(LAYERS, 2, -1)
        gain_grad = lax.psum_scatter(
            lax.psum(gain_part, "mp"), "dp", scatter_dimension=2, tiled=True
        )
    qkv_grad = whole_projection(gq.astype(f32))
    out_grad = jnp.concatenate([go[0], go[1]], axis=-1).astype(f32)
    gate_up_grad = gg.reshape(LAYERS, own, 2, ff).astype(f32)
    down_grad = gd.astype(f32)
    results = [act, input_grad]
    results.extend(adamw(qkv_weight, qkv_first, qkv_second, qkv_average, qkv_grad, 0.03, 0.01))
    results.extend(adamw(out_weight, out_first, out_second, out_average, out_grad, 0.5, 0.01))
    results.extend(
        adamw(
            gate_up_weight, gate_up_first, gate_up_second, gate_up_average, gate_up_grad, 0.03, 0.01
        )
    )
    results.extend(
        adamw(down_weight, down_first, down_second, down_average, down_grad, 0.02, 0.01)
    )
    results.extend(adamw(norm_gain, gain_first, gain_second, gain_average, gain_grad, 0.6, 0.0))
    return tuple(results)


def solution(mesh):
    spreading = mesh.shape["dp"] == 2 * DEPTH
    return jax.shard_map(
        functools.partial(shards, spreading),
        mesh=mesh,
        in_specs=(
            P(("dp", "mp"), None),
            P(("dp", "mp"), None),
            P("dp", None),
            P("dp"),
            P(None, "dp", None),
            P(None, "dp", None),
            P(None, "dp", None),
            P(None, "dp", None),
            P(None, "dp", None),
            P(None, "dp", None),
            P(None, "dp", None),
            P(None, "dp", None),
            P(None, "dp", None, "mp"),
            P(None, "dp", None, "mp"),
            P(None, "dp", None, "mp"),
            P(None, "dp", None, "mp"),
            P(None, "dp", "mp"),
            P(None, "dp", "mp"),
            P(None, "dp", "mp"),
            P(None, "dp", "mp"),
            P(None, None, "dp"),
            P(None, None, "dp"),
            P(None, None, "dp"),
            P(None, None, "dp"),
        ),
        out_specs=(
            P(("dp", "mp"), None),
            P(("dp", "mp"), None),
            P(None, "dp", None),
            P(None, "dp", None),
            P(None, "dp", None),
            P(None, "dp", None),
            P(None, "dp", None),
            P(None, "dp", None),
            P(None, "dp", None),
            P(None, "dp", None),
            P(None, "dp", None),
            P(None, "dp", None),
            P(None, "dp", None, "mp"),
            P(None, "dp", None, "mp"),
            P(None, "dp", None, "mp"),
            P(None, "dp", None, "mp"),
            P(None, "dp", None, "mp"),
            P(None, "dp", "mp"),
            P(None, "dp", "mp"),
            P(None, "dp", "mp"),
            P(None, "dp", "mp"),
            P(None, "dp", "mp"),
            P(None, None, "dp"),
            P(None, None, "dp"),
            P(None, None, "dp"),
            P(None, None, "dp"),
            P(None, None, "dp"),
        ),
        check_vma=False,
    )
```

```python
import functools
import math

import jax
import jax.numpy as jnp
import numpy as np
from jax import lax
from jax.experimental import pallas as pl
from jax.experimental.pallas import tpu as pltpu
from jax.sharding import PartitionSpec as P

HEADS = 12
HEAD_DIM = 64
LAYERS = 2
STEP = 10
GROUP = 4
DEPTH = 4
LEAD = 1
PIECES = 4
OWN_HEADS = HEADS // GROUP
TILE = 2 * HEAD_DIM
PROJ = 5 * TILE

rotary_base = 1000.0
norm_epsilon = 1e-05
masked_score = -1e30
beta_first = 0.5
beta_second = 0.5
adam_epsilon = 1e-08
average_decay = 0.5
score_scale = HEAD_DIM ** (-0.5)
log2e = math.log2(math.e)

MESH = pl.DeviceIdType.MESH
ANY = pl.BlockSpec(memory_space=pl.ANY)
VMEM = pl.BlockSpec(memory_space=pltpu.VMEM)
f32 = jnp.float32
bf16 = jnp.bfloat16
VMEM_LIMIT = 127 * 2**19


def dot(a, b):
    return jnp.dot(a, b, preferred_element_type=f32)


def dot_nt(a, b):
    return lax.dot_general(a, b, (((1,), (1,)), ((), ())), preferred_element_type=f32)


def dot_tn(a, b):
    return lax.dot_general(a, b, (((0,), (0,)), ((), ())), preferred_element_type=f32)


def places():
    me = lax.axis_index("mp")
    core = lax.rem(me, 2)
    side = lax.div(me, 2)
    return me, me + 1 - 2 * core, me + 2 - 4 * side, 3 - me, core


def push(src, dst, sems, layer, number, who):
    return pltpu.make_async_remote_copy(
        src_ref=src,
        dst_ref=dst,
        send_sem=sems.at[0, layer, number],
        recv_sem=sems.at[1, layer, number],
        device_id={"mp": who},
        device_id_type=MESH,
    )


class Spread:
    def __init__(self, own):
        index = lax.axis_index("dp")
        self.own = own
        self.z, self.x = lax.div(index, 2), lax.rem(index, 2)

    def device(self, step):
        return 2 * lax.rem(self.z + step, DEPTH) + self.x

    def beside(self, step):
        return 2 * lax.rem(self.z + step, DEPTH) + 1 - self.x

    def rows(self, index):
        return pl.ds(pl.multiple_of(index * self.own, self.own), self.own)


def greet(mate, across, far=None, spread=None):
    barrier = pltpu.get_barrier_semaphore()
    packs = [mate, across] if far is None else [mate, across, far]
    for who in packs:
        pl.semaphore_signal(barrier, inc=1, device_id={"mp": who}, device_id_type=MESH)
    others = []
    if spread is not None:
        others = [spread.beside(0)] + [spread.device(step) for step in range(1, DEPTH)]
        for who in others:
            pl.semaphore_signal(barrier, inc=1, device_id={"dp": who}, device_id_type=MESH)
    pl.semaphore_wait(barrier, len(packs) + len(others))


def ship(src, dst, sems, piece, number, who):
    return pltpu.make_async_remote_copy(
        src_ref=src,
        dst_ref=dst,
        send_sem=sems.at[0, piece, number],
        recv_sem=sems.at[1, piece, number],
        device_id={"dp": who},
        device_id_type=MESH,
    )


class WeightGather:
    def __init__(self, source, target, layer, piece, sems, local, spread, cols=None):
        self.target, self.layer, self.cols = target, layer, cols
        self.piece, self.sems, self.spread = piece, sems, spread
        z, x = spread.z, spread.x
        own = self.own_part(source)
        place = self.view(z, x)
        self.local = pltpu.make_async_copy(own, place, local)
        self.beside = self.send(own, place, 0, 0, 2 * z + 1 - x)
        self.up = self.send(own, place, 1, 1 + z, 2 * jnp.minimum(z + 1, DEPTH - 1) + x)
        self.down = self.send(own, place, 2, 1 + z, 2 * jnp.maximum(z - 1, 0) + x)
        self.hops = [(far, way) for far in range(1, DEPTH) for way in (-1, 1)]
        self.todo = list(self.hops)

    def own_part(self, source):
        return source.at[self.layer]

    def view(self, z, x):
        return self.target.at[self.layer, self.spread.rows(2 * z + x)]

    def send(self, src, dst, out, into, who):
        return pltpu.make_async_remote_copy(
            src_ref=src,
            dst_ref=dst,
            send_sem=self.sems.at[0, self.piece, out],
            recv_sem=self.sems.at[1, self.piece, into],
            device_id={"dp": who},
            device_id_type=MESH,
        )

    def start(self):
        self.local.start()
        pl.when(self.spread.z < DEPTH - 1)(self.up.start)
        pl.when(self.spread.z > 0)(self.down.start)
        self.beside.start()

    def hop(self, far, way):
        z, x = self.spread.z, self.spread.x
        source = jnp.clip(z + way * far, 0, DEPTH - 1)
        block = self.view(source, x)
        onward = jnp.clip(z - way, 0, DEPTH - 1)
        arrive = self.send(block, block, 3 + source, 1 + source, 2 * source + x)
        over = self.send(block, block, 3 + source, 1 + DEPTH + source, 2 * z + 1 - x)
        along = self.send(block, block, 3 + DEPTH + source, 1 + source, 2 * onward + x)
        comes = z >= far if way < 0 else z + far < DEPTH
        goes = z > 0 if way > 0 else z < DEPTH - 1
        return arrive, over, along, comes, jnp.logical_and(comes, goes)

    def serve(self, count=2 * DEPTH):
        while self.todo and count:
            count -= 1
            arrive, over, along, comes, goes = self.hop(*self.todo.pop(0))

            pl.when(comes)(arrive.wait_recv)
            pl.when(goes)(along.start)
            pl.when(comes)(over.start)

    def wait(self):
        self.serve()
        self.local.wait()
        self.beside.wait_recv()
        z, x = self.spread.z, self.spread.x
        for step in range(1, DEPTH):
            source = lax.rem(z + step, DEPTH)
            block = self.view(source, 1 - x)
            self.send(block, block, 3, 1 + DEPTH + source, 2 * z + 1 - x).wait_recv()

    def finish(self):
        self.beside.wait_send()
        pl.when(self.spread.z < DEPTH - 1)(self.up.wait_send)
        pl.when(self.spread.z > 0)(self.down.wait_send)
        for far, way in self.hops:
            arrive, over, along, comes, goes = self.hop(far, way)
            pl.when(comes)(over.wait_send)
            pl.when(goes)(along.wait_send)


class QuarterGather(WeightGather):
    def __init__(self, source, target, layer, piece, sems, local, spread, half, pack_sems, where):
        me, mate, across, far, core = where
        self.side, self.rows = lax.div(me, 2), spread.own // 2
        cols = pl.ds(pl.multiple_of(core * half, half), half)
        super().__init__(source, target, layer, piece, sems, local, spread, cols)
        here = spread.rows(2 * spread.z + spread.x)
        self.local = pltpu.make_async_copy(source.at[layer], target.at[layer, here], local)
        self.over, self.swap = [], []
        for step in range(DEPTH):
            z = lax.rem(spread.z + step, DEPTH)
            for number, x in enumerate((spread.x, 1 - spread.x)):
                if step or number:
                    spot = 2 * step + number - 1
                    block = self.view(z, x)
                    self.over.append(push(block, block, pack_sems, layer, spot, across))
                    block = target.at[layer, spread.rows(2 * z + x), cols]
                    self.swap.append(push(block, block, pack_sems, layer, 7 + spot, mate))

    def part_rows(self, start):
        return pl.ds(pl.multiple_of(start + self.side * self.rows, self.rows), self.rows)

    def own_part(self, source):
        return source.at[self.layer, self.part_rows(0), self.cols]

    def view(self, z, x):
        rows = self.part_rows((2 * z + x) * self.spread.own)
        return self.target.at[self.layer, rows, self.cols]

    def share_across(self):
        super().wait()
        for copy in self.over:
            copy.start()

    def share(self):
        for copy, onward in zip(self.over, self.swap):
            copy.wait_recv()
            onward.start()

    def wait(self):
        for copy in self.swap:
            copy.wait_recv()

    def finish(self):
        super().finish()
        for copy in self.over + self.swap:
            copy.wait_send()


class WeightSum:
    def __init__(self, grad, near, apart, piece, sems, spread, credits, again, more, total, part):
        self.grad, self.near, self.apart, self.spread = grad, near, apart, spread
        self.near_credit, self.apart_credit = credits
        self.again, self.more = again, more
        self.sum, self.part = total, part
        self.beside = [
            ship(grad.at[self.rows(spread.beside(step))], near.at[step], sems, piece, step,
                 spread.beside(0))
            for step in range(DEPTH)
        ]
        self.along = [
            ship(grad.at[self.rows(spread.device(step))], apart.at[step - 1], sems, piece,
                 DEPTH - 1 + step, spread.device(step))
            for step in range(1, DEPTH)
        ]

    def rows(self, index):
        if self.part is None:
            return self.spread.rows(index)
        half = self.spread.own // 2
        return pl.ds(pl.multiple_of(index * self.spread.own + self.part * half, half), half)

    def start(self):
        if self.again:
            pl.semaphore_wait(self.near_credit, 1)
        for copy in self.beside[1:] + self.beside[:1]:
            copy.start()

    def credit(self, sem, who):
        pl.semaphore_signal(sem, inc=1, device_id={"dp": who}, device_id_type=MESH)

    def add(self):
        if self.again:
            pl.semaphore_wait(self.apart_credit, DEPTH - 1)
        for step in range(1, DEPTH):
            self.beside[step].wait_recv()
            rows = self.rows(self.spread.device(step))
            self.grad[rows, :] = (
                self.grad[rows, :].astype(f32) + self.near[step].astype(f32)
            ).astype(bf16)
            self.along[step - 1].start()
        self.beside[0].wait_recv()
        rows = self.rows(self.spread.device(0))
        self.sum[...] = self.grad[rows, :].astype(f32) + self.near[0].astype(f32)
        if self.more:
            self.credit(self.near_credit, self.spread.beside(0))

    def total(self):
        for copy in self.along:
            copy.wait_recv()
        result = self.sum[...]
        for step in range(DEPTH - 1):
            result = result + self.apart[step].astype(f32)
        if self.more:
            for step in range(1, DEPTH):
                self.credit(self.apart_credit, self.spread.device(step))
        return result

    def finish(self):
        for copy in self.beside + self.along:
            copy.wait_send()


def rows_of(block, size, extent):
    return pl.ds(pl.multiple_of(block * size, size), extent)


def lane_iota(shape):
    return lax.broadcasted_iota(jnp.int32, shape, len(shape) - 1)


def half_masks():
    low = (lane_iota((1, TILE)) < HEAD_DIM).astype(f32)
    return low.astype(bf16), (1.0 - low).astype(bf16)


def turn(tile, cos_rows, sin_rows):
    lane = lane_iota(tile.shape) % HEAD_DIM
    half = HEAD_DIM // 2
    partner = jnp.where(
        lane < half, pltpu.roll(tile, TILE - half, 1), pltpu.roll(tile, half, 1)
    )
    return tile * cos_rows + partner * sin_rows


def write_bias(bias, doc_keys, doc_queries):
    seq = bias.shape[0]
    step = 128

    def body(i, carry):
        rows = rows_of(i, step, step)
        keys = doc_keys[rows, :][:, :1]
        same = keys == doc_queries[:1, :]
        spot = lax.broadcasted_iota(jnp.int32, (step, seq), 0) + i * step
        own = spot == lax.broadcasted_iota(jnp.int32, (step, seq), 1)
        bias[rows, :] = jnp.where(jnp.logical_or(same, own), 0.0, masked_score)
        return carry

    lax.fori_loop(0, seq // step, body, 0)


def write_tables(lengths, mask_row, freq, cos_rows, sin_rows, doc_keys, doc_queries):
    ends = []
    for doc in range(lengths.shape[1]):
        ends.append(lengths[0, doc] + (ends[-1] if ends else 0))

    def document(spots):
        number = jnp.zeros(spots.shape, jnp.int32)
        for end in ends:
            number = number + (spots >= end).astype(jnp.int32)
        return number

    seq = cos_rows.shape[0]
    doc_queries[...] = document(lane_iota(doc_queries.shape))
    step = 128

    def body(i, carry):
        rows = rows_of(i, step, step)
        spots = lax.broadcasted_iota(jnp.int32, (step, 128), 0) + i * step
        start = jnp.zeros(spots.shape, jnp.int32)
        for end in ends:
            start = jnp.maximum(start, jnp.where(spots >= end, end, 0))
        seen = jnp.broadcast_to(mask_row[:, rows].astype(f32), (step, step)).T
        doc_keys[rows, :] = jnp.where(seen > 0.5, document(spots), -1)
        angle = (spots - start).astype(f32) * freq[:1, :]
        sine = jnp.sin(angle)
        cos_rows[rows, :] = jnp.cos(angle)
        lower = lane_iota(spots.shape) % HEAD_DIM < HEAD_DIM // 2
        sin_rows[rows, :] = jnp.where(lower, -sine, sine)
        return carry

    lax.fori_loop(0, seq // step, body, 0)


class Gather:
    def __init__(self, ref, slot, layer, sems, first_sem, size, where):
        me, mate, across, far, core = where
        self.across, self.mate = [], []
        self.forward = []
        half = size // 2

        def piece(block, part):
            start = pl.multiple_of(block * size + part * half, half)
            return ref.at[slot, pl.ds(start, half)]

        for part in range(2):
            own = piece(me, part)
            theirs = piece(across, part)
            self.across.append(push(own, own, sems, layer, first_sem + part, across))
            self.mate.append(push(own, own, sems, layer, first_sem + 2 + part, mate))
            self.forward.append(push(theirs, theirs, sems, layer, first_sem + 4 + part, mate))

    def start(self):
        for copy in self.across + self.mate:
            copy.start()

    def wait_mate(self):
        for copy in self.mate:
            copy.wait_recv()

    def wait_across(self):
        for copy, onward in zip(self.across, self.forward):
            copy.wait_recv()
            onward.start()

    def wait_far(self):
        for copy in self.forward:
            copy.wait_recv()

    def finish(self):
        for copy in self.across + self.mate + self.forward:
            copy.wait_send()


class Share:
    def __init__(self, ref, layer, sems, first_sem, where):
        me, mate, across, far, core = where
        own, theirs = ref.at[layer, me], ref.at[layer, across]
        self.ref, self.layer, self.me = ref, layer, me
        self.over = push(own, own, sems, layer, first_sem, across)
        self.near = push(own, own, sems, layer, first_sem + 1, mate)
        self.onward = push(theirs, theirs, sems, layer, first_sem + 2, mate)

    def start(self, block):
        self.ref[self.layer, self.me] = block
        self.over.start()
        self.near.start()

    def serve(self):
        self.over.wait_recv()
        self.onward.start()

    def finish(self):
        self.near.wait_recv()
        self.onward.wait_recv()
        for copy in (self.over, self.near, self.onward):
            copy.wait_send()


class Scatter:
    def __init__(self, part, slot, got, layer, sems, first_sem, where):
        me, mate, across, far, core = where
        self.part, self.slot, self.got = part, slot, got
        self.far = push(part.at[slot, 0], got.at[slot, 0], sems, layer, first_sem, mate)
        self.over = push(part.at[slot, 1], got.at[slot, 1], sems, layer, first_sem + 1, across)
        self.near = push(part.at[slot, 2], got.at[slot, 2], sems, layer, first_sem + 2, mate)

    def send_far(self, block):
        self.part[self.slot, 0] = block.astype(bf16)
        self.far.start()

    def send_across(self, block):
        self.far.wait_recv()
        self.part[self.slot, 1] = (block + self.got[self.slot, 0].astype(f32)).astype(bf16)
        self.over.start()

    def send_mate(self, block):
        self.part[self.slot, 2] = block.astype(bf16)
        self.near.start()

    def total(self, block):
        self.near.wait_recv()
        self.over.wait_recv()
        return (
            block
            + self.got[self.slot, 1].astype(f32)
            + self.got[self.slot, 2].astype(f32)
        )

    def finish(self):
        for copy in (self.far, self.over, self.near):
            copy.wait_send()


def normed_rows(rows):
    centered = rows - jnp.mean(rows, axis=-1, keepdims=True)
    inverse = lax.rsqrt(jnp.mean(centered * centered, axis=-1, keepdims=True) + norm_epsilon)
    return centered * inverse, inverse


def forward_kernel(
    spreading, tok, wq_in, wo_in, wg_in, wd_in, gain_in, lengths, mask_row, freq,
    act_out, xf_out, qkv_out, lse_out, att_out, flow_out, gu_out, hid_out,
    n1_out, s1_out, n2_out, s2_out, wq_out, wo_out, wg_out, wd_out, gain,
    cos_rows, sin_rows, doc_keys, doc_queries,
    wq, wo, wg, wd, xf, qkv, att, flow, gu, hid, bias, vt, k2, lse,
    n1, s1, n2, s2, first, act, part, got, sems, wsems, osems, dsems, ssems, gside, gdeep, gsems, *own_low,
):
    where = places()
    me, mate, across, far, core = where
    weight_outs = (wq_out, wo_out, wg_out, wd_out)
    size = tok.shape[0]
    seq = size * GROUP
    ff = hid.shape[2]
    spread = Spread(wq_in.shape[1]) if spreading else None
    weights = []
    cast = ()
    if spreading:
        cast = ((wo_in, own_low[0]), (wg_in, own_low[1]), (wd_in, own_low[2]))
        wo_in, wg_in, wd_in = own_low
    parts = (
        (wq_in, wq, None), (wo_in, wo, None), (wg_in, wg, None), (wd_in, wd, None),
    )
    for layer in range(LAYERS):
        for number, (source, target, cols) in enumerate(parts):
            local = wsems.at[layer, number]
            piece = PIECES * layer + number
            if not spreading:
                if cols is not None:
                    source, target = source.at[:, :, cols], target.at[:, :, cols]
                weights.append(pltpu.make_async_copy(source.at[layer], target.at[layer], local))
            elif number == 1:
                weights.append(
                    QuarterGather(source, target, layer, piece, dsems, local, spread,
                                  wo.shape[2] // 2, ssems, where)
                )
            else:
                weights.append(
                    WeightGather(source, target, layer, piece, dsems, local, spread, cols)
                )
    xf[0, rows_of(me, size, size), :] = tok[...]
    greet(mate, across, None, spread)
    gains = []
    if spreading:
        gdeep[spread.z] = gain_in[...]
        own = gdeep.at[spread.z]
        for step in range(1, DEPTH):
            gains.append(ship(own, own, gsems, 0, step, spread.device(step)))
            gains[-1].start()
    else:
        gain[...] = gain_in[...]
    ahead = LEAD if spreading else len(weights)
    for item in weights[:ahead]:
        item.start()

    def gain_stage(stage):
        if not spreading:
            return
        if stage == 0:
            for copy in gains:
                copy.wait_recv()
            gside[spread.x] = gdeep[0] + gdeep[1] + gdeep[2] + gdeep[3]
            own = gside.at[spread.x]
            gains.append(ship(own, own, gsems, 0, 0, spread.beside(0)))
            gains[-1].start()
        else:
            gains[-1].wait_recv()
            gain[...] = gside[0] + gside[1]
            for copy in gains:
                copy.wait_send()

    queue = [(k, hop) for k in range(len(weights)) for hop in range(6)] if spreading else []

    def pump(count):
        for number in range(min(count, len(queue))):
            k, hop = queue.pop(0)
            if hop == 0 and k + ahead < len(weights):
                weights[k + ahead].start()
            weights[k].serve(1)

    pending = []
    stores = []

    def store(number, layer, source, target):
        copy = pltpu.make_async_copy(source.at[layer], target.at[layer], osems.at[layer, number])
        copy.start()
        stores.append(copy)

    row_gather = Gather(xf, 0, 0, sems, 0, size, where)
    row_gather.start()
    for source, target in cast:
        if len(source.shape) == 3:
            target[...] = source[...].astype(bf16)
        else:
            for layer in range(LAYERS):
                for half in range(2):
                    target[layer, :, half * ff:(half + 1) * ff] = source[layer, :, half, :].astype(bf16)
    write_tables(lengths, mask_row, freq, cos_rows, sin_rows, doc_keys, doc_queries)
    write_bias(bias, doc_keys, doc_queries)
    low_mask, high_mask = half_masks()

    for layer in range(LAYERS):
        if layer == 0:
            pump(12)
        weights[PIECES * layer].wait()

        def project(block, layer=layer):
            rows = rows_of(block, size, size)
            proj = dot(xf[layer, rows, :], wq[layer])
            c, s = cos_rows[rows, :], sin_rows[rows, :]
            for tile in (0, 1, 3):
                piece = proj[:, tile * TILE:(tile + 1) * TILE]
                qkv[layer, rows, tile * TILE:(tile + 1) * TILE] = turn(piece, c, s).astype(bf16)
            for tile in (2, 4):
                piece = proj[:, tile * TILE:(tile + 1) * TILE]
                qkv[layer, rows, tile * TILE:(tile + 1) * TILE] = piece.astype(bf16)

        project(me)
        row_gather.wait_mate()
        project(mate)
        row_gather.wait_across()
        pump(2)
        project(across)
        row_gather.wait_far()
        project(far)
        if layer == 0:
            gain_stage(0)
        pending.append(row_gather)
        store(0, layer, xf, xf_out)
        store(1, layer, qkv, qkv_out)
        vt[0] = qkv[layer, :, 2 * TILE:3 * TILE].T
        vt[1] = qkv[layer, :, 4 * TILE:5 * TILE].T
        k2[...] = pltpu.roll(qkv[layer, :, 3 * TILE:4 * TILE].astype(f32), HEAD_DIM, 1).astype(bf16)

        sends = []
        forwards = []
        for head in range(OWN_HEADS):
            query_tile = (0, 0, 3)[head]
            mask = (low_mask, high_mask, low_mask)[head]

            def attend(i, carry, layer=layer, head=head, query_tile=query_tile, mask=mask):
                rows = rows_of(i, size, size)
                queries = qkv[layer, rows, query_tile * TILE:(query_tile + 1) * TILE] * mask
                keys = k2[...] if head == 2 else qkv[layer, :, TILE:2 * TILE]
                values = (vt.at[0, :HEAD_DIM], vt.at[0, HEAD_DIM:], vt.at[1, HEAD_DIM:])[head][...]
                scores = dot_nt(keys, queries) * (score_scale * log2e) + bias[:, rows]
                top = jnp.max(scores, axis=0, keepdims=True)
                probs = jnp.exp2(scores - top)
                total = jnp.sum(probs, axis=0, keepdims=True)
                result = dot(values, probs.astype(bf16)) / total
                spot = pl.ds(
                    pl.multiple_of(me * (OWN_HEADS * HEAD_DIM) + head * HEAD_DIM, HEAD_DIM), HEAD_DIM
                )
                att[layer, spot, rows] = result.astype(bf16)
                lse[layer, head:head + 1, rows] = top + jnp.log(total) * log2e
                return carry

            lax.fori_loop(0, seq // size, attend, 0)

            def features(block, head=head, layer=layer):
                start = block * (OWN_HEADS * HEAD_DIM) + head * HEAD_DIM
                return att.at[layer, pl.ds(pl.multiple_of(start, HEAD_DIM), HEAD_DIM)]

            own, theirs = features(me), features(across)
            to_across = push(own, own, sems, layer, 6 + head, across)
            to_mate = push(own, own, sems, layer, 9 + head, mate)
            onward = push(theirs, theirs, sems, layer, 12 + head, mate)
            to_across.start()
            to_mate.start()
            if head:
                sends[-2].wait_recv()
                forwards[-1].start()
            if spreading and head == 0:
                weights[PIECES * layer + 1].share_across()
            if spreading and head == 2:
                weights[PIECES * layer + 1].share()
            pump(2)
            sends += [to_across, to_mate]
            forwards.append(onward)
        sends[-2].wait_recv()
        forwards[-1].start()
        for head in range(OWN_HEADS):
            sends[2 * head + 1].wait_recv()
            forwards[head].wait_recv()
        store(2, layer, lse, lse_out)
        store(3, layer, att, att_out)
        if layer == 0:
            gain_stage(1)
        pump(2)
        for number in (1, 2):
            weights[PIECES * layer + number].wait()

        def feed(block, keep, layer=layer):
            rows = rows_of(block, size, size)
            branch = dot_tn(att[layer, :, rows], wo[layer])
            normed, inverse = normed_rows(xf[layer, rows, :].astype(f32) + branch)
            first_rows = normed * gain[2 * layer:2 * layer + 1, :]
            if keep:
                n1[layer] = normed
                s1[layer] = jnp.broadcast_to(inverse, s1.shape[1:])
                first[...] = first_rows
            first_low = first_rows.astype(bf16)
            flow[layer, rows, :] = first_low
            gate_up = dot(first_low, wg[layer])
            gate, upward = gate_up[:, :ff], gate_up[:, ff:]
            gu[layer, rows, :] = gate_up.astype(bf16)
            hid[layer, rows, :] = (gate / (1.0 + jnp.exp(-gate)) * upward).astype(bf16)

        def down(block, layer=layer):
            return dot_nt(hid[layer, rows_of(block, size, size), :], wd[layer])

        for number, block in enumerate((far, across, mate, me)):
            feed(block, number == 3)
            pump(2)
        weights[PIECES * layer + 3].wait()
        for number, held in enumerate((wq, wo, wg, wd)):
            store(12 + number, layer, held, weight_outs[number])
        scatter = Scatter(part, layer, got, layer, sems, 15, where)
        scatter.send_far(down(far))
        scatter.send_across(down(across))
        scatter.send_mate(down(mate))
        own_part = down(me)
        pump(2)
        store(4, layer, flow, flow_out)
        store(5, layer, gu, gu_out)
        store(6, layer, hid, hid_out)
        store(7, layer, n1, n1_out)
        store(8, layer, s1, s1_out)
        pump(4)
        ffn = scatter.total(own_part)
        pending.append(scatter)
        normed, inverse = normed_rows(first[...] + ffn)
        n2[layer] = normed
        s2[layer] = jnp.broadcast_to(inverse, s2.shape[1:])
        result = (normed * gain[2 * layer + 1:2 * layer + 2, :]).astype(bf16)
        store(9, layer, n2, n2_out)
        store(10, layer, s2, s2_out)
        if layer + 1 < LAYERS:
            xf[layer + 1, rows_of(me, size, size), :] = result
            row_gather = Gather(xf, layer + 1, layer + 1, sems, 0, size, where)
            row_gather.start()
            pump(2)
        else:
            act[...] = result
            copy = pltpu.make_async_copy(act, act_out, osems.at[0, 11])
            copy.start()
            stores.append(copy)
        for copy in sends + forwards:
            copy.wait_send()
    if spreading:
        pending += weights
    for item in pending:
        item.finish()
    for copy in stores:
        copy.wait()


BACK_LOADED = (
    "n1", "s1", "n2", "s2", "xf", "qkv", "lse", "att", "flow", "gu", "hid", "wq", "wo", "wg", "wd",
)
BACK_TABLES = ("gain", "cos_rows", "sin_rows", "doc_keys", "doc_queries")
BACK_SCRATCH = (
    "bias", "dff", "dbr", "datt", "dproj", "dk", "dv", "dqt", "kt", "k2", "grad", "part", "got",
    "gq", "go", "gg", "gd", "sems", "lsems", "osems",
)

def backward_kernel(spreading, names, *refs):
    r = dict(zip(names, refs))
    cot = r["cot"]
    gain, cos_rows, sin_rows, doc_keys, doc_queries = (r[n] for n in BACK_TABLES)
    (
        bias, dff, dbr, datt, dproj, dk, dv, dqt, kt, k2, grad, part, got,
        gq, go, gg, gd, sems, lsems, osems,
    ) = (r[n] for n in BACK_SCRATCH)
    n1, s1, n2, s2, qkv, lse, att, gu, hid, wq, wo, wg, wd = (
        r[n] for n in BACK_LOADED if n not in ("xf", "flow")
    )
    xf = flow = r["rows"]
    where = places()
    me, mate, across, far, core = where
    size = cot.shape[0]
    seq = size * GROUP
    ff = hid.shape[1]
    feats = xf.shape[1]
    own_feats = OWN_HEADS * HEAD_DIM
    held = {n: (r[n + "_in"], r.get(n, r["rows"])) for n in BACK_LOADED}
    order = list(held)
    loads = {}

    def load(name, layer):
        if layer < 0:
            return
        source, target = held[name]
        copy = pltpu.make_async_copy(source.at[layer], target, lsems.at[order.index(name)])
        copy.start()
        loads[name] = copy

    for name in ("n2", "s2", "wd", "gu", "wg", "hid", "n1", "s1", "flow", "wo", "qkv", "lse", "att", "wq"):
        load(name, LAYERS - 1)
    spread = Spread(feats // (2 * DEPTH)) if spreading else None
    greet(mate, across, far if spreading else None, spread)
    low_mask, high_mask = half_masks()
    grad[...] = cot[...]
    pending = []
    scatters = []
    stores = {}
    sums = {}
    shares = []
    pieces = dict(
        d=gd.at[:, :], g=gg.at[:, :ff], u=gg.at[:, ff:],
        a=gq.at[:, :3 * TILE], b=gq.at[:, 3 * TILE:], o=go.at[:, :],
    )
    gsum = r["gsum"] if spreading else r["gain_out"]
    gsum[...] = jnp.zeros_like(gsum)

    def begin(name, layer):
        if not spreading:
            if name not in "ga":
                number = "boud".index(name)
                store(number, layer, (gq, go, gg, gd)[number], r["qogd"[number] + "_out"])
            return
        index = "dguabo".index(name)
        item = WeightSum(
            pieces[name], r["near_" + name], r["apart_" + name], 6 * layer + index, r["dsems"],
            spread, (r["csems"].at[0, index], r["csems"].at[1, index]),
            layer < LAYERS - 1, layer > 0, r["sum_" + name],
            lax.div(me, 2) if name == "o" else None,
        )
        item.start()
        sums[name, layer] = item

    def add(name, layer):
        if spreading and (name, layer) in sums:
            sums[name, layer].add()

    def total(name, layer):
        if not spreading or (name, layer) not in sums:
            return
        result = sums[name, layer].total()
        if name in "abo":
            share = Share(r[name + "share"], layer, sems, 15 + 3 * "abo".index(name), where)
            share.start(result.astype(bf16))
            shares.append(share)
        elif name == "d":
            r["d_res"][layer] = result
        else:
            half = "gu".index(name)
            r["g_res"][layer, :, half * ff:(half + 1) * ff] = result

    def ready(name, layer):
        if not spreading:
            if name not in "ub":
                stored("aogd".index(name))
        elif (name, layer + 1) in sums:
            sums[name, layer + 1].finish()

    gains = []

    def gain_stage(stage):
        if not spreading:
            return
        gpack, gside, gdeep, gsems = (r[n] for n in ("gpack", "gside", "gdeep", "gsems"))
        if stage == 0:
            gpack[me] = gsum[...]
            for number, who in enumerate((mate, across, far)):
                gains.append(push(gpack.at[me], gpack.at[me], gsems, 0, number, who))
        elif stage == 1:
            for copy in gains[:3]:
                copy.wait_recv()
            gside[spread.x] = gpack[0] + gpack[1] + gpack[2] + gpack[3]
            own = gside.at[spread.x]
            gains.append(ship(own, own, gsems, 0, 3, spread.beside(0)))
        elif stage == 2:
            gains[3].wait_recv()
            gdeep[spread.z] = gside[0] + gside[1]
            own = gdeep.at[spread.z]
            for step in range(1, DEPTH):
                gains.append(ship(own, own, gsems, 0, 3 + step, spread.device(step)))
        else:
            for copy in gains[4:]:
                copy.wait_recv()
            r["gain_out"][...] = gdeep[0] + gdeep[1] + gdeep[2] + gdeep[3]
            for copy in gains:
                copy.wait_send()
            return
        for copy in gains[(0, 3, 4)[stage]:]:
            copy.start()

    def store(number, layer, source, target):
        copy = pltpu.make_async_copy(source, target.at[layer], osems.at[layer, number])
        copy.start()
        stores[number] = copy

    def stored(number):
        if number in stores:
            stores.pop(number).wait()

    for layer in range(LAYERS - 1, -1, -1):

        def norm_back(grad_rows, normed, inverse, row, layer=layer):
            gsum[2 * layer + row:2 * layer + row + 1, :] = jnp.sum(
                grad_rows * normed, axis=0, keepdims=True
            )
            scaled = grad_rows * gain[2 * layer + row:2 * layer + row + 1, :]
            return (
                scaled
                - jnp.mean(scaled, axis=-1, keepdims=True)
                - normed * jnp.mean(scaled * normed, axis=-1, keepdims=True)
            ) * inverse

        loads["n2"].wait()
        loads["s2"].wait()
        dz = norm_back(grad[...], n2[...], s2[:, :1], 1)
        load("n2", layer - 1)
        load("s2", layer - 1)
        grad[...] = dz
        dff[0, rows_of(me, size, size), :] = dz.astype(bf16)
        gather = Gather(dff, 0, layer, sems, 0, size, where)
        gather.start()
        if layer == LAYERS - 1:
            write_bias(bias, doc_keys, doc_queries)
        for name in ("wd", "gu", "wg"):
            loads[name].wait()
        add("o", layer + 1)

        def feed_back(block):
            rows = rows_of(block, size, size)
            grad_hidden = dot(dff[0, rows, :], wd[...])
            gate = gu[rows, :ff].astype(f32)
            upward = gu[rows, ff:].astype(f32)
            sigma = 1.0 / (1.0 + jnp.exp(-gate))
            up_grad = grad_hidden * gate * sigma
            gate_grad = grad_hidden * upward * sigma * (1.0 + gate * (1.0 - sigma))
            gu[rows, :ff] = gate_grad.astype(bf16)
            gu[rows, ff:] = up_grad.astype(bf16)
            return dot_nt(gu[rows, :], wg[...])

        if len(scatters) > 1:
            scatters[-2].finish()
        scatter = Scatter(part, 0, got, 2 * layer, sems, 6, where)
        scatters.append(scatter)
        own_part = feed_back(me)
        gather.wait_mate()
        scatter.send_mate(feed_back(mate))
        gather.wait_across()
        loads["hid"].wait()
        add("a", layer + 1)
        gather.wait_far()
        ready("d", layer)

        def down_weight(i, carry):
            cols = rows_of(i, 256, 256)
            gd[cols, :] = dot_tn(dff[0, :, cols], hid[...]).astype(bf16)
            return carry

        lax.fori_loop(0, feats // 256, down_weight, 0)
        begin("d", layer)
        scatter.send_far(feed_back(far))
        scatter.send_across(feed_back(across))
        gather.finish()
        load("hid", layer - 1)
        load("wd", layer - 1)
        load("wg", layer - 1)
        add("b", layer + 1)
        loads["flow"].wait()
        for name, first_col in (("g", 0), ("u", ff)):
            ready(name, layer)

            def gate_up_weight(i, carry, first_col=first_col):
                cols = rows_of(i, 256, 256)
                gg[cols, first_col:first_col + ff] = dot_tn(
                    flow[:, cols], gu[:, first_col:first_col + ff]
                ).astype(bf16)
                return carry

            lax.fori_loop(0, feats // 256, gate_up_weight, 0)
            begin(name, layer)
        load("gu", layer - 1)
        load("xf", layer)
        for name in "dgu":
            total(name, layer + 1)

        if layer == 0:
            add("d", layer)
        dfirst = grad[...] + scatter.total(own_part)
        loads["n1"].wait()
        loads["s1"].wait()
        dr = norm_back(dfirst, n1[...], s1[:, :1], 0)
        load("n1", layer - 1)
        load("s1", layer - 1)
        grad[...] = dr
        dbr[layer, rows_of(me, size, size), :] = dr.astype(bf16)
        gather = Gather(dbr, layer, layer, sems, 9, size, where)
        gather.start()
        if layer == 0:
            gain_stage(0)
        for name in ("wo", "qkv", "lse"):
            loads[name].wait()

        def att_back(block, layer=layer):
            rows = rows_of(block, size, size)
            for tile, start in enumerate((0, HEAD_DIM)):
                spot = pl.ds(pl.multiple_of(me * own_feats + start, HEAD_DIM), TILE)
                datt[rows, tile * TILE:(tile + 1) * TILE] = dot_nt(
                    dbr[layer, rows, :], wo[spot, :]
                ).astype(bf16)

        kt[0] = qkv[:, TILE:2 * TILE].T
        kt[1] = qkv[:, 3 * TILE:4 * TILE].T
        k2[...] = pltpu.roll(qkv[:, 3 * TILE:4 * TILE].astype(f32), HEAD_DIM, 1).astype(bf16)
        dk[...] = jnp.zeros_like(dk)
        dv[...] = jnp.zeros_like(dv)

        def attend(head, first, second):
            tile = head // 2
            query_tile = (0, 0, 3)[head]
            value_tile = (2, 2, 4)[head]
            query_mask = (low_mask, high_mask, low_mask)[head]
            value_mask = (low_mask, high_mask, high_mask)[head]

            def body(i, carry):
                rows = rows_of(first + i * (second - first), size, size)
                queries = qkv[rows, query_tile * TILE:(query_tile + 1) * TILE] * query_mask
                keys = k2[...] if head == 2 else qkv[:, TILE:2 * TILE]
                scores = dot_nt(keys, queries) * (score_scale * log2e) + bias[:, rows]
                probs = jnp.exp2(scores - lse[head:head + 1, rows])
                outs = datt[rows, tile * TILE:(tile + 1) * TILE] * value_mask
                grad_probs = dot_nt(qkv[:, value_tile * TILE:(value_tile + 1) * TILE], outs)
                delta = jnp.sum(probs * grad_probs, axis=0, keepdims=True)
                grad_scores = (probs * (grad_probs - delta)).astype(bf16)
                dv[tile] = dv[tile] + dot(probs.astype(bf16), outs)
                dk[tile] = dk[tile] + dot(grad_scores, queries)
                keys_t = (kt.at[0, :HEAD_DIM], kt.at[0, HEAD_DIM:], kt.at[1, HEAD_DIM:])[head][...]
                spot = (0, HEAD_DIM, 0)[head]
                dqt[tile, spot:spot + HEAD_DIM, rows] = dot(keys_t, grad_scores)
                return carry

            lax.fori_loop(0, 2, body, 0)

        att_back(me)
        gather.wait_mate()
        att_back(mate)
        for head in range(OWN_HEADS):
            attend(head, me, mate)
        gather.wait_across()
        att_back(across)
        if layer == 0:
            gain_stage(1)
            add("g", layer)
        else:
            add("d", layer)
        gather.wait_far()
        att_back(far)
        pending.append(gather)
        load("wo", layer - 1)
        loads["att"].wait()
        ready("o", layer)

        def out_weight(i, carry, layer=layer):
            rows = rows_of(i, 256, 256)
            half = feats // 2
            cols = pl.ds(pl.multiple_of(core * half, half), half)
            go[rows, :] = dot(att[rows, :], dbr[layer, :, cols]).astype(bf16)
            return carry

        lax.fori_loop(0, feats // 256, out_weight, 0)
        begin("o", layer)
        load("att", layer - 1)
        for name in "oab":
            total(name, layer + 1)
        attend(0, across, far)
        attend(1, across, far)
        for share in shares:
            share.serve()

        def unrotate_pairs(i, carry):
            rows = rows_of(i, size, size)
            c, s = cos_rows[rows, :], -sin_rows[rows, :]
            dproj[rows, :TILE] = turn(dqt[0, :, rows].T * score_scale, c, s).astype(bf16)
            dproj[rows, TILE:2 * TILE] = turn(dk[0, rows, :] * score_scale, c, s).astype(bf16)
            dproj[rows, 2 * TILE:3 * TILE] = dv[0, rows, :].astype(bf16)
            return carry

        def unrotate_last(i, carry):
            rows = rows_of(i, size, size)
            c, s = cos_rows[rows, :], -sin_rows[rows, :]
            lower = lane_iota((size, TILE)) < HEAD_DIM
            mixed = jnp.where(lower, dqt[1, :, rows].T, pltpu.roll(dk[1, rows, :], HEAD_DIM, 1))
            dproj[rows, 3 * TILE:4 * TILE] = turn(mixed * score_scale, c, s).astype(bf16)
            dproj[rows, 4 * TILE:] = dv[1, rows, :].astype(bf16)
            return carry

        def weigh_projection(first, last):
            def qkv_weight(i, carry):
                cols = rows_of(i, 256, 256)
                gq[cols, first:last] = dot_tn(xf[:, cols], dproj[:, first:last]).astype(bf16)
                return carry

            lax.fori_loop(0, feats // 256, qkv_weight, 0)

        lax.fori_loop(0, seq // size, unrotate_pairs, 0)
        loads["xf"].wait()
        ready("a", layer)
        weigh_projection(0, 3 * TILE)
        begin("a", layer)
        if layer:
            add("g", layer)
        else:
            gain_stage(2)
            add("u", layer)
        attend(2, across, far)
        lax.fori_loop(0, seq // size, unrotate_last, 0)
        load("qkv", layer - 1)
        load("lse", layer - 1)
        loads["wq"].wait()

        def input_part(block):
            return dot_nt(dproj[rows_of(block, size, size), :], wq[...])

        if len(scatters) > 1:
            scatters[-2].finish()
        scatter = Scatter(part, 1, got, 2 * layer + 1, sems, 6, where)
        scatters.append(scatter)
        if layer == 0:
            ready("b", layer)
            weigh_projection(3 * TILE, PROJ)
            begin("b", layer)
        scatter.send_far(input_part(far))
        scatter.send_across(input_part(across))
        scatter.send_mate(input_part(mate))
        own_part = input_part(me)
        load("wq", layer - 1)
        if layer:
            ready("b", layer)
            weigh_projection(3 * TILE, PROJ)
            begin("b", layer)
            add("u", layer)
        else:
            gain_stage(3)
            add("o", layer)
            add("a", layer)
            for name in "dg":
                total(name, 0)
            add("b", layer)
        load("flow", layer - 1)
        grad[...] = grad[...] + scatter.total(own_part)
    input_copy = pltpu.make_async_copy(grad, r["ig_out"], osems.at[0, 4])
    input_copy.start()
    for name in "uoab":
        total(name, 0)
    if spreading:
        for share in shares[-3:]:
            share.serve()
    input_copy.wait()
    for item in pending + scatters[-2:]:
        item.finish()
    for number in range(4):
        stored(number)
    for item in shares:
        item.finish()
    if spreading:
        for name in "dguabo":
            sums[name, 0].finish()
        q_out = r["q_out"]
        ends = (
            (r["ashare"], q_out.at[:, :, :, pl.ds(0, 3 * TILE)]),
            (r["bshare"], q_out.at[:, :, :, pl.ds(3 * TILE, 2 * TILE)]),
            (r["oshare"], r["o_out"]),
        )
        last = []
        for number, held in enumerate(ends):
            last.append(pltpu.make_async_copy(*held, osems.at[1, number]))
            last[-1].start()
        for copy in last:
            copy.wait()


RATES = ((0.03, 0.01), (0.5, 0.01), (0.03, 0.01), (0.02, 0.01), (0.6, 0.0))


def adam_step(weight, first, second, average, gradient, rate, decay):
    first_new = beta_first * first + (1.0 - beta_first) * gradient
    second_new = beta_second * second + (1.0 - beta_second) * gradient * gradient
    first_hat = first_new / (1.0 - beta_first**STEP)
    second_hat = second_new / (1.0 - beta_second**STEP)
    weight_new = weight - rate * (
        first_hat / (jnp.sqrt(second_hat) + adam_epsilon) + decay * weight
    )
    average_new = average_decay * average + (1.0 - average_decay) * weight_new
    return first_new, second_new, weight_new, average_new


def adam_kernel(*refs):
    states = [refs[4 * f:4 * f + 4] for f in range(5)]
    grads = refs[20:25]
    outs = [refs[25 + 5 * f:30 + 5 * f] for f in range(5)]
    (qs, os, ds, gs, qg, og, gg, qb, ob, gb, db, gsems, isems, usems) = refs[50:]
    width = ob.shape[3]
    for number, target in enumerate((qs, os, gs, ds)):
        pltpu.make_async_copy(grads[number], target, gsems.at[number]).start()
    chunks = []
    for family, held, grad in ((3, db, ds), (2, gb, gg), (1, ob, og), (0, qb, qg)):
        for layer in range(LAYERS):
            for part in range(3 if family == 0 else 1):
                spot = 3 * layer + part if family == 0 else layer
                chunks.append((family, held, grad, layer, part, spot))

    def view(ref, family, layer, part):
        if family:
            return ref.at[layer]
        return ref.at[layer, :, pl.ds(part * width, width)]

    arrivals = []
    for number, (family, held, grad, layer, part, spot) in enumerate(chunks):
        copies = [
            pltpu.make_async_copy(
                view(states[family][k], family, layer, part), held.at[k, spot], isems.at[number, k]
            )
            for k in range(4)
        ]
        for copy in copies:
            copy.start()
        arrivals.append(copies)

    def wait_grad(number, target):
        pltpu.make_async_copy(grads[number], target, gsems.at[number]).wait()

    gain = [ref[...] for ref in states[4]]
    gradient = grads[4][...]
    new = adam_step(*gain, gradient, *RATES[4])
    for ref, value in zip(outs[4], (gradient,) + new):
        ref[...] = value

    low = lane_iota((qs.shape[2], TILE)) < HEAD_DIM
    leaving = []
    for number, (family, held, grad, layer, part, spot) in enumerate(chunks):
        first_of = layer == 0 and part == 0
        if family == 3 and first_of:
            wait_grad(3, ds)
        if family == 2:
            if first_of:
                wait_grad(2, gs)
            for half in range(2):
                gg[layer, :, half, :] = gs[layer, :, half * width:(half + 1) * width]
        if family == 1:
            if first_of:
                wait_grad(1, os)
            high, wide = os.shape[2], os.shape[3]
            for side in range(2):
                for core in range(2):
                    og[layer, side * high:(side + 1) * high, core * wide:(core + 1) * wide] = os[
                        layer, 2 * side + core
                    ].astype(f32)
        if family == 0:
            if first_of:
                wait_grad(0, qs)

            def pair(j):
                return qs[layer, j, :, part * TILE:(part + 1) * TILE].astype(f32)

            def last(j, upper):
                tile = 4 if part == 2 else 3
                value = qs[layer, j, :, tile * TILE:(tile + 1) * TILE].astype(f32)
                return value if upper == (part > 0) else pltpu.roll(value, HEAD_DIM, 1)

            for j in (0, 2):
                turned = pltpu.roll(pair(j + 1), HEAD_DIM, 1)
                tiles = (
                    pair(j),
                    jnp.where(low, last(j, False), turned),
                    jnp.where(low, turned, last(j + 1, True)),
                )
                for k, value in enumerate(tiles):
                    start = (3 * (j // 2) + k) * TILE
                    qg[spot, :, start:start + TILE] = value
        for copy in arrivals[number]:
            copy.wait()
        rows = 32

        def body(i, carry, family=family, held=held, grad=grad, spot=spot):
            at = pl.ds(pl.multiple_of(i * rows, rows), rows)
            values = [held[k, spot, at] for k in range(4)]
            first, second, weight, average = adam_step(*values, grad[spot, at], *RATES[family])
            for k, value in enumerate((weight, first, second, average)):
                held[k, spot, at] = value
            return carry

        lax.fori_loop(0, ob.shape[2] // rows, body, 0)
        sources = (grad.at[spot],) + tuple(held.at[k, spot] for k in (1, 2, 0, 3))
        for k, source in enumerate(sources):
            copy = pltpu.make_async_copy(
                source, view(outs[family][k], family, layer, part), usems.at[number, k]
            )
            copy.start()
            leaving.append(copy)
    for copy in leaving:
        copy.wait()


def frequencies():
    half = HEAD_DIM // 2
    freq = rotary_base ** (-2.0 * np.arange(half) / HEAD_DIM)
    return jnp.asarray(np.tile(freq, (8, 4)).astype(np.float32))


def own_projection(weight, me):
    layers, rows, _ = weight.shape
    split = weight.reshape(layers, rows, 3, HEADS * HEAD_DIM)
    own = lax.dynamic_slice_in_dim(split, me * OWN_HEADS * HEAD_DIM, OWN_HEADS * HEAD_DIM, 3)
    own = own.astype(bf16)
    pairs = own[..., :TILE].reshape(layers, rows, 3 * TILE)
    last = own[..., TILE:]
    return jnp.concatenate(
        [pairs, last[:, :, 0], last[:, :, 1], jnp.zeros_like(last[:, :, 0]), last[:, :, 2]], axis=-1
    )


def whole_projection(grad):
    group, layers, rows, _ = grad.shape
    pairs = grad[..., :3 * TILE].reshape(group, layers, rows, 3, TILE)
    last = jnp.stack(
        [
            grad[..., 3 * TILE:3 * TILE + HEAD_DIM],
            grad[..., 3 * TILE + HEAD_DIM:4 * TILE],
            grad[..., 4 * TILE + HEAD_DIM:],
        ],
        axis=3,
    )
    full = jnp.concatenate([pairs, last], axis=-1)
    return full.transpose(1, 2, 3, 0, 4).reshape(layers, rows, 3 * HEADS * HEAD_DIM)


def run_forward(spreading, tokens, weights, gain, lengths, mask_row):
    size, feats = tokens.shape
    seq = size * GROUP
    ff = weights[3].shape[2]
    own = weights[0].shape[1]
    shapes = dict(
        act=((size, feats), bf16),
        xf=((LAYERS, seq, feats), bf16),
        qkv=((LAYERS, seq, PROJ), bf16),
        lse=((LAYERS, 8, seq), f32),
        att=((LAYERS, feats, seq), bf16),
        flow=((LAYERS, seq, feats), bf16),
        gu=((LAYERS, seq, 2 * ff), bf16),
        hid=((LAYERS, seq, ff), bf16),
        n1=((LAYERS, size, feats), f32),
        s1=((LAYERS, size, 128), f32),
        n2=((LAYERS, size, feats), f32),
        s2=((LAYERS, size, 128), f32),
        wq=((LAYERS, feats, PROJ), bf16),
        wo=((LAYERS, feats, feats), bf16),
        wg=((LAYERS, feats, 2 * ff), bf16),
        wd=((LAYERS, feats, ff), bf16),
        gain=((8, feats), f32),
        cos_rows=((seq, 128), f32),
        sin_rows=((seq, 128), f32),
        doc_keys=((seq, 128), jnp.int32),
        doc_queries=((8, seq), jnp.int32),
    )
    held = {name: pltpu.VMEM(*shape) for name, shape in shapes.items()}
    scratch = [held[n] for n in ("wq", "wo", "wg", "wd", "xf", "qkv", "att", "flow", "gu", "hid")]
    scratch += [
        pltpu.VMEM((seq, seq), f32),
        pltpu.VMEM((2, TILE, seq), bf16),
        pltpu.VMEM((seq, TILE), bf16),
        held["lse"],
    ]
    scratch += [held[n] for n in ("n1", "s1", "n2", "s2")]
    scratch += [
        pltpu.VMEM((size, feats), f32),
        held["act"],
        pltpu.VMEM((LAYERS, 3, size, feats), bf16),
        pltpu.VMEM((LAYERS, 3, size, feats), bf16),
        pltpu.SemaphoreType.DMA((2, LAYERS, 18)),
        pltpu.SemaphoreType.DMA((LAYERS, PIECES)),
        pltpu.SemaphoreType.DMA((LAYERS, 16)),
        pltpu.SemaphoreType.DMA((2, PIECES * LAYERS, 3 + 2 * DEPTH)),
        pltpu.SemaphoreType.DMA((2, LAYERS, 14)),
        pltpu.VMEM((2, 8, feats), f32),
        pltpu.VMEM((DEPTH, 8, feats), f32),
        pltpu.SemaphoreType.DMA((2, 1, DEPTH)),
    ]
    if spreading:
        scratch += [
            pltpu.VMEM((LAYERS, own, feats), bf16),
            pltpu.VMEM((LAYERS, own, 2 * ff), bf16),
            pltpu.VMEM((LAYERS, own, ff), bf16),
        ]
    return pl.pallas_call(
        functools.partial(forward_kernel, spreading),
        out_shape=[jax.ShapeDtypeStruct(*shape) for shape in shapes.values()],
        in_specs=[VMEM, ANY] + [VMEM if spreading else ANY] * 3
        + [VMEM, pl.BlockSpec(memory_space=pltpu.SMEM), VMEM, VMEM],
        out_specs=[ANY] * (len(shapes) - 5) + [VMEM] * 5,
        scratch_shapes=scratch,
        compiler_params=pltpu.CompilerParams(
            collective_id=0, has_side_effects=True, vmem_limit_bytes=VMEM_LIMIT
        ),
        cost_estimate=pl.CostEstimate(
            flops=12 * 10**9, bytes_accessed=60 * 10**6, transcendentals=10**7
        ),
        name="forward",
    )(tokens, *weights, gain, lengths, mask_row, frequencies())


def run_backward(spreading, cotangent, kept, weights, gain, tables):
    size, feats = cotangent.shape
    seq = size * GROUP
    xf, qkv, lse, att, flow, gu, hid, n1, s1, n2, s2 = kept
    ff = hid.shape[2]
    wq, wo, wg, wd = weights
    loaded = [n1, s1, n2, s2, xf, qkv, lse, att, flow, gu, hid, wq, wo, wg, wd]
    own = feats // (2 * DEPTH)
    half = feats // 2
    widths = dict(d=ff, g=ff, u=ff, a=3 * TILE, b=2 * TILE, o=half)
    if spreading:
        outs = dict(
            ig_out=((size, feats), f32),
            q_out=((LAYERS, GROUP, own, PROJ), bf16),
            o_out=((LAYERS, GROUP, own // 2, half), bf16),
            d_res=((LAYERS, own, ff), f32),
            g_res=((LAYERS, own, 2 * ff), f32),
            gain_out=((8, feats), f32),
        )
    else:
        outs = dict(
            ig_out=((size, feats), f32),
            q_out=(wq.shape, bf16),
            o_out=((LAYERS, feats, half), bf16),
            d_out=(wd.shape, bf16),
            g_out=(wg.shape, bf16),
            gain_out=((8, feats), f32),
        )
    names = ["cot"] + [n + "_in" for n in BACK_LOADED] + list(BACK_TABLES) + list(outs)
    scratch = dict(
        bias=pltpu.VMEM((seq, seq), f32),
        dff=pltpu.VMEM((1, seq, feats), bf16),
        dbr=pltpu.VMEM((LAYERS, seq, feats), bf16),
        datt=pltpu.VMEM((seq, 2 * TILE), bf16),
        dproj=pltpu.VMEM((seq, PROJ), bf16),
        dk=pltpu.VMEM((2, seq, TILE), f32),
        dv=pltpu.VMEM((2, seq, TILE), f32),
        dqt=pltpu.VMEM((2, TILE, seq), f32),
        kt=pltpu.VMEM((2, TILE, seq), bf16),
        k2=pltpu.VMEM((seq, TILE), bf16),
        grad=pltpu.VMEM((size, feats), f32),
        part=pltpu.VMEM((2, 3, size, feats), bf16),
        got=pltpu.VMEM((2, 3, size, feats), bf16),
        gq=pltpu.VMEM((feats, PROJ), bf16),
        go=pltpu.VMEM((feats, half), bf16),
        gg=pltpu.VMEM((feats, 2 * ff), bf16),
        gd=pltpu.VMEM((feats, ff), bf16),
        sems=pltpu.SemaphoreType.DMA((2, 2 * LAYERS, 24)),
        lsems=pltpu.SemaphoreType.DMA((len(loaded),)),
        osems=pltpu.SemaphoreType.DMA((LAYERS, 5)),
        rows=pltpu.VMEM((seq, feats), bf16),
    )
    for name, array in zip(BACK_LOADED, loaded):
        if name not in ("xf", "flow"):
            scratch[name] = pltpu.VMEM(array.shape[1:], array.dtype)
    if spreading:
        scratch.update(
            gsum=pltpu.VMEM((8, feats), f32),
            gpack=pltpu.VMEM((GROUP, 8, feats), f32),
            gside=pltpu.VMEM((2, 8, feats), f32),
            gdeep=pltpu.VMEM((DEPTH, 8, feats), f32),
            gsems=pltpu.SemaphoreType.DMA((2, 1, 7)),
            csems=pltpu.SemaphoreType.REGULAR((2, 6)),
            ashare=pltpu.VMEM((LAYERS, GROUP, own, 3 * TILE), bf16),
            bshare=pltpu.VMEM((LAYERS, GROUP, own, 2 * TILE), bf16),
            oshare=pltpu.VMEM((LAYERS, GROUP, own // 2, half), bf16),
            dsems=pltpu.SemaphoreType.DMA((2, 6 * LAYERS, 7)),
        )
        for name, width in widths.items():
            high = own // 2 if name == "o" else own
            scratch["near_" + name] = pltpu.VMEM((DEPTH, high, width), bf16)
            scratch["apart_" + name] = pltpu.VMEM((DEPTH - 1, high, width), bf16)
            scratch["sum_" + name] = pltpu.VMEM((high, width), f32)
    in_vmem = ("d_res", "g_res", "gain_out")
    return pl.pallas_call(
        functools.partial(backward_kernel, spreading, tuple(names + list(scratch))),
        out_shape=[jax.ShapeDtypeStruct(*shape) for shape in outs.values()],
        in_specs=[VMEM] + [ANY] * 15 + [VMEM] * 5,
        out_specs=[VMEM if name in in_vmem else ANY for name in outs],
        scratch_shapes=list(scratch.values()),
        compiler_params=pltpu.CompilerParams(
            collective_id=1, has_side_effects=True, vmem_limit_bytes=VMEM_LIMIT
        ),
        cost_estimate=pl.CostEstimate(
            flops=24 * 10**9, bytes_accessed=60 * 10**6, transcendentals=10**7
        ),
        name="backward",
    )(cotangent, *loaded, gain, *tables)


def run_adam(states, grads):
    outs = []
    for family in range(5):
        shape = jax.ShapeDtypeStruct(states[4 * family].shape, f32)
        outs += [shape] * 5
    layers, own, _, width = states[8].shape
    scratch = [
        pltpu.VMEM(grads[0].shape, bf16),
        pltpu.VMEM(grads[1].shape, bf16),
        pltpu.VMEM(grads[3].shape, f32),
        pltpu.VMEM(grads[2].shape, f32),
        pltpu.VMEM((3 * layers, own, width), f32),
        pltpu.VMEM((layers, own, width), f32),
        pltpu.VMEM((layers, own, 2, width), f32),
        pltpu.VMEM((4, 3 * layers, own, width), f32),
        pltpu.VMEM((4, layers, own, width), f32),
        pltpu.VMEM((4, layers, own, 2, width), f32),
        pltpu.VMEM((4, layers, own, width), f32),
        pltpu.SemaphoreType.DMA((4,)),
        pltpu.SemaphoreType.DMA((6 * layers, 4)),
        pltpu.SemaphoreType.DMA((6 * layers, 5)),
    ]
    return pl.pallas_call(
        adam_kernel,
        out_shape=outs,
        in_specs=[ANY] * 16 + [VMEM] * 4 + [ANY] * 4 + [VMEM],
        out_specs=[ANY] * 20 + [VMEM] * 5,
        scratch_shapes=scratch,
        compiler_params=pltpu.CompilerParams(vmem_limit_bytes=VMEM_LIMIT),
        cost_estimate=pl.CostEstimate(
            flops=2 * 10**7, bytes_accessed=37 * 10**6, transcendentals=10**6
        ),
        name="adam",
    )(*states, *grads)


def adamw(weight, first, second, average, gradient, rate, decay):
    first_new = beta_first * first + (1.0 - beta_first) * gradient
    second_new = beta_second * second + (1.0 - beta_second) * gradient * gradient
    first_hat = first_new / (1.0 - beta_first**STEP)
    second_hat = second_new / (1.0 - beta_second**STEP)
    weight_new = weight - rate * (
        first_hat / (jnp.sqrt(second_hat) + adam_epsilon) + decay * weight
    )
    average_new = average_decay * average + (1.0 - average_decay) * weight_new
    return (gradient, first_new, second_new, weight_new, average_new)


def shards(
    spreading,
    tokens,
    cotangent,
    lengths,
    key_mask,
    qkv_weight,
    qkv_first,
    qkv_second,
    qkv_average,
    out_weight,
    out_first,
    out_second,
    out_average,
    gate_up_weight,
    gate_up_first,
    gate_up_second,
    gate_up_average,
    down_weight,
    down_first,
    down_second,
    down_average,
    norm_gain,
    gain_first,
    gain_second,
    gain_average,
):
    me = lax.axis_index("mp")
    own = gate_up_weight.shape[1]
    ff = gate_up_weight.shape[3]
    feats = tokens.shape[1]
    if spreading:
        gain = jnp.zeros((8, feats), f32)
        gain = lax.dynamic_update_slice(
            gain, norm_gain.reshape(2 * LAYERS, own), (0, lax.axis_index("dp") * own)
        )
    else:
        gain = lax.all_gather(norm_gain, "dp", axis=2, tiled=True).reshape(2 * LAYERS, feats)
        gain = jnp.concatenate([gain, jnp.zeros((8 - 2 * LAYERS, feats), f32)], axis=0)
    if spreading:
        owned = (own_projection(qkv_weight, me), out_weight, gate_up_weight, down_weight)
    else:
        owned = (
            own_projection(qkv_weight, me),
            out_weight.astype(bf16),
            gate_up_weight.reshape(LAYERS, own, 2 * ff).astype(bf16),
            down_weight.astype(bf16),
        )
        owned = [lax.all_gather(w, "dp", axis=1, tiled=True) for w in owned]
    act, *kept = run_forward(spreading, tokens, owned, gain, lengths, key_mask[None, :])
    weights, gain, tables, kept = kept[-9:-5], kept[-5], kept[-4:], kept[:-9]
    backward = run_backward(spreading, cotangent, kept, weights, gain, tables)
    if spreading:
        input_grad, gq, go, gd, gg, gain_sum = backward
        gain_grad = lax.dynamic_slice_in_dim(
            gain_sum[:2 * LAYERS].reshape(LAYERS, 2, -1), lax.axis_index("dp") * own, own, 2
        )
        states = (
            qkv_weight, qkv_first, qkv_second, qkv_average,
            out_weight, out_first, out_second, out_average,
            gate_up_weight, gate_up_first, gate_up_second, gate_up_average,
            down_weight, down_first, down_second, down_average,
            norm_gain, gain_first, gain_second, gain_average,
        )
        return (act, input_grad, *run_adam(states, (gq, go, gg, gd, gain_grad)))
    else:
        input_grad, gq, go, gd, gg, gain_sum = backward
        gq, go, gg, gd = [
            lax.psum_scatter(g, "dp", scatter_dimension=1, tiled=True) for g in (gq, go, gg, gd)
        ]
        gq, go = lax.all_gather(gq, "mp"), lax.all_gather(go, "mp")
        gain_part = gain_sum[:2 * LAYERS].reshape(LAYERS, 2, -1)
        gain_grad = lax.psum_scatter(
            lax.psum(gain_part, "mp"), "dp", scatter_dimension=2, tiled=True
        )
    qkv_grad = whole_projection(gq.astype(f32))
    out_grad = jnp.concatenate([go[0], go[1]], axis=-1).astype(f32)
    gate_up_grad = gg.reshape(LAYERS, own, 2, ff).astype(f32)
    down_grad = gd.astype(f32)
    results = [act, input_grad]
    results.extend(adamw(qkv_weight, qkv_first, qkv_second, qkv_average, qkv_grad, 0.03, 0.01))
    results.extend(adamw(out_weight, out_first, out_second, out_average, out_grad, 0.5, 0.01))
    results.extend(
        adamw(
            gate_up_weight, gate_up_first, gate_up_second, gate_up_average, gate_up_grad, 0.03, 0.01
        )
    )
    results.extend(
        adamw(down_weight, down_first, down_second, down_average, down_grad, 0.02, 0.01)
    )
    results.extend(adamw(norm_gain, gain_first, gain_second, gain_average, gain_grad, 0.6, 0.0))
    return tuple(results)


def solution(mesh):
    spreading = mesh.shape["dp"] == 2 * DEPTH
    return jax.shard_map(
        functools.partial(shards, spreading),
        mesh=mesh,
        in_specs=(
            P(("dp", "mp"), None),
            P(("dp", "mp"), None),
            P("dp", None),
            P("dp"),
            P(None, "dp", None),
            P(None, "dp", None),
            P(None, "dp", None),
            P(None, "dp", None),
            P(None, "dp", None),
            P(None, "dp", None),
            P(None, "dp", None),
            P(None, "dp", None),
            P(None, "dp", None, "mp"),
            P(None, "dp", None, "mp"),
            P(None, "dp", None, "mp"),
            P(None, "dp", None, "mp"),
            P(None, "dp", "mp"),
            P(None, "dp", "mp"),
            P(None, "dp", "mp"),
            P(None, "dp", "mp"),
            P(None, None, "dp"),
            P(None, None, "dp"),
            P(None, None, "dp"),
            P(None, None, "dp"),
        ),
        out_specs=(
            P(("dp", "mp"), None),
            P(("dp", "mp"), None),
            P(None, "dp", None),
            P(None, "dp", None),
            P(None, "dp", None),
            P(None, "dp", None),
            P(None, "dp", None),
            P(None, "dp", None),
            P(None, "dp", None),
            P(None, "dp", None),
            P(None, "dp", None),
            P(None, "dp", None),
            P(None, "dp", None, "mp"),
            P(None, "dp", None, "mp"),
            P(None, "dp", None, "mp"),
            P(None, "dp", None, "mp"),
            P(None, "dp", None, "mp"),
            P(None, "dp", "mp"),
            P(None, "dp", "mp"),
            P(None, "dp", "mp"),
            P(None, "dp", "mp"),
            P(None, "dp", "mp"),
            P(None, None, "dp"),
            P(None, None, "dp"),
            P(None, None, "dp"),
            P(None, None, "dp"),
            P(None, None, "dp"),
        ),
        check_vma=False,
    )
```

```python
import functools
import math

import jax
import jax.numpy as jnp
import numpy as np
from jax import lax
from jax.experimental import pallas as pl
from jax.experimental.pallas import tpu as pltpu
from jax.sharding import PartitionSpec as P

HEADS = 12
HEAD_DIM = 64
LAYERS = 2
STEP = 10
GROUP = 4
DEPTH = 4
LEAD = 1
PIECES = 4
OWN_HEADS = HEADS // GROUP
TILE = 2 * HEAD_DIM
PROJ = 5 * TILE

rotary_base = 1000.0
norm_epsilon = 1e-05
masked_score = -1e30
beta_first = 0.5
beta_second = 0.5
adam_epsilon = 1e-08
average_decay = 0.5
score_scale = HEAD_DIM ** (-0.5)
log2e = math.log2(math.e)

MESH = pl.DeviceIdType.MESH
ANY = pl.BlockSpec(memory_space=pl.ANY)
VMEM = pl.BlockSpec(memory_space=pltpu.VMEM)
f32 = jnp.float32
bf16 = jnp.bfloat16
VMEM_LIMIT = 127 * 2**19


def dot(a, b):
    return jnp.dot(a, b, preferred_element_type=f32)


def dot_nt(a, b):
    return lax.dot_general(a, b, (((1,), (1,)), ((), ())), preferred_element_type=f32)


def dot_tn(a, b):
    return lax.dot_general(a, b, (((0,), (0,)), ((), ())), preferred_element_type=f32)


def places():
    me = lax.axis_index("mp")
    core = lax.rem(me, 2)
    side = lax.div(me, 2)
    return me, me + 1 - 2 * core, me + 2 - 4 * side, 3 - me, core


def push(src, dst, sems, layer, number, who):
    return pltpu.make_async_remote_copy(
        src_ref=src,
        dst_ref=dst,
        send_sem=sems.at[0, layer, number],
        recv_sem=sems.at[1, layer, number],
        device_id={"mp": who},
        device_id_type=MESH,
    )


class Spread:
    def __init__(self, own):
        index = lax.axis_index("dp")
        self.own = own
        self.z, self.x = lax.div(index, 2), lax.rem(index, 2)

    def device(self, step):
        return 2 * lax.rem(self.z + step, DEPTH) + self.x

    def beside(self, step):
        return 2 * lax.rem(self.z + step, DEPTH) + 1 - self.x

    def rows(self, index):
        return pl.ds(pl.multiple_of(index * self.own, self.own), self.own)


def greet(mate, across, far=None, spread=None):
    barrier = pltpu.get_barrier_semaphore()
    packs = [mate, across] if far is None else [mate, across, far]
    for who in packs:
        pl.semaphore_signal(barrier, inc=1, device_id={"mp": who}, device_id_type=MESH)
    others = []
    if spread is not None:
        others = [spread.beside(0)] + [spread.device(step) for step in range(1, DEPTH)]
        for who in others:
            pl.semaphore_signal(barrier, inc=1, device_id={"dp": who}, device_id_type=MESH)
    pl.semaphore_wait(barrier, len(packs) + len(others))


def ship(src, dst, sems, piece, number, who):
    return pltpu.make_async_remote_copy(
        src_ref=src,
        dst_ref=dst,
        send_sem=sems.at[0, piece, number],
        recv_sem=sems.at[1, piece, number],
        device_id={"dp": who},
        device_id_type=MESH,
    )


class WeightGather:
    def __init__(self, source, target, layer, piece, sems, local, spread, cols=None):
        self.target, self.layer, self.cols = target, layer, cols
        self.piece, self.sems, self.spread = piece, sems, spread
        z, x = spread.z, spread.x
        own = self.own_part(source)
        place = self.view(z, x)
        self.local = pltpu.make_async_copy(own, place, local)
        self.beside = self.send(own, place, 0, 0, 2 * z + 1 - x)
        self.up = self.send(own, place, 1, 1 + z, 2 * jnp.minimum(z + 1, DEPTH - 1) + x)
        self.down = self.send(own, place, 2, 1 + z, 2 * jnp.maximum(z - 1, 0) + x)
        self.hops = [(far, way) for far in range(1, DEPTH) for way in (-1, 1)]
        self.todo = list(self.hops)

    def own_part(self, source):
        return source.at[self.layer]

    def view(self, z, x):
        return self.target.at[self.layer, self.spread.rows(2 * z + x)]

    def send(self, src, dst, out, into, who):
        return pltpu.make_async_remote_copy(
            src_ref=src,
            dst_ref=dst,
            send_sem=self.sems.at[0, self.piece, out],
            recv_sem=self.sems.at[1, self.piece, into],
            device_id={"dp": who},
            device_id_type=MESH,
        )

    def start(self):
        self.local.start()
        pl.when(self.spread.z < DEPTH - 1)(self.up.start)
        pl.when(self.spread.z > 0)(self.down.start)
        self.beside.start()

    def hop(self, far, way):
        z, x = self.spread.z, self.spread.x
        source = jnp.clip(z + way * far, 0, DEPTH - 1)
        block = self.view(source, x)
        onward = jnp.clip(z - way, 0, DEPTH - 1)
        arrive = self.send(block, block, 3 + source, 1 + source, 2 * source + x)
        over = self.send(block, block, 3 + source, 1 + DEPTH + source, 2 * z + 1 - x)
        along = self.send(block, block, 3 + DEPTH + source, 1 + source, 2 * onward + x)
        comes = z >= far if way < 0 else z + far < DEPTH
        goes = z > 0 if way > 0 else z < DEPTH - 1
        return arrive, over, along, comes, jnp.logical_and(comes, goes)

    def serve(self, count=2 * DEPTH):
        while self.todo and count:
            count -= 1
            arrive, over, along, comes, goes = self.hop(*self.todo.pop(0))

            pl.when(comes)(arrive.wait_recv)
            pl.when(goes)(along.start)
            pl.when(comes)(over.start)

    def wait(self):
        self.serve()
        self.local.wait()
        self.beside.wait_recv()
        z, x = self.spread.z, self.spread.x
        for step in range(1, DEPTH):
            source = lax.rem(z + step, DEPTH)
            block = self.view(source, 1 - x)
            self.send(block, block, 3, 1 + DEPTH + source, 2 * z + 1 - x).wait_recv()

    def finish(self):
        self.beside.wait_send()
        pl.when(self.spread.z < DEPTH - 1)(self.up.wait_send)
        pl.when(self.spread.z > 0)(self.down.wait_send)
        for far, way in self.hops:
            arrive, over, along, comes, goes = self.hop(far, way)
            pl.when(comes)(over.wait_send)
            pl.when(goes)(along.wait_send)


class QuarterGather(WeightGather):
    def __init__(self, source, target, layer, piece, sems, local, spread, half, pack_sems, where):
        me, mate, across, far, core = where
        self.side, self.rows = lax.div(me, 2), spread.own // 2
        cols = pl.ds(pl.multiple_of(core * half, half), half)
        super().__init__(source, target, layer, piece, sems, local, spread, cols)
        here = spread.rows(2 * spread.z + spread.x)
        self.local = pltpu.make_async_copy(source.at[layer], target.at[layer, here], local)
        self.over, self.swap = [], []
        for step in range(DEPTH):
            z = lax.rem(spread.z + step, DEPTH)
            for number, x in enumerate((spread.x, 1 - spread.x)):
                if step or number:
                    spot = 2 * step + number - 1
                    block = self.view(z, x)
                    self.over.append(push(block, block, pack_sems, layer, spot, across))
                    block = target.at[layer, spread.rows(2 * z + x), cols]
                    self.swap.append(push(block, block, pack_sems, layer, 7 + spot, mate))

    def part_rows(self, start):
        return pl.ds(pl.multiple_of(start + self.side * self.rows, self.rows), self.rows)

    def own_part(self, source):
        return source.at[self.layer, self.part_rows(0), self.cols]

    def view(self, z, x):
        rows = self.part_rows((2 * z + x) * self.spread.own)
        return self.target.at[self.layer, rows, self.cols]

    def share_across(self):
        super().wait()
        for copy in self.over:
            copy.start()

    def share(self):
        for copy, onward in zip(self.over, self.swap):
            copy.wait_recv()
            onward.start()

    def wait(self):
        for copy in self.swap:
            copy.wait_recv()

    def finish(self):
        super().finish()
        for copy in self.over + self.swap:
            copy.wait_send()


class WeightSum:
    def __init__(self, grad, near, apart, piece, sems, spread, credits, again, more, total, part):
        self.grad, self.near, self.apart, self.spread = grad, near, apart, spread
        self.near_credit, self.apart_credit = credits
        self.again, self.more = again, more
        self.sum, self.part = total, part
        self.beside = [
            ship(grad.at[self.rows(spread.beside(step))], near.at[step], sems, piece, step,
                 spread.beside(0))
            for step in range(DEPTH)
        ]
        self.along = [
            ship(grad.at[self.rows(spread.device(step))], apart.at[step - 1], sems, piece,
                 DEPTH - 1 + step, spread.device(step))
            for step in range(1, DEPTH)
        ]

    def rows(self, index):
        if self.part is None:
            return self.spread.rows(index)
        half = self.spread.own // 2
        return pl.ds(pl.multiple_of(index * self.spread.own + self.part * half, half), half)

    def start(self):
        if self.again:
            pl.semaphore_wait(self.near_credit, 1)
        for copy in self.beside[1:] + self.beside[:1]:
            copy.start()

    def credit(self, sem, who):
        pl.semaphore_signal(sem, inc=1, device_id={"dp": who}, device_id_type=MESH)

    def add(self):
        if self.again:
            pl.semaphore_wait(self.apart_credit, DEPTH - 1)
        for step in range(1, DEPTH):
            self.beside[step].wait_recv()
            rows = self.rows(self.spread.device(step))
            self.grad[rows, :] = (
                self.grad[rows, :].astype(f32) + self.near[step].astype(f32)
            ).astype(bf16)
            self.along[step - 1].start()
        self.beside[0].wait_recv()
        rows = self.rows(self.spread.device(0))
        self.sum[...] = self.grad[rows, :].astype(f32) + self.near[0].astype(f32)
        if self.more:
            self.credit(self.near_credit, self.spread.beside(0))

    def total(self):
        for copy in self.along:
            copy.wait_recv()
        result = self.sum[...]
        for step in range(DEPTH - 1):
            result = result + self.apart[step].astype(f32)
        if self.more:
            for step in range(1, DEPTH):
                self.credit(self.apart_credit, self.spread.device(step))
        return result

    def finish(self):
        for copy in self.beside + self.along:
            copy.wait_send()


def rows_of(block, size, extent):
    return pl.ds(pl.multiple_of(block * size, size), extent)


def lane_iota(shape):
    return lax.broadcasted_iota(jnp.int32, shape, len(shape) - 1)


def half_masks():
    low = (lane_iota((1, TILE)) < HEAD_DIM).astype(f32)
    return low.astype(bf16), (1.0 - low).astype(bf16)


def turn(tile, cos_rows, sin_rows):
    lane = lane_iota(tile.shape) % HEAD_DIM
    half = HEAD_DIM // 2
    partner = jnp.where(
        lane < half, pltpu.roll(tile, TILE - half, 1), pltpu.roll(tile, half, 1)
    )
    return tile * cos_rows + partner * sin_rows


def write_bias(bias, doc_keys, doc_queries):
    seq = bias.shape[0]
    step = 128

    def body(i, carry):
        rows = rows_of(i, step, step)
        keys = doc_keys[rows, :][:, :1]
        same = keys == doc_queries[:1, :]
        spot = lax.broadcasted_iota(jnp.int32, (step, seq), 0) + i * step
        own = spot == lax.broadcasted_iota(jnp.int32, (step, seq), 1)
        bias[rows, :] = jnp.where(jnp.logical_or(same, own), 0.0, masked_score)
        return carry

    lax.fori_loop(0, seq // step, body, 0)


def write_tables(lengths, mask_row, freq, cos_rows, sin_rows, doc_keys, doc_queries):
    ends = []
    for doc in range(lengths.shape[1]):
        ends.append(lengths[0, doc] + (ends[-1] if ends else 0))

    def document(spots):
        number = jnp.zeros(spots.shape, jnp.int32)
        for end in ends:
            number = number + (spots >= end).astype(jnp.int32)
        return number

    seq = cos_rows.shape[0]
    doc_queries[...] = document(lane_iota(doc_queries.shape))
    step = 128

    def body(i, carry):
        rows = rows_of(i, step, step)
        spots = lax.broadcasted_iota(jnp.int32, (step, 128), 0) + i * step
        start = jnp.zeros(spots.shape, jnp.int32)
        for end in ends:
            start = jnp.maximum(start, jnp.where(spots >= end, end, 0))
        seen = jnp.broadcast_to(mask_row[:, rows].astype(f32), (step, step)).T
        doc_keys[rows, :] = jnp.where(seen > 0.5, document(spots), -1)
        angle = (spots - start).astype(f32) * freq[:1, :]
        sine = jnp.sin(angle)
        cos_rows[rows, :] = jnp.cos(angle)
        lower = lane_iota(spots.shape) % HEAD_DIM < HEAD_DIM // 2
        sin_rows[rows, :] = jnp.where(lower, -sine, sine)
        return carry

    lax.fori_loop(0, seq // step, body, 0)


class Gather:
    def __init__(self, ref, slot, layer, sems, first_sem, size, where):
        me, mate, across, far, core = where
        self.across, self.mate = [], []
        self.forward = []
        half = size // 2

        def piece(block, part):
            start = pl.multiple_of(block * size + part * half, half)
            return ref.at[slot, pl.ds(start, half)]

        for part in range(2):
            own = piece(me, part)
            theirs = piece(across, part)
            self.across.append(push(own, own, sems, layer, first_sem + part, across))
            self.mate.append(push(own, own, sems, layer, first_sem + 2 + part, mate))
            self.forward.append(push(theirs, theirs, sems, layer, first_sem + 4 + part, mate))

    def start(self):
        for copy in self.across + self.mate:
            copy.start()

    def wait_mate(self):
        for copy in self.mate:
            copy.wait_recv()

    def wait_across(self):
        for copy, onward in zip(self.across, self.forward):
            copy.wait_recv()
            onward.start()

    def wait_far(self):
        for copy in self.forward:
            copy.wait_recv()

    def finish(self):
        for copy in self.across + self.mate + self.forward:
            copy.wait_send()


class Share:
    def __init__(self, ref, layer, sems, first_sem, where):
        me, mate, across, far, core = where
        own, theirs = ref.at[layer, me], ref.at[layer, across]
        self.ref, self.layer, self.me = ref, layer, me
        self.over = push(own, own, sems, layer, first_sem, across)
        self.near = push(own, own, sems, layer, first_sem + 1, mate)
        self.onward = push(theirs, theirs, sems, layer, first_sem + 2, mate)

    def start(self, block):
        self.ref[self.layer, self.me] = block
        self.over.start()
        self.near.start()

    def serve(self):
        self.over.wait_recv()
        self.onward.start()

    def finish(self):
        self.near.wait_recv()
        self.onward.wait_recv()
        for copy in (self.over, self.near, self.onward):
            copy.wait_send()


class Scatter:
    def __init__(self, part, slot, got, layer, sems, first_sem, where):
        me, mate, across, far, core = where
        self.part, self.slot, self.got = part, slot, got
        self.far = push(part.at[slot, 0], got.at[slot, 0], sems, layer, first_sem, mate)
        self.over = push(part.at[slot, 1], got.at[slot, 1], sems, layer, first_sem + 1, across)
        self.near = push(part.at[slot, 2], got.at[slot, 2], sems, layer, first_sem + 2, mate)

    def send_far(self, block):
        self.part[self.slot, 0] = block.astype(bf16)
        self.far.start()

    def send_across(self, block):
        self.far.wait_recv()
        self.part[self.slot, 1] = (block + self.got[self.slot, 0].astype(f32)).astype(bf16)
        self.over.start()

    def send_mate(self, block):
        self.part[self.slot, 2] = block.astype(bf16)
        self.near.start()

    def total(self, block):
        self.near.wait_recv()
        self.over.wait_recv()
        return (
            block
            + self.got[self.slot, 1].astype(f32)
            + self.got[self.slot, 2].astype(f32)
        )

    def finish(self):
        for copy in (self.far, self.over, self.near):
            copy.wait_send()


def normed_rows(rows):
    centered = rows - jnp.mean(rows, axis=-1, keepdims=True)
    inverse = lax.rsqrt(jnp.mean(centered * centered, axis=-1, keepdims=True) + norm_epsilon)
    return centered * inverse, inverse


def forward_kernel(
    spreading, tok, wq_in, wo_in, wg_in, wd_in, gain_in, lengths, mask_row, freq,
    act_out, xf_out, qkv_out, lse_out, att_out, flow_out, gu_out, hid_out,
    n1_out, s1_out, n2_out, s2_out, wq_out, wo_out, wg_out, wd_out, gain,
    cos_rows, sin_rows, doc_keys, doc_queries,
    wq, wo, wg, wd, xf, qkv, att, flow, gu, hid, bias, vt, k2, lse,
    n1, s1, n2, s2, first, act, part, got, sems, wsems, osems, dsems, ssems, gside, gdeep, gsems, *own_low,
):
    where = places()
    me, mate, across, far, core = where
    weight_outs = (wq_out, wo_out, wg_out, wd_out)
    size = tok.shape[0]
    seq = size * GROUP
    ff = hid.shape[2]
    spread = Spread(wq_in.shape[1]) if spreading else None
    weights = []
    cast = ()
    if spreading:
        cast = ((wo_in, own_low[0]), (wg_in, own_low[1]), (wd_in, own_low[2]))
        wo_in, wg_in, wd_in = own_low
    parts = (
        (wq_in, wq, None), (wo_in, wo, None), (wg_in, wg, None), (wd_in, wd, None),
    )
    for layer in range(LAYERS):
        for number, (source, target, cols) in enumerate(parts):
            local = wsems.at[layer, number]
            piece = PIECES * layer + number
            if not spreading:
                if cols is not None:
                    source, target = source.at[:, :, cols], target.at[:, :, cols]
                weights.append(pltpu.make_async_copy(source.at[layer], target.at[layer], local))
            elif number == 1:
                weights.append(
                    QuarterGather(source, target, layer, piece, dsems, local, spread,
                                  wo.shape[2] // 2, ssems, where)
                )
            else:
                weights.append(
                    WeightGather(source, target, layer, piece, dsems, local, spread, cols)
                )
    xf[0, rows_of(me, size, size), :] = tok[...]
    greet(mate, across, None, spread)
    gains = []
    if spreading:
        gdeep[spread.z] = gain_in[...]
        own = gdeep.at[spread.z]
        for step in range(1, DEPTH):
            gains.append(ship(own, own, gsems, 0, step, spread.device(step)))
            gains[-1].start()
    else:
        gain[...] = gain_in[...]
    ahead = LEAD if spreading else len(weights)
    for item in weights[:ahead]:
        item.start()

    def gain_stage(stage):
        if not spreading:
            return
        if stage == 0:
            for copy in gains:
                copy.wait_recv()
            gside[spread.x] = gdeep[0] + gdeep[1] + gdeep[2] + gdeep[3]
            own = gside.at[spread.x]
            gains.append(ship(own, own, gsems, 0, 0, spread.beside(0)))
            gains[-1].start()
        else:
            gains[-1].wait_recv()
            gain[...] = gside[0] + gside[1]
            for copy in gains:
                copy.wait_send()

    queue = [(k, hop) for k in range(len(weights)) for hop in range(6)] if spreading else []

    def pump(count):
        for number in range(min(count, len(queue))):
            k, hop = queue.pop(0)
            if hop == 0 and k + ahead < len(weights):
                weights[k + ahead].start()
            weights[k].serve(1)

    pending = []
    stores = []

    def store(number, layer, source, target):
        copy = pltpu.make_async_copy(source.at[layer], target.at[layer], osems.at[layer, number])
        copy.start()
        stores.append(copy)

    row_gather = Gather(xf, 0, 0, sems, 0, size, where)
    row_gather.start()
    for source, target in cast:
        if len(source.shape) == 3:
            target[...] = source[...].astype(bf16)
        else:
            for layer in range(LAYERS):
                for half in range(2):
                    target[layer, :, half * ff:(half + 1) * ff] = source[layer, :, half, :].astype(bf16)
    write_tables(lengths, mask_row, freq, cos_rows, sin_rows, doc_keys, doc_queries)
    write_bias(bias, doc_keys, doc_queries)
    low_mask, high_mask = half_masks()

    for layer in range(LAYERS):
        if layer == 0:
            pump(12)
        weights[PIECES * layer].wait()

        def project(block, layer=layer):
            rows = rows_of(block, size, size)
            proj = dot(xf[layer, rows, :], wq[layer])
            c, s = cos_rows[rows, :], sin_rows[rows, :]
            for tile in (0, 1, 3):
                piece = proj[:, tile * TILE:(tile + 1) * TILE]
                qkv[layer, rows, tile * TILE:(tile + 1) * TILE] = turn(piece, c, s).astype(bf16)
            for tile in (2, 4):
                piece = proj[:, tile * TILE:(tile + 1) * TILE]
                qkv[layer, rows, tile * TILE:(tile + 1) * TILE] = piece.astype(bf16)

        project(me)
        row_gather.wait_mate()
        project(mate)
        row_gather.wait_across()
        pump(2)
        project(across)
        row_gather.wait_far()
        project(far)
        if layer == 0:
            gain_stage(0)
        pending.append(row_gather)
        store(0, layer, xf, xf_out)
        store(1, layer, qkv, qkv_out)
        vt[0] = qkv[layer, :, 2 * TILE:3 * TILE].T
        vt[1] = qkv[layer, :, 4 * TILE:5 * TILE].T
        k2[...] = pltpu.roll(qkv[layer, :, 3 * TILE:4 * TILE].astype(f32), HEAD_DIM, 1).astype(bf16)

        sends = []
        forwards = []
        for head in range(OWN_HEADS):
            query_tile = (0, 0, 3)[head]
            mask = (low_mask, high_mask, low_mask)[head]

            def attend(i, carry, layer=layer, head=head, query_tile=query_tile, mask=mask):
                rows = rows_of(i, size, size)
                queries = qkv[layer, rows, query_tile * TILE:(query_tile + 1) * TILE] * mask
                keys = k2[...] if head == 2 else qkv[layer, :, TILE:2 * TILE]
                values = (vt.at[0, :HEAD_DIM], vt.at[0, HEAD_DIM:], vt.at[1, HEAD_DIM:])[head][...]
                scores = dot_nt(keys, queries) * (score_scale * log2e) + bias[:, rows]
                top = jnp.max(scores, axis=0, keepdims=True)
                probs = jnp.exp2(scores - top)
                total = jnp.sum(probs, axis=0, keepdims=True)
                result = dot(values, probs.astype(bf16)) / total
                spot = pl.ds(
                    pl.multiple_of(me * (OWN_HEADS * HEAD_DIM) + head * HEAD_DIM, HEAD_DIM), HEAD_DIM
                )
                att[layer, spot, rows] = result.astype(bf16)
                lse[layer, head:head + 1, rows] = top + jnp.log(total) * log2e
                return carry

            lax.fori_loop(0, seq // size, attend, 0)

            def features(block, head=head, layer=layer):
                start = block * (OWN_HEADS * HEAD_DIM) + head * HEAD_DIM
                return att.at[layer, pl.ds(pl.multiple_of(start, HEAD_DIM), HEAD_DIM)]

            own, theirs = features(me), features(across)
            to_across = push(own, own, sems, layer, 6 + head, across)
            to_mate = push(own, own, sems, layer, 9 + head, mate)
            onward = push(theirs, theirs, sems, layer, 12 + head, mate)
            to_across.start()
            to_mate.start()
            if head:
                sends[-2].wait_recv()
                forwards[-1].start()
            if spreading and head == 0:
                weights[PIECES * layer + 1].share_across()
            if spreading and head == 2:
                weights[PIECES * layer + 1].share()
            pump(2)
            sends += [to_across, to_mate]
            forwards.append(onward)
        sends[-2].wait_recv()
        forwards[-1].start()
        for head in range(OWN_HEADS):
            sends[2 * head + 1].wait_recv()
            forwards[head].wait_recv()
        store(2, layer, lse, lse_out)
        store(3, layer, att, att_out)
        if layer == 0:
            gain_stage(1)
        pump(2)
        for number in (1, 2):
            weights[PIECES * layer + number].wait()

        def feed(block, keep, layer=layer):
            rows = rows_of(block, size, size)
            branch = dot_tn(att[layer, :, rows], wo[layer])
            normed, inverse = normed_rows(xf[layer, rows, :].astype(f32) + branch)
            first_rows = normed * gain[2 * layer:2 * layer + 1, :]
            if keep:
                n1[layer] = normed
                s1[layer] = jnp.broadcast_to(inverse, s1.shape[1:])
                first[...] = first_rows
            first_low = first_rows.astype(bf16)
            flow[layer, rows, :] = first_low
            gate_up = dot(first_low, wg[layer])
            gate, upward = gate_up[:, :ff], gate_up[:, ff:]
            gu[layer, rows, :] = gate_up.astype(bf16)
            hid[layer, rows, :] = (gate / (1.0 + jnp.exp(-gate)) * upward).astype(bf16)

        def down(block, layer=layer):
            return dot_nt(hid[layer, rows_of(block, size, size), :], wd[layer])

        for number, block in enumerate((far, across, mate, me)):
            feed(block, number == 3)
            pump(2)
        weights[PIECES * layer + 3].wait()
        for number, held in enumerate((wq, wo, wg, wd)):
            store(12 + number, layer, held, weight_outs[number])
        scatter = Scatter(part, layer, got, layer, sems, 15, where)
        scatter.send_far(down(far))
        scatter.send_across(down(across))
        scatter.send_mate(down(mate))
        own_part = down(me)
        pump(2)
        store(4, layer, flow, flow_out)
        store(5, layer, gu, gu_out)
        store(6, layer, hid, hid_out)
        store(7, layer, n1, n1_out)
        store(8, layer, s1, s1_out)
        pump(4)
        ffn = scatter.total(own_part)
        pending.append(scatter)
        normed, inverse = normed_rows(first[...] + ffn)
        n2[layer] = normed
        s2[layer] = jnp.broadcast_to(inverse, s2.shape[1:])
        result = (normed * gain[2 * layer + 1:2 * layer + 2, :]).astype(bf16)
        store(9, layer, n2, n2_out)
        store(10, layer, s2, s2_out)
        if layer + 1 < LAYERS:
            xf[layer + 1, rows_of(me, size, size), :] = result
            row_gather = Gather(xf, layer + 1, layer + 1, sems, 0, size, where)
            row_gather.start()
            pump(2)
        else:
            act[...] = result
            copy = pltpu.make_async_copy(act, act_out, osems.at[0, 11])
            copy.start()
            stores.append(copy)
        for copy in sends + forwards:
            copy.wait_send()
    if spreading:
        pending += weights
    for item in pending:
        item.finish()
    for copy in stores:
        copy.wait()


BACK_LOADED = (
    "n1", "s1", "n2", "s2", "xf", "qkv", "lse", "att", "flow", "gu", "hid", "wq", "wo", "wg", "wd",
)
BACK_TABLES = ("gain", "cos_rows", "sin_rows", "doc_keys", "doc_queries")
BACK_SCRATCH = (
    "bias", "dff", "dbr", "datt", "dproj", "dk", "dv", "dqt", "kt", "k2", "grad", "part", "got",
    "gq", "go", "gg", "gd", "sems", "lsems", "osems",
)

def backward_kernel(spreading, names, *refs):
    r = dict(zip(names, refs))
    cot = r["cot"]
    gain, cos_rows, sin_rows, doc_keys, doc_queries = (r[n] for n in BACK_TABLES)
    (
        bias, dff, dbr, datt, dproj, dk, dv, dqt, kt, k2, grad, part, got,
        gq, go, gg, gd, sems, lsems, osems,
    ) = (r[n] for n in BACK_SCRATCH)
    n1, s1, n2, s2, qkv, lse, att, gu, hid, wq, wo, wg, wd = (
        r[n] for n in BACK_LOADED if n not in ("xf", "flow")
    )
    xf = flow = r["rows"]
    where = places()
    me, mate, across, far, core = where
    size = cot.shape[0]
    seq = size * GROUP
    ff = hid.shape[1]
    feats = xf.shape[1]
    own_feats = OWN_HEADS * HEAD_DIM
    held = {n: (r[n + "_in"], r.get(n, r["rows"])) for n in BACK_LOADED}
    order = list(held)
    loads = {}

    def load(name, layer):
        if layer < 0:
            return
        source, target = held[name]
        copy = pltpu.make_async_copy(source.at[layer], target, lsems.at[order.index(name)])
        copy.start()
        loads[name] = copy

    for name in ("n2", "s2", "wd", "gu", "wg", "hid", "n1", "s1", "flow", "wo", "qkv", "lse", "att", "wq"):
        load(name, LAYERS - 1)
    spread = Spread(feats // (2 * DEPTH)) if spreading else None
    greet(mate, across, far if spreading else None, spread)
    low_mask, high_mask = half_masks()
    grad[...] = cot[...]
    pending = []
    scatters = []
    stores = {}
    sums = {}
    shares = []
    pieces = dict(
        d=gd.at[:, :], g=gg.at[:, :ff], u=gg.at[:, ff:],
        a=gq.at[:, :3 * TILE], b=gq.at[:, 3 * TILE:], o=go.at[:, :],
    )
    gsum = r["gsum"] if spreading else r["gain_out"]
    gsum[...] = jnp.zeros_like(gsum)

    def begin(name, layer):
        if not spreading:
            if name not in "ga":
                number = "boud".index(name)
                store(number, layer, (gq, go, gg, gd)[number], r["qogd"[number] + "_out"])
            return
        index = "dguabo".index(name)
        item = WeightSum(
            pieces[name], r["near_" + name], r["apart_" + name], 6 * layer + index, r["dsems"],
            spread, (r["csems"].at[0, index], r["csems"].at[1, index]),
            layer < LAYERS - 1, layer > 0, r["sum_" + name],
            lax.div(me, 2) if name == "o" else None,
        )
        item.start()
        sums[name, layer] = item

    def add(name, layer):
        if spreading and (name, layer) in sums:
            sums[name, layer].add()

    def total(name, layer):
        if not spreading or (name, layer) not in sums:
            return
        result = sums[name, layer].total()
        if name in "abo":
            share = Share(r[name + "share"], layer, sems, 15 + 3 * "abo".index(name), where)
            share.start(result.astype(bf16))
            shares.append(share)
        elif name == "d":
            r["d_res"][layer] = result
        else:
            half = "gu".index(name)
            r["g_res"][layer, :, half * ff:(half + 1) * ff] = result

    def ready(name, layer):
        if not spreading:
            if name not in "ub":
                stored("aogd".index(name))
        elif (name, layer + 1) in sums:
            sums[name, layer + 1].finish()

    gains = []

    def gain_stage(stage):
        if not spreading:
            return
        gpack, gside, gdeep, gsems = (r[n] for n in ("gpack", "gside", "gdeep", "gsems"))
        if stage == 0:
            gpack[me] = gsum[...]
            for number, who in enumerate((mate, across, far)):
                gains.append(push(gpack.at[me], gpack.at[me], gsems, 0, number, who))
        elif stage == 1:
            for copy in gains[:3]:
                copy.wait_recv()
            gside[spread.x] = gpack[0] + gpack[1] + gpack[2] + gpack[3]
            own = gside.at[spread.x]
            gains.append(ship(own, own, gsems, 0, 3, spread.beside(0)))
        elif stage == 2:
            gains[3].wait_recv()
            gdeep[spread.z] = gside[0] + gside[1]
            own = gdeep.at[spread.z]
            for step in range(1, DEPTH):
                gains.append(ship(own, own, gsems, 0, 3 + step, spread.device(step)))
        else:
            for copy in gains[4:]:
                copy.wait_recv()
            r["gain_out"][...] = gdeep[0] + gdeep[1] + gdeep[2] + gdeep[3]
            for copy in gains:
                copy.wait_send()
            return
        for copy in gains[(0, 3, 4)[stage]:]:
            copy.start()

    def store(number, layer, source, target):
        copy = pltpu.make_async_copy(source, target.at[layer], osems.at[layer, number])
        copy.start()
        stores[number] = copy

    def stored(number):
        if number in stores:
            stores.pop(number).wait()

    for layer in range(LAYERS - 1, -1, -1):

        def norm_back(grad_rows, normed, inverse, row, layer=layer):
            gsum[2 * layer + row:2 * layer + row + 1, :] = jnp.sum(
                grad_rows * normed, axis=0, keepdims=True
            )
            scaled = grad_rows * gain[2 * layer + row:2 * layer + row + 1, :]
            return (
                scaled
                - jnp.mean(scaled, axis=-1, keepdims=True)
                - normed * jnp.mean(scaled * normed, axis=-1, keepdims=True)
            ) * inverse

        loads["n2"].wait()
        loads["s2"].wait()
        dz = norm_back(grad[...], n2[...], s2[:, :1], 1)
        load("n2", layer - 1)
        load("s2", layer - 1)
        grad[...] = dz
        dff[0, rows_of(me, size, size), :] = dz.astype(bf16)
        gather = Gather(dff, 0, layer, sems, 0, size, where)
        gather.start()
        if layer == LAYERS - 1:
            write_bias(bias, doc_keys, doc_queries)
        for name in ("wd", "gu", "wg"):
            loads[name].wait()
        add("o", layer + 1)

        def feed_back(block):
            rows = rows_of(block, size, size)
            grad_hidden = dot(dff[0, rows, :], wd[...])
            gate = gu[rows, :ff].astype(f32)
            upward = gu[rows, ff:].astype(f32)
            sigma = 1.0 / (1.0 + jnp.exp(-gate))
            up_grad = grad_hidden * gate * sigma
            gate_grad = grad_hidden * upward * sigma * (1.0 + gate * (1.0 - sigma))
            gu[rows, :ff] = gate_grad.astype(bf16)
            gu[rows, ff:] = up_grad.astype(bf16)
            return dot_nt(gu[rows, :], wg[...])

        if len(scatters) > 1:
            scatters[-2].finish()
        scatter = Scatter(part, 0, got, 2 * layer, sems, 6, where)
        scatters.append(scatter)
        own_part = feed_back(me)
        gather.wait_mate()
        scatter.send_mate(feed_back(mate))
        gather.wait_across()
        loads["hid"].wait()
        add("a", layer + 1)
        gather.wait_far()
        ready("d", layer)

        def down_weight(i, carry):
            cols = rows_of(i, 256, 256)
            gd[cols, :] = dot_tn(dff[0, :, cols], hid[...]).astype(bf16)
            return carry

        lax.fori_loop(0, feats // 256, down_weight, 0)
        begin("d", layer)
        scatter.send_far(feed_back(far))
        scatter.send_across(feed_back(across))
        gather.finish()
        load("hid", layer - 1)
        load("wd", layer - 1)
        load("wg", layer - 1)
        add("b", layer + 1)
        loads["flow"].wait()
        for name, first_col in (("g", 0), ("u", ff)):
            ready(name, layer)

            def gate_up_weight(i, carry, first_col=first_col):
                cols = rows_of(i, 256, 256)
                gg[cols, first_col:first_col + ff] = dot_tn(
                    flow[:, cols], gu[:, first_col:first_col + ff]
                ).astype(bf16)
                return carry

            lax.fori_loop(0, feats // 256, gate_up_weight, 0)
            begin(name, layer)
        load("gu", layer - 1)
        load("xf", layer)
        for name in "dgu":
            total(name, layer + 1)

        if layer == 0:
            add("d", layer)
        dfirst = grad[...] + scatter.total(own_part)
        loads["n1"].wait()
        loads["s1"].wait()
        dr = norm_back(dfirst, n1[...], s1[:, :1], 0)
        load("n1", layer - 1)
        load("s1", layer - 1)
        grad[...] = dr
        dbr[layer, rows_of(me, size, size), :] = dr.astype(bf16)
        gather = Gather(dbr, layer, layer, sems, 9, size, where)
        gather.start()
        if layer == 0:
            gain_stage(0)
        for name in ("wo", "qkv", "lse"):
            loads[name].wait()

        def att_back(block, layer=layer):
            rows = rows_of(block, size, size)
            for tile, start in enumerate((0, HEAD_DIM)):
                spot = pl.ds(pl.multiple_of(me * own_feats + start, HEAD_DIM), TILE)
                datt[rows, tile * TILE:(tile + 1) * TILE] = dot_nt(
                    dbr[layer, rows, :], wo[spot, :]
                ).astype(bf16)

        kt[0] = qkv[:, TILE:2 * TILE].T
        kt[1] = qkv[:, 3 * TILE:4 * TILE].T
        k2[...] = pltpu.roll(qkv[:, 3 * TILE:4 * TILE].astype(f32), HEAD_DIM, 1).astype(bf16)
        dk[...] = jnp.zeros_like(dk)
        dv[...] = jnp.zeros_like(dv)

        def attend(head, first, second):
            tile = head // 2
            query_tile = (0, 0, 3)[head]
            value_tile = (2, 2, 4)[head]
            query_mask = (low_mask, high_mask, low_mask)[head]
            value_mask = (low_mask, high_mask, high_mask)[head]

            def body(i, carry):
                rows = rows_of(first + i * (second - first), size, size)
                queries = qkv[rows, query_tile * TILE:(query_tile + 1) * TILE] * query_mask
                keys = k2[...] if head == 2 else qkv[:, TILE:2 * TILE]
                scores = dot_nt(keys, queries) * (score_scale * log2e) + bias[:, rows]
                probs = jnp.exp2(scores - lse[head:head + 1, rows])
                outs = datt[rows, tile * TILE:(tile + 1) * TILE] * value_mask
                grad_probs = dot_nt(qkv[:, value_tile * TILE:(value_tile + 1) * TILE], outs)
                delta = jnp.sum(probs * grad_probs, axis=0, keepdims=True)
                grad_scores = (probs * (grad_probs - delta)).astype(bf16)
                dv[tile] = dv[tile] + dot(probs.astype(bf16), outs)
                dk[tile] = dk[tile] + dot(grad_scores, queries)
                keys_t = (kt.at[0, :HEAD_DIM], kt.at[0, HEAD_DIM:], kt.at[1, HEAD_DIM:])[head][...]
                spot = (0, HEAD_DIM, 0)[head]
                dqt[tile, spot:spot + HEAD_DIM, rows] = dot(keys_t, grad_scores)
                return carry

            lax.fori_loop(0, 2, body, 0)

        att_back(me)
        gather.wait_mate()
        att_back(mate)
        for head in range(OWN_HEADS):
            attend(head, me, mate)
        gather.wait_across()
        att_back(across)
        if layer == 0:
            gain_stage(1)
            add("g", layer)
        else:
            add("d", layer)
        gather.wait_far()
        att_back(far)
        pending.append(gather)
        load("wo", layer - 1)
        loads["att"].wait()
        ready("o", layer)

        def out_weight(i, carry, layer=layer):
            rows = rows_of(i, 256, 256)
            half = feats // 2
            cols = pl.ds(pl.multiple_of(core * half, half), half)
            go[rows, :] = dot(att[rows, :], dbr[layer, :, cols]).astype(bf16)
            return carry

        lax.fori_loop(0, feats // 256, out_weight, 0)
        begin("o", layer)
        load("att", layer - 1)
        for name in "oab":
            total(name, layer + 1)
        attend(0, across, far)
        attend(1, across, far)
        for share in shares:
            share.serve()

        def unrotate_pairs(i, carry):
            rows = rows_of(i, size, size)
            c, s = cos_rows[rows, :], -sin_rows[rows, :]
            dproj[rows, :TILE] = turn(dqt[0, :, rows].T * score_scale, c, s).astype(bf16)
            dproj[rows, TILE:2 * TILE] = turn(dk[0, rows, :] * score_scale, c, s).astype(bf16)
            dproj[rows, 2 * TILE:3 * TILE] = dv[0, rows, :].astype(bf16)
            return carry

        def unrotate_last(i, carry):
            rows = rows_of(i, size, size)
            c, s = cos_rows[rows, :], -sin_rows[rows, :]
            lower = lane_iota((size, TILE)) < HEAD_DIM
            mixed = jnp.where(lower, dqt[1, :, rows].T, pltpu.roll(dk[1, rows, :], HEAD_DIM, 1))
            dproj[rows, 3 * TILE:4 * TILE] = turn(mixed * score_scale, c, s).astype(bf16)
            dproj[rows, 4 * TILE:] = dv[1, rows, :].astype(bf16)
            return carry

        def weigh_projection(first, last):
            def qkv_weight(i, carry):
                cols = rows_of(i, 256, 256)
                gq[cols, first:last] = dot_tn(xf[:, cols], dproj[:, first:last]).astype(bf16)
                return carry

            lax.fori_loop(0, feats // 256, qkv_weight, 0)

        lax.fori_loop(0, seq // size, unrotate_pairs, 0)
        loads["xf"].wait()
        ready("a", layer)
        weigh_projection(0, 3 * TILE)
        begin("a", layer)
        if layer:
            add("g", layer)
        else:
            gain_stage(2)
            add("u", layer)
        attend(2, across, far)
        lax.fori_loop(0, seq // size, unrotate_last, 0)
        load("qkv", layer - 1)
        load("lse", layer - 1)
        loads["wq"].wait()

        def input_part(block):
            return dot_nt(dproj[rows_of(block, size, size), :], wq[...])

        if len(scatters) > 1:
            scatters[-2].finish()
        scatter = Scatter(part, 1, got, 2 * layer + 1, sems, 6, where)
        scatters.append(scatter)
        if layer == 0:
            ready("b", layer)
            weigh_projection(3 * TILE, PROJ)
            begin("b", layer)
        scatter.send_far(input_part(far))
        scatter.send_across(input_part(across))
        scatter.send_mate(input_part(mate))
        own_part = input_part(me)
        load("wq", layer - 1)
        if layer:
            ready("b", layer)
            weigh_projection(3 * TILE, PROJ)
            begin("b", layer)
            add("u", layer)
        else:
            gain_stage(3)
            add("o", layer)
            add("a", layer)
            for name in "dg":
                total(name, 0)
            add("b", layer)
        load("flow", layer - 1)
        grad[...] = grad[...] + scatter.total(own_part)
    input_copy = pltpu.make_async_copy(grad, r["ig_out"], osems.at[0, 4])
    input_copy.start()
    for name in "uoab":
        total(name, 0)
    if spreading:
        for share in shares[-3:]:
            share.serve()
    input_copy.wait()
    for item in pending + scatters[-2:]:
        item.finish()
    for number in range(4):
        stored(number)
    for item in shares:
        item.finish()
    if spreading:
        for name in "dguabo":
            sums[name, 0].finish()
        q_out = r["q_out"]
        ends = (
            (r["ashare"], q_out.at[:, :, :, pl.ds(0, 3 * TILE)]),
            (r["bshare"], q_out.at[:, :, :, pl.ds(3 * TILE, 2 * TILE)]),
            (r["oshare"], r["o_out"]),
        )
        last = []
        for number, held in enumerate(ends):
            last.append(pltpu.make_async_copy(*held, osems.at[1, number]))
            last[-1].start()
        for copy in last:
            copy.wait()


RATES = ((0.03, 0.01), (0.5, 0.01), (0.03, 0.01), (0.02, 0.01), (0.6, 0.0))


def adam_step(weight, first, second, average, gradient, rate, decay):
    first_new = beta_first * first + (1.0 - beta_first) * gradient
    second_new = beta_second * second + (1.0 - beta_second) * gradient * gradient
    first_hat = first_new * (1.0 / (1.0 - beta_first**STEP))
    second_hat = second_new * (1.0 / (1.0 - beta_second**STEP))
    weight_new = weight - rate * (
        first_hat / (jnp.sqrt(second_hat) + adam_epsilon) + decay * weight
    )
    average_new = average_decay * average + (1.0 - average_decay) * weight_new
    return first_new, second_new, weight_new, average_new


def adam_kernel(*refs):
    states = [refs[4 * f:4 * f + 4] for f in range(5)]
    grads = refs[20:25]
    outs = [refs[27 + 5 * f:32 + 5 * f] for f in range(5)]
    (qs, os, ds, gs, qg, og, gg, qb, ob, gb, db, gsems, isems, usems, psems, act, ig) = refs[54:]
    passed = []
    for k, held in enumerate((act, ig)):
        passed.append(pltpu.make_async_copy(refs[25 + k], held, psems.at[k]))
        passed[-1].start()
    width = ob.shape[3]
    for number, target in enumerate((qs, os, gs, ds)):
        pltpu.make_async_copy(grads[number], target, gsems.at[number]).start()
    chunks = []
    for family, held, grad in ((3, db, ds), (2, gb, gg), (1, ob, og), (0, qb, qg)):
        for layer in range(LAYERS):
            for part in range(3 if family == 0 else 1):
                spot = 3 * layer + part if family == 0 else layer
                chunks.append((family, held, grad, layer, part, spot))

    def view(ref, family, layer, part):
        if family:
            return ref.at[layer]
        return ref.at[layer, :, pl.ds(part * width, width)]

    arrivals = []
    for number, (family, held, grad, layer, part, spot) in enumerate(chunks):
        copies = [
            pltpu.make_async_copy(
                view(states[family][k], family, layer, part), held.at[k, spot], isems.at[number, k]
            )
            for k in range(4)
        ]
        for copy in copies:
            copy.start()
        arrivals.append(copies)

    def wait_grad(number, target):
        pltpu.make_async_copy(grads[number], target, gsems.at[number]).wait()

    gain = [ref[...] for ref in states[4]]
    gradient = grads[4][...]
    new = adam_step(*gain, gradient, *RATES[4])
    for ref, value in zip(outs[4], (gradient,) + new):
        ref[...] = value

    for k, held in enumerate((act, ig)):
        passed[k].wait()
        passed[k] = pltpu.make_async_copy(held, refs[52 + k], psems.at[k])
        passed[k].start()
    low = lane_iota((qs.shape[2], TILE)) < HEAD_DIM
    leaving = []
    for number, (family, held, grad, layer, part, spot) in enumerate(chunks):
        first_of = layer == 0 and part == 0
        if family == 3 and first_of:
            wait_grad(3, ds)
        if family == 2:
            if first_of:
                wait_grad(2, gs)
            for half in range(2):
                gg[layer, :, half, :] = gs[layer, :, half * width:(half + 1) * width]
        if family == 1:
            if first_of:
                wait_grad(1, os)
            high, wide = os.shape[2], os.shape[3]
            for side in range(2):
                for core in range(2):
                    og[layer, side * high:(side + 1) * high, core * wide:(core + 1) * wide] = os[
                        layer, 2 * side + core
                    ].astype(f32)
        if family == 0:
            if first_of:
                wait_grad(0, qs)

            def pair(j):
                return qs[layer, j, :, part * TILE:(part + 1) * TILE].astype(f32)

            def last(j, upper):
                tile = 4 if part == 2 else 3
                value = qs[layer, j, :, tile * TILE:(tile + 1) * TILE].astype(f32)
                return value if upper == (part > 0) else pltpu.roll(value, HEAD_DIM, 1)

            for j in (0, 2):
                turned = pltpu.roll(pair(j + 1), HEAD_DIM, 1)
                tiles = (
                    pair(j),
                    jnp.where(low, last(j, False), turned),
                    jnp.where(low, turned, last(j + 1, True)),
                )
                for k, value in enumerate(tiles):
                    start = (3 * (j // 2) + k) * TILE
                    qg[spot, :, start:start + TILE] = value
        for copy in arrivals[number]:
            copy.wait()
        rows = 32

        def body(i, carry, family=family, held=held, grad=grad, spot=spot):
            at = pl.ds(pl.multiple_of(i * rows, rows), rows)
            values = [held[k, spot, at] for k in range(4)]
            first, second, weight, average = adam_step(*values, grad[spot, at], *RATES[family])
            for k, value in enumerate((weight, first, second, average)):
                held[k, spot, at] = value
            return carry

        lax.fori_loop(0, ob.shape[2] // rows, body, 0)
        sources = (grad.at[spot],) + tuple(held.at[k, spot] for k in (1, 2, 0, 3))
        for k, source in enumerate(sources):
            copy = pltpu.make_async_copy(
                source, view(outs[family][k], family, layer, part), usems.at[number, k]
            )
            copy.start()
            leaving.append(copy)
    for copy in leaving + passed:
        copy.wait()


def frequencies():
    half = HEAD_DIM // 2
    freq = rotary_base ** (-2.0 * np.arange(half) / HEAD_DIM)
    return jnp.asarray(np.tile(freq, (8, 4)).astype(np.float32))


def own_projection(weight, me):
    layers, rows, _ = weight.shape
    split = weight.reshape(layers, rows, 3, HEADS * HEAD_DIM)
    own = lax.dynamic_slice_in_dim(split, me * OWN_HEADS * HEAD_DIM, OWN_HEADS * HEAD_DIM, 3)
    own = own.astype(bf16)
    pairs = own[..., :TILE].reshape(layers, rows, 3 * TILE)
    last = own[..., TILE:]
    return jnp.concatenate(
        [pairs, last[:, :, 0], last[:, :, 1], jnp.zeros_like(last[:, :, 0]), last[:, :, 2]], axis=-1
    )


def whole_projection(grad):
    group, layers, rows, _ = grad.shape
    pairs = grad[..., :3 * TILE].reshape(group, layers, rows, 3, TILE)
    last = jnp.stack(
        [
            grad[..., 3 * TILE:3 * TILE + HEAD_DIM],
            grad[..., 3 * TILE + HEAD_DIM:4 * TILE],
            grad[..., 4 * TILE + HEAD_DIM:],
        ],
        axis=3,
    )
    full = jnp.concatenate([pairs, last], axis=-1)
    return full.transpose(1, 2, 3, 0, 4).reshape(layers, rows, 3 * HEADS * HEAD_DIM)


def run_forward(spreading, tokens, weights, gain, lengths, mask_row):
    size, feats = tokens.shape
    seq = size * GROUP
    ff = weights[3].shape[2]
    own = weights[0].shape[1]
    shapes = dict(
        act=((size, feats), bf16),
        xf=((LAYERS, seq, feats), bf16),
        qkv=((LAYERS, seq, PROJ), bf16),
        lse=((LAYERS, 8, seq), f32),
        att=((LAYERS, feats, seq), bf16),
        flow=((LAYERS, seq, feats), bf16),
        gu=((LAYERS, seq, 2 * ff), bf16),
        hid=((LAYERS, seq, ff), bf16),
        n1=((LAYERS, size, feats), f32),
        s1=((LAYERS, size, 128), f32),
        n2=((LAYERS, size, feats), f32),
        s2=((LAYERS, size, 128), f32),
        wq=((LAYERS, feats, PROJ), bf16),
        wo=((LAYERS, feats, feats), bf16),
        wg=((LAYERS, feats, 2 * ff), bf16),
        wd=((LAYERS, feats, ff), bf16),
        gain=((8, feats), f32),
        cos_rows=((seq, 128), f32),
        sin_rows=((seq, 128), f32),
        doc_keys=((seq, 128), jnp.int32),
        doc_queries=((8, seq), jnp.int32),
    )
    held = {name: pltpu.VMEM(*shape) for name, shape in shapes.items()}
    scratch = [held[n] for n in ("wq", "wo", "wg", "wd", "xf", "qkv", "att", "flow", "gu", "hid")]
    scratch += [
        pltpu.VMEM((seq, seq), f32),
        pltpu.VMEM((2, TILE, seq), bf16),
        pltpu.VMEM((seq, TILE), bf16),
        held["lse"],
    ]
    scratch += [held[n] for n in ("n1", "s1", "n2", "s2")]
    scratch += [
        pltpu.VMEM((size, feats), f32),
        held["act"],
        pltpu.VMEM((LAYERS, 3, size, feats), bf16),
        pltpu.VMEM((LAYERS, 3, size, feats), bf16),
        pltpu.SemaphoreType.DMA((2, LAYERS, 18)),
        pltpu.SemaphoreType.DMA((LAYERS, PIECES)),
        pltpu.SemaphoreType.DMA((LAYERS, 16)),
        pltpu.SemaphoreType.DMA((2, PIECES * LAYERS, 3 + 2 * DEPTH)),
        pltpu.SemaphoreType.DMA((2, LAYERS, 14)),
        pltpu.VMEM((2, 8, feats), f32),
        pltpu.VMEM((DEPTH, 8, feats), f32),
        pltpu.SemaphoreType.DMA((2, 1, DEPTH)),
    ]
    if spreading:
        scratch += [
            pltpu.VMEM((LAYERS, own, feats), bf16),
            pltpu.VMEM((LAYERS, own, 2 * ff), bf16),
            pltpu.VMEM((LAYERS, own, ff), bf16),
        ]
    return pl.pallas_call(
        functools.partial(forward_kernel, spreading),
        out_shape=[jax.ShapeDtypeStruct(*shape) for shape in shapes.values()],
        in_specs=[VMEM, ANY] + [VMEM if spreading else ANY] * 3
        + [VMEM, pl.BlockSpec(memory_space=pltpu.SMEM), VMEM, VMEM],
        out_specs=[ANY] * (len(shapes) - 5) + [VMEM] * 5,
        scratch_shapes=scratch,
        compiler_params=pltpu.CompilerParams(
            collective_id=0, has_side_effects=True, vmem_limit_bytes=VMEM_LIMIT
        ),
        cost_estimate=pl.CostEstimate(
            flops=12 * 10**9, bytes_accessed=60 * 10**6, transcendentals=10**7
        ),
        name="forward",
    )(tokens, *weights, gain, lengths, mask_row, frequencies())


def run_backward(spreading, cotangent, kept, weights, gain, tables):
    size, feats = cotangent.shape
    seq = size * GROUP
    xf, qkv, lse, att, flow, gu, hid, n1, s1, n2, s2 = kept
    ff = hid.shape[2]
    wq, wo, wg, wd = weights
    loaded = [n1, s1, n2, s2, xf, qkv, lse, att, flow, gu, hid, wq, wo, wg, wd]
    own = feats // (2 * DEPTH)
    half = feats // 2
    widths = dict(d=ff, g=ff, u=ff, a=3 * TILE, b=2 * TILE, o=half)
    if spreading:
        outs = dict(
            ig_out=((size, feats), f32),
            q_out=((LAYERS, GROUP, own, PROJ), bf16),
            o_out=((LAYERS, GROUP, own // 2, half), bf16),
            d_res=((LAYERS, own, ff), f32),
            g_res=((LAYERS, own, 2 * ff), f32),
            gain_out=((8, feats), f32),
        )
    else:
        outs = dict(
            ig_out=((size, feats), f32),
            q_out=(wq.shape, bf16),
            o_out=((LAYERS, feats, half), bf16),
            d_out=(wd.shape, bf16),
            g_out=(wg.shape, bf16),
            gain_out=((8, feats), f32),
        )
    names = ["cot"] + [n + "_in" for n in BACK_LOADED] + list(BACK_TABLES) + list(outs)
    scratch = dict(
        bias=pltpu.VMEM((seq, seq), f32),
        dff=pltpu.VMEM((1, seq, feats), bf16),
        dbr=pltpu.VMEM((LAYERS, seq, feats), bf16),
        datt=pltpu.VMEM((seq, 2 * TILE), bf16),
        dproj=pltpu.VMEM((seq, PROJ), bf16),
        dk=pltpu.VMEM((2, seq, TILE), f32),
        dv=pltpu.VMEM((2, seq, TILE), f32),
        dqt=pltpu.VMEM((2, TILE, seq), f32),
        kt=pltpu.VMEM((2, TILE, seq), bf16),
        k2=pltpu.VMEM((seq, TILE), bf16),
        grad=pltpu.VMEM((size, feats), f32),
        part=pltpu.VMEM((2, 3, size, feats), bf16),
        got=pltpu.VMEM((2, 3, size, feats), bf16),
        gq=pltpu.VMEM((feats, PROJ), bf16),
        go=pltpu.VMEM((feats, half), bf16),
        gg=pltpu.VMEM((feats, 2 * ff), bf16),
        gd=pltpu.VMEM((feats, ff), bf16),
        sems=pltpu.SemaphoreType.DMA((2, 2 * LAYERS, 24)),
        lsems=pltpu.SemaphoreType.DMA((len(loaded),)),
        osems=pltpu.SemaphoreType.DMA((LAYERS, 5)),
        rows=pltpu.VMEM((seq, feats), bf16),
    )
    for name, array in zip(BACK_LOADED, loaded):
        if name not in ("xf", "flow"):
            scratch[name] = pltpu.VMEM(array.shape[1:], array.dtype)
    if spreading:
        scratch.update(
            gsum=pltpu.VMEM((8, feats), f32),
            gpack=pltpu.VMEM((GROUP, 8, feats), f32),
            gside=pltpu.VMEM((2, 8, feats), f32),
            gdeep=pltpu.VMEM((DEPTH, 8, feats), f32),
            gsems=pltpu.SemaphoreType.DMA((2, 1, 7)),
            csems=pltpu.SemaphoreType.REGULAR((2, 6)),
            ashare=pltpu.VMEM((LAYERS, GROUP, own, 3 * TILE), bf16),
            bshare=pltpu.VMEM((LAYERS, GROUP, own, 2 * TILE), bf16),
            oshare=pltpu.VMEM((LAYERS, GROUP, own // 2, half), bf16),
            dsems=pltpu.SemaphoreType.DMA((2, 6 * LAYERS, 7)),
        )
        for name, width in widths.items():
            high = own // 2 if name == "o" else own
            scratch["near_" + name] = pltpu.VMEM((DEPTH, high, width), bf16)
            scratch["apart_" + name] = pltpu.VMEM((DEPTH - 1, high, width), bf16)
            scratch["sum_" + name] = pltpu.VMEM((high, width), f32)
    in_vmem = ("d_res", "g_res", "gain_out")
    return pl.pallas_call(
        functools.partial(backward_kernel, spreading, tuple(names + list(scratch))),
        out_shape=[jax.ShapeDtypeStruct(*shape) for shape in outs.values()],
        in_specs=[VMEM] + [ANY] * 15 + [VMEM] * 5,
        out_specs=[VMEM if name in in_vmem else ANY for name in outs],
        scratch_shapes=list(scratch.values()),
        compiler_params=pltpu.CompilerParams(
            collective_id=1, has_side_effects=True, vmem_limit_bytes=VMEM_LIMIT
        ),
        cost_estimate=pl.CostEstimate(
            flops=24 * 10**9, bytes_accessed=60 * 10**6, transcendentals=10**7
        ),
        name="backward",
    )(cotangent, *loaded, gain, *tables)


def run_adam(states, grads, rows):
    outs = []
    for family in range(5):
        shape = jax.ShapeDtypeStruct(states[4 * family].shape, f32)
        outs += [shape] * 5
    outs += [jax.ShapeDtypeStruct(a.shape, a.dtype) for a in rows]
    layers, own, _, width = states[8].shape
    scratch = [
        pltpu.VMEM(grads[0].shape, bf16),
        pltpu.VMEM(grads[1].shape, bf16),
        pltpu.VMEM(grads[3].shape, f32),
        pltpu.VMEM(grads[2].shape, f32),
        pltpu.VMEM((3 * layers, own, width), f32),
        pltpu.VMEM((layers, own, width), f32),
        pltpu.VMEM((layers, own, 2, width), f32),
        pltpu.VMEM((4, 3 * layers, own, width), f32),
        pltpu.VMEM((4, layers, own, width), f32),
        pltpu.VMEM((4, layers, own, 2, width), f32),
        pltpu.VMEM((4, layers, own, width), f32),
        pltpu.SemaphoreType.DMA((4,)),
        pltpu.SemaphoreType.DMA((6 * layers, 4)),
        pltpu.SemaphoreType.DMA((6 * layers, 5)),
        pltpu.SemaphoreType.DMA((2,)),
    ]
    scratch += [pltpu.VMEM(a.shape, a.dtype) for a in rows]
    return pl.pallas_call(
        adam_kernel,
        out_shape=outs,
        in_specs=[ANY] * 16 + [VMEM] * 4 + [ANY] * 4 + [VMEM] + [ANY] * 2,
        out_specs=[ANY] * 20 + [VMEM] * 5 + [ANY] * 2,
        scratch_shapes=scratch,
        compiler_params=pltpu.CompilerParams(vmem_limit_bytes=VMEM_LIMIT),
        cost_estimate=pl.CostEstimate(
            flops=2 * 10**7, bytes_accessed=37 * 10**6, transcendentals=10**6
        ),
        name="adam",
    )(*states, *grads, *rows)


def adamw(weight, first, second, average, gradient, rate, decay):
    first_new = beta_first * first + (1.0 - beta_first) * gradient
    second_new = beta_second * second + (1.0 - beta_second) * gradient * gradient
    first_hat = first_new / (1.0 - beta_first**STEP)
    second_hat = second_new / (1.0 - beta_second**STEP)
    weight_new = weight - rate * (
        first_hat / (jnp.sqrt(second_hat) + adam_epsilon) + decay * weight
    )
    average_new = average_decay * average + (1.0 - average_decay) * weight_new
    return (gradient, first_new, second_new, weight_new, average_new)


def shards(
    spreading,
    tokens,
    cotangent,
    lengths,
    key_mask,
    qkv_weight,
    qkv_first,
    qkv_second,
    qkv_average,
    out_weight,
    out_first,
    out_second,
    out_average,
    gate_up_weight,
    gate_up_first,
    gate_up_second,
    gate_up_average,
    down_weight,
    down_first,
    down_second,
    down_average,
    norm_gain,
    gain_first,
    gain_second,
    gain_average,
):
    me = lax.axis_index("mp")
    own = gate_up_weight.shape[1]
    ff = gate_up_weight.shape[3]
    feats = tokens.shape[1]
    if spreading:
        gain = jnp.zeros((8, feats), f32)
        gain = lax.dynamic_update_slice(
            gain, norm_gain.reshape(2 * LAYERS, own), (0, lax.axis_index("dp") * own)
        )
    else:
        gain = lax.all_gather(norm_gain, "dp", axis=2, tiled=True).reshape(2 * LAYERS, feats)
        gain = jnp.concatenate([gain, jnp.zeros((8 - 2 * LAYERS, feats), f32)], axis=0)
    if spreading:
        owned = (own_projection(qkv_weight, me), out_weight, gate_up_weight, down_weight)
    else:
        owned = (
            own_projection(qkv_weight, me),
            out_weight.astype(bf16),
            gate_up_weight.reshape(LAYERS, own, 2 * ff).astype(bf16),
            down_weight.astype(bf16),
        )
        owned = [lax.all_gather(w, "dp", axis=1, tiled=True) for w in owned]
    act, *kept = run_forward(spreading, tokens, owned, gain, lengths, key_mask[None, :])
    weights, gain, tables, kept = kept[-9:-5], kept[-5], kept[-4:], kept[:-9]
    backward = run_backward(spreading, cotangent, kept, weights, gain, tables)
    if spreading:
        input_grad, gq, go, gd, gg, gain_sum = backward
        gain_grad = lax.dynamic_slice_in_dim(
            gain_sum[:2 * LAYERS].reshape(LAYERS, 2, -1), lax.axis_index("dp") * own, own, 2
        )
        states = (
            qkv_weight, qkv_first, qkv_second, qkv_average,
            out_weight, out_first, out_second, out_average,
            gate_up_weight, gate_up_first, gate_up_second, gate_up_average,
            down_weight, down_first, down_second, down_average,
            norm_gain, gain_first, gain_second, gain_average,
        )
        grads = (gq, go, gg, gd, gain_grad)
        *results, act, input_grad = run_adam(states, grads, (act, input_grad))
        return (act, input_grad, *results)
    else:
        input_grad, gq, go, gd, gg, gain_sum = backward
        gq, go, gg, gd = [
            lax.psum_scatter(g, "dp", scatter_dimension=1, tiled=True) for g in (gq, go, gg, gd)
        ]
        gq, go = lax.all_gather(gq, "mp"), lax.all_gather(go, "mp")
        gain_part = gain_sum[:2 * LAYERS].reshape(LAYERS, 2, -1)
        gain_grad = lax.psum_scatter(
            lax.psum(gain_part, "mp"), "dp", scatter_dimension=2, tiled=True
        )
    qkv_grad = whole_projection(gq.astype(f32))
    out_grad = jnp.concatenate([go[0], go[1]], axis=-1).astype(f32)
    gate_up_grad = gg.reshape(LAYERS, own, 2, ff).astype(f32)
    down_grad = gd.astype(f32)
    results = [act, input_grad]
    results.extend(adamw(qkv_weight, qkv_first, qkv_second, qkv_average, qkv_grad, 0.03, 0.01))
    results.extend(adamw(out_weight, out_first, out_second, out_average, out_grad, 0.5, 0.01))
    results.extend(
        adamw(
            gate_up_weight, gate_up_first, gate_up_second, gate_up_average, gate_up_grad, 0.03, 0.01
        )
    )
    results.extend(
        adamw(down_weight, down_first, down_second, down_average, down_grad, 0.02, 0.01)
    )
    results.extend(adamw(norm_gain, gain_first, gain_second, gain_average, gain_grad, 0.6, 0.0))
    return tuple(results)


def solution(mesh):
    spreading = mesh.shape["dp"] == 2 * DEPTH
    return jax.shard_map(
        functools.partial(shards, spreading),
        mesh=mesh,
        in_specs=(
            P(("dp", "mp"), None),
            P(("dp", "mp"), None),
            P("dp", None),
            P("dp"),
            P(None, "dp", None),
            P(None, "dp", None),
            P(None, "dp", None),
            P(None, "dp", None),
            P(None, "dp", None),
            P(None, "dp", None),
            P(None, "dp", None),
            P(None, "dp", None),
            P(None, "dp", None, "mp"),
            P(None, "dp", None, "mp"),
            P(None, "dp", None, "mp"),
            P(None, "dp", None, "mp"),
            P(None, "dp", "mp"),
            P(None, "dp", "mp"),
            P(None, "dp", "mp"),
            P(None, "dp", "mp"),
            P(None, None, "dp"),
            P(None, None, "dp"),
            P(None, None, "dp"),
            P(None, None, "dp"),
        ),
        out_specs=(
            P(("dp", "mp"), None),
            P(("dp", "mp"), None),
            P(None, "dp", None),
            P(None, "dp", None),
            P(None, "dp", None),
            P(None, "dp", None),
            P(None, "dp", None),
            P(None, "dp", None),
            P(None, "dp", None),
            P(None, "dp", None),
            P(None, "dp", None),
            P(None, "dp", None),
            P(None, "dp", None, "mp"),
            P(None, "dp", None, "mp"),
            P(None, "dp", None, "mp"),
            P(None, "dp", None, "mp"),
            P(None, "dp", None, "mp"),
            P(None, "dp", "mp"),
            P(None, "dp", "mp"),
            P(None, "dp", "mp"),
            P(None, "dp", "mp"),
            P(None, "dp", "mp"),
            P(None, None, "dp"),
            P(None, None, "dp"),
            P(None, None, "dp"),
            P(None, None, "dp"),
            P(None, None, "dp"),
        ),
        check_vma=False,
    )
```

```python
import functools
import math

import jax
import jax.numpy as jnp
import numpy as np
from jax import lax
from jax.experimental import pallas as pl
from jax.experimental.pallas import tpu as pltpu
from jax.sharding import PartitionSpec as P

HEADS = 12
HEAD_DIM = 64
LAYERS = 2
STEP = 10
GROUP = 4
DEPTH = 4
LEAD = 1
PIECES = 4
OWN_HEADS = HEADS // GROUP
TILE = 2 * HEAD_DIM
PROJ = 5 * TILE

rotary_base = 1000.0
norm_epsilon = 1e-05
masked_score = -1e30
beta_first = 0.5
beta_second = 0.5
adam_epsilon = 1e-08
average_decay = 0.5
score_scale = HEAD_DIM ** (-0.5)
log2e = math.log2(math.e)

MESH = pl.DeviceIdType.MESH
ANY = pl.BlockSpec(memory_space=pl.ANY)
VMEM = pl.BlockSpec(memory_space=pltpu.VMEM)
f32 = jnp.float32
bf16 = jnp.bfloat16
VMEM_LIMIT = 127 * 2**19


def dot(a, b):
    return jnp.dot(a, b, preferred_element_type=f32)


def dot_nt(a, b):
    return lax.dot_general(a, b, (((1,), (1,)), ((), ())), preferred_element_type=f32)


def dot_tn(a, b):
    return lax.dot_general(a, b, (((0,), (0,)), ((), ())), preferred_element_type=f32)


def places():
    me = lax.axis_index("mp")
    core = lax.rem(me, 2)
    side = lax.div(me, 2)
    return me, me + 1 - 2 * core, me + 2 - 4 * side, 3 - me, core


def push(src, dst, sems, layer, number, who):
    return pltpu.make_async_remote_copy(
        src_ref=src,
        dst_ref=dst,
        send_sem=sems.at[0, layer, number],
        recv_sem=sems.at[1, layer, number],
        device_id={"mp": who},
        device_id_type=MESH,
    )


class Spread:
    def __init__(self, own):
        index = lax.axis_index("dp")
        self.own = own
        self.z, self.x = lax.div(index, 2), lax.rem(index, 2)

    def device(self, step):
        return 2 * lax.rem(self.z + step, DEPTH) + self.x

    def beside(self, step):
        return 2 * lax.rem(self.z + step, DEPTH) + 1 - self.x

    def rows(self, index):
        return pl.ds(pl.multiple_of(index * self.own, self.own), self.own)


def greet(mate, across, far=None, spread=None):
    barrier = pltpu.get_barrier_semaphore()
    packs = [mate, across] if far is None else [mate, across, far]
    for who in packs:
        pl.semaphore_signal(barrier, inc=1, device_id={"mp": who}, device_id_type=MESH)
    others = []
    if spread is not None:
        others = [spread.beside(0)] + [spread.device(step) for step in range(1, DEPTH)]
        for who in others:
            pl.semaphore_signal(barrier, inc=1, device_id={"dp": who}, device_id_type=MESH)
    pl.semaphore_wait(barrier, len(packs) + len(others))


def ship(src, dst, sems, piece, number, who):
    return pltpu.make_async_remote_copy(
        src_ref=src,
        dst_ref=dst,
        send_sem=sems.at[0, piece, number],
        recv_sem=sems.at[1, piece, number],
        device_id={"dp": who},
        device_id_type=MESH,
    )


class WeightGather:
    def __init__(self, source, target, layer, piece, sems, local, spread, cols=None):
        self.target, self.layer, self.cols = target, layer, cols
        self.piece, self.sems, self.spread = piece, sems, spread
        z, x = spread.z, spread.x
        own = self.own_part(source)
        place = self.view(z, x)
        self.local = pltpu.make_async_copy(own, place, local)
        self.beside = self.send(own, place, 0, 0, 2 * z + 1 - x)
        self.up = self.send(own, place, 1, 1 + z, 2 * jnp.minimum(z + 1, DEPTH - 1) + x)
        self.down = self.send(own, place, 2, 1 + z, 2 * jnp.maximum(z - 1, 0) + x)
        self.hops = [(far, way) for far in range(1, DEPTH) for way in (-1, 1)]
        self.todo = list(self.hops)

    def own_part(self, source):
        return source.at[self.layer]

    def view(self, z, x):
        return self.target.at[self.layer, self.spread.rows(2 * z + x)]

    def send(self, src, dst, out, into, who):
        return pltpu.make_async_remote_copy(
            src_ref=src,
            dst_ref=dst,
            send_sem=self.sems.at[0, self.piece, out],
            recv_sem=self.sems.at[1, self.piece, into],
            device_id={"dp": who},
            device_id_type=MESH,
        )

    def start(self):
        self.local.start()
        pl.when(self.spread.z < DEPTH - 1)(self.up.start)
        pl.when(self.spread.z > 0)(self.down.start)
        self.beside.start()

    def hop(self, far, way):
        z, x = self.spread.z, self.spread.x
        source = jnp.clip(z + way * far, 0, DEPTH - 1)
        block = self.view(source, x)
        onward = jnp.clip(z - way, 0, DEPTH - 1)
        arrive = self.send(block, block, 3 + source, 1 + source, 2 * source + x)
        over = self.send(block, block, 3 + source, 1 + DEPTH + source, 2 * z + 1 - x)
        along = self.send(block, block, 3 + DEPTH + source, 1 + source, 2 * onward + x)
        comes = z >= far if way < 0 else z + far < DEPTH
        goes = z > 0 if way > 0 else z < DEPTH - 1
        return arrive, over, along, comes, jnp.logical_and(comes, goes)

    def serve(self, count=2 * DEPTH):
        while self.todo and count:
            count -= 1
            arrive, over, along, comes, goes = self.hop(*self.todo.pop(0))

            pl.when(comes)(arrive.wait_recv)
            pl.when(goes)(along.start)
            pl.when(comes)(over.start)

    def wait(self):
        self.serve()
        self.local.wait()
        self.beside.wait_recv()
        z, x = self.spread.z, self.spread.x
        for step in range(1, DEPTH):
            source = lax.rem(z + step, DEPTH)
            block = self.view(source, 1 - x)
            self.send(block, block, 3, 1 + DEPTH + source, 2 * z + 1 - x).wait_recv()

    def finish(self):
        self.beside.wait_send()
        pl.when(self.spread.z < DEPTH - 1)(self.up.wait_send)
        pl.when(self.spread.z > 0)(self.down.wait_send)
        for far, way in self.hops:
            arrive, over, along, comes, goes = self.hop(far, way)
            pl.when(comes)(over.wait_send)
            pl.when(goes)(along.wait_send)


class QuarterGather(WeightGather):
    def __init__(self, source, target, layer, piece, sems, local, spread, half, pack_sems, where):
        me, mate, across, far, core = where
        self.side, self.rows = lax.div(me, 2), spread.own // 2
        cols = pl.ds(pl.multiple_of(core * half, half), half)
        super().__init__(source, target, layer, piece, sems, local, spread, cols)
        here = spread.rows(2 * spread.z + spread.x)
        self.local = pltpu.make_async_copy(source.at[layer], target.at[layer, here], local)
        self.over, self.swap = [], []
        for step in range(DEPTH):
            z = lax.rem(spread.z + step, DEPTH)
            for number, x in enumerate((spread.x, 1 - spread.x)):
                if step or number:
                    spot = 2 * step + number - 1
                    block = self.view(z, x)
                    self.over.append(push(block, block, pack_sems, layer, spot, across))
                    block = target.at[layer, spread.rows(2 * z + x), cols]
                    self.swap.append(push(block, block, pack_sems, layer, 7 + spot, mate))

    def part_rows(self, start):
        return pl.ds(pl.multiple_of(start + self.side * self.rows, self.rows), self.rows)

    def own_part(self, source):
        return source.at[self.layer, self.part_rows(0), self.cols]

    def view(self, z, x):
        rows = self.part_rows((2 * z + x) * self.spread.own)
        return self.target.at[self.layer, rows, self.cols]

    def share_across(self):
        super().wait()
        for copy in self.over:
            copy.start()

    def share(self):
        for copy, onward in zip(self.over, self.swap):
            copy.wait_recv()
            onward.start()

    def wait(self):
        for copy in self.swap:
            copy.wait_recv()

    def finish(self):
        super().finish()
        for copy in self.over + self.swap:
            copy.wait_send()


class WeightSum:
    def __init__(self, grad, near, apart, piece, sems, spread, credits, again, more, total, part):
        self.grad, self.near, self.apart, self.spread = grad, near, apart, spread
        self.near_credit, self.apart_credit = credits
        self.again, self.more = again, more
        self.sum, self.part = total, part
        self.beside = [
            ship(grad.at[self.rows(spread.beside(step))], near.at[step], sems, piece, step,
                 spread.beside(0))
            for step in range(DEPTH)
        ]
        self.along = [
            ship(grad.at[self.rows(spread.device(step))], apart.at[step - 1], sems, piece,
                 DEPTH - 1 + step, spread.device(step))
            for step in range(1, DEPTH)
        ]

    def rows(self, index):
        if self.part is None:
            return self.spread.rows(index)
        half = self.spread.own // 2
        return pl.ds(pl.multiple_of(index * self.spread.own + self.part * half, half), half)

    def start(self):
        if self.again:
            pl.semaphore_wait(self.near_credit, 1)
        for copy in self.beside[1:] + self.beside[:1]:
            copy.start()

    def credit(self, sem, who):
        pl.semaphore_signal(sem, inc=1, device_id={"dp": who}, device_id_type=MESH)

    def add(self):
        if self.again:
            pl.semaphore_wait(self.apart_credit, DEPTH - 1)
        for step in range(1, DEPTH):
            self.beside[step].wait_recv()
            rows = self.rows(self.spread.device(step))
            self.grad[rows, :] = (
                self.grad[rows, :].astype(f32) + self.near[step].astype(f32)
            ).astype(bf16)
            self.along[step - 1].start()
        self.beside[0].wait_recv()
        rows = self.rows(self.spread.device(0))
        self.sum[...] = self.grad[rows, :].astype(f32) + self.near[0].astype(f32)
        if self.more:
            self.credit(self.near_credit, self.spread.beside(0))

    def total(self):
        for copy in self.along:
            copy.wait_recv()
        result = self.sum[...]
        for step in range(DEPTH - 1):
            result = result + self.apart[step].astype(f32)
        if self.more:
            for step in range(1, DEPTH):
                self.credit(self.apart_credit, self.spread.device(step))
        return result

    def finish(self):
        for copy in self.beside + self.along:
            copy.wait_send()


def rows_of(block, size, extent):
    return pl.ds(pl.multiple_of(block * size, size), extent)


def lane_iota(shape):
    return lax.broadcasted_iota(jnp.int32, shape, len(shape) - 1)


def half_masks():
    low = (lane_iota((1, TILE)) < HEAD_DIM).astype(f32)
    return low.astype(bf16), (1.0 - low).astype(bf16)


def turn(tile, cos_rows, sin_rows):
    lane = lane_iota(tile.shape) % HEAD_DIM
    half = HEAD_DIM // 2
    partner = jnp.where(
        lane < half, pltpu.roll(tile, TILE - half, 1), pltpu.roll(tile, half, 1)
    )
    return tile * cos_rows + partner * sin_rows


def write_bias(bias, doc_keys, doc_queries):
    seq = bias.shape[0]
    step = 128

    def body(i, carry):
        rows = rows_of(i, step, step)
        keys = doc_keys[rows, :][:, :1]
        same = keys == doc_queries[:1, :]
        spot = lax.broadcasted_iota(jnp.int32, (step, seq), 0) + i * step
        own = spot == lax.broadcasted_iota(jnp.int32, (step, seq), 1)
        bias[rows, :] = jnp.where(jnp.logical_or(same, own), 0.0, masked_score)
        return carry

    lax.fori_loop(0, seq // step, body, 0)


def write_tables(lengths, mask_row, freq, cos_rows, sin_rows, doc_keys, doc_queries):
    ends = []
    for doc in range(lengths.shape[1]):
        ends.append(lengths[0, doc] + (ends[-1] if ends else 0))

    def document(spots):
        number = jnp.zeros(spots.shape, jnp.int32)
        for end in ends:
            number = number + (spots >= end).astype(jnp.int32)
        return number

    seq = cos_rows.shape[0]
    doc_queries[...] = document(lane_iota(doc_queries.shape))
    step = 128

    def body(i, carry):
        rows = rows_of(i, step, step)
        spots = lax.broadcasted_iota(jnp.int32, (step, 128), 0) + i * step
        start = jnp.zeros(spots.shape, jnp.int32)
        for end in ends:
            start = jnp.maximum(start, jnp.where(spots >= end, end, 0))
        seen = jnp.broadcast_to(mask_row[:, rows].astype(f32), (step, step)).T
        doc_keys[rows, :] = jnp.where(seen > 0.5, document(spots), -1)
        angle = (spots - start).astype(f32) * freq[:1, :]
        sine = jnp.sin(angle)
        cos_rows[rows, :] = jnp.cos(angle)
        lower = lane_iota(spots.shape) % HEAD_DIM < HEAD_DIM // 2
        sin_rows[rows, :] = jnp.where(lower, -sine, sine)
        return carry

    lax.fori_loop(0, seq // step, body, 0)


class Gather:
    def __init__(self, ref, slot, layer, sems, first_sem, size, where):
        me, mate, across, far, core = where
        self.across, self.mate = [], []
        self.forward = []
        half = size // 2

        def piece(block, part):
            start = pl.multiple_of(block * size + part * half, half)
            return ref.at[slot, pl.ds(start, half)]

        for part in range(2):
            own = piece(me, part)
            theirs = piece(across, part)
            self.across.append(push(own, own, sems, layer, first_sem + part, across))
            self.mate.append(push(own, own, sems, layer, first_sem + 2 + part, mate))
            self.forward.append(push(theirs, theirs, sems, layer, first_sem + 4 + part, mate))

    def start(self):
        for copy in self.across + self.mate:
            copy.start()

    def wait_mate(self):
        for copy in self.mate:
            copy.wait_recv()

    def wait_across(self):
        for copy, onward in zip(self.across, self.forward):
            copy.wait_recv()
            onward.start()

    def wait_far(self):
        for copy in self.forward:
            copy.wait_recv()

    def finish(self):
        for copy in self.across + self.mate + self.forward:
            copy.wait_send()


class Share:
    def __init__(self, ref, layer, sems, first_sem, where):
        me, mate, across, far, core = where
        own, theirs = ref.at[layer, me], ref.at[layer, across]
        self.ref, self.layer, self.me = ref, layer, me
        self.over = push(own, own, sems, layer, first_sem, across)
        self.near = push(own, own, sems, layer, first_sem + 1, mate)
        self.onward = push(theirs, theirs, sems, layer, first_sem + 2, mate)

    def start(self, block):
        self.ref[self.layer, self.me] = block
        self.over.start()
        self.near.start()

    def serve(self):
        self.over.wait_recv()
        self.onward.start()

    def finish(self):
        self.near.wait_recv()
        self.onward.wait_recv()
        for copy in (self.over, self.near, self.onward):
            copy.wait_send()


class Scatter:
    def __init__(self, part, slot, got, layer, sems, first_sem, where):
        me, mate, across, far, core = where
        self.part, self.slot, self.got = part, slot, got
        self.far = push(part.at[slot, 0], got.at[slot, 0], sems, layer, first_sem, mate)
        self.over = push(part.at[slot, 1], got.at[slot, 1], sems, layer, first_sem + 1, across)
        self.near = push(part.at[slot, 2], got.at[slot, 2], sems, layer, first_sem + 2, mate)

    def send_far(self, block):
        self.part[self.slot, 0] = block.astype(bf16)
        self.far.start()

    def send_across(self, block):
        self.far.wait_recv()
        self.part[self.slot, 1] = (block + self.got[self.slot, 0].astype(f32)).astype(bf16)
        self.over.start()

    def send_mate(self, block):
        self.part[self.slot, 2] = block.astype(bf16)
        self.near.start()

    def total(self, block):
        self.near.wait_recv()
        self.over.wait_recv()
        return (
            block
            + self.got[self.slot, 1].astype(f32)
            + self.got[self.slot, 2].astype(f32)
        )

    def finish(self):
        for copy in (self.far, self.over, self.near):
            copy.wait_send()


def normed_rows(rows):
    centered = rows - jnp.mean(rows, axis=-1, keepdims=True)
    inverse = lax.rsqrt(jnp.mean(centered * centered, axis=-1, keepdims=True) + norm_epsilon)
    return centered * inverse, inverse


def forward_kernel(
    spreading, tok, wq_in, wo_in, wg_in, wd_in, gain_in, lengths, mask_row, freq,
    act_out, xf_out, qkv_out, lse_out, att_out, flow_out, gu_out, hid_out,
    n1_out, s1_out, n2_out, s2_out, wq_out, wo_out, wg_out, wd_out, gain,
    cos_rows, sin_rows, doc_keys, doc_queries,
    wq, wo, wg, wd, xf, qkv, att, flow, gu, hid, bias, vt, k2, lse,
    n1, s1, n2, s2, first, act, part, got, sems, wsems, osems, dsems, ssems, gside, gdeep, gsems, *own_low,
):
    where = places()
    me, mate, across, far, core = where
    weight_outs = (wq_out, wo_out, wg_out, wd_out)
    size = tok.shape[0]
    seq = size * GROUP
    ff = hid.shape[2]
    spread = Spread(wq_in.shape[1]) if spreading else None
    weights = []
    cast = ()
    if spreading:
        cast = ((wo_in, own_low[0]), (wg_in, own_low[1]), (wd_in, own_low[2]))
        wo_in, wg_in, wd_in = own_low
    parts = (
        (wq_in, wq, None), (wo_in, wo, None), (wg_in, wg, None), (wd_in, wd, None),
    )
    for layer in range(LAYERS):
        for number, (source, target, cols) in enumerate(parts):
            local = wsems.at[layer, number]
            piece = PIECES * layer + number
            if not spreading:
                if cols is not None:
                    source, target = source.at[:, :, cols], target.at[:, :, cols]
                weights.append(pltpu.make_async_copy(source.at[layer], target.at[layer], local))
            elif number == 1:
                weights.append(
                    QuarterGather(source, target, layer, piece, dsems, local, spread,
                                  wo.shape[2] // 2, ssems, where)
                )
            else:
                weights.append(
                    WeightGather(source, target, layer, piece, dsems, local, spread, cols)
                )
    xf[0, rows_of(me, size, size), :] = tok[...]
    greet(mate, across, None, spread)
    gains = []
    if spreading:
        gdeep[spread.z] = gain_in[...]
        own = gdeep.at[spread.z]
        for step in range(1, DEPTH):
            gains.append(ship(own, own, gsems, 0, step, spread.device(step)))
            gains[-1].start()
    else:
        gain[...] = gain_in[...]
    ahead = LEAD if spreading else len(weights)
    for item in weights[:ahead]:
        item.start()

    def gain_stage(stage):
        if not spreading:
            return
        if stage == 0:
            for copy in gains:
                copy.wait_recv()
            gside[spread.x] = gdeep[0] + gdeep[1] + gdeep[2] + gdeep[3]
            own = gside.at[spread.x]
            gains.append(ship(own, own, gsems, 0, 0, spread.beside(0)))
            gains[-1].start()
        else:
            gains[-1].wait_recv()
            gain[...] = gside[0] + gside[1]
            for copy in gains:
                copy.wait_send()

    queue = [(k, hop) for k in range(len(weights)) for hop in range(6)] if spreading else []

    def pump(count):
        for number in range(min(count, len(queue))):
            k, hop = queue.pop(0)
            if hop == 0 and k + ahead < len(weights):
                weights[k + ahead].start()
            weights[k].serve(1)

    pending = []
    stores = []

    def store(number, layer, source, target):
        copy = pltpu.make_async_copy(source.at[layer], target.at[layer], osems.at[layer, number])
        copy.start()
        stores.append(copy)

    row_gather = Gather(xf, 0, 0, sems, 0, size, where)
    row_gather.start()
    for source, target in cast:
        if len(source.shape) == 3:
            target[...] = source[...].astype(bf16)
        else:
            for layer in range(LAYERS):
                for half in range(2):
                    target[layer, :, half * ff:(half + 1) * ff] = source[layer, :, half, :].astype(bf16)
    write_tables(lengths, mask_row, freq, cos_rows, sin_rows, doc_keys, doc_queries)
    write_bias(bias, doc_keys, doc_queries)
    low_mask, high_mask = half_masks()

    for layer in range(LAYERS):
        if layer == 0:
            pump(12)
        weights[PIECES * layer].wait()

        def project(block, layer=layer):
            rows = rows_of(block, size, size)
            proj = dot(xf[layer, rows, :], wq[layer])
            c, s = cos_rows[rows, :], sin_rows[rows, :]
            for tile in (0, 1, 3):
                piece = proj[:, tile * TILE:(tile + 1) * TILE]
                qkv[layer, rows, tile * TILE:(tile + 1) * TILE] = turn(piece, c, s).astype(bf16)
            for tile in (2, 4):
                piece = proj[:, tile * TILE:(tile + 1) * TILE]
                qkv[layer, rows, tile * TILE:(tile + 1) * TILE] = piece.astype(bf16)

        project(me)
        row_gather.wait_mate()
        project(mate)
        row_gather.wait_across()
        pump(2)
        project(across)
        row_gather.wait_far()
        project(far)
        if layer == 0:
            gain_stage(0)
        pending.append(row_gather)
        store(0, layer, xf, xf_out)
        store(1, layer, qkv, qkv_out)
        vt[0] = qkv[layer, :, 2 * TILE:3 * TILE].T
        vt[1] = qkv[layer, :, 4 * TILE:5 * TILE].T
        k2[...] = pltpu.roll(qkv[layer, :, 3 * TILE:4 * TILE].astype(f32), HEAD_DIM, 1).astype(bf16)

        sends = []
        forwards = []
        for head in range(OWN_HEADS):
            query_tile = (0, 0, 3)[head]
            mask = (low_mask, high_mask, low_mask)[head]

            def attend(i, carry, layer=layer, head=head, query_tile=query_tile, mask=mask):
                rows = rows_of(i, size, size)
                queries = qkv[layer, rows, query_tile * TILE:(query_tile + 1) * TILE] * mask
                keys = k2[...] if head == 2 else qkv[layer, :, TILE:2 * TILE]
                values = (vt.at[0, :HEAD_DIM], vt.at[0, HEAD_DIM:], vt.at[1, HEAD_DIM:])[head][...]
                scores = dot_nt(keys, queries) * (score_scale * log2e) + bias[:, rows]
                top = jnp.max(scores, axis=0, keepdims=True)
                probs = jnp.exp2(scores - top)
                total = jnp.sum(probs, axis=0, keepdims=True)
                result = dot(values, probs.astype(bf16)) / total
                spot = pl.ds(
                    pl.multiple_of(me * (OWN_HEADS * HEAD_DIM) + head * HEAD_DIM, HEAD_DIM), HEAD_DIM
                )
                att[layer, spot, rows] = result.astype(bf16)
                lse[layer, head:head + 1, rows] = top + jnp.log(total) * log2e
                return carry

            lax.fori_loop(0, seq // size, attend, 0)

            def features(block, head=head, layer=layer):
                start = block * (OWN_HEADS * HEAD_DIM) + head * HEAD_DIM
                return att.at[layer, pl.ds(pl.multiple_of(start, HEAD_DIM), HEAD_DIM)]

            own, theirs = features(me), features(across)
            to_across = push(own, own, sems, layer, 6 + head, across)
            to_mate = push(own, own, sems, layer, 9 + head, mate)
            onward = push(theirs, theirs, sems, layer, 12 + head, mate)
            to_across.start()
            to_mate.start()
            if head:
                sends[-2].wait_recv()
                forwards[-1].start()
            if spreading and head == 0:
                weights[PIECES * layer + 1].share_across()
            if spreading and head == 2:
                weights[PIECES * layer + 1].share()
            pump(2)
            sends += [to_across, to_mate]
            forwards.append(onward)
        sends[-2].wait_recv()
        forwards[-1].start()
        for head in range(OWN_HEADS):
            sends[2 * head + 1].wait_recv()
            forwards[head].wait_recv()
        store(2, layer, lse, lse_out)
        store(3, layer, att, att_out)
        if layer == 0:
            gain_stage(1)
        pump(2)
        for number in (1, 2):
            weights[PIECES * layer + number].wait()

        def feed(block, keep, layer=layer):
            rows = rows_of(block, size, size)
            branch = dot_tn(att[layer, :, rows], wo[layer])
            normed, inverse = normed_rows(xf[layer, rows, :].astype(f32) + branch)
            first_rows = normed * gain[2 * layer:2 * layer + 1, :]
            if keep:
                n1[layer] = normed
                s1[layer] = jnp.broadcast_to(inverse, s1.shape[1:])
                first[...] = first_rows
            first_low = first_rows.astype(bf16)
            flow[layer, rows, :] = first_low
            gate_up = dot(first_low, wg[layer])
            gate, upward = gate_up[:, :ff], gate_up[:, ff:]
            gu[layer, rows, :] = gate_up.astype(bf16)
            hid[layer, rows, :] = (gate / (1.0 + jnp.exp(-gate)) * upward).astype(bf16)

        def down(block, layer=layer):
            return dot_nt(hid[layer, rows_of(block, size, size), :], wd[layer])

        for number, block in enumerate((far, across, mate, me)):
            feed(block, number == 3)
            pump(2)
        weights[PIECES * layer + 3].wait()
        for number, held in enumerate((wq, wo, wg, wd)):
            store(12 + number, layer, held, weight_outs[number])
        scatter = Scatter(part, layer, got, layer, sems, 15, where)
        scatter.send_far(down(far))
        scatter.send_across(down(across))
        scatter.send_mate(down(mate))
        own_part = down(me)
        pump(2)
        store(4, layer, flow, flow_out)
        store(5, layer, gu, gu_out)
        store(6, layer, hid, hid_out)
        store(7, layer, n1, n1_out)
        store(8, layer, s1, s1_out)
        pump(4)
        ffn = scatter.total(own_part)
        pending.append(scatter)
        normed, inverse = normed_rows(first[...] + ffn)
        n2[layer] = normed
        s2[layer] = jnp.broadcast_to(inverse, s2.shape[1:])
        result = (normed * gain[2 * layer + 1:2 * layer + 2, :]).astype(bf16)
        store(9, layer, n2, n2_out)
        store(10, layer, s2, s2_out)
        if layer + 1 < LAYERS:
            xf[layer + 1, rows_of(me, size, size), :] = result
            row_gather = Gather(xf, layer + 1, layer + 1, sems, 0, size, where)
            row_gather.start()
            pump(2)
        else:
            act[...] = result
            copy = pltpu.make_async_copy(act, act_out, osems.at[0, 11])
            copy.start()
            stores.append(copy)
        for copy in sends + forwards:
            copy.wait_send()
    if spreading:
        pending += weights
    for item in pending:
        item.finish()
    for copy in stores:
        copy.wait()


BACK_LOADED = (
    "n1", "s1", "n2", "s2", "xf", "qkv", "lse", "att", "flow", "gu", "hid", "wq", "wo", "wg", "wd",
)
BACK_TABLES = ("gain", "cos_rows", "sin_rows", "doc_keys", "doc_queries")
BACK_SCRATCH = (
    "bias", "dff", "dbr", "datt", "dproj", "dk", "dv", "dqt", "kt", "k2", "grad", "part", "got",
    "gq", "go", "gg", "gd", "sems", "lsems", "osems",
)

def backward_kernel(spreading, names, *refs):
    r = dict(zip(names, refs))
    cot = r["cot"]
    gain, cos_rows, sin_rows, doc_keys, doc_queries = (r[n] for n in BACK_TABLES)
    (
        bias, dff, dbr, datt, dproj, dk, dv, dqt, kt, k2, grad, part, got,
        gq, go, gg, gd, sems, lsems, osems,
    ) = (r[n] for n in BACK_SCRATCH)
    n1, s1, n2, s2, qkv, lse, att, gu, hid, wq, wo, wg, wd = (
        r[n] for n in BACK_LOADED if n not in ("xf", "flow")
    )
    xf = flow = r["rows"]
    where = places()
    me, mate, across, far, core = where
    size = cot.shape[0]
    seq = size * GROUP
    ff = hid.shape[1]
    feats = xf.shape[1]
    own_feats = OWN_HEADS * HEAD_DIM
    held = {n: (r[n + "_in"], r.get(n, r["rows"])) for n in BACK_LOADED}
    order = list(held)
    loads = {}

    def load(name, layer):
        if layer < 0:
            return
        source, target = held[name]
        copy = pltpu.make_async_copy(source.at[layer], target, lsems.at[order.index(name)])
        copy.start()
        loads[name] = copy

    for name in ("n2", "s2", "wd", "gu", "wg", "hid", "n1", "s1", "flow", "wo", "qkv", "lse", "att", "wq"):
        load(name, LAYERS - 1)
    spread = Spread(feats // (2 * DEPTH)) if spreading else None
    greet(mate, across, far if spreading else None, spread)
    low_mask, high_mask = half_masks()
    grad[...] = cot[...]
    pending = []
    scatters = []
    stores = {}
    sums = {}
    shares = []
    pieces = dict(
        d=gd.at[:, :], g=gg.at[:, :ff], u=gg.at[:, ff:],
        a=gq.at[:, :3 * TILE], b=gq.at[:, 3 * TILE:], o=go.at[:, :],
    )
    gsum = r["gsum"] if spreading else r["gain_out"]
    gsum[...] = jnp.zeros_like(gsum)

    def begin(name, layer):
        if not spreading:
            if name not in "ga":
                number = "boud".index(name)
                store(number, layer, (gq, go, gg, gd)[number], r["qogd"[number] + "_out"])
            return
        index = "dguabo".index(name)
        item = WeightSum(
            pieces[name], r["near_" + name], r["apart_" + name], 6 * layer + index, r["dsems"],
            spread, (r["csems"].at[0, index], r["csems"].at[1, index]),
            layer < LAYERS - 1, layer > 0, r["sum_" + name],
            lax.div(me, 2) if name == "o" else None,
        )
        item.start()
        sums[name, layer] = item

    def add(name, layer):
        if spreading and (name, layer) in sums:
            sums[name, layer].add()

    def total(name, layer):
        if not spreading or (name, layer) not in sums:
            return
        result = sums[name, layer].total()
        if name in "abo":
            share = Share(r[name + "share"], layer, sems, 15 + 3 * "abo".index(name), where)
            share.start(result.astype(bf16))
            shares.append(share)
        elif name == "d":
            r["d_res"][layer] = result
        else:
            half = "gu".index(name)
            r["g_res"][layer, :, half * ff:(half + 1) * ff] = result

    def ready(name, layer):
        if not spreading:
            if name not in "ub":
                stored("aogd".index(name))
        elif (name, layer + 1) in sums:
            sums[name, layer + 1].finish()

    gains = []

    def gain_stage(stage):
        if not spreading:
            return
        gpack, gside, gdeep, gsems = (r[n] for n in ("gpack", "gside", "gdeep", "gsems"))
        if stage == 0:
            gpack[me] = gsum[...]
            for number, who in enumerate((mate, across, far)):
                gains.append(push(gpack.at[me], gpack.at[me], gsems, 0, number, who))
        elif stage == 1:
            for copy in gains[:3]:
                copy.wait_recv()
            gside[spread.x] = gpack[0] + gpack[1] + gpack[2] + gpack[3]
            own = gside.at[spread.x]
            gains.append(ship(own, own, gsems, 0, 3, spread.beside(0)))
        elif stage == 2:
            gains[3].wait_recv()
            gdeep[spread.z] = gside[0] + gside[1]
            own = gdeep.at[spread.z]
            for step in range(1, DEPTH):
                gains.append(ship(own, own, gsems, 0, 3 + step, spread.device(step)))
        else:
            for copy in gains[4:]:
                copy.wait_recv()
            r["gain_out"][...] = gdeep[0] + gdeep[1] + gdeep[2] + gdeep[3]
            for copy in gains:
                copy.wait_send()
            return
        for copy in gains[(0, 3, 4)[stage]:]:
            copy.start()

    def store(number, layer, source, target):
        copy = pltpu.make_async_copy(source, target.at[layer], osems.at[layer, number])
        copy.start()
        stores[number] = copy

    def stored(number):
        if number in stores:
            stores.pop(number).wait()

    for layer in range(LAYERS - 1, -1, -1):

        def norm_back(grad_rows, normed, inverse, row, layer=layer):
            gsum[2 * layer + row:2 * layer + row + 1, :] = jnp.sum(
                grad_rows * normed, axis=0, keepdims=True
            )
            scaled = grad_rows * gain[2 * layer + row:2 * layer + row + 1, :]
            return (
                scaled
                - jnp.mean(scaled, axis=-1, keepdims=True)
                - normed * jnp.mean(scaled * normed, axis=-1, keepdims=True)
            ) * inverse

        loads["n2"].wait()
        loads["s2"].wait()
        dz = norm_back(grad[...], n2[...], s2[:, :1], 1)
        load("n2", layer - 1)
        load("s2", layer - 1)
        grad[...] = dz
        dff[0, rows_of(me, size, size), :] = dz.astype(bf16)
        gather = Gather(dff, 0, layer, sems, 0, size, where)
        gather.start()
        if layer == LAYERS - 1:
            write_bias(bias, doc_keys, doc_queries)
        for name in ("wd", "gu", "wg"):
            loads[name].wait()
        add("o", layer + 1)

        def feed_back(block):
            rows = rows_of(block, size, size)
            grad_hidden = dot(dff[0, rows, :], wd[...])
            gate = gu[rows, :ff].astype(f32)
            upward = gu[rows, ff:].astype(f32)
            sigma = 1.0 / (1.0 + jnp.exp(-gate))
            up_grad = grad_hidden * gate * sigma
            gate_grad = grad_hidden * upward * sigma * (1.0 + gate * (1.0 - sigma))
            gu[rows, :ff] = gate_grad.astype(bf16)
            gu[rows, ff:] = up_grad.astype(bf16)
            return dot_nt(gu[rows, :], wg[...])

        if len(scatters) > 1:
            scatters[-2].finish()
        scatter = Scatter(part, 0, got, 2 * layer, sems, 6, where)
        scatters.append(scatter)
        own_part = feed_back(me)
        gather.wait_mate()
        scatter.send_mate(feed_back(mate))
        gather.wait_across()
        loads["hid"].wait()
        add("a", layer + 1)
        gather.wait_far()
        ready("d", layer)

        def down_weight(i, carry):
            cols = rows_of(i, 256, 256)
            gd[cols, :] = dot_tn(dff[0, :, cols], hid[...]).astype(bf16)
            return carry

        lax.fori_loop(0, feats // 256, down_weight, 0)
        begin("d", layer)
        scatter.send_far(feed_back(far))
        scatter.send_across(feed_back(across))
        gather.finish()
        load("hid", layer - 1)
        load("wd", layer - 1)
        load("wg", layer - 1)
        add("b", layer + 1)
        loads["flow"].wait()
        for name, first_col in (("g", 0), ("u", ff)):
            ready(name, layer)

            def gate_up_weight(i, carry, first_col=first_col):
                cols = rows_of(i, 256, 256)
                gg[cols, first_col:first_col + ff] = dot_tn(
                    flow[:, cols], gu[:, first_col:first_col + ff]
                ).astype(bf16)
                return carry

            lax.fori_loop(0, feats // 256, gate_up_weight, 0)
            begin(name, layer)
        load("gu", layer - 1)
        load("xf", layer)
        for name in "dgu":
            total(name, layer + 1)

        if layer == 0:
            add("d", layer)
        dfirst = grad[...] + scatter.total(own_part)
        loads["n1"].wait()
        loads["s1"].wait()
        dr = norm_back(dfirst, n1[...], s1[:, :1], 0)
        load("n1", layer - 1)
        load("s1", layer - 1)
        grad[...] = dr
        dbr[layer, rows_of(me, size, size), :] = dr.astype(bf16)
        gather = Gather(dbr, layer, layer, sems, 9, size, where)
        gather.start()
        if layer == 0:
            gain_stage(0)
        for name in ("wo", "qkv", "lse"):
            loads[name].wait()

        def att_back(block, layer=layer):
            rows = rows_of(block, size, size)
            for tile, start in enumerate((0, HEAD_DIM)):
                spot = pl.ds(pl.multiple_of(me * own_feats + start, HEAD_DIM), TILE)
                datt[rows, tile * TILE:(tile + 1) * TILE] = dot_nt(
                    dbr[layer, rows, :], wo[spot, :]
                ).astype(bf16)

        kt[0] = qkv[:, TILE:2 * TILE].T
        kt[1] = qkv[:, 3 * TILE:4 * TILE].T
        k2[...] = pltpu.roll(qkv[:, 3 * TILE:4 * TILE].astype(f32), HEAD_DIM, 1).astype(bf16)
        dk[...] = jnp.zeros_like(dk)
        dv[...] = jnp.zeros_like(dv)

        def attend(head, first, second):
            tile = head // 2
            query_tile = (0, 0, 3)[head]
            value_tile = (2, 2, 4)[head]
            query_mask = (low_mask, high_mask, low_mask)[head]
            value_mask = (low_mask, high_mask, high_mask)[head]

            def body(i, carry):
                rows = rows_of(first + i * (second - first), size, size)
                queries = qkv[rows, query_tile * TILE:(query_tile + 1) * TILE] * query_mask
                keys = k2[...] if head == 2 else qkv[:, TILE:2 * TILE]
                scores = dot_nt(keys, queries) * (score_scale * log2e) + bias[:, rows]
                probs = jnp.exp2(scores - lse[head:head + 1, rows])
                outs = datt[rows, tile * TILE:(tile + 1) * TILE] * value_mask
                grad_probs = dot_nt(qkv[:, value_tile * TILE:(value_tile + 1) * TILE], outs)
                delta = jnp.sum(probs * grad_probs, axis=0, keepdims=True)
                grad_scores = (probs * (grad_probs - delta)).astype(bf16)
                dv[tile] = dv[tile] + dot(probs.astype(bf16), outs)
                dk[tile] = dk[tile] + dot(grad_scores, queries)
                keys_t = (kt.at[0, :HEAD_DIM], kt.at[0, HEAD_DIM:], kt.at[1, HEAD_DIM:])[head][...]
                spot = (0, HEAD_DIM, 0)[head]
                dqt[tile, spot:spot + HEAD_DIM, rows] = dot(keys_t, grad_scores)
                return carry

            lax.fori_loop(0, 2, body, 0)

        att_back(me)
        gather.wait_mate()
        att_back(mate)
        for head in range(OWN_HEADS):
            attend(head, me, mate)
        gather.wait_across()
        att_back(across)
        if layer == 0:
            gain_stage(1)
            add("g", layer)
        else:
            add("d", layer)
        gather.wait_far()
        att_back(far)
        pending.append(gather)
        load("wo", layer - 1)
        loads["att"].wait()
        ready("o", layer)

        def out_weight(i, carry, layer=layer):
            rows = rows_of(i, 256, 256)
            half = feats // 2
            cols = pl.ds(pl.multiple_of(core * half, half), half)
            go[rows, :] = dot(att[rows, :], dbr[layer, :, cols]).astype(bf16)
            return carry

        lax.fori_loop(0, feats // 256, out_weight, 0)
        begin("o", layer)
        load("att", layer - 1)
        for name in "oab":
            total(name, layer + 1)
        attend(0, across, far)
        attend(1, across, far)
        for share in shares:
            share.serve()

        def unrotate_pairs(i, carry):
            rows = rows_of(i, size, size)
            c, s = cos_rows[rows, :], -sin_rows[rows, :]
            dproj[rows, :TILE] = turn(dqt[0, :, rows].T * score_scale, c, s).astype(bf16)
            dproj[rows, TILE:2 * TILE] = turn(dk[0, rows, :] * score_scale, c, s).astype(bf16)
            dproj[rows, 2 * TILE:3 * TILE] = dv[0, rows, :].astype(bf16)
            return carry

        def unrotate_last(i, carry):
            rows = rows_of(i, size, size)
            c, s = cos_rows[rows, :], -sin_rows[rows, :]
            lower = lane_iota((size, TILE)) < HEAD_DIM
            mixed = jnp.where(lower, dqt[1, :, rows].T, pltpu.roll(dk[1, rows, :], HEAD_DIM, 1))
            dproj[rows, 3 * TILE:4 * TILE] = turn(mixed * score_scale, c, s).astype(bf16)
            dproj[rows, 4 * TILE:] = dv[1, rows, :].astype(bf16)
            return carry

        def weigh_projection(first, last):
            def qkv_weight(i, carry):
                cols = rows_of(i, 256, 256)
                gq[cols, first:last] = dot_tn(xf[:, cols], dproj[:, first:last]).astype(bf16)
                return carry

            lax.fori_loop(0, feats // 256, qkv_weight, 0)

        lax.fori_loop(0, seq // size, unrotate_pairs, 0)
        loads["xf"].wait()
        ready("a", layer)
        weigh_projection(0, 3 * TILE)
        begin("a", layer)
        if layer:
            add("g", layer)
        else:
            gain_stage(2)
            add("u", layer)
        attend(2, across, far)
        lax.fori_loop(0, seq // size, unrotate_last, 0)
        load("qkv", layer - 1)
        load("lse", layer - 1)
        loads["wq"].wait()

        def input_part(block):
            return dot_nt(dproj[rows_of(block, size, size), :], wq[...])

        if len(scatters) > 1:
            scatters[-2].finish()
        scatter = Scatter(part, 1, got, 2 * layer + 1, sems, 6, where)
        scatters.append(scatter)
        if layer == 0:
            ready("b", layer)
            weigh_projection(3 * TILE, PROJ)
            begin("b", layer)
        scatter.send_far(input_part(far))
        scatter.send_across(input_part(across))
        scatter.send_mate(input_part(mate))
        own_part = input_part(me)
        load("wq", layer - 1)
        if layer:
            ready("b", layer)
            weigh_projection(3 * TILE, PROJ)
            begin("b", layer)
            add("u", layer)
        else:
            gain_stage(3)
            add("o", layer)
            add("a", layer)
            for name in "dg":
                total(name, 0)
            add("b", layer)
        load("flow", layer - 1)
        grad[...] = grad[...] + scatter.total(own_part)
    input_copy = pltpu.make_async_copy(grad, r["ig_out"], osems.at[0, 4])
    input_copy.start()
    for name in "uoab":
        total(name, 0)
    if spreading:
        for share in shares[-3:]:
            share.serve()
    input_copy.wait()
    for item in pending + scatters[-2:]:
        item.finish()
    for number in range(4):
        stored(number)
    for item in shares:
        item.finish()
    if spreading:
        for name in "dguabo":
            sums[name, 0].finish()
        q_out = r["q_out"]
        ends = (
            (r["ashare"], q_out.at[:, :, :, pl.ds(0, 3 * TILE)]),
            (r["bshare"], q_out.at[:, :, :, pl.ds(3 * TILE, 2 * TILE)]),
            (r["oshare"], r["o_out"]),
        )
        last = []
        for number, held in enumerate(ends):
            last.append(pltpu.make_async_copy(*held, osems.at[1, number]))
            last[-1].start()
        for copy in last:
            copy.wait()


RATES = ((0.03, 0.01), (0.5, 0.01), (0.03, 0.01), (0.02, 0.01), (0.6, 0.0))


def adam_step(weight, first, second, average, gradient, rate, decay):
    first_new = beta_first * first + (1.0 - beta_first) * gradient
    second_new = beta_second * second + (1.0 - beta_second) * gradient * gradient
    first_hat = first_new * (1.0 / (1.0 - beta_first**STEP))
    second_hat = second_new * (1.0 / (1.0 - beta_second**STEP))
    weight_new = weight - rate * (
        first_hat / (jnp.sqrt(second_hat) + adam_epsilon) + decay * weight
    )
    average_new = average_decay * average + (1.0 - average_decay) * weight_new
    return first_new, second_new, weight_new, average_new


def adam_kernel(*refs):
    states = [refs[4 * f:4 * f + 4] for f in range(5)]
    grads = refs[20:25]
    outs = [refs[27 + 5 * f:32 + 5 * f] for f in range(5)]
    (qs, os, ds, gs, qg, og, gg, qb, ob, gb, db, gsems, isems, usems, psems, act, ig) = refs[54:]
    passed = []
    for k, held in enumerate((act, ig)):
        passed.append(pltpu.make_async_copy(refs[25 + k], held, psems.at[k]))
        passed[-1].start()
    width = ob.shape[3]
    for number, target in enumerate((qs, os, gs, ds)):
        pltpu.make_async_copy(grads[number], target, gsems.at[number]).start()
    chunks = []
    for family, held, grad in ((3, db, ds), (2, gb, gg), (1, ob, og), (0, qb, qg)):
        for layer in range(LAYERS):
            for part in range(3 if family == 0 else 1):
                spot = 3 * layer + part if family == 0 else layer
                chunks.append((family, held, grad, layer, part, spot))

    def view(ref, family, layer, part):
        if family:
            return ref.at[layer]
        return ref.at[layer, :, pl.ds(part * width, width)]

    arrivals = []
    for number, (family, held, grad, layer, part, spot) in enumerate(chunks):
        copies = [
            pltpu.make_async_copy(
                view(states[family][k], family, layer, part), held.at[k, spot], isems.at[number, k]
            )
            for k in range(4)
        ]
        for copy in copies:
            copy.start()
        arrivals.append(copies)

    def wait_grad(number, target):
        pltpu.make_async_copy(grads[number], target, gsems.at[number]).wait()

    gain = [ref[...] for ref in states[4]]
    gradient = grads[4][...]
    new = adam_step(*gain, gradient, *RATES[4])
    for ref, value in zip(outs[4], (gradient,) + new):
        ref[...] = value

    for k, held in enumerate((act, ig)):
        passed[k].wait()
        passed[k] = pltpu.make_async_copy(held, refs[52 + k], psems.at[k])
        passed[k].start()
    low = lane_iota((qs.shape[2], TILE)) < HEAD_DIM
    leaving = []
    for number, (family, held, grad, layer, part, spot) in enumerate(chunks):
        first_of = layer == 0 and part == 0
        if family == 3 and first_of:
            wait_grad(3, ds)
        if family == 2:
            if first_of:
                wait_grad(2, gs)
            for half in range(2):
                gg[layer, :, half, :] = gs[layer, :, half * width:(half + 1) * width]
        if family == 1:
            if first_of:
                wait_grad(1, os)
            high, wide = os.shape[2], os.shape[3]
            for side in range(2):
                for core in range(2):
                    og[layer, side * high:(side + 1) * high, core * wide:(core + 1) * wide] = os[
                        layer, 2 * side + core
                    ].astype(f32)
        if family == 0:
            if first_of:
                wait_grad(0, qs)

            def pair(j):
                return qs[layer, j, :, part * TILE:(part + 1) * TILE].astype(f32)

            def last(j, upper):
                tile = 4 if part == 2 else 3
                value = qs[layer, j, :, tile * TILE:(tile + 1) * TILE].astype(f32)
                return value if upper == (part > 0) else pltpu.roll(value, HEAD_DIM, 1)

            for j in (0, 2):
                turned = pltpu.roll(pair(j + 1), HEAD_DIM, 1)
                tiles = (
                    pair(j),
                    jnp.where(low, last(j, False), turned),
                    jnp.where(low, turned, last(j + 1, True)),
                )
                for k, value in enumerate(tiles):
                    start = (3 * (j // 2) + k) * TILE
                    qg[spot, :, start:start + TILE] = value
        for copy in arrivals[number]:
            copy.wait()
        rows = 8

        def body(i, carry, family=family, held=held, grad=grad, spot=spot):
            at = pl.ds(pl.multiple_of(i * rows, rows), rows)
            values = [held[k, spot, at] for k in range(4)]
            first, second, weight, average = adam_step(*values, grad[spot, at], *RATES[family])
            for k, value in enumerate((weight, first, second, average)):
                held[k, spot, at] = value
            return carry

        lax.fori_loop(0, ob.shape[2] // rows, body, 0)
        sources = (grad.at[spot],) + tuple(held.at[k, spot] for k in (1, 2, 0, 3))
        for k, source in enumerate(sources):
            copy = pltpu.make_async_copy(
                source, view(outs[family][k], family, layer, part), usems.at[number, k]
            )
            copy.start()
            leaving.append(copy)
    for copy in leaving + passed:
        copy.wait()


def frequencies():
    half = HEAD_DIM // 2
    freq = rotary_base ** (-2.0 * np.arange(half) / HEAD_DIM)
    return jnp.asarray(np.tile(freq, (8, 4)).astype(np.float32))


def own_projection(weight, me):
    layers, rows, _ = weight.shape
    split = weight.reshape(layers, rows, 3, HEADS * HEAD_DIM)
    own = lax.dynamic_slice_in_dim(split, me * OWN_HEADS * HEAD_DIM, OWN_HEADS * HEAD_DIM, 3)
    own = own.astype(bf16)
    pairs = own[..., :TILE].reshape(layers, rows, 3 * TILE)
    last = own[..., TILE:]
    return jnp.concatenate(
        [pairs, last[:, :, 0], last[:, :, 1], jnp.zeros_like(last[:, :, 0]), last[:, :, 2]], axis=-1
    )


def whole_projection(grad):
    group, layers, rows, _ = grad.shape
    pairs = grad[..., :3 * TILE].reshape(group, layers, rows, 3, TILE)
    last = jnp.stack(
        [
            grad[..., 3 * TILE:3 * TILE + HEAD_DIM],
            grad[..., 3 * TILE + HEAD_DIM:4 * TILE],
            grad[..., 4 * TILE + HEAD_DIM:],
        ],
        axis=3,
    )
    full = jnp.concatenate([pairs, last], axis=-1)
    return full.transpose(1, 2, 3, 0, 4).reshape(layers, rows, 3 * HEADS * HEAD_DIM)


def run_forward(spreading, tokens, weights, gain, lengths, mask_row):
    size, feats = tokens.shape
    seq = size * GROUP
    ff = weights[3].shape[2]
    own = weights[0].shape[1]
    shapes = dict(
        act=((size, feats), bf16),
        xf=((LAYERS, seq, feats), bf16),
        qkv=((LAYERS, seq, PROJ), bf16),
        lse=((LAYERS, 8, seq), f32),
        att=((LAYERS, feats, seq), bf16),
        flow=((LAYERS, seq, feats), bf16),
        gu=((LAYERS, seq, 2 * ff), bf16),
        hid=((LAYERS, seq, ff), bf16),
        n1=((LAYERS, size, feats), f32),
        s1=((LAYERS, size, 128), f32),
        n2=((LAYERS, size, feats), f32),
        s2=((LAYERS, size, 128), f32),
        wq=((LAYERS, feats, PROJ), bf16),
        wo=((LAYERS, feats, feats), bf16),
        wg=((LAYERS, feats, 2 * ff), bf16),
        wd=((LAYERS, feats, ff), bf16),
        gain=((8, feats), f32),
        cos_rows=((seq, 128), f32),
        sin_rows=((seq, 128), f32),
        doc_keys=((seq, 128), jnp.int32),
        doc_queries=((8, seq), jnp.int32),
    )
    held = {name: pltpu.VMEM(*shape) for name, shape in shapes.items()}
    scratch = [held[n] for n in ("wq", "wo", "wg", "wd", "xf", "qkv", "att", "flow", "gu", "hid")]
    scratch += [
        pltpu.VMEM((seq, seq), f32),
        pltpu.VMEM((2, TILE, seq), bf16),
        pltpu.VMEM((seq, TILE), bf16),
        held["lse"],
    ]
    scratch += [held[n] for n in ("n1", "s1", "n2", "s2")]
    scratch += [
        pltpu.VMEM((size, feats), f32),
        held["act"],
        pltpu.VMEM((LAYERS, 3, size, feats), bf16),
        pltpu.VMEM((LAYERS, 3, size, feats), bf16),
        pltpu.SemaphoreType.DMA((2, LAYERS, 18)),
        pltpu.SemaphoreType.DMA((LAYERS, PIECES)),
        pltpu.SemaphoreType.DMA((LAYERS, 16)),
        pltpu.SemaphoreType.DMA((2, PIECES * LAYERS, 3 + 2 * DEPTH)),
        pltpu.SemaphoreType.DMA((2, LAYERS, 14)),
        pltpu.VMEM((2, 8, feats), f32),
        pltpu.VMEM((DEPTH, 8, feats), f32),
        pltpu.SemaphoreType.DMA((2, 1, DEPTH)),
    ]
    if spreading:
        scratch += [
            pltpu.VMEM((LAYERS, own, feats), bf16),
            pltpu.VMEM((LAYERS, own, 2 * ff), bf16),
            pltpu.VMEM((LAYERS, own, ff), bf16),
        ]
    return pl.pallas_call(
        functools.partial(forward_kernel, spreading),
        out_shape=[jax.ShapeDtypeStruct(*shape) for shape in shapes.values()],
        in_specs=[VMEM, ANY] + [VMEM if spreading else ANY] * 3
        + [VMEM, pl.BlockSpec(memory_space=pltpu.SMEM), VMEM, VMEM],
        out_specs=[ANY] * (len(shapes) - 5) + [VMEM] * 5,
        scratch_shapes=scratch,
        compiler_params=pltpu.CompilerParams(
            collective_id=0, has_side_effects=True, vmem_limit_bytes=VMEM_LIMIT
        ),
        cost_estimate=pl.CostEstimate(
            flops=12 * 10**9, bytes_accessed=60 * 10**6, transcendentals=10**7
        ),
        name="forward",
    )(tokens, *weights, gain, lengths, mask_row, frequencies())


def run_backward(spreading, cotangent, kept, weights, gain, tables):
    size, feats = cotangent.shape
    seq = size * GROUP
    xf, qkv, lse, att, flow, gu, hid, n1, s1, n2, s2 = kept
    ff = hid.shape[2]
    wq, wo, wg, wd = weights
    loaded = [n1, s1, n2, s2, xf, qkv, lse, att, flow, gu, hid, wq, wo, wg, wd]
    own = feats // (2 * DEPTH)
    half = feats // 2
    widths = dict(d=ff, g=ff, u=ff, a=3 * TILE, b=2 * TILE, o=half)
    if spreading:
        outs = dict(
            ig_out=((size, feats), f32),
            q_out=((LAYERS, GROUP, own, PROJ), bf16),
            o_out=((LAYERS, GROUP, own // 2, half), bf16),
            d_res=((LAYERS, own, ff), f32),
            g_res=((LAYERS, own, 2 * ff), f32),
            gain_out=((8, feats), f32),
        )
    else:
        outs = dict(
            ig_out=((size, feats), f32),
            q_out=(wq.shape, bf16),
            o_out=((LAYERS, feats, half), bf16),
            d_out=(wd.shape, bf16),
            g_out=(wg.shape, bf16),
            gain_out=((8, feats), f32),
        )
    names = ["cot"] + [n + "_in" for n in BACK_LOADED] + list(BACK_TABLES) + list(outs)
    scratch = dict(
        bias=pltpu.VMEM((seq, seq), f32),
        dff=pltpu.VMEM((1, seq, feats), bf16),
        dbr=pltpu.VMEM((LAYERS, seq, feats), bf16),
        datt=pltpu.VMEM((seq, 2 * TILE), bf16),
        dproj=pltpu.VMEM((seq, PROJ), bf16),
        dk=pltpu.VMEM((2, seq, TILE), f32),
        dv=pltpu.VMEM((2, seq, TILE), f32),
        dqt=pltpu.VMEM((2, TILE, seq), f32),
        kt=pltpu.VMEM((2, TILE, seq), bf16),
        k2=pltpu.VMEM((seq, TILE), bf16),
        grad=pltpu.VMEM((size, feats), f32),
        part=pltpu.VMEM((2, 3, size, feats), bf16),
        got=pltpu.VMEM((2, 3, size, feats), bf16),
        gq=pltpu.VMEM((feats, PROJ), bf16),
        go=pltpu.VMEM((feats, half), bf16),
        gg=pltpu.VMEM((feats, 2 * ff), bf16),
        gd=pltpu.VMEM((feats, ff), bf16),
        sems=pltpu.SemaphoreType.DMA((2, 2 * LAYERS, 24)),
        lsems=pltpu.SemaphoreType.DMA((len(loaded),)),
        osems=pltpu.SemaphoreType.DMA((LAYERS, 5)),
        rows=pltpu.VMEM((seq, feats), bf16),
    )
    for name, array in zip(BACK_LOADED, loaded):
        if name not in ("xf", "flow"):
            scratch[name] = pltpu.VMEM(array.shape[1:], array.dtype)
    if spreading:
        scratch.update(
            gsum=pltpu.VMEM((8, feats), f32),
            gpack=pltpu.VMEM((GROUP, 8, feats), f32),
            gside=pltpu.VMEM((2, 8, feats), f32),
            gdeep=pltpu.VMEM((DEPTH, 8, feats), f32),
            gsems=pltpu.SemaphoreType.DMA((2, 1, 7)),
            csems=pltpu.SemaphoreType.REGULAR((2, 6)),
            ashare=pltpu.VMEM((LAYERS, GROUP, own, 3 * TILE), bf16),
            bshare=pltpu.VMEM((LAYERS, GROUP, own, 2 * TILE), bf16),
            oshare=pltpu.VMEM((LAYERS, GROUP, own // 2, half), bf16),
            dsems=pltpu.SemaphoreType.DMA((2, 6 * LAYERS, 7)),
        )
        for name, width in widths.items():
            high = own // 2 if name == "o" else own
            scratch["near_" + name] = pltpu.VMEM((DEPTH, high, width), bf16)
            scratch["apart_" + name] = pltpu.VMEM((DEPTH - 1, high, width), bf16)
            scratch["sum_" + name] = pltpu.VMEM((high, width), f32)
    in_vmem = ("d_res", "g_res", "gain_out")
    return pl.pallas_call(
        functools.partial(backward_kernel, spreading, tuple(names + list(scratch))),
        out_shape=[jax.ShapeDtypeStruct(*shape) for shape in outs.values()],
        in_specs=[VMEM] + [ANY] * 15 + [VMEM] * 5,
        out_specs=[VMEM if name in in_vmem else ANY for name in outs],
        scratch_shapes=list(scratch.values()),
        compiler_params=pltpu.CompilerParams(
            collective_id=1, has_side_effects=True, vmem_limit_bytes=VMEM_LIMIT
        ),
        cost_estimate=pl.CostEstimate(
            flops=24 * 10**9, bytes_accessed=60 * 10**6, transcendentals=10**7
        ),
        name="backward",
    )(cotangent, *loaded, gain, *tables)


def run_adam(states, grads, rows):
    outs = []
    for family in range(5):
        shape = jax.ShapeDtypeStruct(states[4 * family].shape, f32)
        outs += [shape] * 5
    outs += [jax.ShapeDtypeStruct(a.shape, a.dtype) for a in rows]
    layers, own, _, width = states[8].shape
    scratch = [
        pltpu.VMEM(grads[0].shape, bf16),
        pltpu.VMEM(grads[1].shape, bf16),
        pltpu.VMEM(grads[3].shape, f32),
        pltpu.VMEM(grads[2].shape, f32),
        pltpu.VMEM((3 * layers, own, width), f32),
        pltpu.VMEM((layers, own, width), f32),
        pltpu.VMEM((layers, own, 2, width), f32),
        pltpu.VMEM((4, 3 * layers, own, width), f32),
        pltpu.VMEM((4, layers, own, width), f32),
        pltpu.VMEM((4, layers, own, 2, width), f32),
        pltpu.VMEM((4, layers, own, width), f32),
        pltpu.SemaphoreType.DMA((4,)),
        pltpu.SemaphoreType.DMA((6 * layers, 4)),
        pltpu.SemaphoreType.DMA((6 * layers, 5)),
        pltpu.SemaphoreType.DMA((2,)),
    ]
    scratch += [pltpu.VMEM(a.shape, a.dtype) for a in rows]
    return pl.pallas_call(
        adam_kernel,
        out_shape=outs,
        in_specs=[ANY] * 16 + [VMEM] * 4 + [ANY] * 4 + [VMEM] + [ANY] * 2,
        out_specs=[ANY] * 20 + [VMEM] * 5 + [ANY] * 2,
        scratch_shapes=scratch,
        compiler_params=pltpu.CompilerParams(vmem_limit_bytes=VMEM_LIMIT),
        cost_estimate=pl.CostEstimate(
            flops=2 * 10**7, bytes_accessed=37 * 10**6, transcendentals=10**6
        ),
        name="adam",
    )(*states, *grads, *rows)


def adamw(weight, first, second, average, gradient, rate, decay):
    first_new = beta_first * first + (1.0 - beta_first) * gradient
    second_new = beta_second * second + (1.0 - beta_second) * gradient * gradient
    first_hat = first_new / (1.0 - beta_first**STEP)
    second_hat = second_new / (1.0 - beta_second**STEP)
    weight_new = weight - rate * (
        first_hat / (jnp.sqrt(second_hat) + adam_epsilon) + decay * weight
    )
    average_new = average_decay * average + (1.0 - average_decay) * weight_new
    return (gradient, first_new, second_new, weight_new, average_new)


def shards(
    spreading,
    tokens,
    cotangent,
    lengths,
    key_mask,
    qkv_weight,
    qkv_first,
    qkv_second,
    qkv_average,
    out_weight,
    out_first,
    out_second,
    out_average,
    gate_up_weight,
    gate_up_first,
    gate_up_second,
    gate_up_average,
    down_weight,
    down_first,
    down_second,
    down_average,
    norm_gain,
    gain_first,
    gain_second,
    gain_average,
):
    me = lax.axis_index("mp")
    own = gate_up_weight.shape[1]
    ff = gate_up_weight.shape[3]
    feats = tokens.shape[1]
    if spreading:
        gain = jnp.zeros((8, feats), f32)
        gain = lax.dynamic_update_slice(
            gain, norm_gain.reshape(2 * LAYERS, own), (0, lax.axis_index("dp") * own)
        )
    else:
        gain = lax.all_gather(norm_gain, "dp", axis=2, tiled=True).reshape(2 * LAYERS, feats)
        gain = jnp.concatenate([gain, jnp.zeros((8 - 2 * LAYERS, feats), f32)], axis=0)
    if spreading:
        owned = (own_projection(qkv_weight, me), out_weight, gate_up_weight, down_weight)
    else:
        owned = (
            own_projection(qkv_weight, me),
            out_weight.astype(bf16),
            gate_up_weight.reshape(LAYERS, own, 2 * ff).astype(bf16),
            down_weight.astype(bf16),
        )
        owned = [lax.all_gather(w, "dp", axis=1, tiled=True) for w in owned]
    act, *kept = run_forward(spreading, tokens, owned, gain, lengths, key_mask[None, :])
    weights, gain, tables, kept = kept[-9:-5], kept[-5], kept[-4:], kept[:-9]
    backward = run_backward(spreading, cotangent, kept, weights, gain, tables)
    if spreading:
        input_grad, gq, go, gd, gg, gain_sum = backward
        gain_grad = lax.dynamic_slice_in_dim(
            gain_sum[:2 * LAYERS].reshape(LAYERS, 2, -1), lax.axis_index("dp") * own, own, 2
        )
        states = (
            qkv_weight, qkv_first, qkv_second, qkv_average,
            out_weight, out_first, out_second, out_average,
            gate_up_weight, gate_up_first, gate_up_second, gate_up_average,
            down_weight, down_first, down_second, down_average,
            norm_gain, gain_first, gain_second, gain_average,
        )
        grads = (gq, go, gg, gd, gain_grad)
        *results, act, input_grad = run_adam(states, grads, (act, input_grad))
        return (act, input_grad, *results)
    else:
        input_grad, gq, go, gd, gg, gain_sum = backward
        gq, go, gg, gd = [
            lax.psum_scatter(g, "dp", scatter_dimension=1, tiled=True) for g in (gq, go, gg, gd)
        ]
        gq, go = lax.all_gather(gq, "mp"), lax.all_gather(go, "mp")
        gain_part = gain_sum[:2 * LAYERS].reshape(LAYERS, 2, -1)
        gain_grad = lax.psum_scatter(
            lax.psum(gain_part, "mp"), "dp", scatter_dimension=2, tiled=True
        )
    qkv_grad = whole_projection(gq.astype(f32))
    out_grad = jnp.concatenate([go[0], go[1]], axis=-1).astype(f32)
    gate_up_grad = gg.reshape(LAYERS, own, 2, ff).astype(f32)
    down_grad = gd.astype(f32)
    results = [act, input_grad]
    results.extend(adamw(qkv_weight, qkv_first, qkv_second, qkv_average, qkv_grad, 0.03, 0.01))
    results.extend(adamw(out_weight, out_first, out_second, out_average, out_grad, 0.5, 0.01))
    results.extend(
        adamw(
            gate_up_weight, gate_up_first, gate_up_second, gate_up_average, gate_up_grad, 0.03, 0.01
        )
    )
    results.extend(
        adamw(down_weight, down_first, down_second, down_average, down_grad, 0.02, 0.01)
    )
    results.extend(adamw(norm_gain, gain_first, gain_second, gain_average, gain_grad, 0.6, 0.0))
    return tuple(results)


def solution(mesh):
    spreading = mesh.shape["dp"] == 2 * DEPTH
    return jax.shard_map(
        functools.partial(shards, spreading),
        mesh=mesh,
        in_specs=(
            P(("dp", "mp"), None),
            P(("dp", "mp"), None),
            P("dp", None),
            P("dp"),
            P(None, "dp", None),
            P(None, "dp", None),
            P(None, "dp", None),
            P(None, "dp", None),
            P(None, "dp", None),
            P(None, "dp", None),
            P(None, "dp", None),
            P(None, "dp", None),
            P(None, "dp", None, "mp"),
            P(None, "dp", None, "mp"),
            P(None, "dp", None, "mp"),
            P(None, "dp", None, "mp"),
            P(None, "dp", "mp"),
            P(None, "dp", "mp"),
            P(None, "dp", "mp"),
            P(None, "dp", "mp"),
            P(None, None, "dp"),
            P(None, None, "dp"),
            P(None, None, "dp"),
            P(None, None, "dp"),
        ),
        out_specs=(
            P(("dp", "mp"), None),
            P(("dp", "mp"), None),
            P(None, "dp", None),
            P(None, "dp", None),
            P(None, "dp", None),
            P(None, "dp", None),
            P(None, "dp", None),
            P(None, "dp", None),
            P(None, "dp", None),
            P(None, "dp", None),
            P(None, "dp", None),
            P(None, "dp", None),
            P(None, "dp", None, "mp"),
            P(None, "dp", None, "mp"),
            P(None, "dp", None, "mp"),
            P(None, "dp", None, "mp"),
            P(None, "dp", None, "mp"),
            P(None, "dp", "mp"),
            P(None, "dp", "mp"),
            P(None, "dp", "mp"),
            P(None, "dp", "mp"),
            P(None, "dp", "mp"),
            P(None, None, "dp"),
            P(None, None, "dp"),
            P(None, None, "dp"),
            P(None, None, "dp"),
            P(None, None, "dp"),
        ),
        check_vma=False,
    )
```
